128 devices in a mesh: dp: 4 (over z), ctx: 8 (over x, core), tensor: 4 (over y).
Axes of the slice: x: 4, y: 4, z: 4, core: 2. Of those that a mesh axis runs over, the one named last changes fastest.
Arguments:
- inputs: float32 [16, 1024, 1024], P('dp', 'ctx'), may hold values from -6 to 6
- segments: int32 [16, 1024], P('dp', 'ctx'), may hold values from 0 to 1023, as said below
- attn_gain: float32 [2, 1024], replicated, may hold values from 0.5 to 1.5
- attn_shift: float32 [2, 1024], replicated, may hold values from -2.5 to 2.5
- mlp_gain: float32 [2, 1024], replicated, may hold values from 0.5 to 1.5
- mlp_shift: float32 [2, 1024], replicated, may hold values from -2.5 to 2.5
- qkv_weight: bfloat16 [2, 3, 1024, 1024], P(None, None, None, 'tensor'), may hold values from -0.1875 to 0.1875
- qkv_bias: float32 [2, 3, 1024], P(None, None, 'tensor'), may hold values from -2.5 to 2.5
- out_weight: bfloat16 [2, 1024, 1024], P(None, 'tensor'), may hold values from -0.75 to 0.75
- out_bias: float32 [2, 1024], replicated, may hold values from -2.5 to 2.5
- up_weight: bfloat16 [2, 1024, 4096], P(None, None, 'tensor'), may hold values from -0.1875 to 0.1875
- up_bias: float32 [2, 4096], P(None, 'tensor'), may hold values from -2.5 to 2.5
- down_weight: bfloat16 [2, 4096, 1024], P(None, 'tensor'), may hold values from -0.09375 to 0.09375
- down_bias: float32 [2, 1024], replicated, may hold values from -2.5 to 2.5
- cotangent: float32 [16, 1024, 1024], P('dp', 'ctx'), may hold values from -6 to 6
Outputs:
- output: float32 [16, 1024, 1024], P('dp', 'ctx')
- input_grad: float32 [16, 1024, 1024], P('dp', 'ctx')
- attn_gain_grad: float32 [2, 1024], replicated
- attn_shift_grad: float32 [2, 1024], replicated
- mlp_gain_grad: float32 [2, 1024], replicated
- mlp_shift_grad: float32 [2, 1024], replicated
- qkv_weight_grad: float32 [2, 3, 1024, 1024], P(None, None, None, 'tensor')
- qkv_bias_grad: float32 [2, 3, 1024], P(None, None, 'tensor')
- out_weight_grad: float32 [2, 1024, 1024], P(None, 'tensor')
- out_bias_grad: float32 [2, 1024], replicated
- up_weight_grad: float32 [2, 1024, 4096], P(None, None, 'tensor')
- up_bias_grad: float32 [2, 4096], P(None, 'tensor')
- down_weight_grad: float32 [2, 4096, 1024], P(None, 'tensor')
- down_bias_grad: float32 [2, 1024], replicated
The draws below stay inside these ranges and needn't reach their ends.
Inputs may be any that keep to these rules, and one draw needn't show every extreme that they name: `segments`: each entry is the place, within its sequence, of the first token of that token's document, so it never falls along a sequence and is at most the token's own place; in one sequence of each index of dp the last token begins a document of its own.
All inputs are finite; a program needn't handle non-finite values.
Results may differ from the reference program's by a relative error of at most 0.033.
Values may be sent and summed in bfloat16 or wider, within the bound.
No kernel may reach another device: no remote copies, remote signals or barrier semaphores. Data moves between devices by JAX's collectives and lax.ppermute only.
A program may use at most 192 MiB of HBM per device.

```python
import jax
import jax.numpy as jnp
from jax import lax

D = 1024
HEADS = 16
HEAD = 64
ROT = 16
FF = 4096
LAYERS = 2
LENGTH = 1024
SEQS = 4
HD = 1024
BATCH = 16
BLOCK = 128
N_DP = 4


def draw_segments(key, part):
    key = jax.random.fold_in(key, 7)
    keys_split = jax.random.split(key, 4)
    places = jnp.arange(LENGTH, dtype=jnp.int32)
    shortest = max(LENGTH // 16, 2)
    count_docs = LENGTH // shortest + 1
    lengths = jax.random.randint(keys_split[0], (BATCH, count_docs), shortest, LENGTH // 2 + 1)
    starts = jnp.cumsum(lengths, axis=1) - lengths
    regular = jnp.max(jnp.where(starts[:, None, :] <= places[None, :, None], starts[:, None, :], 0), axis=2)
    span_begin = jax.random.randint(keys_split[1], (BATCH, 1), 1, BLOCK)
    span_end = jax.random.randint(keys_split[2], (BATCH, 1), LENGTH - BLOCK + 1, LENGTH + 1)
    offsets = jnp.clip(places[None, :] - span_end, 0, LENGTH - 1)
    shifted = jnp.take_along_axis(regular, offsets, axis=1) + span_end
    spanning = jnp.where(places[None, :] < span_begin, 0, jnp.where(places[None, :] < span_end, span_begin, shifted))
    spanning = jnp.where(places[None, :] == LENGTH - 1, LENGTH - 1, spanning)
    chosen = jax.random.randint(keys_split[3], (N_DP, 1), 0, SEQS)
    picked = (jnp.arange(SEQS, dtype=jnp.int32)[None, :] == chosen).reshape(BATCH, 1)
    return jnp.where(picked, spanning, regular).astype(jnp.int32)


def block_scale(stream_key, extent, cuts, smallest, largest):
    def one(position, parts):
        heights = jax.random.uniform(jax.random.fold_in(jax.random.fold_in(stream_key, 6), position), (parts,), jnp.float32, smallest / len(cuts), largest / len(cuts))
        return jnp.repeat(jnp.exp(heights), extent[position] // parts).reshape((-1,) + (1,) * (len(extent) - position - 1))

    loudness = one(*cuts[0])
    for cut in cuts[1:]:
        loudness = loudness * one(*cut)
    return loudness


def noise(stream_key, extent, deviation, bound, cuts=(), kind=jnp.bfloat16):
    array = jax.random.normal(stream_key, extent, jnp.float32) * deviation
    if len(cuts) > 0:
        array = block_scale(stream_key, extent, cuts, -0.22, 0.18) * array
    return jnp.clip(array, min=-bound, max=bound).astype(kind)


def setup_inputs(seed: int = 0) -> dict:
    key_list = jax.random.split(jax.random.key(seed), 16)
    return {
        "inputs": noise(key_list[0], (BATCH, LENGTH, D), 1.0, 6.0, ((0, 4), (1, 8)), jnp.float32),
        "segments": draw_segments(jax.random.fold_in(key_list[15], 71), 0),
        "attn_gain": jnp.clip(1.0 + 0.1 * jax.random.normal(key_list[2], (LAYERS, D), jnp.float32), 0.5, 1.5),
        "attn_shift": noise(key_list[3], (LAYERS, D), 0.3, 2.5, (), jnp.float32),
        "mlp_gain": jnp.clip(1.0 + 0.1 * jax.random.normal(key_list[4], (LAYERS, D), jnp.float32), 0.5, 1.5),
        "mlp_shift": noise(key_list[5], (LAYERS, D), 0.3, 2.5, (), jnp.float32),
        "qkv_weight": noise(key_list[6], (LAYERS, 3, D, HD), D ** -0.5, 0.1875, ((3, 4),)),
        "qkv_bias": noise(key_list[7], (LAYERS, 3, HD), 0.3, 2.5, ((2, 4),), jnp.float32),
        "out_weight": noise(key_list[8], (LAYERS, HD, D), (HD // 16) ** -0.5, 0.75, ((1, 4),)),
        "out_bias": noise(key_list[9], (LAYERS, D), 0.3, 2.5, (), jnp.float32),
        "up_weight": noise(key_list[10], (LAYERS, D, FF), D ** -0.5, 0.1875, ((2, 4),)),
        "up_bias": noise(key_list[11], (LAYERS, FF), 0.3, 2.5, ((1, 4),), jnp.float32),
        "down_weight": noise(key_list[12], (LAYERS, FF, D), FF ** -0.5, 0.09375, ((1, 4),)),
        "down_bias": noise(key_list[13], (LAYERS, D), 0.3, 2.5, (), jnp.float32),
        "cotangent": noise(key_list[14], (BATCH, LENGTH, D), 1.0, 6.0, ((0, 4), (1, 8)), jnp.float32),
    }


@jax.custom_vjp
def low(v):
    return lax.optimization_barrier(v.astype(jnp.bfloat16)).astype(jnp.float32)

@jax.custom_vjp
def low_back(v):
    return v

def low_keep(v):
    return (low(v), None)

def low_pass(kept, grad):
    return (grad,)

def back_keep(v):
    return (v, None)

def back_low(kept, grad):
    return (low(grad),)
low.defvjp(low_keep, low_pass)
low_back.defvjp(back_keep, back_low)

def layer_norm(values, gain_row, shift_row):
    average = lax.optimization_barrier(jnp.mean(values, axis=-1, keepdims=True))
    centred = values - average
    spread = lax.optimization_barrier(jnp.mean(centred * centred, axis=-1, keepdims=True))
    return centred * lax.rsqrt(spread + 1e-05) * gain_row + shift_row

def turn_half(values):
    return jnp.concatenate([-values[..., ROT // 2:ROT], values[..., :ROT // 2], values[..., ROT:]], axis=-1)

def rotary_tables(places):
    frequency = 10000.0 ** (-2.0 * jnp.arange(ROT // 2, dtype=jnp.float32) / ROT)
    angles = places[..., None] * frequency
    padding = jnp.ones(places.shape + (HEAD - ROT,), jnp.float32)
    cos_table = jnp.concatenate([jnp.cos(angles), jnp.cos(angles), padding], axis=-1)
    sin_table = jnp.concatenate([jnp.sin(angles), jnp.sin(angles), 0.0 * padding], axis=-1)
    return (cos_table, sin_table)

def attend(packed):
    queries, key_rows, value_rows, starts = packed
    scores = jnp.einsum('qhe,khe->hqk', queries, key_rows, precision=lax.Precision.HIGHEST) * HEAD ** (-0.5)
    scores = low_back(scores)
    places = jnp.arange(LENGTH, dtype=jnp.int32)
    allowed = (places[None, :] <= places[:, None]) & (places[None, :] >= starts[:, None])
    scores = jnp.where(allowed[None], scores, -1e+30)
    weights = low(jax.nn.softmax(scores, axis=-1))
    return jnp.einsum('hqk,khe->qhe', weights, value_rows, precision=lax.Precision.HIGHEST)

def layer_block(stream, segments, layer_index, params):
    attn_gain, attn_shift, mlp_gain, mlp_shift, qkv_weight, qkv_bias, out_weight, out_bias, up_weight, up_bias, down_weight, down_bias = params
    attn_in = low(layer_norm(stream, attn_gain[layer_index], attn_shift[layer_index]))
    mlp_in = low(layer_norm(stream, mlp_gain[layer_index], mlp_shift[layer_index]))
    projected = jnp.einsum('bld,jde->jble', attn_in, qkv_weight[layer_index], precision=lax.Precision.HIGHEST)
    projected = low_back(projected) + qkv_bias[layer_index][:, None, None, :]
    projected = projected.reshape(3, BATCH, LENGTH, HEADS, HEAD)
    places = (jnp.arange(LENGTH, dtype=jnp.int32)[None, :] - segments).astype(jnp.float32)
    cos_table, sin_table = rotary_tables(places)
    cos_table = cos_table[:, :, None, :]
    sin_table = sin_table[:, :, None, :]
    queries = low(projected[0] * cos_table + turn_half(projected[0]) * sin_table)
    key_rows = low(projected[1] * cos_table + turn_half(projected[1]) * sin_table)
    value_rows = low(projected[2])
    attended = lax.map(jax.checkpoint(attend), (queries, key_rows, value_rows, segments))
    attended = low(low_back(attended.reshape(BATCH, LENGTH, HD)))
    attn_out = low_back(jnp.einsum('ble,ed->bld', attended, out_weight[layer_index], precision=lax.Precision.HIGHEST)) + out_bias[layer_index]
    hidden = low_back(jnp.einsum('bld,df->blf', mlp_in, up_weight[layer_index], precision=lax.Precision.HIGHEST)) + up_bias[layer_index]
    active = low(jax.nn.gelu(hidden, approximate=False))
    mlp_out = low_back(jnp.einsum('blf,fd->bld', active, down_weight[layer_index], precision=lax.Precision.HIGHEST)) + down_bias[layer_index]
    return stream + attn_out + mlp_out

def forward(stream, segments, params):
    for layer_index in range(LAYERS):
        stream = layer_block(stream, segments, layer_index, params)
    return stream

def reference(inputs, segments, attn_gain, attn_shift, mlp_gain, mlp_shift, qkv_weight, qkv_bias, out_weight, out_bias, up_weight, up_bias, down_weight, down_bias, cotangent):
    params = tuple((member.astype(jnp.float32) for member in (attn_gain, attn_shift, mlp_gain, mlp_shift, qkv_weight, qkv_bias, out_weight, out_bias, up_weight, up_bias, down_weight, down_bias)))

    def whole(stream, weights):
        return forward(stream, segments, weights)
    output, pullback = jax.vjp(whole, inputs.astype(jnp.float32), params)
    input_grad, gradients = pullback(cotangent.astype(jnp.float32))
    g_attn_gain, g_attn_shift, g_mlp_gain, g_mlp_shift, g_qkv_weight, g_qkv_bias, g_out_weight, g_out_bias, g_up_weight, g_up_bias, g_down_weight, g_down_bias = gradients
    return (output, input_grad, g_attn_gain, g_attn_shift, g_mlp_gain, g_mlp_shift, g_qkv_weight, g_qkv_bias, g_out_weight, g_out_bias, g_up_weight, g_up_bias, g_down_weight, g_down_bias)
```

```python
import functools

import jax
import jax.numpy as jnp
from jax import lax
from jax.experimental import pallas as pl
from jax.experimental.pallas import tpu as pltpu
from jax.sharding import PartitionSpec as P

HEAD = 64
ROT = 16
LAYERS = 2
LANES = 128
F32 = jnp.float32
BF16 = jnp.bfloat16


def shape_of(shape, dtype):
    return jax.ShapeDtypeStruct(tuple(shape), dtype)


def whole(array):
    rank = array.ndim
    return pl.BlockSpec(array.shape, lambda i, *_: (0,) * rank)


def layer_spec(array, layer):
    rank = array.ndim
    return pl.BlockSpec((1,) + array.shape[1:], lambda i, *_: (layer,) + (0,) * (rank - 1))


def run(body, me, operands, outs, scratch=(), name=None, limit=32, out_specs=None, aliases=None):
    arrays, specs = [], []
    for operand in operands:
        array, spec = operand if isinstance(operand, tuple) else (operand, None)
        arrays.append(array)
        specs.append(whole(array) if spec is None else spec)
    return pl.pallas_call(
        body,
        grid_spec=pltpu.PrefetchScalarGridSpec(
            num_scalar_prefetch=1,
            grid=(1,),
            in_specs=specs,
            out_specs=[whole(o) for o in outs] if out_specs is None else out_specs,
            scratch_shapes=list(scratch),
        ),
        out_shape=list(outs),
        input_output_aliases=aliases or {},
        compiler_params=pltpu.CompilerParams(vmem_limit_bytes=limit * 1024 * 1024),
        cost_estimate=pl.CostEstimate(flops=1, bytes_accessed=1, transcendentals=0),
        name=name,
    )(me, *arrays)


def matmul(left, right):
    return jnp.dot(left, right, preferred_element_type=F32)


def matmul_nt(left, right):
    return lax.dot_general(left, right, (((1,), (1,)), ((), ())), preferred_element_type=F32)


def matmul_tn(left, right):
    return lax.dot_general(left, right, (((0,), (0,)), ((), ())), preferred_element_type=F32)


def normalize(values):
    average = jnp.mean(values, axis=-1, keepdims=True)
    centred = values - average
    factor = lax.rsqrt(jnp.mean(centred * centred, axis=-1, keepdims=True) + 1e-05)
    return centred * factor, factor


def wrap4(value):
    return lax.rem(value + 4, 4)


def rows(index, size):
    return pl.ds(pl.multiple_of(index * size, size), size)


def rotary_rows(place_row):
    count = place_row.shape[1]
    which = lax.broadcasted_iota(jnp.int32, (8, count), 0)
    frequency = jnp.zeros((8, count), F32)
    for index in range(8):
        frequency = jnp.where(which == index, 10000.0 ** (-2.0 * index / ROT), frequency)
    angles = frequency * place_row
    trig = jnp.concatenate([jnp.cos(angles), jnp.sin(angles)], axis=0)
    row = lax.broadcasted_iota(jnp.int32, (16, LANES), 0)
    lane = lax.broadcasted_iota(jnp.int32, (16, LANES), 1) & (HEAD - 1)
    same = (lane & 7) == (row & 7)
    is_cos = row < 8
    pick_cos = jnp.where(is_cos & same & (lane < 16), 1.0, 0.0)
    pick_low = jnp.where((row >= 8) & same & (lane < 8), 1.0, 0.0)
    pick_high = jnp.where((row >= 8) & same & (lane >= 8) & (lane < 16), 1.0, 0.0)
    picks = jnp.concatenate([pick_cos, pick_low, pick_high], axis=1).astype(F32)
    spread = lax.dot_general(
        trig, picks, (((0,), (0,)), ((), ())), preferred_element_type=F32, precision=lax.Precision.HIGHEST
    )
    lane_row = lax.broadcasted_iota(jnp.int32, (1, LANES), 1) & (HEAD - 1)
    cos_table = spread[:, :LANES] + jnp.where(lane_row >= ROT, 1.0, 0.0)
    return cos_table, spread[:, LANES : 2 * LANES], spread[:, 2 * LANES :]


def rotate(values, tables, back=False):
    cos_table, low_sin, high_sin = tables
    below = pltpu.roll(values, LANES - ROT // 2, 1) * low_sin
    above = pltpu.roll(values, ROT // 2, 1) * high_sin
    turned = below - above if back else above - below
    return values * cos_table + turned


def project_rows(layer, tok_shape, me_ref, seg_ref, weight, bias, a_ref, p_refs, proj_ref, with_seg):
    seq_count, block_len, width = tok_shape
    chip, core = me_ref[0], me_ref[1]
    base = (chip * 2 + core) * block_len
    for j in range(3):
        proj_ref[:, j * 2 * LANES : (j + 1) * 2 * LANES] = matmul(a_ref[...], weight(j)) + bias[j : j + 1, :]
    for k in range(4):
        seq = wrap4(chip + k)
        place = rows(seq, block_len)
        seg_row = seg_ref[pl.ds(seq, 1), :]
        spots = lax.broadcasted_iota(jnp.int32, (1, block_len), 1) + base
        tables = rotary_rows((spots - seg_row).astype(F32))
        for j in range(3):
            for pair in range(2):
                at = (2 * j + pair) * LANES
                part = proj_ref[place, at : at + LANES]
                if j < 2:
                    part = rotate(part, tables)
                p_refs[k][pair, 0:block_len, j * LANES : (j + 1) * LANES] = part.astype(BF16)
        if with_seg:
            coded = seg_row.astype(F32)
            high = jnp.floor(coded * 0.125)
            packed = jnp.concatenate([high, coded - 8.0 * high, jnp.zeros_like(high)], axis=1)
            packed = jnp.broadcast_to(packed, (16, 3 * LANES)).astype(BF16)
            for pair in range(2):
                p_refs[k][pair, block_len : block_len + 16, :] = packed


def project_first_body(tok_shape, me_ref, *refs):
    seq_count, block_len, width = tok_shape
    in_refs, refs = refs[:8], refs[8:]
    a_ref, m_ref, *p_refs = refs[:6]
    proj_ref, *held, sems = refs[6:]
    x_ref, seg_ref, ag_ref, as_ref, mg_ref, ms_ref, w_ref, b_ref = held
    copies = []
    for index in (1, 2, 3, 4, 5):
        copies.append(pltpu.make_async_copy(in_refs[index], held[index], sems.at[len(copies)]))
    copies.append(pltpu.make_async_copy(in_refs[7].at[0], b_ref, sems.at[len(copies)]))
    small_count = len(copies)
    for seq in range(seq_count):
        place = pl.ds(seq * block_len, block_len)
        copies.append(pltpu.make_async_copy(in_refs[0].at[place], x_ref.at[place], sems.at[len(copies)]))
    copies.append(pltpu.make_async_copy(in_refs[6].at[0], w_ref, sems.at[len(copies)]))
    for copy in copies:
        copy.start()
    for copy in copies[:small_count]:
        copy.wait()
    for seq in range(seq_count):
        copies[small_count + seq].wait()
        place = slice(seq * block_len, (seq + 1) * block_len)
        normed, _ = normalize(x_ref[place, :])
        a_ref[place, :] = (normed * ag_ref[0:1, :] + as_ref[0:1, :]).astype(BF16)
        m_ref[place, :] = (normed * mg_ref[0:1, :] + ms_ref[0:1, :]).astype(BF16)
    copies[-1].wait()
    project_rows(0, tok_shape, me_ref, seg_ref, lambda j: w_ref[j], b_ref[...], a_ref, p_refs, proj_ref, True)


def project_body(layer, tok_shape, me_ref, *refs):
    seq_count, block_len, width = tok_shape
    x_ref, seg_ref, *refs = refs
    u_refs, refs = refs[:4], refs[4:]
    ob_ref, db_ref, ag_ref, as_ref, mg_ref, ms_ref, w_ref, b_ref, x_out, a_ref, m_ref, *p_refs, proj_ref = refs
    tensor = me_ref[2]
    shift = ob_ref[layer - 1 : layer, :] + db_ref[layer - 1 : layer, :]
    for k in range(4):
        place = rows(wrap4(tensor - k), block_len)
        value = x_ref[place, :] + u_refs[k][...].astype(F32) + shift
        x_out[place, :] = value
        normed, _ = normalize(value)
        a_ref[place, :] = (normed * ag_ref[layer : layer + 1, :] + as_ref[layer : layer + 1, :]).astype(BF16)
        m_ref[place, :] = (normed * mg_ref[layer : layer + 1, :] + ms_ref[layer : layer + 1, :]).astype(BF16)
    project_rows(layer, tok_shape, me_ref, seg_ref, lambda j: w_ref[0, j], b_ref[0], a_ref, p_refs, proj_ref, False)


def gather_pieces(me_ref, refs, targets, block_len, seg_target=None):
    chip, core = me_ref[0], me_ref[1]
    for k in range(4):
        owner = wrap4(chip - k)
        for side, ref in ((core, refs[k]), (1 - core, refs[4 + k])):
            place = rows(owner * 2 + side, block_len)
            for index, target in enumerate(targets):
                target[place, :] = ref[core, 0:block_len, index * LANES : (index + 1) * LANES]
            if seg_target is not None:
                row = ref[core, block_len : block_len + 16, :].astype(F32)[0:1, :]
                starts = row[:, 0:LANES] * 8.0 + row[:, LANES : 2 * LANES]
                seg_target[:, place] = jnp.broadcast_to(starts, (8, block_len))


def head_stack(values):
    lane = lax.broadcasted_iota(jnp.int32, values.shape, 1)
    zero = jnp.zeros_like(values)
    return jnp.concatenate(
        [jnp.where(lane < HEAD, values, zero), jnp.where(lane >= HEAD, values, zero)], axis=0
    )


def own_halves(product, width):
    return jnp.concatenate([product[0:HEAD, 0:width], product[HEAD:, width : 2 * width]], axis=0)


def chances_t(q_ref, k_ref, seg_ref, step, chunk):
    start, keys = step * chunk, (step + 1) * chunk
    stacked = head_stack(q_ref[start:keys, :]) * jnp.asarray(HEAD ** (-0.5), BF16)
    scores = matmul_nt(k_ref[0:keys, :], stacked)
    key_place = lax.broadcasted_iota(jnp.int32, (keys, 2 * chunk), 0).astype(F32)
    query_place = (lax.broadcasted_iota(jnp.int32, (1, 2 * chunk), 1) & (chunk - 1)).astype(F32) + start
    seg_row = seg_ref[0:1, start:keys]
    seg_row = jnp.concatenate([seg_row, seg_row], axis=1)
    allowed = (key_place >= seg_row) & (key_place <= query_place)
    scores = jnp.where(allowed, scores, -1e30)
    raised = jnp.exp(scores - jnp.max(scores, axis=0, keepdims=True))
    total = jnp.sum(raised, axis=0, keepdims=True)
    return raised * (1.0 / total), stacked


def attend_body(block_len, chunk, me_ref, *refs):
    piece_refs, refs = refs[:8], refs[8:]
    seg_out, qkv_ref, *refs = refs
    o_refs, refs = refs[:4], refs[4:]
    vt_ref, o_ref = refs
    q_ref, k_ref, v_ref = qkv_ref.at[0], qkv_ref.at[1], qkv_ref.at[2]
    gather_pieces(me_ref, piece_refs, (q_ref, k_ref, v_ref), block_len, seg_out)
    vt_ref[...] = v_ref[...].T
    length = q_ref.shape[0]
    for step in range(length // chunk):
        keys = (step + 1) * chunk
        chances, _ = chances_t(q_ref, k_ref, seg_out, step, chunk)
        mixed = matmul(vt_ref[:, 0:keys], chances.astype(BF16))
        o_ref[step * chunk : keys, :] = own_halves(mixed, chunk).T.astype(BF16)
    send_blocks(me_ref, o_ref, o_refs, block_len)


def send_blocks(me_ref, source, targets, block_len):
    chip = me_ref[0]
    for k in range(4):
        dest = wrap4(chip + k)
        for side in range(2):
            targets[k][side] = source[rows(dest * 2 + side, block_len), :]


def attend_both_body(block_len, chunk, with_out, me_ref, *refs):
    if with_out:
        piece_refs, refs = refs[:8], refs[8:]
    else:
        qkv_ref, *refs = refs
    grad_refs, refs = refs[:8], refs[8:]
    seg_ref, *refs = refs
    d_refs, refs = refs[:4], refs[4:]
    if with_out:
        qkv_ref, *refs = refs
    q_ref, k_ref, v_ref = qkv_ref.at[0], qkv_ref.at[1], qkv_ref.at[2]
    g_ref, t_ref, o_ref, dq_ref, dk_ref, dv_ref = refs
    if with_out:
        gather_pieces(me_ref, piece_refs, (q_ref, k_ref, v_ref), block_len)
    gather_pieces(me_ref, grad_refs, (g_ref,), block_len)
    length = q_ref.shape[0]
    t_ref[0] = k_ref[...].T
    if with_out:
        t_ref[1] = v_ref[...].T
    dk_ref[...] = jnp.zeros_like(dk_ref)
    dv_ref[...] = jnp.zeros_like(dv_ref)
    for step in range(length // chunk):
        start, keys = step * chunk, (step + 1) * chunk
        chances, stacked = chances_t(q_ref, k_ref, seg_ref, step, chunk)
        low = chances.astype(BF16)
        if with_out:
            mixed = matmul(t_ref[1, :, 0:keys], low)
            o_ref[start:keys, :] = own_halves(mixed, chunk).T.astype(BF16)
        grads = head_stack(g_ref[start:keys, :])
        chance_grad = matmul_nt(v_ref[0:keys, :], grads)
        delta = jnp.sum(chances * chance_grad, axis=0, keepdims=True)
        score_grad = (chances * (chance_grad - delta)).astype(BF16)
        dv_ref[0:keys, :] += matmul(low, grads)
        dk_ref[0:keys, :] += matmul(score_grad, stacked)
        query = matmul(t_ref[0, :, 0:keys], score_grad)
        dq_ref[start:keys, :] = own_halves(query, chunk).T * HEAD ** (-0.5)
    chip = me_ref[0]
    for k in range(4):
        dest = wrap4(chip + k)
        for side in range(2):
            place = rows(dest * 2 + side, block_len)
            spots = (lax.broadcasted_iota(jnp.int32, (1, block_len), 1) + (dest * 2 + side) * block_len).astype(F32)
            tables = rotary_rows(spots - seg_ref[0:1, place])
            d_refs[k][side, :, 0:LANES] = rotate(dq_ref[place, :], tables, True).astype(BF16)
            d_refs[k][side, :, LANES : 2 * LANES] = rotate(dk_ref[place, :], tables, True).astype(BF16)
            d_refs[k][side, :, 2 * LANES : 3 * LANES] = dv_ref[place, :].astype(BF16)
            if with_out:
                d_refs[k][side, :, 3 * LANES :] = o_ref[place, :]


def land_heads(me_ref, refs, target, block_len, groups, first=0):
    chip, core = me_ref[0], me_ref[1]
    for k in range(4):
        place = rows(wrap4(chip - k), block_len)
        mine, other = refs[k][core], refs[4 + k][core]
        is_low = core == 0
        for group in range(groups):
            span = slice((first + group) * LANES, (first + group + 1) * LANES)
            at = group * 2 * LANES
            target[place, at : at + LANES] = jnp.where(is_low, mine[:, span], other[:, span])
            target[place, at + LANES : at + 2 * LANES] = jnp.where(is_low, other[:, span], mine[:, span])


def combine_body(block_len, fused, me_ref, *refs):
    piece_refs, refs = refs[:8], refs[8:]
    w_ref, *refs = refs
    if fused:
        g_ref, down_ref, *refs = refs
    else:
        part_ref, *refs = refs
    o_ref, *refs = refs
    q_refs, scr = refs[:4], refs[4]
    tensor = me_ref[2]
    land_heads(me_ref, piece_refs, o_ref, block_len, 1, 3 if fused else 0)
    part = matmul(g_ref[...], down_ref[0]) if fused else part_ref[...]
    scr[...] = (matmul(o_ref[...], w_ref[0]) + part).astype(BF16)
    for k in range(4):
        q_refs[k][...] = scr[rows(wrap4(tensor + k), block_len), :]


def send_grad_body(block_len, me_ref, x_ref, w_ref, *refs):
    chip = me_ref[0]
    for k in range(4):
        value = x_ref[rows(wrap4(chip + k), block_len), :].astype(BF16)
        grad = matmul_nt(value, w_ref[0]).astype(BF16)
        for pair in range(2):
            refs[k][pair] = grad[:, pair * LANES : (pair + 1) * LANES]


def join_body(block_len, me_ref, *refs):
    q_refs, refs = refs[:4], refs[4:]
    w_ref, r_ref, *g_refs = refs
    chip, tensor = me_ref[0], me_ref[2]
    for k in range(4):
        r_ref[rows(wrap4(tensor - k), block_len), :] = q_refs[k][...]
    for k in range(4):
        value = r_ref[rows(wrap4(chip + k), block_len), :]
        grad = matmul_nt(value, w_ref[0]).astype(BF16)
        for pair in range(2):
            g_refs[k][pair] = grad[:, pair * LANES : (pair + 1) * LANES]


def project_back_body(block_len, layer, me_ref, *refs):
    piece_refs, refs = refs[:8], refs[8:]
    w_ref, dm_ref, ag_ref, mg_ref, dp_ref, da_ref, bias_ref, *refs = refs
    q_refs, scr = refs[:4], refs[4]
    tensor = me_ref[2]
    land_heads(me_ref, piece_refs, dp_ref, block_len, 3)
    for j in range(3):
        span = slice(j * 2 * LANES, (j + 1) * 2 * LANES)
        bias_ref[j : j + 1, :] = jnp.sum(dp_ref[:, span].astype(F32), axis=0, keepdims=True)
    total = None
    for j in range(3):
        term = matmul_nt(dp_ref[:, j * 2 * LANES : (j + 1) * 2 * LANES], w_ref[0, j])
        total = term if total is None else total + term
    da_ref[...] = total.astype(BF16)
    scr[...] = (total * ag_ref[layer : layer + 1, :] + dm_ref[...] * mg_ref[layer : layer + 1, :]).astype(BF16)
    for k in range(4):
        q_refs[k][...] = scr[rows(wrap4(tensor + k), block_len), :]


def norm_back_body(me_ref, *refs):
    e_refs, refs = refs[:4], refs[4:]
    x_ref, dy_ref, dx_ref, low_ref, bias_ref = refs
    upstream = dy_ref[...]
    total = e_refs[0][...].astype(F32)
    for k in range(1, 4):
        total = total + e_refs[k][...].astype(F32)
    normed, factor = normalize(x_ref[...])
    inner = jnp.mean(total * normed, axis=-1, keepdims=True)
    result = upstream + factor * (total - jnp.mean(total, axis=-1, keepdims=True) - normed * inner)
    dx_ref[...] = result
    low_ref[...] = result.astype(BF16)
    bias_ref[...] = jnp.sum(upstream, axis=0, keepdims=True)


def gains_body(me_ref, x_ref, da_ref, dm_ref, out_ref):
    normed, _ = normalize(x_ref[...])
    da = da_ref[...].astype(F32)
    dm = dm_ref[...]
    out_ref[0:1, :] = jnp.sum(da * normed, axis=0, keepdims=True)
    out_ref[1:2, :] = jnp.sum(da, axis=0, keepdims=True)
    out_ref[2:3, :] = jnp.sum(dm * normed, axis=0, keepdims=True)
    out_ref[3:4, :] = jnp.sum(dm, axis=0, keepdims=True)


def gelu_parts(hidden):
    cdf = 0.5 * (1.0 + lax.erf(hidden * (0.5**0.5)))
    density = jnp.exp(-0.5 * hidden * hidden) * 0.3989422804014327
    return cdf, density


def feed_body(layer, me_ref, m_ref, up_ref, ub_ref, down_ref, g_ref, slope_ref, part_ref):
    size = 2 * LANES
    for step in range(up_ref.shape[2] // size):
        span = slice(step * size, (step + 1) * size)
        hidden = matmul(m_ref[...], up_ref[0, :, span]) + ub_ref[layer : layer + 1, span]
        cdf, density = gelu_parts(hidden)
        g_ref[:, span] = (hidden * cdf).astype(BF16)
        slope_ref[:, span] = cdf + hidden * density
    part_ref[...] = matmul(g_ref[...], down_ref[0])


def feed_back_body(me_ref, r_ref, slope_ref, up_ref, down_ref, dh_ref, dm_ref, bias_ref):
    size = 2 * LANES
    for step in range(down_ref.shape[1] // size):
        span = slice(step * size, (step + 1) * size)
        grad = matmul_nt(r_ref[...], down_ref[0, span, :]) * slope_ref[:, span]
        bias_ref[:, span] = jnp.sum(grad, axis=0, keepdims=True)
        dh_ref[:, span] = grad.astype(BF16)
    dm_ref[...] = matmul_nt(dh_ref[...], up_ref[0])


def feed_both_body(layer, me_ref, m_ref, dy_ref, up_ref, ub_ref, down_ref, g_ref, r_ref, dh_ref, dm_ref, bias_ref):
    size = 2 * LANES
    r_ref[...] = dy_ref[...].astype(BF16)
    for step in range(up_ref.shape[2] // size):
        span = slice(step * size, (step + 1) * size)
        hidden = matmul(m_ref[...], up_ref[0, :, span]) + ub_ref[layer : layer + 1, span]
        cdf, density = gelu_parts(hidden)
        g_ref[:, span] = (hidden * cdf).astype(BF16)
        grad = matmul_nt(r_ref[...], down_ref[0, span, :]) * (cdf + hidden * density)
        bias_ref[:, span] = jnp.sum(grad, axis=0, keepdims=True)
        dh_ref[:, span] = grad.astype(BF16)
    dm_ref[...] = matmul_nt(dh_ref[...], up_ref[0])


def feed_weights_body(me_ref, m_ref, dh_ref, g_ref, r_ref, keep_ref, send_ref):
    core = me_ref[1]
    half = m_ref.shape[1] // 2
    for side, out in ((core, keep_ref), (1 - core, send_ref)):
        out[0:half, :] = matmul_tn(m_ref[:, rows(side, half)], dh_ref[...]).astype(BF16)
        out[half:, :] = matmul_tn(g_ref[:, rows(side, half)], r_ref[...]).astype(BF16)


def head_weights_body(me_ref, a_ref, dp_ref, o_ref, r_ref, keep_ref, send_ref):
    core = me_ref[1]
    half = a_ref.shape[1] // 2
    wide = dp_ref.shape[1]
    for side, out in ((core, keep_ref), (1 - core, send_ref)):
        out[:, 0:wide] = matmul_tn(a_ref[:, rows(side, half)], dp_ref[...]).astype(BF16)
        grad = matmul_tn(o_ref[:, rows(side, LANES)], r_ref[...]).astype(BF16)
        for part in range(4):
            out[part * LANES : (part + 1) * LANES, wide:] = grad[:, part * 2 * LANES : (part + 1) * 2 * LANES]


def halve_body(me_ref, feed_keep, feed_came, head_keep, head_came, *refs):
    a_keep, a_send, b_keep, b_send, scr = refs
    high, low = feed_keep.shape[0], head_keep.shape[0]
    scr[0:high, :] = (feed_keep[...].astype(F32) + feed_came[...].astype(F32)).astype(BF16)
    scr[high:, :] = (head_keep[...].astype(F32) + head_came[...].astype(F32)).astype(BF16)
    place = me_ref[3]
    near, far = place ^ 1, 3 - place
    size = a_keep.shape[0] // 2
    for ref, first, second in (
        (a_keep, place, far),
        (a_send, near, 3 - near),
        (b_keep, 4 + place, 4 + near),
        (b_send, 4 + far, 4 + (far ^ 1)),
    ):
        ref[0:size, :] = scr[rows(first, size), :]
        ref[size:, :] = scr[rows(second, size), :]


def halve_again_body(me_ref, a_keep, a_came, b_keep, b_came, *outs):
    size = outs[0].shape[0]
    for keep, came, mine, send in ((a_keep, a_came, outs[0], outs[1]), (b_keep, b_came, outs[2], outs[3])):
        total = (keep[...].astype(F32) + came[...].astype(F32)).astype(BF16)
        mine[...] = total[0:size, :]
        send[...] = total[size:, :]


def line_up_body(axis, me_ref, *refs):
    size = refs[0].shape[0]
    for k in range(4):
        refs[4][rows(wrap4(me_ref[axis] - k), size), :] = refs[k][...]


def add_packs_body(me_ref, feed_keep, feed_came, head_keep, head_came, out_ref):
    high = feed_keep.shape[0]
    out_ref[0:high, :] = (feed_keep[...].astype(F32) + feed_came[...].astype(F32)).astype(BF16)
    out_ref[high:, :] = (head_keep[...].astype(F32) + head_came[...].astype(F32)).astype(BF16)


def merge_body(me_ref, a_keep, a_came, b_keep, b_came, small_ref, *refs):
    out_refs, scr = refs[:4], refs[4]
    size = a_keep.shape[0]
    scr[0:size, :] = (a_keep[...].astype(F32) + a_came[...].astype(F32)).astype(BF16)
    scr[size:, :] = (b_keep[...].astype(F32) + b_came[...].astype(F32)).astype(BF16)
    few = scr.shape[0] // 4
    for k in range(4):
        out_refs[k][0:few, :] = scr[rows(wrap4(me_ref[0] + k), few), :]
        out_refs[k][few:, :] = small_ref[...]


def settle_body(me_ref, *refs):
    in_refs, (first_ref, second_ref, shared_ref, local_ref) = refs[:4], refs[4:]
    even = in_refs[0][...].astype(F32) + in_refs[2][...].astype(F32)
    odd = in_refs[1][...].astype(F32) + in_refs[3][...].astype(F32)
    total = (even + odd).astype(BF16)
    size, few = first_ref.shape[0], shared_ref.shape[0]
    first_ref[...] = total[0:size, :]
    second_ref[...] = total[size : 2 * size, :]
    shared_ref[...] = total[2 * size : 2 * size + few, :]
    local_ref[...] = total[2 * size + few :, :]


def write_rows(ref, start, count, at, side, outs):
    up_ref, down_ref, qkv_ref, out_ref = outs
    size = 2 * LANES
    half = up_ref.shape[1] // 2
    value = ref[start : start + count, :].astype(F32)
    weight = lax.div(at, half)
    inside = pl.multiple_of(lax.rem(at, half) + side * half, 16)

    @pl.when(weight == 0)
    def _():
        up_ref[0, pl.ds(inside, count), :] = value

    @pl.when(weight == 1)
    def _():
        down_ref[0, pl.ds(inside, count), :] = value

    @pl.when(weight == 2)
    def _():
        for j in range(3):
            qkv_ref[0, j, pl.ds(inside, count), :] = value[:, j * size : (j + 1) * size]
        part = lax.div(lax.rem(at, half), LANES)
        place = pl.multiple_of(lax.rem(at, LANES) + side * LANES, 16)
        for index in range(4):

            @pl.when(part == index)
            def _():
                out_ref[0, pl.ds(place, count), index * size : (index + 1) * size] = value[:, 3 * size :]


def unpack_body(few, me_ref, *refs):
    outs = refs[24:28]
    chip, core, place_z = me_ref[0], me_ref[1], me_ref[3]
    block = 3 * few
    for side, group in ((core, refs[:10]), (1 - core, refs[10:20])):
        for along, me in ((0, place_z), (1, chip)):
            pieces = group[5 * along : 5 * along + 5]
            half = pieces[3].shape[0]
            spans = [(pieces[0], me, 0), (pieces[1], me ^ 1, 0), (pieces[2], 3 - me, 0)]
            spans += [(pieces[3], me ^ 2, 0), (pieces[4], me ^ 2, half)]
            for ref, owner, offset in spans:
                for start in range(0, ref.shape[0], few):
                    row = offset + start
                    other, inner_row = row // block, row % block
                    place_here, chip_here = (owner, other) if along == 0 else (other, owner)
                    row_in_chunk = chip_here * (2 * block) + along * block + inner_row
                    size = 4 * block
                    way = lax.div(row_in_chunk, size)
                    at = way * (4 * size) + place_here * size + lax.rem(row_in_chunk, size)
                    write_rows(ref, start, few, at, side, outs)


def unpack_whole_body(me_ref, mine_ref, other_ref, *outs):
    core = me_ref[1]
    up_ref, down_ref, qkv_ref, out_ref = outs
    size = 2 * LANES
    half = up_ref.shape[1] // 2
    for side, pack in ((core, mine_ref), (1 - core, other_ref)):
        place = rows(side, half)
        up_ref[0, place, :] = pack[0:half, :].astype(F32)
        down_ref[0, place, :] = pack[half : 2 * half, :].astype(F32)
        for j in range(3):
            qkv_ref[0, j, place, :] = pack[2 * half :, j * size : (j + 1) * size].astype(F32)
        for part in range(4):
            at = 2 * half + part * LANES
            out_ref[0, rows(side, LANES), part * size : (part + 1) * size] = pack[at : at + LANES, 3 * size :].astype(F32)


def pack_small_body(me_ref, *refs):
    ins, small_ref = refs[:8], refs[8]
    width = small_ref.shape[1]
    blank = jnp.zeros((1, width), F32)
    shared = [ins[0][...], ins[1][...], ins[2][...], ins[3][...]] + [blank] * 6
    small_ref[0:16, :] = jnp.concatenate(shared, axis=0).astype(BF16)
    local = [ins[6][...], ins[7][...]]
    for ref in ins[4:6]:
        values = ref[...]
        flat = [values[j : j + 1, :] for j in range(3)]
        local.append(jnp.concatenate(flat + [jnp.zeros((1, width - 3 * values.shape[1]), F32)], axis=1))
    small_ref[16:32, :] = jnp.concatenate(local + [blank] * 12, axis=0).astype(BF16)


def add_body(count, me_ref, *refs):
    total = refs[0][...].astype(F32)
    for ref in refs[1:count]:
        total = total + ref[...].astype(F32)
    refs[count][...] = total.astype(refs[count].dtype)


def small_out_body(me_ref, small_ref, *outs):
    shared, local = small_ref[0:16, :], small_ref[16:32, :]
    for index in range(5):
        outs[index][0:1, :] = shared[index : index + 1, :]
        outs[index][1:2, :] = shared[index + 5 : index + 6, :]
    outs[5][...] = local[0:2, :]
    size = outs[6].shape[2]
    for layer in range(2):
        for j in range(3):
            outs[6][layer, j : j + 1, :] = local[2 + layer : 3 + layer, j * size : (j + 1) * size]


def place_body(block_len, with_sum, me_ref, *refs):
    q_refs, refs = refs[:4], refs[4:]
    tensor = me_ref[2]
    out_ref = refs[-1]
    if with_sum:
        x_ref, ob_ref, db_ref = refs[:3]
        shift = ob_ref[1:2, :] + db_ref[1:2, :]
    for k in range(4):
        place = rows(wrap4(tensor - k), block_len)
        value = q_refs[k][...].astype(F32)
        out_ref[place, :] = x_ref[place, :] + value + shift if with_sum else value


def chip_turn(shift):
    return [(2 * x + c, 2 * ((x + shift) % 4) + c) for x in range(4) for c in range(2)]


CORE_SWAP = [(i, i ^ 1) for i in range(8)]


def over_chips(pieces, beside=()):
    mine, beside = lax.optimization_barrier((over_x(pieces), beside))
    return mine + [swap_core(piece) for piece in mine], beside


def ring_turn(shift):
    return [(i, (i + shift) % 4) for i in range(4)]


def over_tensor(pieces):
    return [pieces[0]] + [lax.ppermute(pieces[k], "tensor", ring_turn(k)) for k in range(1, 4)]


def share_tensor(piece):
    return over_tensor([piece] * 4)


def over_dp(pieces):
    return [pieces[0]] + [lax.ppermute(pieces[k], "dp", ring_turn(k)) for k in range(1, 4)]


def over_x(pieces):
    return [pieces[0]] + [lax.ppermute(pieces[k], "ctx", chip_turn(k)) for k in range(1, 4)]


def swap_core(piece):
    return lax.ppermute(piece, "ctx", CORE_SWAP)


NEXT_PAIR = [(0, 1), (1, 0), (2, 3), (3, 2)]
WRAP_PAIR = [(0, 3), (3, 0), (1, 2), (2, 1)]


def halves_both_ways(first, second, axis, again=False):
    ways = (WRAP_PAIR, NEXT_PAIR) if again else (NEXT_PAIR, WRAP_PAIR)
    return lax.ppermute(first, axis, ways[0]), lax.ppermute(second, axis, ways[1])


def chips_of(pairs):
    return [(2 * a + c, 2 * b + c) for a, b in pairs for c in range(2)]


def spread_near(piece, axis):
    name, move = ("dp", lambda pairs: pairs) if axis == "dp" else ("ctx", chips_of)
    return [piece] + [lax.ppermute(piece, name, move(pairs)) for pairs in (NEXT_PAIR, WRAP_PAIR)]


def spread_far(pieces, axis):
    name, move = ("dp", lambda pairs: pairs) if axis == "dp" else ("ctx", chips_of)
    half = pieces[0].shape[0] // 2
    return pieces + [
        lax.ppermute(pieces[1][:half], name, move(WRAP_PAIR)),
        lax.ppermute(pieces[2][half:], name, move(NEXT_PAIR)),
    ]


def tie(first, second):
    return lax.optimization_barrier((first, second))


def after(values, token):
    return lax.optimization_barrier((values, token))[0]


def add_up(pieces):
    total = pieces[0].astype(F32)
    for piece in pieces[1:]:
        total = total + piece.astype(F32)
    return total


def on_device(
    inputs,
    segments,
    attn_gain,
    attn_shift,
    mlp_gain,
    mlp_shift,
    qkv_weight,
    qkv_bias,
    out_weight,
    out_bias,
    up_weight,
    up_bias,
    down_weight,
    down_bias,
    cotangent,
):
    seq_count, block_len, width = inputs.shape
    tokens = seq_count * block_len
    inner = qkv_weight.shape[3]
    hidden = up_weight.shape[2]
    length = block_len * 8
    chunk = 256
    place = lax.axis_index("ctx")
    me = jnp.stack([place // 2, place % 2, lax.axis_index("tensor"), lax.axis_index("dp")]).astype(jnp.int32)
    x0 = inputs.reshape(tokens, width)
    dy1 = cotangent.reshape(tokens, width)
    tok_shape = inputs.shape
    wide = shape_of((tokens, width), BF16)
    norms = (attn_gain, attn_shift, mlp_gain, mlp_shift)

    def project_first(x):
        sources = [x, segments, *norms, qkv_weight, qkv_bias]
        held = [v.shape for v in sources[:6]] + [qkv_weight.shape[1:], qkv_bias.shape[1:]]
        piece = shape_of((2, block_len + 16, 3 * LANES), BF16)
        return run(
            functools.partial(project_first_body, tok_shape),
            me,
            [(v, pl.BlockSpec(memory_space=pltpu.HBM)) for v in sources],
            [wide, wide] + [piece] * 4,
            scratch=[pltpu.VMEM((tokens, 3 * inner), F32)]
            + [pltpu.VMEM(size, v.dtype) for size, v in zip(held, sources)]
            + [pltpu.SemaphoreType.DMA((11,))],
            name="norm_project",
            limit=62,
        )

    def project(layer, x, extra):
        piece = shape_of((2, block_len, 3 * LANES), BF16)
        return run(
            functools.partial(project_body, layer, tok_shape),
            me,
            [x, segments, *extra, *norms]
            + [(qkv_weight, layer_spec(qkv_weight, layer)), (qkv_bias, layer_spec(qkv_bias, layer))],
            [shape_of((tokens, width), F32), wide, wide] + [piece] * 4,
            scratch=[pltpu.VMEM((tokens, 3 * inner), F32)],
            name="norm_project",
            limit=24,
        )

    def feed(layer, m):
        return run(
            functools.partial(feed_body, layer),
            me,
            [m, (up_weight, layer_spec(up_weight, layer)), up_bias, (down_weight, layer_spec(down_weight, layer))],
            [shape_of((tokens, hidden), BF16), shape_of((tokens, hidden), F32), shape_of((tokens, width), F32)],
            name="feed", limit=24,
        )

    def feed_back(layer, r, slope):
        return run(
            feed_back_body,
            me,
            [r, slope, (up_weight, layer_spec(up_weight, layer)), (down_weight, layer_spec(down_weight, layer))],
            [shape_of((tokens, hidden), BF16), shape_of((tokens, width), F32), shape_of((1, hidden), F32)],
            name="feed_back", limit=24,
        )

    def feed_both(layer, m, dy):
        return run(
            functools.partial(feed_both_body, layer),
            me,
            [m, dy, (up_weight, layer_spec(up_weight, layer)), up_bias, (down_weight, layer_spec(down_weight, layer))],
            [shape_of((tokens, hidden), BF16), wide, shape_of((tokens, hidden), BF16)]
            + [shape_of((tokens, width), F32), shape_of((1, hidden), F32)],
            name="feed_both", limit=24,
        )

    def combine(layer, pieces, part, active=None):
        fused = part is None
        got = run(
            functools.partial(combine_body, block_len, fused),
            me,
            [*pieces, (out_weight, layer_spec(out_weight, layer))]
            + ([active, (down_weight, layer_spec(down_weight, layer))] if fused else [part]),
            [shape_of((tokens, inner), BF16)] + [shape_of((block_len, width), BF16)] * 4,
            scratch=[pltpu.VMEM((tokens, width), BF16)],
            name="combine", limit=20,
        )
        return got[0], got[1:]

    def add_all(values, dtype=BF16):
        out = shape_of(values[0].shape, dtype)
        return run(functools.partial(add_body, len(values)), me, values, [out], name="add_all", limit=16)[0]

    def line_up(axis, values):
        high, wide_here = values[0].shape
        out = shape_of((high * 4, wide_here), BF16)
        return run(functools.partial(line_up_body, axis), me, values, [out], name="line_up", limit=8)[0]

    seq_bf16 = pltpu.VMEM((length, LANES), BF16)
    seq_f32 = pltpu.VMEM((length, LANES), F32)
    o_shapes = [shape_of((2, block_len, LANES), BF16)] * 4

    def attend_both(pieces, grads, seg_rows, with_out):
        return run(
            functools.partial(attend_both_body, block_len, chunk, with_out),
            me,
            [*pieces, *grads, seg_rows],
            [shape_of((2, block_len, (4 if with_out else 3) * LANES), BF16)] * 4,
            scratch=([pltpu.VMEM((3, length, LANES), BF16)] if with_out else [])
            + [seq_bf16, pltpu.VMEM((2, LANES, length), BF16), seq_bf16]
            + [seq_f32] * 3,
            name="attend_both", limit=24,
        )

    def project_back(layer, pieces, dm):
        got = run(
            functools.partial(project_back_body, block_len, layer),
            me,
            [*pieces, (qkv_weight, layer_spec(qkv_weight, layer)), dm, attn_gain, mlp_gain],
            [shape_of((tokens, 3 * inner), BF16), wide, shape_of((3, inner), F32)]
            + [shape_of((block_len, width), BF16)] * 4,
            scratch=[pltpu.VMEM((tokens, width), BF16)],
            name="project_back", limit=24,
        )
        return got[0], got[1], got[2], got[3:]

    def norm_back(pieces, x, dy, dy_quarter):
        by_tensor = pl.BlockSpec((block_len, width), lambda i, me_ref: (me_ref[2], 0))
        quarter = shape_of((block_len, width), F32)
        return run(
            norm_back_body,
            me,
            [*pieces, (x, by_tensor), dy if dy_quarter else (dy, by_tensor)],
            [quarter, shape_of((block_len, width), BF16), shape_of((1, width), F32)],
            name="norm_back", limit=10,
        )

    def gains(x, da, dm):
        return run(gains_body, me, [x, da, dm], [shape_of((4, width), F32)], name="gains", limit=16)[0]

    half = width // 2
    columns = [[8 * z + 2 * chip + core for z in range(4) for chip in range(4)] for core in range(2)]

    def feed_weights(m, dh, active, r):
        pack = shape_of((2 * half, width), BF16)
        return run(feed_weights_body, me, [m, dh, active, r], [pack] * 2, name="feed_weights", limit=24)

    def head_weights(attn_in, dproj, attended, r):
        pack = shape_of((half, width), BF16)
        return run(head_weights_body, me, [attn_in, dproj, attended, r], [pack] * 2, name="head_weights", limit=20)

    a0, m0, *pieces = project_first(x0)
    fed0 = feed(0, m0)
    pieces0, (active0, slope0, part0) = over_chips(pieces, fed0)
    got = run(
        functools.partial(attend_body, block_len, chunk),
        me,
        pieces0,
        [shape_of((8, length), F32), shape_of((3, length, LANES), BF16)] + o_shapes,
        scratch=[pltpu.VMEM((LANES, length), BF16), seq_bf16],
        name="attend", limit=20,
    )
    seg_rows, qkv0 = got[:2]
    out0, _ = over_chips(got[2:])
    attended0, u0 = combine(0, out0, part0)
    grads1 = run(
        functools.partial(send_grad_body, block_len),
        me,
        [after(dy1, u0[0]), (out_weight, layer_spec(out_weight, 1))],
        o_shapes,
        name="out_back", limit=14,
    )
    u0, grads1 = tie(over_tensor(u0), over_x(grads1))
    u0 = share_tensor(add_up(u0).astype(BF16))
    u0, grads1_other = tie(u0, [swap_core(piece) for piece in grads1])

    x1, a1, m1, *pieces = project(1, x0, [*u0, out_bias, down_bias])
    fed1 = feed_both(1, m1, dy1)
    pieces1, (active1, r1, dh1, dm1, up_b1) = over_chips(pieces, fed1)
    got = attend_both(pieces1, grads1 + grads1_other, seg_rows, True)
    feed_pack1 = feed_weights(after(m1, got[0]), dh1, active1, r1)
    back1, feed_pack1 = over_chips(got, feed_pack1)
    dproj1, da1, qkv_b1, e1 = project_back(1, back1, dm1)
    feed_keep, feed_send, back1 = after((*feed_pack1, back1), e1[0])
    feed_came = swap_core(feed_send)
    attended1, u1 = combine(1, back1, None, active1)
    head_keep, head_send = head_weights(a1, dproj1, attended1, r1)
    pack1 = run(
        add_packs_body,
        me,
        [feed_keep, feed_came, head_keep, swap_core(head_send)],
        [shape_of((3 * half, width), BF16)],
        name="add_packs",
        limit=28,
    )[0]
    e1, (u1, _) = tie(over_tensor(e1), (u1, pack1))
    part1 = lax.psum_scatter(pack1, ("dp", "ctx"), axis_index_groups=columns, tiled=True)
    dx1, low1, bias1 = norm_back(e1, x1, dy1, False)
    gains1 = gains(after(x1, low1), da1, dm1)
    quarters, gains1 = tie(share_tensor(low1), gains1)

    r0, *grads0 = run(
        functools.partial(join_body, block_len),
        me,
        [*quarters, (out_weight, layer_spec(out_weight, 0))],
        [wide] + o_shapes,
        name="join_out_back", limit=14,
    )
    dh0, dm0, up_b0 = feed_back(0, r0, slope0)
    grads0, (dh0, dm0) = over_chips(grads0, (dh0, dm0))
    back0 = attend_both([qkv0], grads0, seg_rows, False)
    feed_pack0 = feed_weights(after(m0, back0[0]), dh0, active0, r0)
    back0, (feed_keep, feed_send) = over_chips(back0, feed_pack0)
    dproj0, da0, qkv_b0, e0 = project_back(0, back0, dm0)
    feed_keep, feed_send, a0, x0_late = after((feed_keep, feed_send, a0, x0), e0[0])
    head_keep, head_send = head_weights(a0, dproj0, attended0, r0)
    way = shape_of((3 * half // 4, width), BF16)
    a_keep, a_send, b_keep, b_send = run(
        halve_body,
        me,
        [feed_keep, swap_core(feed_send), head_keep, swap_core(head_send)],
        [way] * 4,
        scratch=[pltpu.VMEM((3 * half, width), BF16)],
        name="halve",
        limit=28,
    )
    gains0 = gains(x0_late, da0, dm0)
    a_came, b_came = halves_both_ways(a_send, b_send, "dp")
    e0, (a_send, gains0, part1) = tie(over_tensor(e0), (a_send, gains0, part1))
    pack1 = lax.all_gather(part1, ("dp", "ctx"), axis_index_groups=columns, tiled=True)
    dx0, low0, bias0 = norm_back(e0, x0, dx1, True)
    last = share_tensor(low0)
    way = shape_of((3 * half // 8, width), BF16)
    a_keep, a_send, b_keep, b_send = run(
        halve_again_body, me, after([a_keep, a_came, b_keep, b_came], low0), [way] * 4, name="halve_again", limit=16
    )
    a_came, b_came = halves_both_ways(a_send, b_send, "dp", True)
    small = run(
        pack_small_body,
        me,
        [gains0, bias0, gains1, bias1, qkv_b0, qkv_b1, up_b0, up_b1],
        [shape_of((32, width), BF16)],
        name="pack_small",
        limit=8,
    )[0]

    few = half // 32
    size = 3 * few
    cut = run(
        merge_body,
        me,
        [a_keep, a_came, b_keep, b_came, small],
        [shape_of((2 * size + 32, width), BF16)] * 4,
        scratch=[pltpu.VMEM((8 * size, width), BF16)],
        name="merge",
        limit=16,
    )
    cut, last = tie(over_x(cut), last)
    row_block = shape_of((16, width), BF16)
    piece = shape_of((size, width), BF16)
    first, second, shared, local = run(settle_body, me, cut, [piece, piece, row_block, row_block], name="settle", limit=8)
    u1 = over_tensor(after(u1, first))
    shared = [shared, lax.ppermute(shared, "tensor", NEXT_PAIR)]
    (first, second), (shared, pack1) = tie((over_x([first] * 4), over_dp([second] * 4)), (shared, pack1))
    first, second = line_up(0, first), line_up(3, second)
    near = (spread_near(first, "dp"), spread_near(second, "x"))

    heavy = [
        shape_of((2, width, hidden), F32),
        shape_of((2, hidden, width), F32),
        shape_of((2, 3, width, inner), F32),
        shape_of((2, inner, width), F32),
    ]
    pack1, last = after((pack1, last), second)
    first_outs = run(
        unpack_whole_body,
        me,
        [pack1, swap_core(pack1)],
        heavy,
        name="unpack_whole",
        limit=44,
        out_specs=[layer_spec(v, 1) for v in heavy],
    )
    shared = add_all(shared)
    shared = add_all([shared, lax.ppermute(shared, "tensor", WRAP_PAIR)])
    u1 = share_tensor(add_up(u1).astype(BF16))
    small = jnp.concatenate([shared, local], axis=0)
    for pairs in (NEXT_PAIR, WRAP_PAIR):
        small = add_all([small, lax.ppermute(small, "dp", pairs)])
    small = add_all([small, swap_core(small)], F32)
    row_pair = shape_of((2, width), F32)
    small = run(
        small_out_body, me, [small], [row_pair] * 6 + [shape_of((2, 3, inner), F32)], name="small_out", limit=8
    )
    tok_out = [shape_of((tokens, width), F32)]
    input_grad = run(functools.partial(place_body, block_len, False), me, last, tok_out, name="place_grad", limit=16)[0]
    output = run(
        functools.partial(place_body, block_len, True),
        me,
        [*u1, x1, out_bias, down_bias],
        tok_out,
        name="place_output",
        limit=20,
    )[0]
    near, first_outs = tie(near, first_outs)
    mine = spread_far(near[0], "dp") + spread_far(near[1], "x")
    mine, (small, input_grad, output) = tie(mine, (small, input_grad, output))
    untouched = pl.BlockSpec(memory_space=pl.ANY)
    up_grad, down_grad, qkv_grad, out_grad = run(
        functools.partial(unpack_body, few),
        me,
        mine + [swap_core(v) for v in mine] + [(v, untouched) for v in first_outs],
        heavy,
        name="unpack",
        limit=44,
        out_specs=[layer_spec(v, 0) for v in heavy],
        aliases={21 + index: index for index in range(4)},
    )
    return (
        output.reshape(tok_shape),
        input_grad.reshape(tok_shape),
        small[0],
        small[1],
        small[2],
        small[3],
        qkv_grad,
        small[6],
        out_grad,
        small[4],
        up_grad,
        small[5],
        down_grad,
        small[4],
    )


def solution(mesh):
    in_specs = (
        P("dp", "ctx", None),
        P("dp", "ctx"),
        P(),
        P(),
        P(),
        P(),
        P(None, None, None, "tensor"),
        P(None, None, "tensor"),
        P(None, "tensor", None),
        P(),
        P(None, None, "tensor"),
        P(None, "tensor"),
        P(None, "tensor", None),
        P(),
        P("dp", "ctx", None),
    )
    out_specs = (
        P("dp", "ctx", None),
        P("dp", "ctx", None),
        P(),
        P(),
        P(),
        P(),
        P(None, None, None, "tensor"),
        P(None, None, "tensor"),
        P(None, "tensor", None),
        P(),
        P(None, None, "tensor"),
        P(None, "tensor"),
        P(None, "tensor", None),
        P(),
    )
    return jax.shard_map(
        on_device, mesh=mesh, in_specs=in_specs, out_specs=out_specs, check_vma=False
    )
```

```python
import functools

import jax
import jax.numpy as jnp
from jax import lax
from jax.experimental import pallas as pl
from jax.experimental.pallas import tpu as pltpu
from jax.sharding import PartitionSpec as P

HEAD = 64
ROT = 16
LAYERS = 2
LANES = 128
F32 = jnp.float32
BF16 = jnp.bfloat16


def shape_of(shape, dtype):
    return jax.ShapeDtypeStruct(tuple(shape), dtype)


def whole(array):
    rank = array.ndim
    return pl.BlockSpec(array.shape, lambda i, *_: (0,) * rank, pipeline_mode=pl.Buffered(1))


def layer_spec(array, layer):
    rank = array.ndim
    return pl.BlockSpec(
        (1,) + array.shape[1:], lambda i, *_: (layer,) + (0,) * (rank - 1), pipeline_mode=pl.Buffered(1)
    )


def run(body, me, operands, outs, scratch=(), name=None, limit=32, out_specs=None, aliases=None):
    arrays, specs = [], []
    for operand in operands:
        array, spec = operand if isinstance(operand, tuple) else (operand, None)
        arrays.append(array)
        specs.append(whole(array) if spec is None else spec)
    return pl.pallas_call(
        body,
        grid_spec=pltpu.PrefetchScalarGridSpec(
            num_scalar_prefetch=1,
            grid=(1,),
            in_specs=specs,
            out_specs=[whole(o) for o in outs] if out_specs is None else out_specs,
            scratch_shapes=list(scratch),
        ),
        out_shape=list(outs),
        input_output_aliases=aliases or {},
        compiler_params=pltpu.CompilerParams(vmem_limit_bytes=limit * 1024 * 1024),
        cost_estimate=pl.CostEstimate(flops=1, bytes_accessed=1, transcendentals=0),
        name=name,
    )(me, *arrays)


def matmul(left, right):
    return jnp.dot(left, right, preferred_element_type=F32)


def matmul_nt(left, right):
    return lax.dot_general(left, right, (((1,), (1,)), ((), ())), preferred_element_type=F32)


def matmul_tn(left, right):
    return lax.dot_general(left, right, (((0,), (0,)), ((), ())), preferred_element_type=F32)


def normalize(values):
    average = jnp.mean(values, axis=-1, keepdims=True)
    centred = values - average
    factor = lax.rsqrt(jnp.mean(centred * centred, axis=-1, keepdims=True) + 1e-05)
    return centred * factor, factor


def wrap4(value):
    return lax.rem(value + 4, 4)


def rows(index, size):
    return pl.ds(pl.multiple_of(index * size, size), size)


def rotary_rows(place_row):
    count = place_row.shape[1]
    which = lax.broadcasted_iota(jnp.int32, (8, count), 0)
    frequency = jnp.zeros((8, count), F32)
    for index in range(8):
        frequency = jnp.where(which == index, 10000.0 ** (-2.0 * index / ROT), frequency)
    angles = frequency * place_row
    trig = jnp.concatenate([jnp.cos(angles), jnp.sin(angles)], axis=0)
    row = lax.broadcasted_iota(jnp.int32, (16, LANES), 0)
    lane = lax.broadcasted_iota(jnp.int32, (16, LANES), 1) & (HEAD - 1)
    same = (lane & 7) == (row & 7)
    is_cos = row < 8
    pick_cos = jnp.where(is_cos & same & (lane < 16), 1.0, 0.0)
    pick_low = jnp.where((row >= 8) & same & (lane < 8), 1.0, 0.0)
    pick_high = jnp.where((row >= 8) & same & (lane >= 8) & (lane < 16), 1.0, 0.0)
    picks = jnp.concatenate([pick_cos, pick_low, pick_high], axis=1).astype(F32)
    spread = lax.dot_general(
        trig, picks, (((0,), (0,)), ((), ())), preferred_element_type=F32, precision=lax.Precision.HIGHEST
    )
    lane_row = lax.broadcasted_iota(jnp.int32, (1, LANES), 1) & (HEAD - 1)
    cos_table = spread[:, :LANES] + jnp.where(lane_row >= ROT, 1.0, 0.0)
    return cos_table, spread[:, LANES : 2 * LANES], spread[:, 2 * LANES :]


def rotate(values, tables, back=False):
    cos_table, low_sin, high_sin = tables
    below = pltpu.roll(values, LANES - ROT // 2, 1) * low_sin
    above = pltpu.roll(values, ROT // 2, 1) * high_sin
    turned = below - above if back else above - below
    return values * cos_table + turned


def project_rows(layer, tok_shape, me_ref, seg_ref, weight, bias, a_ref, p_refs, proj_ref, with_seg):
    seq_count, block_len, width = tok_shape
    chip, core = me_ref[0], me_ref[1]
    base = (chip * 2 + core) * block_len
    for j in range(3):
        proj_ref[:, j * 2 * LANES : (j + 1) * 2 * LANES] = matmul(a_ref[...], weight(j)) + bias[j : j + 1, :]
    for k in range(4):
        seq = wrap4(chip + k)
        place = rows(seq, block_len)
        seg_row = seg_ref[pl.ds(seq, 1), :]
        spots = lax.broadcasted_iota(jnp.int32, (1, block_len), 1) + base
        tables = rotary_rows((spots - seg_row).astype(F32))
        for j in range(3):
            for pair in range(2):
                at = (2 * j + pair) * LANES
                part = proj_ref[place, at : at + LANES]
                if j < 2:
                    part = rotate(part, tables)
                p_refs[k][pair, 0:block_len, j * LANES : (j + 1) * LANES] = part.astype(BF16)
        if with_seg:
            coded = seg_row.astype(F32)
            high = jnp.floor(coded * 0.125)
            packed = jnp.concatenate([high, coded - 8.0 * high, jnp.zeros_like(high)], axis=1)
            packed = jnp.broadcast_to(packed, (16, 3 * LANES)).astype(BF16)
            for pair in range(2):
                p_refs[k][pair, block_len : block_len + 16, :] = packed


def project_first_body(tok_shape, me_ref, *refs):
    seq_count, block_len, width = tok_shape
    in_refs, refs = refs[:8], refs[8:]
    xq_ref, a_ref, m_ref, *p_refs = refs[:7]
    proj_ref, *held, sems = refs[7:]
    x_ref, seg_ref, ag_ref, as_ref, mg_ref, ms_ref, w_ref, b_ref = held
    copies = []
    for index in (1, 2, 3, 4, 5):
        copies.append(pltpu.make_async_copy(in_refs[index], held[index], sems.at[len(copies)]))
    copies.append(pltpu.make_async_copy(in_refs[7].at[0], b_ref, sems.at[len(copies)]))
    small_count = len(copies)
    for seq in range(seq_count):
        place = pl.ds(seq * block_len, block_len)
        copies.append(pltpu.make_async_copy(in_refs[0].at[place], x_ref.at[place], sems.at[len(copies)]))
    copies.append(pltpu.make_async_copy(in_refs[6].at[0], w_ref, sems.at[len(copies)]))
    for copy in copies:
        copy.start()
    for copy in copies[:small_count]:
        copy.wait()
    for seq in range(seq_count):
        copies[small_count + seq].wait()
        place = slice(seq * block_len, (seq + 1) * block_len)
        normed, _ = normalize(x_ref[place, :])
        a_ref[place, :] = (normed * ag_ref[0:1, :] + as_ref[0:1, :]).astype(BF16)
        m_ref[place, :] = (normed * mg_ref[0:1, :] + ms_ref[0:1, :]).astype(BF16)
    xq_ref[...] = x_ref[rows(me_ref[2], block_len), :]
    copies[-1].wait()
    project_rows(0, tok_shape, me_ref, seg_ref, lambda j: w_ref[j], b_ref[...], a_ref, p_refs, proj_ref, True)


def project_body(layer, tok_shape, me_ref, *refs):
    seq_count, block_len, width = tok_shape
    x_ref, seg_ref, *refs = refs
    u_refs, refs = refs[:4], refs[4:]
    ob_ref, db_ref, ag_ref, as_ref, mg_ref, ms_ref, w_ref, b_ref, x_out, xq_ref, a_ref, m_ref, *p_refs, proj_ref = refs
    tensor = me_ref[2]
    shift = ob_ref[layer - 1 : layer, :] + db_ref[layer - 1 : layer, :]
    for k in range(4):
        place = rows(wrap4(tensor - k), block_len)
        value = x_ref[place, :] + u_refs[k][...].astype(F32) + shift
        x_out[place, :] = value
        if k == 0:
            xq_ref[...] = value
        normed, _ = normalize(value)
        a_ref[place, :] = (normed * ag_ref[layer : layer + 1, :] + as_ref[layer : layer + 1, :]).astype(BF16)
        m_ref[place, :] = (normed * mg_ref[layer : layer + 1, :] + ms_ref[layer : layer + 1, :]).astype(BF16)
    project_rows(layer, tok_shape, me_ref, seg_ref, lambda j: w_ref[0, j], b_ref[0], a_ref, p_refs, proj_ref, False)


def gather_pieces(me_ref, refs, targets, block_len, seg_target=None):
    chip, core = me_ref[0], me_ref[1]
    for k in range(4):
        owner = wrap4(chip - k)
        for side, ref in ((core, refs[k]), (1 - core, refs[4 + k])):
            place = rows(owner * 2 + side, block_len)
            for index, target in enumerate(targets):
                target[place, :] = ref[core, 0:block_len, index * LANES : (index + 1) * LANES]
            if seg_target is not None:
                row = ref[core, block_len : block_len + 16, :].astype(F32)[0:1, :]
                starts = row[:, 0:LANES] * 8.0 + row[:, LANES : 2 * LANES]
                seg_target[:, place] = jnp.broadcast_to(starts, (8, block_len))


def head_stack(values):
    lane = lax.broadcasted_iota(jnp.int32, values.shape, 1)
    zero = jnp.zeros_like(values)
    return jnp.concatenate(
        [jnp.where(lane < HEAD, values, zero), jnp.where(lane >= HEAD, values, zero)], axis=0
    )


def own_halves(product, width):
    return jnp.concatenate([product[0:HEAD, 0:width], product[HEAD:, width : 2 * width]], axis=0)


def chances_t(q_ref, k_ref, seg_ref, step, chunk):
    start, keys = step * chunk, (step + 1) * chunk
    stacked = head_stack(q_ref[start:keys, :]) * jnp.asarray(HEAD ** (-0.5), BF16)
    scores = matmul_nt(k_ref[0:keys, :], stacked)
    key_place = lax.broadcasted_iota(jnp.int32, (keys, 2 * chunk), 0).astype(F32)
    query_place = (lax.broadcasted_iota(jnp.int32, (1, 2 * chunk), 1) & (chunk - 1)).astype(F32) + start
    seg_row = seg_ref[0:1, start:keys]
    seg_row = jnp.concatenate([seg_row, seg_row], axis=1)
    allowed = (key_place >= seg_row) & (key_place <= query_place)
    scores = jnp.where(allowed, scores, -1e30)
    raised = jnp.exp(scores - jnp.max(scores, axis=0, keepdims=True))
    total = jnp.sum(raised, axis=0, keepdims=True)
    return raised * (1.0 / total), stacked


def attend_body(block_len, chunk, me_ref, *refs):
    piece_refs, refs = refs[:8], refs[8:]
    seg_out, qkv_ref, *refs = refs
    o_refs, refs = refs[:4], refs[4:]
    vt_ref, o_ref = refs
    q_ref, k_ref, v_ref = qkv_ref.at[0], qkv_ref.at[1], qkv_ref.at[2]
    gather_pieces(me_ref, piece_refs, (q_ref, k_ref, v_ref), block_len, seg_out)
    vt_ref[...] = v_ref[...].T
    length = q_ref.shape[0]
    for step in range(length // chunk):
        keys = (step + 1) * chunk
        chances, _ = chances_t(q_ref, k_ref, seg_out, step, chunk)
        mixed = matmul(vt_ref[:, 0:keys], chances.astype(BF16))
        o_ref[step * chunk : keys, :] = own_halves(mixed, chunk).T.astype(BF16)
    send_blocks(me_ref, o_ref, o_refs, block_len)


def send_blocks(me_ref, source, targets, block_len):
    chip = me_ref[0]
    for k in range(4):
        dest = wrap4(chip + k)
        for side in range(2):
            targets[k][side] = source[rows(dest * 2 + side, block_len), :]


def attend_both_body(block_len, chunk, with_out, me_ref, *refs):
    if with_out:
        piece_refs, refs = refs[:8], refs[8:]
    else:
        qkv_ref, *refs = refs
    grad_refs, refs = refs[:8], refs[8:]
    seg_ref, *refs = refs
    d_refs, refs = refs[:4], refs[4:]
    if with_out:
        qkv_ref, *refs = refs
    q_ref, k_ref, v_ref = qkv_ref.at[0], qkv_ref.at[1], qkv_ref.at[2]
    g_ref, t_ref, o_ref, dq_ref, dk_ref, dv_ref = refs
    if with_out:
        gather_pieces(me_ref, piece_refs, (q_ref, k_ref, v_ref), block_len)
    gather_pieces(me_ref, grad_refs, (g_ref,), block_len)
    length = q_ref.shape[0]
    t_ref[0] = k_ref[...].T
    if with_out:
        t_ref[1] = v_ref[...].T
    dk_ref[...] = jnp.zeros_like(dk_ref)
    dv_ref[...] = jnp.zeros_like(dv_ref)
    for step in range(length // chunk):
        start, keys = step * chunk, (step + 1) * chunk
        chances, stacked = chances_t(q_ref, k_ref, seg_ref, step, chunk)
        low = chances.astype(BF16)
        if with_out:
            mixed = matmul(t_ref[1, :, 0:keys], low)
            o_ref[start:keys, :] = own_halves(mixed, chunk).T.astype(BF16)
        grads = head_stack(g_ref[start:keys, :])
        chance_grad = matmul_nt(v_ref[0:keys, :], grads)
        delta = jnp.sum(chances * chance_grad, axis=0, keepdims=True)
        score_grad = (chances * (chance_grad - delta)).astype(BF16)
        dv_ref[0:keys, :] += matmul(low, grads)
        dk_ref[0:keys, :] += matmul(score_grad, stacked)
        query = matmul(t_ref[0, :, 0:keys], score_grad)
        dq_ref[start:keys, :] = own_halves(query, chunk).T * HEAD ** (-0.5)
    chip = me_ref[0]
    for k in range(4):
        dest = wrap4(chip + k)
        for side in range(2):
            place = rows(dest * 2 + side, block_len)
            spots = (lax.broadcasted_iota(jnp.int32, (1, block_len), 1) + (dest * 2 + side) * block_len).astype(F32)
            tables = rotary_rows(spots - seg_ref[0:1, place])
            d_refs[k][side, :, 0:LANES] = rotate(dq_ref[place, :], tables, True).astype(BF16)
            d_refs[k][side, :, LANES : 2 * LANES] = rotate(dk_ref[place, :], tables, True).astype(BF16)
            d_refs[k][side, :, 2 * LANES : 3 * LANES] = dv_ref[place, :].astype(BF16)
            if with_out:
                d_refs[k][side, :, 3 * LANES :] = o_ref[place, :]


def land_heads(me_ref, refs, target, block_len, groups, first=0):
    chip, core = me_ref[0], me_ref[1]
    for k in range(4):
        place = rows(wrap4(chip - k), block_len)
        mine, other = refs[k][core], refs[4 + k][core]
        is_low = core == 0
        for group in range(groups):
            span = slice((first + group) * LANES, (first + group + 1) * LANES)
            at = group * 2 * LANES
            target[place, at : at + LANES] = jnp.where(is_low, mine[:, span], other[:, span])
            target[place, at + LANES : at + 2 * LANES] = jnp.where(is_low, other[:, span], mine[:, span])


def combine_body(block_len, fused, me_ref, *refs):
    piece_refs, refs = refs[:8], refs[8:]
    w_ref, *refs = refs
    if fused:
        g_ref, down_ref, *refs = refs
    else:
        part_ref, *refs = refs
    o_ref, *refs = refs
    q_refs, scr = refs[:4], refs[4]
    tensor = me_ref[2]
    land_heads(me_ref, piece_refs, o_ref, block_len, 1, 3 if fused else 0)
    part = matmul(g_ref[...], down_ref[0]) if fused else part_ref[...]
    scr[...] = (matmul(o_ref[...], w_ref[0]) + part).astype(BF16)
    for k in range(4):
        q_refs[k][...] = scr[rows(wrap4(tensor + k), block_len), :]


def send_grad_body(block_len, me_ref, x_ref, w_ref, *refs):
    chip, tensor = me_ref[0], me_ref[2]
    quarter_ref, *refs = refs
    quarter_ref[...] = x_ref[rows(tensor, block_len), :]
    for k in range(4):
        value = x_ref[rows(wrap4(chip + k), block_len), :].astype(BF16)
        grad = matmul_nt(value, w_ref[0]).astype(BF16)
        for pair in range(2):
            refs[k][pair] = grad[:, pair * LANES : (pair + 1) * LANES]


def join_body(block_len, me_ref, *refs):
    q_refs, refs = refs[:4], refs[4:]
    w_ref, r_ref, *g_refs = refs
    chip, tensor = me_ref[0], me_ref[2]
    for k in range(4):
        r_ref[rows(wrap4(tensor - k), block_len), :] = q_refs[k][...]
    for k in range(4):
        value = r_ref[rows(wrap4(chip + k), block_len), :]
        grad = matmul_nt(value, w_ref[0]).astype(BF16)
        for pair in range(2):
            g_refs[k][pair] = grad[:, pair * LANES : (pair + 1) * LANES]


def project_back_body(block_len, layer, me_ref, *refs):
    piece_refs, refs = refs[:8], refs[8:]
    w_ref, dm_ref, ag_ref, mg_ref, dp_ref, da_ref, bias_ref, *refs = refs
    q_refs, scr = refs[:4], refs[4]
    tensor = me_ref[2]
    land_heads(me_ref, piece_refs, dp_ref, block_len, 3)
    for j in range(3):
        span = slice(j * 2 * LANES, (j + 1) * 2 * LANES)
        bias_ref[j : j + 1, :] = jnp.sum(dp_ref[:, span].astype(F32), axis=0, keepdims=True)
    total = None
    for j in range(3):
        term = matmul_nt(dp_ref[:, j * 2 * LANES : (j + 1) * 2 * LANES], w_ref[0, j])
        total = term if total is None else total + term
    da_ref[...] = total.astype(BF16)
    scr[...] = (total * ag_ref[layer : layer + 1, :] + dm_ref[...] * mg_ref[layer : layer + 1, :]).astype(BF16)
    for k in range(4):
        q_refs[k][...] = scr[rows(wrap4(tensor + k), block_len), :]


def norm_back_body(me_ref, *refs):
    e_refs, refs = refs[:4], refs[4:]
    x_ref, dy_ref, dx_ref, low_ref, bias_ref = refs
    upstream = dy_ref[...]
    total = e_refs[0][...].astype(F32)
    for k in range(1, 4):
        total = total + e_refs[k][...].astype(F32)
    normed, factor = normalize(x_ref[...])
    inner = jnp.mean(total * normed, axis=-1, keepdims=True)
    result = upstream + factor * (total - jnp.mean(total, axis=-1, keepdims=True) - normed * inner)
    dx_ref[...] = result
    low_ref[...] = result.astype(BF16)
    bias_ref[...] = jnp.sum(upstream, axis=0, keepdims=True)


def gains_body(me_ref, x_ref, da_ref, dm_ref, out_ref):
    normed, _ = normalize(x_ref[...])
    da = da_ref[...].astype(F32)
    dm = dm_ref[...]
    out_ref[0:1, :] = jnp.sum(da * normed, axis=0, keepdims=True)
    out_ref[1:2, :] = jnp.sum(da, axis=0, keepdims=True)
    out_ref[2:3, :] = jnp.sum(dm * normed, axis=0, keepdims=True)
    out_ref[3:4, :] = jnp.sum(dm, axis=0, keepdims=True)


def gelu_parts(hidden):
    cdf = 0.5 * (1.0 + lax.erf(hidden * (0.5**0.5)))
    density = jnp.exp(-0.5 * hidden * hidden) * 0.3989422804014327
    return cdf, density


def feed_body(layer, me_ref, m_ref, up_ref, ub_ref, down_ref, g_ref, slope_ref, part_ref):
    size = 2 * LANES
    for step in range(up_ref.shape[2] // size):
        span = slice(step * size, (step + 1) * size)
        hidden = matmul(m_ref[...], up_ref[0, :, span]) + ub_ref[layer : layer + 1, span]
        cdf, density = gelu_parts(hidden)
        g_ref[:, span] = (hidden * cdf).astype(BF16)
        slope_ref[:, span] = cdf + hidden * density
    part_ref[...] = matmul(g_ref[...], down_ref[0])


def feed_back_body(me_ref, r_ref, slope_ref, up_ref, down_ref, dh_ref, dm_ref, bias_ref):
    size = 2 * LANES
    for step in range(down_ref.shape[1] // size):
        span = slice(step * size, (step + 1) * size)
        grad = matmul_nt(r_ref[...], down_ref[0, span, :]) * slope_ref[:, span]
        bias_ref[:, span] = jnp.sum(grad, axis=0, keepdims=True)
        dh_ref[:, span] = grad.astype(BF16)
    dm_ref[...] = matmul_nt(dh_ref[...], up_ref[0])


def feed_both_body(layer, me_ref, m_ref, dy_ref, up_ref, ub_ref, down_ref, g_ref, r_ref, dh_ref, dm_ref, bias_ref):
    size = 2 * LANES
    r_ref[...] = dy_ref[...].astype(BF16)
    for step in range(up_ref.shape[2] // size):
        span = slice(step * size, (step + 1) * size)
        hidden = matmul(m_ref[...], up_ref[0, :, span]) + ub_ref[layer : layer + 1, span]
        cdf, density = gelu_parts(hidden)
        g_ref[:, span] = (hidden * cdf).astype(BF16)
        grad = matmul_nt(r_ref[...], down_ref[0, span, :]) * (cdf + hidden * density)
        bias_ref[:, span] = jnp.sum(grad, axis=0, keepdims=True)
        dh_ref[:, span] = grad.astype(BF16)
    dm_ref[...] = matmul_nt(dh_ref[...], up_ref[0])


def feed_weights_body(me_ref, m_ref, dh_ref, g_ref, r_ref, keep_ref, send_ref):
    core = me_ref[1]
    half = m_ref.shape[1] // 2
    for side, out in ((core, keep_ref), (1 - core, send_ref)):
        out[0:half, :] = matmul_tn(m_ref[:, rows(side, half)], dh_ref[...]).astype(BF16)
        out[half:, :] = matmul_tn(g_ref[:, rows(side, half)], r_ref[...]).astype(BF16)


def head_weights_body(me_ref, a_ref, dp_ref, o_ref, r_ref, keep_ref, send_ref):
    core = me_ref[1]
    half = a_ref.shape[1] // 2
    wide = dp_ref.shape[1]
    for side, out in ((core, keep_ref), (1 - core, send_ref)):
        out[:, 0:wide] = matmul_tn(a_ref[:, rows(side, half)], dp_ref[...]).astype(BF16)
        grad = matmul_tn(o_ref[:, rows(side, LANES)], r_ref[...]).astype(BF16)
        for part in range(4):
            out[part * LANES : (part + 1) * LANES, wide:] = grad[:, part * 2 * LANES : (part + 1) * 2 * LANES]


def near_far(place):
    return place ^ 1, 3 - place


def halve_feed_body(me_ref, keep_ref, came_ref, *refs):
    outs, scr = refs[:4], refs[4]
    scr[...] = (keep_ref[...].astype(F32) + came_ref[...].astype(F32)).astype(BF16)
    place = me_ref[3]
    near, far = near_far(place)
    half = scr.shape[0] // 2
    size = outs[0].shape[0] // 4
    orders = ((place, far), (near, 3 - near), (4 + place, 4 + near), (4 + far, 4 + (far ^ 1)))
    for ref, order in zip(outs, orders):
        for index, block in enumerate(order):
            at = 2 * size * index
            ref[at : at + size, :] = scr[rows(block, size), :]
            ref[at + size : at + 2 * size, :] = scr[pl.ds(pl.multiple_of(half + block * size, size), size), :]


def halve_head_body(me_ref, a_keep, a_came, b_keep, b_came, keep_ref, came_ref, *refs):
    feed_ref, head_ref, next_ref, wrap_ref, scr = refs
    scr[...] = (keep_ref[...].astype(F32) + came_ref[...].astype(F32)).astype(BF16)
    high = a_keep.shape[0] // 2
    for index, (keep, came, out) in enumerate(((a_keep, a_came, wrap_ref), (b_keep, b_came, next_ref))):
        total = (keep[...].astype(F32) + came[...].astype(F32)).astype(BF16)
        feed_ref[index * high : (index + 1) * high, :] = total[0:high, :]
        out[0:high, :] = total[high:, :]
    place = me_ref[3]
    near, far = near_far(place)
    size = scr.shape[0] // 8
    for ref, start, order in (
        (head_ref, 0, (place, far, 4 + place, 4 + near)),
        (next_ref, high, (near, 3 - near)),
        (wrap_ref, high, (4 + far, 4 + (far ^ 1))),
    ):
        for index, block in enumerate(order):
            at = start + size * index
            ref[at : at + size, :] = scr[rows(block, size), :]


def halve_last_body(me_ref, feed_ref, head_ref, next_came, wrap_came, *outs):
    feed_out, head_out, next_ref, wrap_ref = outs
    high = feed_ref.shape[0] // 2
    for index, came in enumerate((wrap_came, next_came)):
        span = slice(index * high, (index + 1) * high)
        feed_out[span, :] = (feed_ref[span, :].astype(F32) + came[0:high, :].astype(F32)).astype(BF16)
    low = head_ref.shape[0] // 4
    for index, (came, send) in enumerate(((next_came, wrap_ref), (wrap_came, next_ref))):
        span = slice(index * 2 * low, (index + 1) * 2 * low)
        total = (head_ref[span, :].astype(F32) + came[high:, :].astype(F32)).astype(BF16)
        head_out[index * low : (index + 1) * low, :] = total[0:low, :]
        send[...] = total[low:, :]


def line_up_body(axis, me_ref, *refs):
    size = refs[0].shape[0]
    for k in range(4):
        refs[4][rows(wrap4(me_ref[axis] - k), size), :] = refs[k][...]


def add_packs_body(me_ref, feed_keep, feed_came, head_keep, head_came, out_ref):
    high = feed_keep.shape[0]
    out_ref[0:high, :] = (feed_keep[...].astype(F32) + feed_came[...].astype(F32)).astype(BF16)
    out_ref[high:, :] = (head_keep[...].astype(F32) + head_came[...].astype(F32)).astype(BF16)


def merge_body(me_ref, feed_ref, head_ref, wrap_came, next_came, small_ref, *refs):
    out_refs, scr = refs[:4], refs[4]
    low = wrap_came.shape[0]
    for index, came in enumerate((wrap_came, next_came)):
        span = slice(index * low, (index + 1) * low)
        scr[span, :] = (head_ref[span, :].astype(F32) + came[...].astype(F32)).astype(BF16)
    few = low // 2
    for k in range(4):
        part = wrap4(me_ref[0] + k)
        way, sub = part >> 1, part & 1
        for index in range(2):
            at = pl.multiple_of((2 * way + index) * low + sub * few, few)
            out_refs[k][index * few : (index + 1) * few, :] = feed_ref[pl.ds(at, few), :]
        at = pl.multiple_of(way * low + sub * few, few)
        out_refs[k][2 * few : 3 * few, :] = scr[pl.ds(at, few), :]
        out_refs[k][3 * few :, :] = small_ref[...]


def settle_body(me_ref, *refs):
    in_refs, (first_ref, second_ref, shared_ref, local_ref) = refs[:4], refs[4:]
    even = in_refs[0][...].astype(F32) + in_refs[2][...].astype(F32)
    odd = in_refs[1][...].astype(F32) + in_refs[3][...].astype(F32)
    total = (even + odd).astype(BF16)
    few, count = first_ref.shape[0] // 3, shared_ref.shape[0]
    for weight in range(3):
        for index, ref in enumerate((first_ref, second_ref)):
            at = (2 * weight + index) * few
            ref[weight * few : (weight + 1) * few, :] = total[at : at + few, :]
    shared_ref[...] = total[6 * few : 6 * few + count, :]
    local_ref[...] = total[6 * few + count :, :]


def flush(held, outs, layer, sems):
    copies = [pltpu.make_async_copy(a, b.at[layer], sems.at[i]) for i, (a, b) in enumerate(zip(held, outs))]
    return copies


def unpack_body(few, me_ref, *refs):
    outs, held, sems = refs[24:28], refs[28:32], refs[32]
    up_ref, down_ref, qkv_ref, out_ref = held
    copies = flush(held, outs, 0, sems)
    chip, core, place_z = me_ref[0], me_ref[1], me_ref[3]
    size = 2 * LANES
    half = up_ref.shape[0] // 2
    for weight in range(3):
        for side, group in ((core, refs[:10]), (1 - core, refs[10:20])):
            for along, me in ((0, place_z), (1, chip)):
                pieces = group[5 * along : 5 * along + 5]
                spans = [(pieces[0], me, 0), (pieces[1], me ^ 1, 0), (pieces[2], 3 - me, 0)]
                spans += [(pieces[3], me ^ 2, 0), (pieces[4], me ^ 2, 2)]
                for ref, owner, first in spans:
                    for index in range(ref.shape[0] // (3 * few)):
                        z, x = (owner, first + index) if along == 0 else (first + index, owner)
                        start = (3 * index + weight) * few
                        value = ref[start : start + few, :].astype(F32)
                        row = (z + 4 * (x >> 1)) * (4 * few) + (x & 1) * (2 * few) + along * few
                        place = pl.ds(pl.multiple_of(row + side * half, few), few)
                        if weight < 2:
                            held[weight][place, :] = value
                        else:
                            for j in range(3):
                                qkv_ref[j, place, :] = value[:, j * size : (j + 1) * size]
                            inner = pl.ds(pl.multiple_of((row & (LANES - 1)) + side * LANES, few), few)
                            lanes = pl.ds(pl.multiple_of((row >> 7) * size, size), size)
                            out_ref[inner, lanes] = value[:, 3 * size :]
        for copy in copies[weight : weight + 1] if weight < 2 else copies[2:]:
            copy.start()
    for copy in copies:
        copy.wait()


def unpack_whole_body(me_ref, mine_ref, other_ref, *refs):
    outs, held, sems = refs[:4], refs[4:8], refs[8]
    up_ref, down_ref, qkv_ref, out_ref = held
    copies = flush(held, outs, 1, sems)
    core = me_ref[1]
    size = 2 * LANES
    half = up_ref.shape[0] // 2
    for weight in range(3):
        for side, pack in ((core, mine_ref), (1 - core, other_ref)):
            place = rows(side, half)
            at = weight * half
            if weight < 2:
                held[weight][place, :] = pack[at : at + half, :].astype(F32)
            else:
                for j in range(3):
                    qkv_ref[j, place, :] = pack[at:, j * size : (j + 1) * size].astype(F32)
                for part in range(4):
                    start = at + part * LANES
                    out_ref[rows(side, LANES), part * size : (part + 1) * size] = pack[
                        start : start + LANES, 3 * size :
                    ].astype(F32)
        for copy in copies[weight : weight + 1] if weight < 2 else copies[2:]:
            copy.start()
    for copy in copies:
        copy.wait()


def pack_small_body(me_ref, *refs):
    ins, small_ref = refs[:8], refs[8]
    width = small_ref.shape[1]
    blank = jnp.zeros((1, width), F32)
    shared = [ins[0][...], ins[1][...], ins[2][...], ins[3][...]] + [blank] * 6
    small_ref[0:16, :] = jnp.concatenate(shared, axis=0).astype(BF16)
    local = [ins[6][...], ins[7][...]]
    for ref in ins[4:6]:
        values = ref[...]
        flat = [values[j : j + 1, :] for j in range(3)]
        local.append(jnp.concatenate(flat + [jnp.zeros((1, width - 3 * values.shape[1]), F32)], axis=1))
    small_ref[16:32, :] = jnp.concatenate(local + [blank] * 12, axis=0).astype(BF16)


def add_body(count, me_ref, *refs):
    total = refs[0][...].astype(F32)
    for ref in refs[1:count]:
        total = total + ref[...].astype(F32)
    refs[count][...] = total.astype(refs[count].dtype)


def small_out_body(me_ref, small_ref, *outs):
    shared, local = small_ref[0:16, :], small_ref[16:32, :]
    for index in range(5):
        outs[index][0:1, :] = shared[index : index + 1, :]
        outs[index][1:2, :] = shared[index + 5 : index + 6, :]
    outs[5][...] = local[0:2, :]
    size = outs[6].shape[2]
    for layer in range(2):
        for j in range(3):
            outs[6][layer, j : j + 1, :] = local[2 + layer : 3 + layer, j * size : (j + 1) * size]


def place_body(block_len, with_sum, me_ref, *refs):
    q_refs, refs = refs[:4], refs[4:]
    tensor = me_ref[2]
    out_ref = refs[-1]
    if with_sum:
        x_ref, ob_ref, db_ref = refs[:3]
        shift = ob_ref[1:2, :] + db_ref[1:2, :]
    for k in range(4):
        place = rows(wrap4(tensor - k), block_len)
        value = q_refs[k][...].astype(F32)
        out_ref[place, :] = x_ref[place, :] + value + shift if with_sum else value


def chip_turn(shift):
    return [(2 * x + c, 2 * ((x + shift) % 4) + c) for x in range(4) for c in range(2)]


CORE_SWAP = [(i, i ^ 1) for i in range(8)]


def over_chips(pieces, beside=()):
    mine, beside = lax.optimization_barrier((over_x(pieces), beside))
    return mine + [swap_core(piece) for piece in mine], beside


def ring_turn(shift):
    return [(i, (i + shift) % 4) for i in range(4)]


def over_tensor(pieces):
    return [pieces[0]] + [lax.ppermute(pieces[k], "tensor", ring_turn(k)) for k in range(1, 4)]


def share_tensor(piece):
    return over_tensor([piece] * 4)


def over_dp(pieces):
    return [pieces[0]] + [lax.ppermute(pieces[k], "dp", ring_turn(k)) for k in range(1, 4)]


def over_x(pieces):
    return [pieces[0]] + [lax.ppermute(pieces[k], "ctx", chip_turn(k)) for k in range(1, 4)]


def swap_core(piece):
    return lax.ppermute(piece, "ctx", CORE_SWAP)


NEXT_PAIR = [(0, 1), (1, 0), (2, 3), (3, 2)]
WRAP_PAIR = [(0, 3), (3, 0), (1, 2), (2, 1)]


def both_ways(to_next, to_wrap):
    return lax.ppermute(to_next, "dp", NEXT_PAIR), lax.ppermute(to_wrap, "dp", WRAP_PAIR)


def chips_of(pairs):
    return [(2 * a + c, 2 * b + c) for a, b in pairs for c in range(2)]


def spread_near(piece, axis):
    name, move = ("dp", lambda pairs: pairs) if axis == "dp" else ("ctx", chips_of)
    return [piece] + [lax.ppermute(piece, name, move(pairs)) for pairs in (NEXT_PAIR, WRAP_PAIR)]


def spread_far(pieces, axis):
    name, move = ("dp", lambda pairs: pairs) if axis == "dp" else ("ctx", chips_of)
    half = pieces[0].shape[0] // 2
    return pieces + [
        lax.ppermute(pieces[1][:half], name, move(WRAP_PAIR)),
        lax.ppermute(pieces[2][half:], name, move(NEXT_PAIR)),
    ]


def tie(first, second):
    return lax.optimization_barrier((first, second))


def after(values, token):
    return lax.optimization_barrier((values, token))[0]


def add_up(pieces):
    total = pieces[0].astype(F32)
    for piece in pieces[1:]:
        total = total + piece.astype(F32)
    return total


def on_device(
    inputs,
    segments,
    attn_gain,
    attn_shift,
    mlp_gain,
    mlp_shift,
    qkv_weight,
    qkv_bias,
    out_weight,
    out_bias,
    up_weight,
    up_bias,
    down_weight,
    down_bias,
    cotangent,
):
    seq_count, block_len, width = inputs.shape
    tokens = seq_count * block_len
    inner = qkv_weight.shape[3]
    hidden = up_weight.shape[2]
    length = block_len * 8
    chunk = 256
    place = lax.axis_index("ctx")
    me = jnp.stack([place // 2, place % 2, lax.axis_index("tensor"), lax.axis_index("dp")]).astype(jnp.int32)
    x0 = inputs.reshape(tokens, width)
    dy1 = cotangent.reshape(tokens, width)
    tok_shape = inputs.shape
    wide = shape_of((tokens, width), BF16)
    norms = (attn_gain, attn_shift, mlp_gain, mlp_shift)

    def project_first(x):
        sources = [x, segments, *norms, qkv_weight, qkv_bias]
        held = [v.shape for v in sources[:6]] + [qkv_weight.shape[1:], qkv_bias.shape[1:]]
        piece = shape_of((2, block_len + 16, 3 * LANES), BF16)
        return run(
            functools.partial(project_first_body, tok_shape),
            me,
            [(v, pl.BlockSpec(memory_space=pltpu.HBM)) for v in sources],
            [shape_of((block_len, width), F32), wide, wide] + [piece] * 4,
            scratch=[pltpu.VMEM((tokens, 3 * inner), F32)]
            + [pltpu.VMEM(size, v.dtype) for size, v in zip(held, sources)]
            + [pltpu.SemaphoreType.DMA((11,))],
            name="norm_project",
            limit=62,
        )

    def project(layer, x, extra):
        piece = shape_of((2, block_len, 3 * LANES), BF16)
        return run(
            functools.partial(project_body, layer, tok_shape),
            me,
            [x, segments, *extra, *norms]
            + [(qkv_weight, layer_spec(qkv_weight, layer)), (qkv_bias, layer_spec(qkv_bias, layer))],
            [shape_of((tokens, width), F32), shape_of((block_len, width), F32), wide, wide] + [piece] * 4,
            scratch=[pltpu.VMEM((tokens, 3 * inner), F32)],
            name="norm_project",
            limit=24,
        )

    def feed(layer, m):
        return run(
            functools.partial(feed_body, layer),
            me,
            [m, (up_weight, layer_spec(up_weight, layer)), up_bias, (down_weight, layer_spec(down_weight, layer))],
            [shape_of((tokens, hidden), BF16), shape_of((tokens, hidden), F32), shape_of((tokens, width), F32)],
            name="feed", limit=24,
        )

    def feed_back(layer, r, slope):
        return run(
            feed_back_body,
            me,
            [r, slope, (up_weight, layer_spec(up_weight, layer)), (down_weight, layer_spec(down_weight, layer))],
            [shape_of((tokens, hidden), BF16), shape_of((tokens, width), F32), shape_of((1, hidden), F32)],
            name="feed_back", limit=24,
        )

    def feed_both(layer, m, dy):
        return run(
            functools.partial(feed_both_body, layer),
            me,
            [m, dy, (up_weight, layer_spec(up_weight, layer)), up_bias, (down_weight, layer_spec(down_weight, layer))],
            [shape_of((tokens, hidden), BF16), wide, shape_of((tokens, hidden), BF16)]
            + [shape_of((tokens, width), F32), shape_of((1, hidden), F32)],
            name="feed_both", limit=24,
        )

    def combine(layer, pieces, part, active=None):
        fused = part is None
        got = run(
            functools.partial(combine_body, block_len, fused),
            me,
            [*pieces, (out_weight, layer_spec(out_weight, layer))]
            + ([active, (down_weight, layer_spec(down_weight, layer))] if fused else [part]),
            [shape_of((tokens, inner), BF16)] + [shape_of((block_len, width), BF16)] * 4,
            scratch=[pltpu.VMEM((tokens, width), BF16)],
            name="combine", limit=20,
        )
        return got[0], got[1:]

    def add_all(values, dtype=BF16):
        out = shape_of(values[0].shape, dtype)
        return run(functools.partial(add_body, len(values)), me, values, [out], name="add_all", limit=16)[0]

    def line_up(axis, values):
        high, wide_here = values[0].shape
        out = shape_of((high * 4, wide_here), BF16)
        return run(functools.partial(line_up_body, axis), me, values, [out], name="line_up", limit=8)[0]

    seq_bf16 = pltpu.VMEM((length, LANES), BF16)
    seq_f32 = pltpu.VMEM((length, LANES), F32)
    o_shapes = [shape_of((2, block_len, LANES), BF16)] * 4

    def attend_both(pieces, grads, seg_rows, with_out):
        return run(
            functools.partial(attend_both_body, block_len, chunk, with_out),
            me,
            [*pieces, *grads, seg_rows],
            [shape_of((2, block_len, (4 if with_out else 3) * LANES), BF16)] * 4,
            scratch=([pltpu.VMEM((3, length, LANES), BF16)] if with_out else [])
            + [seq_bf16, pltpu.VMEM((2, LANES, length), BF16), seq_bf16]
            + [seq_f32] * 3,
            name="attend_both", limit=24,
        )

    def project_back(layer, pieces, dm):
        got = run(
            functools.partial(project_back_body, block_len, layer),
            me,
            [*pieces, (qkv_weight, layer_spec(qkv_weight, layer)), dm, attn_gain, mlp_gain],
            [shape_of((tokens, 3 * inner), BF16), wide, shape_of((3, inner), F32)]
            + [shape_of((block_len, width), BF16)] * 4,
            scratch=[pltpu.VMEM((tokens, width), BF16)],
            name="project_back", limit=24,
        )
        return got[0], got[1], got[2], got[3:]

    def norm_back(pieces, x, dy):
        quarter = shape_of((block_len, width), F32)
        return run(
            norm_back_body,
            me,
            [*pieces, x, dy],
            [quarter, shape_of((block_len, width), BF16), shape_of((1, width), F32)],
            name="norm_back",
            limit=10,
        )

    def gains(x, da, dm):
        return run(gains_body, me, [x, da, dm], [shape_of((4, width), F32)], name="gains", limit=16)[0]

    half = width // 2
    columns = [[8 * z + 2 * chip + core for z in range(4) for chip in range(4)] for core in range(2)]

    def feed_weights(m, dh, active, r):
        pack = shape_of((2 * half, width), BF16)
        return run(feed_weights_body, me, [m, dh, active, r], [pack] * 2, name="feed_weights", limit=24)

    def head_weights(attn_in, dproj, attended, r):
        pack = shape_of((half, width), BF16)
        return run(head_weights_body, me, [attn_in, dproj, attended, r], [pack] * 2, name="head_weights", limit=20)

    x0_quarter, a0, m0, *pieces = project_first(x0)
    fed0 = feed(0, m0)
    pieces0, (active0, slope0, part0) = over_chips(pieces, fed0)
    got = run(
        functools.partial(attend_body, block_len, chunk),
        me,
        pieces0,
        [shape_of((8, length), F32), shape_of((3, length, LANES), BF16)] + o_shapes,
        scratch=[pltpu.VMEM((LANES, length), BF16), seq_bf16],
        name="attend", limit=20,
    )
    seg_rows, qkv0 = got[:2]
    out0, _ = over_chips(got[2:])
    attended0, u0 = combine(0, out0, part0)
    dy1_quarter, *grads1 = run(
        functools.partial(send_grad_body, block_len),
        me,
        [after(dy1, u0[0]), (out_weight, layer_spec(out_weight, 1))],
        [shape_of((block_len, width), F32)] + o_shapes,
        name="out_back", limit=14,
    )
    grads1 = over_x(grads1)
    u0 = share_tensor(add_up(over_tensor(u0)).astype(BF16))
    u0, grads1 = tie(u0, grads1)
    grads1_other = [swap_core(piece) for piece in grads1]

    x1, x1_quarter, a1, m1, *pieces = project(1, x0, [*u0, out_bias, down_bias])
    fed1 = feed_both(1, m1, dy1)
    pieces1, ((active1, r1, dh1, dm1, up_b1), grads1_other) = over_chips(pieces, (fed1, grads1_other))
    got = attend_both(pieces1, grads1 + grads1_other, seg_rows, True)
    feed_pack1 = feed_weights(after(m1, got[0]), dh1, active1, r1)
    back1, feed_pack1 = over_chips(got, feed_pack1)
    dproj1, da1, qkv_b1, e1 = project_back(1, back1, dm1)
    feed_keep, feed_send, back1 = after((*feed_pack1, back1), e1[0])
    feed_came = swap_core(feed_send)
    attended1, u1 = combine(1, back1, None, active1)
    head_keep, head_send = head_weights(a1, dproj1, attended1, r1)
    pack1 = run(
        add_packs_body,
        me,
        [feed_keep, feed_came, head_keep, swap_core(head_send)],
        [shape_of((3 * half, width), BF16)],
        name="add_packs",
        limit=28,
    )[0]
    e1, (u1, pack1) = tie(over_tensor(e1), (u1, pack1))
    part1 = lax.psum_scatter(pack1, ("dp", "ctx"), axis_index_groups=columns, tiled=True)
    dx1, low1, bias1 = norm_back(e1, x1_quarter, dy1_quarter)
    gains1 = gains(after(x1, low1), da1, dm1)
    quarters, gains1 = tie(share_tensor(low1), gains1)

    r0, *grads0 = run(
        functools.partial(join_body, block_len),
        me,
        [*quarters, (out_weight, layer_spec(out_weight, 0))],
        [wide] + o_shapes,
        name="join_out_back", limit=14,
    )
    dh0, dm0, up_b0 = feed_back(0, r0, slope0)
    grads0, (dh0, dm0) = over_chips(grads0, (dh0, dm0))
    back0 = attend_both([qkv0], grads0, seg_rows, False)
    feed_keep, feed_send = feed_weights(after(m0, back0[0]), dh0, active0, r0)
    way = shape_of((half // 2, width), BF16)
    a_keep, a_send, b_keep, b_send = run(
        halve_feed_body,
        me,
        [feed_keep, swap_core(feed_send)],
        [way] * 4,
        scratch=[pltpu.VMEM((2 * half, width), BF16)],
        name="halve_feed",
        limit=16,
    )
    u1 = over_tensor(after(u1, feed_keep))
    back0, (a_keep, a_send, b_keep, b_send) = over_chips(back0, (a_keep, a_send, b_keep, b_send))
    a_came, b_came = both_ways(a_send, b_send)
    dproj0, da0, qkv_b0, e0 = project_back(0, back0, dm0)
    head_keep, head_send = head_weights(a0, dproj0, attended0, r0)
    e0 = after(e0, head_keep)
    feed_sums, head_sums, to_next, to_wrap = run(
        halve_head_body,
        me,
        [a_keep, a_came, b_keep, b_came, head_keep, swap_core(head_send)],
        [way] * 4,
        scratch=[pltpu.VMEM((half, width), BF16)],
        name="halve_head",
        limit=16,
    )
    gains0 = gains(after(x0, to_next), da0, dm0)
    next_came, wrap_came = both_ways(to_next, to_wrap)
    e0, (gains0, part1, u1, next_came, wrap_came) = tie(over_tensor(e0), (gains0, part1, u1, next_came, wrap_came))
    pack1 = lax.all_gather(part1, ("dp", "ctx"), axis_index_groups=columns, tiled=True)
    low_way = shape_of((half // 8, width), BF16)
    feed_sums, head_sums, to_next, to_wrap = run(
        halve_last_body,
        me,
        [feed_sums, head_sums, next_came, wrap_came],
        [way, shape_of((half // 4, width), BF16), low_way, low_way],
        name="halve_last",
        limit=8,
    )
    next_came, wrap_came = both_ways(to_next, to_wrap)
    dx0, low0, bias0 = norm_back(after(e0, to_next), x0_quarter, dx1)
    last = share_tensor(low0)
    small = run(
        pack_small_body,
        me,
        [gains0, bias0, gains1, bias1, qkv_b0, qkv_b1, up_b0, up_b1],
        [shape_of((32, width), BF16)],
        name="pack_small",
        limit=8,
    )[0]

    few = half // 32
    cut = run(
        merge_body,
        me,
        [feed_sums, head_sums, wrap_came, next_came, small],
        [shape_of((6 * few + 32, width), BF16)] * 4,
        scratch=[pltpu.VMEM((half // 4, width), BF16)],
        name="merge",
        limit=8,
    )
    cut, last = tie(over_x(cut), last)
    row_block = shape_of((16, width), BF16)
    piece = shape_of((3 * few, width), BF16)
    first, second, shared, local = run(settle_body, me, cut, [piece, piece, row_block, row_block], name="settle", limit=8)
    shared = [shared, lax.ppermute(shared, "tensor", NEXT_PAIR)]
    (first, second), (shared, pack1) = tie((over_x([first] * 4), over_dp([second] * 4)), (shared, pack1))
    first, second = line_up(0, first), line_up(3, second)
    near = (spread_near(first, "dp"), spread_near(second, "x"))
    pack1, last, u1, shared = after((pack1, last, u1, shared), second)

    heavy = [
        shape_of((2, width, hidden), F32),
        shape_of((2, hidden, width), F32),
        shape_of((2, 3, width, inner), F32),
        shape_of((2, inner, width), F32),
    ]
    in_place = pl.BlockSpec(memory_space=pl.ANY)
    held = [pltpu.VMEM(v.shape[1:], F32) for v in heavy] + [pltpu.SemaphoreType.DMA((4,))]
    first_outs = run(
        unpack_whole_body,
        me,
        [pack1, swap_core(pack1)],
        heavy,
        name="unpack_whole",
        limit=28,
        out_specs=[in_place] * 4,
        scratch=held,
    )
    u1 = share_tensor(add_up(u1).astype(BF16))
    near, first_outs = tie(near, first_outs)
    shared = add_all(after(shared, near[0][1]))
    shared = add_all([shared, lax.ppermute(shared, "tensor", WRAP_PAIR)])
    small = jnp.concatenate([shared, local], axis=0)
    for pairs in (NEXT_PAIR, WRAP_PAIR):
        small = add_all([small, lax.ppermute(small, "dp", pairs)])
    small = add_all([small, swap_core(small)], F32)
    row_pair = shape_of((2, width), F32)
    small = run(
        small_out_body, me, [small], [row_pair] * 6 + [shape_of((2, 3, inner), F32)], name="small_out", limit=8
    )
    tok_out = [shape_of((tokens, width), F32)]
    input_grad = run(functools.partial(place_body, block_len, False), me, last, tok_out, name="place_grad", limit=16)[0]
    output = run(
        functools.partial(place_body, block_len, True),
        me,
        [*u1, x1, out_bias, down_bias],
        tok_out,
        name="place_output",
        limit=20,
    )[0]
    mine = spread_far(near[0], "dp") + spread_far(near[1], "x")
    other = [swap_core(v) for v in near[0] + near[1]]
    mine, (small, input_grad, output, other) = tie(mine, (small, input_grad, output, other))
    far = [swap_core(v) for v in mine[3:5] + mine[8:10]]
    other = other[0:3] + far[0:2] + other[3:6] + far[2:4]
    up_grad, down_grad, qkv_grad, out_grad = run(
        functools.partial(unpack_body, few),
        me,
        mine + other + [(v, in_place) for v in first_outs],
        heavy,
        name="unpack",
        limit=28,
        out_specs=[in_place] * 4,
        scratch=held,
        aliases={21 + index: index for index in range(4)},
    )
    return (
        output.reshape(tok_shape),
        input_grad.reshape(tok_shape),
        small[0],
        small[1],
        small[2],
        small[3],
        qkv_grad,
        small[6],
        out_grad,
        small[4],
        up_grad,
        small[5],
        down_grad,
        small[4],
    )


def solution(mesh):
    in_specs = (
        P("dp", "ctx", None),
        P("dp", "ctx"),
        P(),
        P(),
        P(),
        P(),
        P(None, None, None, "tensor"),
        P(None, None, "tensor"),
        P(None, "tensor", None),
        P(),
        P(None, None, "tensor"),
        P(None, "tensor"),
        P(None, "tensor", None),
        P(),
        P("dp", "ctx", None),
    )
    out_specs = (
        P("dp", "ctx", None),
        P("dp", "ctx", None),
        P(),
        P(),
        P(),
        P(),
        P(None, None, None, "tensor"),
        P(None, None, "tensor"),
        P(None, "tensor", None),
        P(),
        P(None, None, "tensor"),
        P(None, "tensor"),
        P(None, "tensor", None),
        P(),
    )
    return jax.shard_map(
        on_device, mesh=mesh, in_specs=in_specs, out_specs=out_specs, check_vma=False
    )
```

```python
import functools

import jax
import jax.numpy as jnp
from jax import lax
from jax.experimental import pallas as pl
from jax.experimental.pallas import tpu as pltpu
from jax.sharding import PartitionSpec as P

HEAD = 64
ROT = 16
LAYERS = 2
LANES = 128
F32 = jnp.float32
BF16 = jnp.bfloat16


def shape_of(shape, dtype):
    return jax.ShapeDtypeStruct(tuple(shape), dtype)


def whole(array):
    rank = array.ndim
    return pl.BlockSpec(array.shape, lambda i, *_: (0,) * rank, pipeline_mode=pl.Buffered(1))


def layer_spec(array, layer):
    rank = array.ndim
    return pl.BlockSpec(
        (1,) + array.shape[1:], lambda i, *_: (layer,) + (0,) * (rank - 1), pipeline_mode=pl.Buffered(1)
    )


def run(body, me, operands, outs, scratch=(), name=None, limit=32, out_specs=None, aliases=None, grid=1):
    arrays, specs = [], []
    for operand in operands:
        array, spec = operand if isinstance(operand, tuple) else (operand, None)
        arrays.append(array)
        specs.append(whole(array) if spec is None else spec)
    return pl.pallas_call(
        body,
        grid_spec=pltpu.PrefetchScalarGridSpec(
            num_scalar_prefetch=1,
            grid=(grid,),
            in_specs=specs,
            out_specs=[whole(o) for o in outs] if out_specs is None else out_specs,
            scratch_shapes=list(scratch),
        ),
        out_shape=list(outs),
        input_output_aliases=aliases or {},
        compiler_params=pltpu.CompilerParams(vmem_limit_bytes=limit * 1024 * 1024),
        cost_estimate=pl.CostEstimate(flops=1, bytes_accessed=1, transcendentals=0),
        name=name,
    )(me, *arrays)


def matmul(left, right):
    return jnp.dot(left, right, preferred_element_type=F32)


def matmul_nt(left, right):
    return lax.dot_general(left, right, (((1,), (1,)), ((), ())), preferred_element_type=F32)


def matmul_tn(left, right):
    return lax.dot_general(left, right, (((0,), (0,)), ((), ())), preferred_element_type=F32)


def normalize(values):
    average = jnp.mean(values, axis=-1, keepdims=True)
    centred = values - average
    factor = lax.rsqrt(jnp.mean(centred * centred, axis=-1, keepdims=True) + 1e-05)
    return centred * factor, factor


def wrap4(value):
    return lax.rem(value + 4, 4)


def rows(index, size):
    return pl.ds(pl.multiple_of(index * size, size), size)


def rotary_rows(place_row):
    count = place_row.shape[1]
    which = lax.broadcasted_iota(jnp.int32, (8, count), 0)
    frequency = jnp.zeros((8, count), F32)
    for index in range(8):
        frequency = jnp.where(which == index, 10000.0 ** (-2.0 * index / ROT), frequency)
    angles = frequency * place_row
    trig = jnp.concatenate([jnp.cos(angles), jnp.sin(angles)], axis=0)
    row = lax.broadcasted_iota(jnp.int32, (16, LANES), 0)
    lane = lax.broadcasted_iota(jnp.int32, (16, LANES), 1) & (HEAD - 1)
    same = (lane & 7) == (row & 7)
    is_cos = row < 8
    pick_cos = jnp.where(is_cos & same & (lane < 16), 1.0, 0.0)
    pick_low = jnp.where((row >= 8) & same & (lane < 8), 1.0, 0.0)
    pick_high = jnp.where((row >= 8) & same & (lane >= 8) & (lane < 16), 1.0, 0.0)
    picks = jnp.concatenate([pick_cos, pick_low, pick_high], axis=1).astype(F32)
    spread = lax.dot_general(
        trig, picks, (((0,), (0,)), ((), ())), preferred_element_type=F32, precision=lax.Precision.HIGHEST
    )
    lane_row = lax.broadcasted_iota(jnp.int32, (1, LANES), 1) & (HEAD - 1)
    cos_table = spread[:, :LANES] + jnp.where(lane_row >= ROT, 1.0, 0.0)
    return cos_table, spread[:, LANES : 2 * LANES], spread[:, 2 * LANES :]


def rotate(values, tables, back=False):
    cos_table, low_sin, high_sin = tables
    below = pltpu.roll(values, LANES - ROT // 2, 1) * low_sin
    above = pltpu.roll(values, ROT // 2, 1) * high_sin
    turned = below - above if back else above - below
    return values * cos_table + turned


def project_rows(layer, tok_shape, me_ref, seg_ref, weight, bias, a_ref, p_refs, proj_ref, with_seg):
    seq_count, block_len, width = tok_shape
    chip, core = me_ref[0], me_ref[1]
    base = (chip * 2 + core) * block_len
    for j in range(3):
        proj_ref[:, j * 2 * LANES : (j + 1) * 2 * LANES] = matmul(a_ref[...], weight(j)) + bias[j, layer : layer + 1, :]
    for k in range(4):
        seq = wrap4(chip + k)
        place = rows(seq, block_len)
        seg_row = seg_ref[pl.ds(seq, 1), :]
        spots = lax.broadcasted_iota(jnp.int32, (1, block_len), 1) + base
        tables = rotary_rows((spots - seg_row).astype(F32))
        for j in range(3):
            for pair in range(2):
                at = (2 * j + pair) * LANES
                part = proj_ref[place, at : at + LANES]
                if j < 2:
                    part = rotate(part, tables)
                p_refs[k][pair, 0:block_len, j * LANES : (j + 1) * LANES] = part.astype(BF16)
        if with_seg:
            coded = seg_row.astype(F32)
            high = jnp.floor(coded * 0.125)
            packed = jnp.concatenate([high, coded - 8.0 * high, jnp.zeros_like(high)], axis=1)
            packed = jnp.broadcast_to(packed, (16, 3 * LANES)).astype(BF16)
            for pair in range(2):
                p_refs[k][pair, block_len : block_len + 16, :] = packed


def project_first_body(tok_shape, me_ref, *refs):
    seq_count, block_len, width = tok_shape
    in_refs, refs = refs[:8], refs[8:]
    xq_ref, a_ref, m_ref, *p_refs = refs[:7]
    proj_ref, *held, sems = refs[7:]
    x_ref, seg_ref, ag_ref, as_ref, mg_ref, ms_ref, w_ref, b_ref = held
    copies = []
    for index in (1, 2, 3, 4, 5):
        copies.append(pltpu.make_async_copy(in_refs[index], held[index], sems.at[len(copies)]))
    copies.append(pltpu.make_async_copy(in_refs[7], b_ref, sems.at[len(copies)]))
    small_count = len(copies)
    for seq in range(seq_count):
        place = pl.ds(seq * block_len, block_len)
        copies.append(pltpu.make_async_copy(in_refs[0].at[place], x_ref.at[place], sems.at[len(copies)]))
    copies.append(pltpu.make_async_copy(in_refs[6].at[0], w_ref, sems.at[len(copies)]))
    for copy in copies:
        copy.start()
    for copy in copies[:small_count]:
        copy.wait()
    for seq in range(seq_count):
        copies[small_count + seq].wait()
        place = slice(seq * block_len, (seq + 1) * block_len)
        normed, _ = normalize(x_ref[place, :])
        a_ref[place, :] = (normed * ag_ref[0:1, :] + as_ref[0:1, :]).astype(BF16)
        m_ref[place, :] = (normed * mg_ref[0:1, :] + ms_ref[0:1, :]).astype(BF16)
    xq_ref[...] = x_ref[rows(me_ref[2], block_len), :]
    copies[-1].wait()
    project_rows(0, tok_shape, me_ref, seg_ref, lambda j: w_ref[j], b_ref, a_ref, p_refs, proj_ref, True)


def project_body(layer, tok_shape, me_ref, *refs):
    seq_count, block_len, width = tok_shape
    x_ref, seg_ref, *refs = refs
    u_refs, refs = refs[:4], refs[4:]
    ob_ref, db_ref, ag_ref, as_ref, mg_ref, ms_ref, w_ref, b_ref, x_out, xq_ref, a_ref, m_ref, *p_refs, proj_ref = refs
    tensor = me_ref[2]
    shift = ob_ref[layer - 1 : layer, :] + db_ref[layer - 1 : layer, :]
    for k in range(4):
        place = rows(wrap4(tensor - k), block_len)
        value = x_ref[place, :] + u_refs[k][...].astype(F32) + shift
        x_out[place, :] = value
        if k == 0:
            xq_ref[...] = value
        normed, _ = normalize(value)
        a_ref[place, :] = (normed * ag_ref[layer : layer + 1, :] + as_ref[layer : layer + 1, :]).astype(BF16)
        m_ref[place, :] = (normed * mg_ref[layer : layer + 1, :] + ms_ref[layer : layer + 1, :]).astype(BF16)
    project_rows(layer, tok_shape, me_ref, seg_ref, lambda j: w_ref[0, j], b_ref, a_ref, p_refs, proj_ref, False)


def gather_pieces(me_ref, refs, targets, block_len, seg_target=None):
    chip, core = me_ref[0], me_ref[1]
    for k in range(4):
        owner = wrap4(chip - k)
        for side, ref in ((core, refs[k]), (1 - core, refs[4 + k])):
            place = rows(owner * 2 + side, block_len)
            for index, target in enumerate(targets):
                target[place, :] = ref[core, 0:block_len, index * LANES : (index + 1) * LANES]
            if seg_target is not None:
                row = ref[core, block_len : block_len + 16, :].astype(F32)[0:1, :]
                starts = row[:, 0:LANES] * 8.0 + row[:, LANES : 2 * LANES]
                seg_target[:, place] = jnp.broadcast_to(starts, (8, block_len))


def head_stack(values):
    lane = lax.broadcasted_iota(jnp.int32, values.shape, 1)
    zero = jnp.zeros_like(values)
    return jnp.concatenate(
        [jnp.where(lane < HEAD, values, zero), jnp.where(lane >= HEAD, values, zero)], axis=0
    )


def own_halves(product, width):
    return jnp.concatenate([product[0:HEAD, 0:width], product[HEAD:, width : 2 * width]], axis=0)


def chances_t(q_ref, k_ref, seg_ref, step, chunk):
    start, keys = step * chunk, (step + 1) * chunk
    stacked = head_stack(q_ref[start:keys, :]) * jnp.asarray(HEAD ** (-0.5), BF16)
    scores = matmul_nt(k_ref[0:keys, :], stacked)
    key_place = lax.broadcasted_iota(jnp.int32, (keys, 2 * chunk), 0).astype(F32)
    query_place = (lax.broadcasted_iota(jnp.int32, (1, 2 * chunk), 1) & (chunk - 1)).astype(F32) + start
    seg_row = seg_ref[0:1, start:keys]
    seg_row = jnp.concatenate([seg_row, seg_row], axis=1)
    allowed = (key_place >= seg_row) & (key_place <= query_place)
    scores = jnp.where(allowed, scores, -1e30)
    raised = jnp.exp(scores - jnp.max(scores, axis=0, keepdims=True))
    total = jnp.sum(raised, axis=0, keepdims=True)
    return raised * (1.0 / total), stacked


def attend_body(block_len, chunk, me_ref, *refs):
    piece_refs, refs = refs[:8], refs[8:]
    seg_out, qkv_ref, *refs = refs
    o_refs, refs = refs[:4], refs[4:]
    vt_ref, o_ref = refs
    q_ref, k_ref, v_ref = qkv_ref.at[0], qkv_ref.at[1], qkv_ref.at[2]
    gather_pieces(me_ref, piece_refs, (q_ref, k_ref, v_ref), block_len, seg_out)
    vt_ref[...] = v_ref[...].T
    length = q_ref.shape[0]
    for step in range(length // chunk):
        keys = (step + 1) * chunk
        chances, _ = chances_t(q_ref, k_ref, seg_out, step, chunk)
        mixed = matmul(vt_ref[:, 0:keys], chances.astype(BF16))
        o_ref[step * chunk : keys, :] = own_halves(mixed, chunk).T.astype(BF16)
    send_blocks(me_ref, o_ref, o_refs, block_len)


def send_blocks(me_ref, source, targets, block_len):
    chip = me_ref[0]
    for k in range(4):
        dest = wrap4(chip + k)
        for side in range(2):
            targets[k][side] = source[rows(dest * 2 + side, block_len), :]


def attend_both_body(block_len, chunk, with_out, me_ref, *refs):
    if with_out:
        piece_refs, refs = refs[:8], refs[8:]
    else:
        qkv_ref, *refs = refs
    grad_refs, refs = refs[:8], refs[8:]
    seg_ref, *refs = refs
    d_refs, refs = refs[:4], refs[4:]
    if with_out:
        qkv_ref, *refs = refs
    q_ref, k_ref, v_ref = qkv_ref.at[0], qkv_ref.at[1], qkv_ref.at[2]
    g_ref, t_ref, o_ref, dq_ref, dk_ref, dv_ref = refs
    if with_out:
        gather_pieces(me_ref, piece_refs, (q_ref, k_ref, v_ref), block_len)
    gather_pieces(me_ref, grad_refs, (g_ref,), block_len)
    length = q_ref.shape[0]
    t_ref[0] = k_ref[...].T
    if with_out:
        t_ref[1] = v_ref[...].T
    dk_ref[...] = jnp.zeros_like(dk_ref)
    dv_ref[...] = jnp.zeros_like(dv_ref)
    for step in range(length // chunk):
        start, keys = step * chunk, (step + 1) * chunk
        chances, stacked = chances_t(q_ref, k_ref, seg_ref, step, chunk)
        low = chances.astype(BF16)
        if with_out:
            mixed = matmul(t_ref[1, :, 0:keys], low)
            o_ref[start:keys, :] = own_halves(mixed, chunk).T.astype(BF16)
        grads = head_stack(g_ref[start:keys, :])
        chance_grad = matmul_nt(v_ref[0:keys, :], grads)
        delta = jnp.sum(chances * chance_grad, axis=0, keepdims=True)
        score_grad = (chances * (chance_grad - delta)).astype(BF16)
        dv_ref[0:keys, :] += matmul(low, grads)
        dk_ref[0:keys, :] += matmul(score_grad, stacked)
        query = matmul(t_ref[0, :, 0:keys], score_grad)
        dq_ref[start:keys, :] = own_halves(query, chunk).T * HEAD ** (-0.5)
    chip = me_ref[0]
    for k in range(4):
        dest = wrap4(chip + k)
        for side in range(2):
            place = rows(dest * 2 + side, block_len)
            spots = (lax.broadcasted_iota(jnp.int32, (1, block_len), 1) + (dest * 2 + side) * block_len).astype(F32)
            tables = rotary_rows(spots - seg_ref[0:1, place])
            d_refs[k][side, :, 0:LANES] = rotate(dq_ref[place, :], tables, True).astype(BF16)
            d_refs[k][side, :, LANES : 2 * LANES] = rotate(dk_ref[place, :], tables, True).astype(BF16)
            d_refs[k][side, :, 2 * LANES : 3 * LANES] = dv_ref[place, :].astype(BF16)
            if with_out:
                d_refs[k][side, :, 3 * LANES :] = o_ref[place, :]


def land_heads(me_ref, refs, target, block_len, groups, first=0):
    chip, core = me_ref[0], me_ref[1]
    for k in range(4):
        place = rows(wrap4(chip - k), block_len)
        mine, other = refs[k][core], refs[4 + k][core]
        is_low = core == 0
        for group in range(groups):
            span = slice((first + group) * LANES, (first + group + 1) * LANES)
            at = group * 2 * LANES
            target[place, at : at + LANES] = jnp.where(is_low, mine[:, span], other[:, span])
            target[place, at + LANES : at + 2 * LANES] = jnp.where(is_low, other[:, span], mine[:, span])


def combine_body(block_len, fused, me_ref, *refs):
    piece_refs, refs = refs[:8], refs[8:]
    w_ref, *refs = refs
    if fused:
        g_ref, down_ref, *refs = refs
    else:
        part_ref, *refs = refs
    o_ref, *refs = refs
    q_refs, scr = refs[:-1], refs[-1]
    tensor = me_ref[2]
    land_heads(me_ref, piece_refs, o_ref, block_len, 1, 3 if fused else 0)
    part = matmul(g_ref[...], down_ref[0]) if fused else part_ref[...]
    scr[...] = (matmul(o_ref[...], w_ref[0]) + part).astype(BF16)
    for k in range(4):
        q_refs[k][...] = scr[rows(wrap4(tensor + k), block_len), :]


def send_grad_body(block_len, me_ref, x_ref, w_ref, *refs):
    chip, tensor = me_ref[0], me_ref[2]
    quarter_ref, *refs = refs
    quarter_ref[...] = x_ref[rows(tensor, block_len), :]
    for k in range(4):
        value = x_ref[rows(wrap4(chip + k), block_len), :].astype(BF16)
        grad = matmul_nt(value, w_ref[0]).astype(BF16)
        for pair in range(2):
            refs[k][pair] = grad[:, pair * LANES : (pair + 1) * LANES]


def join_body(block_len, me_ref, *refs):
    q_refs, refs = refs[:4], refs[4:]
    w_ref, r_ref, *g_refs = refs
    chip, tensor = me_ref[0], me_ref[2]
    for k in range(4):
        r_ref[rows(wrap4(tensor - k), block_len), :] = q_refs[k][...]
    for k in range(4):
        value = r_ref[rows(wrap4(chip + k), block_len), :]
        grad = matmul_nt(value, w_ref[0]).astype(BF16)
        for pair in range(2):
            g_refs[k][pair] = grad[:, pair * LANES : (pair + 1) * LANES]


def project_back_body(block_len, layer, me_ref, *refs):
    piece_refs, refs = refs[:8], refs[8:]
    w_ref, dm_ref, ag_ref, mg_ref, *refs = refs
    riders, refs = refs[:-8], refs[-8:]
    dp_ref, da_ref, bias_ref, *q_refs, scr = refs
    tensor = me_ref[2]
    land_heads(me_ref, piece_refs, dp_ref, block_len, 3)
    for j in range(3):
        span = slice(j * 2 * LANES, (j + 1) * 2 * LANES)
        bias_ref[j : j + 1, :] = jnp.sum(dp_ref[:, span].astype(F32), axis=0, keepdims=True)
    total = None
    for j in range(3):
        term = matmul_nt(dp_ref[:, j * 2 * LANES : (j + 1) * 2 * LANES], w_ref[0, j])
        total = term if total is None else total + term
    da_ref[...] = total.astype(BF16)
    scr[...] = (total * ag_ref[layer : layer + 1, :] + dm_ref[...] * mg_ref[layer : layer + 1, :]).astype(BF16)
    for k in range(4):
        q_refs[k][0:block_len, :] = scr[rows(wrap4(tensor + k), block_len), :]
        if riders:
            q_refs[k][block_len:, :] = riders[k][...]


def norm_back_body(me_ref, *refs):
    e_ref, x_ref, dy_ref, dx_ref, low_ref, bias_ref = refs
    upstream = dy_ref[...]
    size = upstream.shape[0]
    total = e_ref[0:size, :]
    normed, factor = normalize(x_ref[...])
    inner = jnp.mean(total * normed, axis=-1, keepdims=True)
    result = upstream + factor * (total - jnp.mean(total, axis=-1, keepdims=True) - normed * inner)
    dx_ref[...] = result
    low_ref[0:size, :] = result.astype(BF16)
    if e_ref.shape[0] > size:
        low_ref[size:, :] = e_ref[size:, :].astype(BF16)
    bias_ref[...] = jnp.sum(upstream, axis=0, keepdims=True)


def gains_body(me_ref, x_ref, da_ref, dm_ref, out_ref):
    normed, _ = normalize(x_ref[...])
    da = da_ref[...].astype(F32)
    dm = dm_ref[...]
    out_ref[0:1, :] = jnp.sum(da * normed, axis=0, keepdims=True)
    out_ref[1:2, :] = jnp.sum(da, axis=0, keepdims=True)
    out_ref[2:3, :] = jnp.sum(dm * normed, axis=0, keepdims=True)
    out_ref[3:4, :] = jnp.sum(dm, axis=0, keepdims=True)


def gelu_parts(hidden):
    cdf = 0.5 * (1.0 + lax.erf(hidden * (0.5**0.5)))
    density = jnp.exp(-0.5 * hidden * hidden) * 0.3989422804014327
    return cdf, density


def feed_body(layer, me_ref, m_ref, up_ref, ub_ref, down_ref, g_ref, slope_ref, part_ref):
    size = 2 * LANES
    for step in range(up_ref.shape[2] // size):
        span = slice(step * size, (step + 1) * size)
        hidden = matmul(m_ref[...], up_ref[0, :, span]) + ub_ref[layer : layer + 1, span]
        cdf, density = gelu_parts(hidden)
        g_ref[:, span] = (hidden * cdf).astype(BF16)
        slope_ref[:, span] = cdf + hidden * density
    part_ref[...] = matmul(g_ref[...], down_ref[0])


def feed_back_body(me_ref, r_ref, slope_ref, up_ref, down_ref, dh_ref, dm_ref, bias_ref):
    size = 2 * LANES
    for step in range(down_ref.shape[1] // size):
        span = slice(step * size, (step + 1) * size)
        grad = matmul_nt(r_ref[...], down_ref[0, span, :]) * slope_ref[:, span]
        bias_ref[:, span] = jnp.sum(grad, axis=0, keepdims=True)
        dh_ref[:, span] = grad.astype(BF16)
    dm_ref[...] = matmul_nt(dh_ref[...], up_ref[0])


def feed_both_body(layer, me_ref, m_ref, dy_ref, up_ref, ub_ref, down_ref, g_ref, r_ref, dh_ref, dm_ref, bias_ref):
    size = 2 * LANES
    r_ref[...] = dy_ref[...].astype(BF16)
    for step in range(up_ref.shape[2] // size):
        span = slice(step * size, (step + 1) * size)
        hidden = matmul(m_ref[...], up_ref[0, :, span]) + ub_ref[layer : layer + 1, span]
        cdf, density = gelu_parts(hidden)
        g_ref[:, span] = (hidden * cdf).astype(BF16)
        grad = matmul_nt(r_ref[...], down_ref[0, span, :]) * (cdf + hidden * density)
        bias_ref[:, span] = jnp.sum(grad, axis=0, keepdims=True)
        dh_ref[:, span] = grad.astype(BF16)
    dm_ref[...] = matmul_nt(dh_ref[...], up_ref[0])


def feed_weights_body(me_ref, m_ref, dh_ref, g_ref, r_ref, keep_ref, send_ref):
    core = me_ref[1]
    half = m_ref.shape[1] // 2
    for side, out in ((core, keep_ref), (1 - core, send_ref)):
        out[0:half, :] = matmul_tn(m_ref[:, rows(side, half)], dh_ref[...]).astype(BF16)
        out[half:, :] = matmul_tn(g_ref[:, rows(side, half)], r_ref[...]).astype(BF16)


def head_weights_body(me_ref, a_ref, dp_ref, o_ref, r_ref, keep_ref, send_ref):
    core = me_ref[1]
    half = a_ref.shape[1] // 2
    wide = dp_ref.shape[1]
    for side, out in ((core, keep_ref), (1 - core, send_ref)):
        out[:, 0:wide] = matmul_tn(a_ref[:, rows(side, half)], dp_ref[...]).astype(BF16)
        grad = matmul_tn(o_ref[:, rows(side, LANES)], r_ref[...]).astype(BF16)
        for part in range(4):
            out[part * LANES : (part + 1) * LANES, wide:] = grad[:, part * 2 * LANES : (part + 1) * 2 * LANES]


def feed_weights_whole_body(me_ref, m_ref, dh_ref, g_ref, r_ref, pack_ref):
    high = m_ref.shape[1]
    pack_ref[0:high, :] = matmul_tn(m_ref[...], dh_ref[...]).astype(BF16)
    pack_ref[high:, :] = matmul_tn(g_ref[...], r_ref[...]).astype(BF16)


def head_weights_whole_body(me_ref, a_ref, dp_ref, o_ref, r_ref, before_ref, pack_ref):
    wide = dp_ref.shape[1]
    pack_ref[:, 0:wide] = matmul_tn(a_ref[...], dp_ref[...]).astype(BF16)
    grad = matmul_tn(o_ref[...], r_ref[...]).astype(BF16)
    high, size = grad.shape[0], 2 * LANES
    for part in range(4):
        pack_ref[part * high : (part + 1) * high, wide:] = grad[:, part * size : (part + 1) * size]


def near_far(place):
    return place ^ 1, 3 - place


def halve_body(me_ref, feed_keep, feed_came, head_keep, head_came, *refs):
    outs, feed_scr, head_scr = refs[:4], refs[4], refs[5]
    feed_scr[...] = (feed_keep[...].astype(F32) + feed_came[...].astype(F32)).astype(BF16)
    head_scr[...] = (head_keep[...].astype(F32) + head_came[...].astype(F32)).astype(BF16)
    place = me_ref[3]
    near, far = near_far(place)
    half = head_scr.shape[0]
    size = half // 8
    orders = ((place, far), (near, 3 - near), (4 + place, 4 + near), (4 + far, 4 + (far ^ 1)))
    for ref, order in zip(outs, orders):
        for index, block in enumerate(order):
            at = 3 * size * index
            ref[at : at + size, :] = feed_scr[rows(block, size), :]
            ref[at + size : at + 2 * size, :] = feed_scr[pl.ds(pl.multiple_of(half + block * size, size), size), :]
            ref[at + 2 * size : at + 3 * size, :] = head_scr[rows(block, size), :]


def halve_again_body(me_ref, a_keep, a_came, b_keep, b_came, *outs):
    size = outs[0].shape[0]
    for keep, came, mine, send in ((a_keep, a_came, outs[0], outs[1]), (b_keep, b_came, outs[2], outs[3])):
        total = (keep[...].astype(F32) + came[...].astype(F32)).astype(BF16)
        mine[...] = total[0:size, :]
        send[...] = total[size:, :]


def line_up_body(axis, me_ref, *refs):
    size = refs[4].shape[0] // 4
    for k in range(4):
        refs[4][rows(wrap4(me_ref[axis] - k), size), :] = refs[k][0:size, :]
    if len(refs) > 5:
        even = refs[0][size:, :].astype(F32) + refs[2][size:, :].astype(F32)
        odd = refs[1][size:, :].astype(F32) + refs[3][size:, :].astype(F32)
        refs[5][...] = (even + odd).astype(BF16)


def merge_body(me_ref, a_keep, a_came, b_keep, b_came, small_ref, *refs):
    out_refs, scr = refs[:4], refs[4]
    high = a_keep.shape[0]
    scr[0:high, :] = (a_keep[...].astype(F32) + a_came[...].astype(F32)).astype(BF16)
    scr[high:, :] = (b_keep[...].astype(F32) + b_came[...].astype(F32)).astype(BF16)
    few = high // 6
    for k in range(4):
        part = wrap4(me_ref[0] + k)
        for weight in range(3):
            at = pl.multiple_of((part >> 1) * high + weight * 2 * few + (part & 1) * few, few)
            out_refs[k][weight * few : (weight + 1) * few, :] = scr[pl.ds(at, few), :]
        out_refs[k][3 * few :, :] = small_ref[...]


def settle_body(me_ref, *refs):
    in_refs, (first_ref, second_ref) = refs[:4], refs[4:]
    even = in_refs[0][...].astype(F32) + in_refs[2][...].astype(F32)
    odd = in_refs[1][...].astype(F32) + in_refs[3][...].astype(F32)
    total = (even + odd).astype(BF16)
    few = first_ref.shape[0] // 3
    for weight in range(3):
        for index, ref in enumerate((first_ref, second_ref)):
            at = (2 * weight + index) * few
            ref[weight * few : (weight + 1) * few, :] = total[at : at + few, :]
    second_ref[3 * few :, :] = total[6 * few :, :]


def flush(held, outs, layer, sems):
    copies = [pltpu.make_async_copy(a, b.at[layer], sems.at[i]) for i, (a, b) in enumerate(zip(held, outs))]
    return copies


def unpack_body(few, me_ref, *refs):
    outs, held, sems = refs[24:28], refs[28:32], refs[32]
    up_ref, down_ref, qkv_ref, out_ref = held
    copies = flush(held, outs, 0, sems)
    chip, core, place_z = me_ref[0], me_ref[1], me_ref[3]
    size = 2 * LANES
    half = up_ref.shape[0] // 2
    for weight in range(3):
        for side, group in ((core, refs[:10]), (1 - core, refs[10:20])):
            for along, me in ((0, place_z), (1, chip)):
                pieces = group[5 * along : 5 * along + 5]
                spans = [(pieces[0], me, 0), (pieces[1], me ^ 1, 0), (pieces[2], 3 - me, 0)]
                spans += [(pieces[3], me ^ 2, 0), (pieces[4], me ^ 2, 2)]
                for ref, owner, first in spans:
                    for index in range(ref.shape[0] // (3 * few)):
                        z, x = (owner, first + index) if along == 0 else (first + index, owner)
                        start = (3 * index + weight) * few
                        value = ref[start : start + few, :].astype(F32)
                        row = (z + 4 * (x >> 1)) * (4 * few) + (x & 1) * (2 * few) + along * few
                        place = pl.ds(pl.multiple_of(row + side * half, few), few)
                        if weight < 2:
                            held[weight][place, :] = value
                        else:
                            for j in range(3):
                                qkv_ref[j, place, :] = value[:, j * size : (j + 1) * size]
                            inner = pl.ds(pl.multiple_of((row & (LANES - 1)) + side * LANES, few), few)
                            lanes = pl.ds(pl.multiple_of((row >> 7) * size, size), size)
                            out_ref[inner, lanes] = value[:, 3 * size :]
        for copy in copies[weight : weight + 1] if weight < 2 else copies[2:]:
            copy.start()
    for copy in copies:
        copy.wait()


def unpack_whole_body(me_ref, up_in, down_in, head_in, up_ref, down_ref, qkv_ref, out_ref):
    size = 2 * LANES
    up_ref[0] = up_in[...].astype(F32)
    down_ref[0] = down_in[...].astype(F32)
    for j in range(3):
        qkv_ref[0, j] = head_in[:, j * size : (j + 1) * size].astype(F32)
    out_ref[0] = head_in[:, 3 * size :].astype(F32)


def pack_small_body(me_ref, *refs):
    ins, small_ref = refs[:8], refs[8]
    width = small_ref.shape[1]
    blank = jnp.zeros((1, width), F32)
    shared = [ins[0][...], ins[1][...], ins[2][...], ins[3][...]] + [blank] * 6
    small_ref[0:16, :] = jnp.concatenate(shared, axis=0).astype(BF16)
    local = [ins[6][...], ins[7][...]]
    for ref in ins[4:6]:
        values = ref[...]
        flat = [values[j : j + 1, :] for j in range(3)]
        local.append(jnp.concatenate(flat + [jnp.zeros((1, width - 3 * values.shape[1]), F32)], axis=1))
    small_ref[16:32, :] = jnp.concatenate(local + [blank] * 12, axis=0).astype(BF16)


def add_cut_body(me_ref, mine_ref, came_ref, shared_ref, local_ref):
    total = (mine_ref[...].astype(F32) + came_ref[...].astype(F32)).astype(BF16)
    half = shared_ref.shape[0]
    shared_ref[...] = total[0:half, :]
    local_ref[...] = total[half:, :]


def add_body(count, me_ref, *refs):
    total = refs[0][...].astype(F32)
    for ref in refs[1:count]:
        total = total + ref[...].astype(F32)
    refs[count][...] = total.astype(refs[count].dtype)


def small_out_body(me_ref, mine_ref, came_ref, local_ref, *outs):
    shared = mine_ref[...].astype(F32) + came_ref[...].astype(F32)
    local = local_ref[...].astype(F32)
    for index in range(5):
        outs[index][0:1, :] = shared[index : index + 1, :]
        outs[index][1:2, :] = shared[index + 5 : index + 6, :]
    outs[5][...] = local[0:2, :]
    size = outs[6].shape[2]
    for layer in range(2):
        for j in range(3):
            outs[6][layer, j : j + 1, :] = local[2 + layer : 3 + layer, j * size : (j + 1) * size]


def place_body(block_len, me_ref, *refs):
    q_refs, (x_ref, ob_ref, db_ref, grad_ref, out_ref) = refs[:4], refs[4:]
    shift = ob_ref[1:2, :] + db_ref[1:2, :]
    for k in range(4):
        place = rows(wrap4(me_ref[2] - k), block_len)
        grad_ref[place, :] = q_refs[k][0:block_len, :].astype(F32)
        out_ref[place, :] = x_ref[place, :] + q_refs[k][block_len:, :].astype(F32) + shift


def chip_turn(shift):
    return [(2 * x + c, 2 * ((x + shift) % 4) + c) for x in range(4) for c in range(2)]


CORE_SWAP = [(i, i ^ 1) for i in range(8)]


def over_chips(pieces, beside=()):
    mine, beside = lax.optimization_barrier((over_x(pieces), beside))
    return mine + [swap_core(piece) for piece in mine], beside


def ring_turn(shift):
    return [(i, (i + shift) % 4) for i in range(4)]


def over_tensor(pieces):
    return [pieces[0]] + [lax.ppermute(pieces[k], "tensor", ring_turn(k)) for k in range(1, 4)]


def share_tensor(piece):
    return over_tensor([piece] * 4)


def over_dp(pieces):
    return [pieces[0]] + [lax.ppermute(pieces[k], "dp", ring_turn(k)) for k in range(1, 4)]


def over_x(pieces):
    return [pieces[0]] + [lax.ppermute(pieces[k], "ctx", chip_turn(k)) for k in range(1, 4)]


def swap_core(piece):
    return lax.ppermute(piece, "ctx", CORE_SWAP)


NEXT_PAIR = [(0, 1), (1, 0), (2, 3), (3, 2)]
WRAP_PAIR = [(0, 3), (3, 0), (1, 2), (2, 1)]


def both_ways(to_next, to_wrap):
    return lax.ppermute(to_next, "dp", NEXT_PAIR), lax.ppermute(to_wrap, "dp", WRAP_PAIR)


def chips_of(pairs):
    return [(2 * a + c, 2 * b + c) for a, b in pairs for c in range(2)]


def spread_near(piece, axis):
    name, move = ("dp", lambda pairs: pairs) if axis == "dp" else ("ctx", chips_of)
    return [piece] + [lax.ppermute(piece, name, move(pairs)) for pairs in (NEXT_PAIR, WRAP_PAIR)]


def spread_far(pieces, axis):
    name, move = ("dp", lambda pairs: pairs) if axis == "dp" else ("ctx", chips_of)
    half = pieces[0].shape[0] // 2
    return pieces + [
        lax.ppermute(pieces[1][:half], name, move(WRAP_PAIR)),
        lax.ppermute(pieces[2][half:], name, move(NEXT_PAIR)),
    ]


def tie(first, second):
    return lax.optimization_barrier((first, second))


def after(values, token):
    return lax.optimization_barrier((values, token))[0]


def add_up(pieces):
    total = pieces[0].astype(F32)
    for piece in pieces[1:]:
        total = total + piece.astype(F32)
    return total


def on_device(
    inputs,
    segments,
    attn_gain,
    attn_shift,
    mlp_gain,
    mlp_shift,
    qkv_weight,
    qkv_bias,
    out_weight,
    out_bias,
    up_weight,
    up_bias,
    down_weight,
    down_bias,
    cotangent,
):
    seq_count, block_len, width = inputs.shape
    tokens = seq_count * block_len
    inner = qkv_weight.shape[3]
    hidden = up_weight.shape[2]
    length = block_len * 8
    chunk = 256
    place = lax.axis_index("ctx")
    me = jnp.stack([place // 2, place % 2, lax.axis_index("tensor"), lax.axis_index("dp")]).astype(jnp.int32)
    x0 = inputs.reshape(tokens, width)
    dy1 = cotangent.reshape(tokens, width)
    tok_shape = inputs.shape
    wide = shape_of((tokens, width), BF16)
    norms = (attn_gain, attn_shift, mlp_gain, mlp_shift)
    biases = qkv_bias.transpose(1, 0, 2)

    def project_first(x):
        sources = [x, segments, *norms, qkv_weight, biases]
        held = [v.shape for v in sources[:6]] + [qkv_weight.shape[1:], biases.shape]
        piece = shape_of((2, block_len + 16, 3 * LANES), BF16)
        return run(
            functools.partial(project_first_body, tok_shape),
            me,
            [(v, pl.BlockSpec(memory_space=pltpu.HBM)) for v in sources],
            [shape_of((block_len, width), F32), wide, wide] + [piece] * 4,
            scratch=[pltpu.VMEM((tokens, 3 * inner), F32)]
            + [pltpu.VMEM(size, v.dtype) for size, v in zip(held, sources)]
            + [pltpu.SemaphoreType.DMA((11,))],
            name="norm_project",
            limit=62,
        )

    def project(layer, x, extra):
        piece = shape_of((2, block_len, 3 * LANES), BF16)
        return run(
            functools.partial(project_body, layer, tok_shape),
            me,
            [x, segments, *extra, *norms]
            + [(qkv_weight, layer_spec(qkv_weight, layer)), biases],
            [shape_of((tokens, width), F32), shape_of((block_len, width), F32), wide, wide] + [piece] * 4,
            scratch=[pltpu.VMEM((tokens, 3 * inner), F32)],
            name="norm_project",
            limit=24,
        )

    def feed(layer, m):
        return run(
            functools.partial(feed_body, layer),
            me,
            [m, (up_weight, layer_spec(up_weight, layer)), up_bias, (down_weight, layer_spec(down_weight, layer))],
            [shape_of((tokens, hidden), BF16), shape_of((tokens, hidden), F32), shape_of((tokens, width), F32)],
            name="feed", limit=24,
        )

    def feed_back(layer, r, slope):
        return run(
            feed_back_body,
            me,
            [r, slope, (up_weight, layer_spec(up_weight, layer)), (down_weight, layer_spec(down_weight, layer))],
            [shape_of((tokens, hidden), BF16), shape_of((tokens, width), F32), shape_of((1, hidden), F32)],
            name="feed_back", limit=24,
        )

    def feed_both(layer, m, dy):
        return run(
            functools.partial(feed_both_body, layer),
            me,
            [m, dy, (up_weight, layer_spec(up_weight, layer)), up_bias, (down_weight, layer_spec(down_weight, layer))],
            [shape_of((tokens, hidden), BF16), wide, shape_of((tokens, hidden), BF16)]
            + [shape_of((tokens, width), F32), shape_of((1, hidden), F32)],
            name="feed_both", limit=24,
        )

    def combine(layer, pieces, part, active=None):
        fused = part is None
        got = run(
            functools.partial(combine_body, block_len, fused),
            me,
            [*pieces, (out_weight, layer_spec(out_weight, layer))]
            + ([active, (down_weight, layer_spec(down_weight, layer))] if fused else [part]),
            [shape_of((tokens, inner), BF16)] + [shape_of((block_len, width), BF16)] * 4,
            scratch=[pltpu.VMEM((tokens, width), BF16)],
            name="combine", limit=20,
        )
        return got[0], got[1:]

    def add_all(values, dtype=BF16):
        out = shape_of(values[0].shape, dtype)
        return run(functools.partial(add_body, len(values)), me, values, [out], name="add_all", limit=16)[0]

    def line_up(axis, values, size):
        extra = values[0].shape[0] - size
        small = [shape_of((extra, width), BF16)] if extra else []
        outs = [shape_of((4 * size, width), BF16)] + small
        return run(functools.partial(line_up_body, axis), me, values, outs, name="line_up", limit=8)

    seq_bf16 = pltpu.VMEM((length, LANES), BF16)
    seq_f32 = pltpu.VMEM((length, LANES), F32)
    o_shapes = [shape_of((2, block_len, LANES), BF16)] * 4

    def attend_both(pieces, grads, seg_rows, with_out):
        return run(
            functools.partial(attend_both_body, block_len, chunk, with_out),
            me,
            [*pieces, *grads, seg_rows],
            [shape_of((2, block_len, (4 if with_out else 3) * LANES), BF16)] * 4,
            scratch=([pltpu.VMEM((3, length, LANES), BF16)] if with_out else [])
            + [seq_bf16, pltpu.VMEM((2, LANES, length), BF16), seq_bf16]
            + [seq_f32] * 3,
            name="attend_both", limit=24,
        )

    def project_back(layer, pieces, dm, riders=()):
        got = run(
            functools.partial(project_back_body, block_len, layer),
            me,
            [*pieces, (qkv_weight, layer_spec(qkv_weight, layer)), dm, attn_gain, mlp_gain, *riders],
            [shape_of((tokens, 3 * inner), BF16), wide, shape_of((3, inner), F32)]
            + [shape_of((block_len * (2 if riders else 1), width), BF16)] * 4,
            scratch=[pltpu.VMEM((tokens, width), BF16)],
            name="project_back", limit=24,
        )
        return got[0], got[1], got[2], got[3:]

    def norm_back(pieces, x, dy):
        quarter = shape_of((block_len, width), F32)
        return run(
            norm_back_body,
            me,
            [add_up(pieces), x, dy],
            [quarter, shape_of(pieces[0].shape, BF16), shape_of((1, width), F32)],
            name="norm_back",
            limit=10,
        )

    def gains(x, da, dm):
        return run(gains_body, me, [x, da, dm], [shape_of((4, width), F32)], name="gains", limit=16)[0]

    half = width // 2

    def feed_weights(m, dh, active, r):
        pack = shape_of((2 * half, width), BF16)
        return run(feed_weights_body, me, [m, dh, active, r], [pack] * 2, name="feed_weights", limit=24)

    def head_weights(attn_in, dproj, attended, r):
        pack = shape_of((half, width), BF16)
        return run(head_weights_body, me, [attn_in, dproj, attended, r], [pack] * 2, name="head_weights", limit=20)

    x0_quarter, a0, m0, *pieces = project_first(x0)
    fed0 = feed(0, m0)
    pieces0, (active0, slope0, part0) = over_chips(pieces, fed0)
    got = run(
        functools.partial(attend_body, block_len, chunk),
        me,
        pieces0,
        [shape_of((8, length), F32), shape_of((3, length, LANES), BF16)] + o_shapes,
        scratch=[pltpu.VMEM((LANES, length), BF16), seq_bf16],
        name="attend", limit=20,
    )
    seg_rows, qkv0 = got[:2]
    out0, _ = over_chips(got[2:])
    attended0, u0 = combine(0, out0, part0)
    dy1_quarter, *grads1 = run(
        functools.partial(send_grad_body, block_len),
        me,
        [after(dy1, u0[0]), (out_weight, layer_spec(out_weight, 1))],
        [shape_of((block_len, width), F32)] + o_shapes,
        name="out_back", limit=14,
    )
    grads1 = over_x(grads1)
    u0 = share_tensor(add_up(over_tensor(u0)).astype(BF16))
    u0, grads1 = tie(u0, grads1)
    grads1_other = [swap_core(piece) for piece in grads1]

    x1, x1_quarter, a1, m1, *pieces = project(1, x0, [*u0, out_bias, down_bias])
    fed1 = feed_both(1, m1, dy1)
    pieces1, ((active1, r1, dh1, dm1, up_b1), grads1_other) = over_chips(pieces, (fed1, grads1_other))
    got = attend_both(pieces1, grads1 + grads1_other, seg_rows, True)
    feed_pack1 = run(
        feed_weights_whole_body,
        me,
        [after(m1, got[0]), dh1, active1, r1],
        [shape_of((3 * width, width), BF16)],
        name="feed_weights",
        limit=24,
        out_specs=[pl.BlockSpec((2 * width, width), lambda i, *_: (0, 0))],
    )[0]
    back1, feed_pack1 = over_chips(got, feed_pack1)
    dproj1, da1, qkv_b1, e1 = project_back(1, back1, dm1)
    back1 = after(back1, e1[0])
    attended1, u1 = combine(1, back1, None, active1)
    pack1 = run(
        head_weights_whole_body,
        me,
        [a1, dproj1, attended1, r1, (feed_pack1, pl.BlockSpec(memory_space=pl.ANY))],
        [shape_of((3 * width, width), BF16)],
        name="head_weights",
        limit=24,
        out_specs=[pl.BlockSpec((width, width), lambda i, *_: (2, 0))],
        aliases={5: 0},
    )[0]
    e1, (u1, pack1) = tie(over_tensor(e1), (u1, pack1))
    part1 = lax.psum_scatter(pack1, ("dp", "ctx"), tiled=True)
    dx1, low1, bias1 = norm_back(e1, x1_quarter, dy1_quarter)
    gains1 = gains(after(x1, low1), da1, dm1)
    quarters, gains1 = tie(share_tensor(low1), gains1)

    r0, *grads0 = run(
        functools.partial(join_body, block_len),
        me,
        [*quarters, (out_weight, layer_spec(out_weight, 0))],
        [wide] + o_shapes,
        name="join_out_back", limit=14,
    )
    dh0, dm0, up_b0 = feed_back(0, r0, slope0)
    grads0, (dh0, dm0) = over_chips(grads0, (dh0, dm0))
    back0 = attend_both([qkv0], grads0, seg_rows, False)
    feed_pack0 = feed_weights(after(m0, back0[0]), dh0, active0, r0)
    back0, (feed_keep, feed_send) = over_chips(back0, feed_pack0)
    dproj0, da0, qkv_b0, e0 = project_back(0, back0, dm0, u1)
    head_keep, head_send = head_weights(a0, dproj0, attended0, r0)
    e0 = after(e0, head_keep)
    way = shape_of((3 * half // 4, width), BF16)
    a_keep, a_send, b_keep, b_send = run(
        halve_body,
        me,
        [feed_keep, swap_core(feed_send), head_keep, swap_core(head_send)],
        [way] * 4,
        scratch=[pltpu.VMEM((2 * half, width), BF16), pltpu.VMEM((half, width), BF16)],
        name="halve",
        limit=20,
    )
    part1 = after(part1, a_send)
    pack1 = lax.all_gather(part1, ("dp", "ctx"), tiled=True)
    gains0 = gains(after(x0, a_send), da0, dm0)
    a_came, b_came = both_ways(a_send, b_send)
    e0, (gains0, a_came, b_came) = tie(over_tensor(e0), (gains0, a_came, b_came))
    way = shape_of((3 * half // 8, width), BF16)
    a_keep, a_send, b_keep, b_send = run(
        halve_again_body, me, [a_keep, a_came, b_keep, b_came], [way] * 4, name="halve_again", limit=12
    )
    b_came, a_came = both_ways(b_send, a_send)
    dx0, low0, bias0 = norm_back(after(e0, a_send), x0_quarter, dx1)
    last = share_tensor(low0)
    small = run(
        pack_small_body,
        me,
        [gains0, bias0, gains1, bias1, qkv_b0, qkv_b1, up_b0, up_b1],
        [shape_of((32, width), BF16)],
        name="pack_small",
        limit=8,
    )[0]

    few = half // 32
    cut = run(
        merge_body,
        me,
        [a_keep, a_came, b_keep, b_came, small],
        [shape_of((6 * few + 32, width), BF16)] * 4,
        scratch=[pltpu.VMEM((24 * few, width), BF16)],
        name="merge",
        limit=12,
    )
    cut, last = tie(over_x(cut), last)
    pieces = [shape_of((3 * few, width), BF16), shape_of((3 * few + 32, width), BF16)]
    first, second = run(settle_body, me, cut, pieces, name="settle", limit=8)
    first, (second, pack1) = tie(over_x([first] * 4), (over_dp([second] * 4), pack1))
    second, small = line_up(3, second, 3 * few)
    first = line_up(0, first, 3 * few)[0]
    near = (spread_near(first, "dp"), spread_near(second, "x"))

    pack1, last = after((pack1, last), first)
    heavy = [
        shape_of((2, width, hidden), F32),
        shape_of((2, hidden, width), F32),
        shape_of((2, 3, width, inner), F32),
        shape_of((2, inner, width), F32),
    ]
    eighth = width // 8
    first_outs = run(
        unpack_whole_body,
        me,
        [
            (pack1, pl.BlockSpec((eighth, width), lambda i, *_, part=part: (8 * part + i, 0)))
            for part in range(3)
        ],
        heavy,
        name="unpack_whole",
        limit=24,
        out_specs=[
            pl.BlockSpec((1, eighth, width), lambda i, *_: (1, i, 0)),
            pl.BlockSpec((1, eighth, width), lambda i, *_: (1, i, 0)),
            pl.BlockSpec((1, 3, eighth, inner), lambda i, *_: (1, 0, i, 0)),
            pl.BlockSpec((1, eighth, 2 * LANES), lambda i, *_: (1, i % 2, i // 2)),
        ],
        grid=8,
    )
    input_grad, output = run(
        functools.partial(place_body, block_len),
        me,
        [*last, x1, out_bias, down_bias],
        [shape_of((tokens, width), F32)] * 2,
        name="place",
        limit=20,
    )
    row_block = shape_of((16, width), BF16)
    shared, local = run(add_cut_body, me, [small, swap_core(small)], [row_block] * 2, name="add_cut", limit=8)
    shared_came = lax.ppermute(shared, "tensor", NEXT_PAIR)
    near, (first_outs, shared_came, input_grad, output) = tie(near, (first_outs, shared_came, input_grad, output))
    far = (spread_far(near[0], "dp"), spread_far(near[1], "x"))
    other = [swap_core(v) for v in near[0] + near[1]]
    shared = add_all([shared, shared_came])
    shared_came = lax.ppermute(shared, "tensor", WRAP_PAIR)
    row_pair = shape_of((2, width), F32)
    small = run(
        small_out_body,
        me,
        [shared, shared_came, local],
        [row_pair] * 6 + [shape_of((2, 3, inner), F32)],
        name="small_out",
        limit=8,
    )
    mine, (small, other) = tie(far[0] + far[1], (small, other))
    far = [swap_core(v) for v in mine[3:5] + mine[8:10]]
    other = other[0:3] + far[0:2] + other[3:6] + far[2:4]
    in_place = pl.BlockSpec(memory_space=pl.ANY)
    held = [pltpu.VMEM(v.shape[1:], F32) for v in heavy] + [pltpu.SemaphoreType.DMA((4,))]
    up_grad, down_grad, qkv_grad, out_grad = run(
        functools.partial(unpack_body, few),
        me,
        mine + other + [(v, in_place) for v in first_outs],
        heavy,
        name="unpack",
        limit=28,
        out_specs=[in_place] * 4,
        scratch=held,
        aliases={21 + index: index for index in range(4)},
    )
    return (
        output.reshape(tok_shape),
        input_grad.reshape(tok_shape),
        small[0],
        small[1],
        small[2],
        small[3],
        qkv_grad,
        small[6],
        out_grad,
        small[4],
        up_grad,
        small[5],
        down_grad,
        small[4],
    )


def solution(mesh):
    in_specs = (
        P("dp", "ctx", None),
        P("dp", "ctx"),
        P(),
        P(),
        P(),
        P(),
        P(None, None, None, "tensor"),
        P(None, None, "tensor"),
        P(None, "tensor", None),
        P(),
        P(None, None, "tensor"),
        P(None, "tensor"),
        P(None, "tensor", None),
        P(),
        P("dp", "ctx", None),
    )
    out_specs = (
        P("dp", "ctx", None),
        P("dp", "ctx", None),
        P(),
        P(),
        P(),
        P(),
        P(None, None, None, "tensor"),
        P(None, None, "tensor"),
        P(None, "tensor", None),
        P(),
        P(None, None, "tensor"),
        P(None, "tensor"),
        P(None, "tensor", None),
        P(),
    )
    return jax.shard_map(
        on_device, mesh=mesh, in_specs=in_specs, out_specs=out_specs, check_vma=False
    )
```

```python
import functools

import jax
import jax.numpy as jnp
from jax import lax
from jax.experimental import pallas as pl
from jax.experimental.pallas import tpu as pltpu
from jax.sharding import PartitionSpec as P

HEAD = 64
ROT = 16
LAYERS = 2
LANES = 128
F32 = jnp.float32
BF16 = jnp.bfloat16


def shape_of(shape, dtype):
    return jax.ShapeDtypeStruct(tuple(shape), dtype)


def whole(array):
    rank = array.ndim
    return pl.BlockSpec(array.shape, lambda i, *_: (0,) * rank, pipeline_mode=pl.Buffered(1))


def layer_spec(array, layer):
    rank = array.ndim
    return pl.BlockSpec(
        (1,) + array.shape[1:], lambda i, *_: (layer,) + (0,) * (rank - 1), pipeline_mode=pl.Buffered(1)
    )


def run(body, me, operands, outs, scratch=(), name=None, limit=32, out_specs=None, aliases=None, grid=1):
    arrays, specs = [], []
    for operand in operands:
        array, spec = operand if isinstance(operand, tuple) else (operand, None)
        arrays.append(array)
        specs.append(whole(array) if spec is None else spec)
    return pl.pallas_call(
        body,
        grid_spec=pltpu.PrefetchScalarGridSpec(
            num_scalar_prefetch=1,
            grid=(grid,),
            in_specs=specs,
            out_specs=[whole(o) for o in outs] if out_specs is None else out_specs,
            scratch_shapes=list(scratch),
        ),
        out_shape=list(outs),
        input_output_aliases=aliases or {},
        compiler_params=pltpu.CompilerParams(vmem_limit_bytes=limit * 1024 * 1024),
        cost_estimate=pl.CostEstimate(flops=1, bytes_accessed=1, transcendentals=0),
        name=name,
    )(me, *arrays)


def matmul(left, right):
    return jnp.dot(left, right, preferred_element_type=F32)


def matmul_nt(left, right):
    return lax.dot_general(left, right, (((1,), (1,)), ((), ())), preferred_element_type=F32)


def matmul_tn(left, right):
    return lax.dot_general(left, right, (((0,), (0,)), ((), ())), preferred_element_type=F32)


def normalize(values):
    average = jnp.mean(values, axis=-1, keepdims=True)
    centred = values - average
    factor = lax.rsqrt(jnp.mean(centred * centred, axis=-1, keepdims=True) + 1e-05)
    return centred * factor, factor


def wrap4(value):
    return lax.rem(value + 4, 4)


def rows(index, size):
    return pl.ds(pl.multiple_of(index * size, size), size)


def rotary_rows(place_row):
    count = place_row.shape[1]
    which = lax.broadcasted_iota(jnp.int32, (8, count), 0)
    frequency = jnp.zeros((8, count), F32)
    for index in range(8):
        frequency = jnp.where(which == index, 10000.0 ** (-2.0 * index / ROT), frequency)
    angles = frequency * place_row
    trig = jnp.concatenate([jnp.cos(angles), jnp.sin(angles)], axis=0)
    row = lax.broadcasted_iota(jnp.int32, (16, LANES), 0)
    lane = lax.broadcasted_iota(jnp.int32, (16, LANES), 1) & (HEAD - 1)
    same = (lane & 7) == (row & 7)
    is_cos = row < 8
    pick_cos = jnp.where(is_cos & same & (lane < 16), 1.0, 0.0)
    pick_low = jnp.where((row >= 8) & same & (lane < 8), 1.0, 0.0)
    pick_high = jnp.where((row >= 8) & same & (lane >= 8) & (lane < 16), 1.0, 0.0)
    picks = jnp.concatenate([pick_cos, pick_low, pick_high], axis=1).astype(F32)
    spread = lax.dot_general(
        trig, picks, (((0,), (0,)), ((), ())), preferred_element_type=F32, precision=lax.Precision.HIGHEST
    )
    lane_row = lax.broadcasted_iota(jnp.int32, (1, LANES), 1) & (HEAD - 1)
    cos_table = spread[:, :LANES] + jnp.where(lane_row >= ROT, 1.0, 0.0)
    return cos_table, spread[:, LANES : 2 * LANES], spread[:, 2 * LANES :]


def rotate(values, tables, back=False):
    cos_table, low_sin, high_sin = tables
    below = pltpu.roll(values, LANES - ROT // 2, 1) * low_sin
    above = pltpu.roll(values, ROT // 2, 1) * high_sin
    turned = below - above if back else above - below
    return values * cos_table + turned


def project_rows(layer, tok_shape, me_ref, seg_ref, weight, bias, a_ref, p_refs, proj_ref, with_seg):
    seq_count, block_len, width = tok_shape
    chip, core = me_ref[0], me_ref[1]
    base = (chip * 2 + core) * block_len
    for j in range(3):
        proj_ref[:, j * 2 * LANES : (j + 1) * 2 * LANES] = matmul(a_ref[...], weight(j)) + bias[j, layer : layer + 1, :]
    for k in range(4):
        seq = wrap4(chip + k)
        place = rows(seq, block_len)
        seg_row = seg_ref[pl.ds(seq, 1), :]
        spots = lax.broadcasted_iota(jnp.int32, (1, block_len), 1) + base
        tables = rotary_rows((spots - seg_row).astype(F32))
        for j in range(3):
            for pair in range(2):
                at = (2 * j + pair) * LANES
                part = proj_ref[place, at : at + LANES]
                if j < 2:
                    part = rotate(part, tables)
                p_refs[k][pair, 0:block_len, j * LANES : (j + 1) * LANES] = part.astype(BF16)
        if with_seg:
            coded = seg_row.astype(F32)
            high = jnp.floor(coded * 0.125)
            packed = jnp.concatenate([high, coded - 8.0 * high, jnp.zeros_like(high)], axis=1)
            packed = jnp.broadcast_to(packed, (16, 3 * LANES)).astype(BF16)
            for pair in range(2):
                p_refs[k][pair, block_len : block_len + 16, :] = packed


def project_first_body(tok_shape, me_ref, *refs):
    seq_count, block_len, width = tok_shape
    in_refs, refs = refs[:8], refs[8:]
    xq_ref, a_ref, m_ref, *p_refs = refs[:7]
    proj_ref, *held, sems = refs[7:]
    x_ref, seg_ref, ag_ref, as_ref, mg_ref, ms_ref, w_ref, b_ref = held
    copies = []
    for index in (1, 2, 3, 4, 5):
        copies.append(pltpu.make_async_copy(in_refs[index], held[index], sems.at[len(copies)]))
    copies.append(pltpu.make_async_copy(in_refs[7], b_ref, sems.at[len(copies)]))
    small_count = len(copies)
    for seq in range(seq_count):
        place = pl.ds(seq * block_len, block_len)
        copies.append(pltpu.make_async_copy(in_refs[0].at[place], x_ref.at[place], sems.at[len(copies)]))
    copies.append(pltpu.make_async_copy(in_refs[6].at[0], w_ref, sems.at[len(copies)]))
    for copy in copies:
        copy.start()
    for copy in copies[:small_count]:
        copy.wait()
    for seq in range(seq_count):
        copies[small_count + seq].wait()
        place = slice(seq * block_len, (seq + 1) * block_len)
        normed, _ = normalize(x_ref[place, :])
        a_ref[place, :] = (normed * ag_ref[0:1, :] + as_ref[0:1, :]).astype(BF16)
        m_ref[place, :] = (normed * mg_ref[0:1, :] + ms_ref[0:1, :]).astype(BF16)
    xq_ref[...] = x_ref[rows(me_ref[2], block_len), :]
    copies[-1].wait()
    project_rows(0, tok_shape, me_ref, seg_ref, lambda j: w_ref[j], b_ref, a_ref, p_refs, proj_ref, True)


def project_body(layer, tok_shape, me_ref, *refs):
    seq_count, block_len, width = tok_shape
    x_ref, seg_ref, *refs = refs
    u_refs, refs = refs[:4], refs[4:]
    ob_ref, db_ref, ag_ref, as_ref, mg_ref, ms_ref, w_ref, b_ref, x_out, xq_ref, a_ref, m_ref, *p_refs, proj_ref = refs
    tensor = me_ref[2]
    shift = ob_ref[layer - 1 : layer, :] + db_ref[layer - 1 : layer, :]
    for k in range(4):
        place = rows(wrap4(tensor - k), block_len)
        value = x_ref[place, :] + u_refs[k][...].astype(F32) + shift
        x_out[place, :] = value
        if k == 0:
            xq_ref[...] = value
        normed, _ = normalize(value)
        a_ref[place, :] = (normed * ag_ref[layer : layer + 1, :] + as_ref[layer : layer + 1, :]).astype(BF16)
        m_ref[place, :] = (normed * mg_ref[layer : layer + 1, :] + ms_ref[layer : layer + 1, :]).astype(BF16)
    project_rows(layer, tok_shape, me_ref, seg_ref, lambda j: w_ref[0, j], b_ref, a_ref, p_refs, proj_ref, False)


def gather_pieces(me_ref, refs, targets, block_len, seg_target=None):
    chip, core = me_ref[0], me_ref[1]
    for k in range(4):
        owner = wrap4(chip - k)
        for side, ref in ((core, refs[k]), (1 - core, refs[4 + k])):
            place = rows(owner * 2 + side, block_len)
            for index, target in enumerate(targets):
                target[place, :] = ref[core, 0:block_len, index * LANES : (index + 1) * LANES]
            if seg_target is not None:
                row = ref[core, block_len : block_len + 16, :].astype(F32)[0:1, :]
                starts = row[:, 0:LANES] * 8.0 + row[:, LANES : 2 * LANES]
                seg_target[:, place] = jnp.broadcast_to(starts, (8, block_len))


def head_stack(values):
    lane = lax.broadcasted_iota(jnp.int32, values.shape, 1)
    zero = jnp.zeros_like(values)
    return jnp.concatenate(
        [jnp.where(lane < HEAD, values, zero), jnp.where(lane >= HEAD, values, zero)], axis=0
    )


def own_halves(product, width):
    return jnp.concatenate([product[0:HEAD, 0:width], product[HEAD:, width : 2 * width]], axis=0)


def chances_t(q_ref, k_ref, seg_ref, step, chunk):
    start, keys = step * chunk, (step + 1) * chunk
    stacked = head_stack(q_ref[start:keys, :]) * jnp.asarray(HEAD ** (-0.5), BF16)
    scores = matmul_nt(k_ref[0:keys, :], stacked)
    key_place = lax.broadcasted_iota(jnp.int32, (keys, 2 * chunk), 0).astype(F32)
    query_place = (lax.broadcasted_iota(jnp.int32, (1, 2 * chunk), 1) & (chunk - 1)).astype(F32) + start
    seg_row = seg_ref[0:1, start:keys]
    seg_row = jnp.concatenate([seg_row, seg_row], axis=1)
    allowed = (key_place >= seg_row) & (key_place <= query_place)
    scores = jnp.where(allowed, scores, -1e30)
    raised = jnp.exp(scores - jnp.max(scores, axis=0, keepdims=True))
    total = jnp.sum(raised, axis=0, keepdims=True)
    return raised * (1.0 / total), stacked


def attend_body(block_len, chunk, me_ref, *refs):
    piece_refs, refs = refs[:8], refs[8:]
    seg_out, qkv_ref, *refs = refs
    o_refs, refs = refs[:4], refs[4:]
    vt_ref, o_ref = refs
    q_ref, k_ref, v_ref = qkv_ref.at[0], qkv_ref.at[1], qkv_ref.at[2]
    gather_pieces(me_ref, piece_refs, (q_ref, k_ref, v_ref), block_len, seg_out)
    vt_ref[...] = v_ref[...].T
    length = q_ref.shape[0]
    for step in range(length // chunk):
        keys = (step + 1) * chunk
        chances, _ = chances_t(q_ref, k_ref, seg_out, step, chunk)
        mixed = matmul(vt_ref[:, 0:keys], chances.astype(BF16))
        o_ref[step * chunk : keys, :] = own_halves(mixed, chunk).T.astype(BF16)
    send_blocks(me_ref, o_ref, o_refs, block_len)


def send_blocks(me_ref, source, targets, block_len):
    chip = me_ref[0]
    for k in range(4):
        dest = wrap4(chip + k)
        for side in range(2):
            targets[k][side] = source[rows(dest * 2 + side, block_len), :]


def attend_both_body(block_len, chunk, with_out, me_ref, *refs):
    if with_out:
        piece_refs, refs = refs[:8], refs[8:]
    else:
        qkv_ref, *refs = refs
    grad_refs, refs = refs[:8], refs[8:]
    seg_ref, *refs = refs
    d_refs, refs = refs[:4], refs[4:]
    if with_out:
        qkv_ref, *refs = refs
    q_ref, k_ref, v_ref = qkv_ref.at[0], qkv_ref.at[1], qkv_ref.at[2]
    g_ref, t_ref, o_ref, dq_ref, dk_ref, dv_ref = refs
    if with_out:
        gather_pieces(me_ref, piece_refs, (q_ref, k_ref, v_ref), block_len)
    gather_pieces(me_ref, grad_refs, (g_ref,), block_len)
    length = q_ref.shape[0]
    t_ref[0] = k_ref[...].T
    if with_out:
        t_ref[1] = v_ref[...].T
    dk_ref[...] = jnp.zeros_like(dk_ref)
    dv_ref[...] = jnp.zeros_like(dv_ref)
    for step in range(length // chunk):
        start, keys = step * chunk, (step + 1) * chunk
        chances, stacked = chances_t(q_ref, k_ref, seg_ref, step, chunk)
        low = chances.astype(BF16)
        if with_out:
            mixed = matmul(t_ref[1, :, 0:keys], low)
            o_ref[start:keys, :] = own_halves(mixed, chunk).T.astype(BF16)
        grads = head_stack(g_ref[start:keys, :])
        chance_grad = matmul_nt(v_ref[0:keys, :], grads)
        delta = jnp.sum(chances * chance_grad, axis=0, keepdims=True)
        score_grad = (chances * (chance_grad - delta)).astype(BF16)
        dv_ref[0:keys, :] += matmul(low, grads)
        dk_ref[0:keys, :] += matmul(score_grad, stacked)
        query = matmul(t_ref[0, :, 0:keys], score_grad)
        dq_ref[start:keys, :] = own_halves(query, chunk).T * HEAD ** (-0.5)
    chip = me_ref[0]
    for k in range(4):
        dest = wrap4(chip + k)
        for side in range(2):
            place = rows(dest * 2 + side, block_len)
            spots = (lax.broadcasted_iota(jnp.int32, (1, block_len), 1) + (dest * 2 + side) * block_len).astype(F32)
            tables = rotary_rows(spots - seg_ref[0:1, place])
            d_refs[k][side, :, 0:LANES] = rotate(dq_ref[place, :], tables, True).astype(BF16)
            d_refs[k][side, :, LANES : 2 * LANES] = rotate(dk_ref[place, :], tables, True).astype(BF16)
            d_refs[k][side, :, 2 * LANES : 3 * LANES] = dv_ref[place, :].astype(BF16)
            if with_out:
                d_refs[k][side, :, 3 * LANES :] = o_ref[place, :]


def land_heads(me_ref, refs, target, block_len, groups, first=0):
    chip, core = me_ref[0], me_ref[1]
    for k in range(4):
        place = rows(wrap4(chip - k), block_len)
        mine, other = refs[k][core], refs[4 + k][core]
        is_low = core == 0
        for group in range(groups):
            span = slice((first + group) * LANES, (first + group + 1) * LANES)
            at = group * 2 * LANES
            target[place, at : at + LANES] = jnp.where(is_low, mine[:, span], other[:, span])
            target[place, at + LANES : at + 2 * LANES] = jnp.where(is_low, other[:, span], mine[:, span])


def combine_body(block_len, fused, me_ref, *refs):
    piece_refs, refs = refs[:8], refs[8:]
    w_ref, *refs = refs
    if fused:
        g_ref, down_ref, *refs = refs
    else:
        part_ref, *refs = refs
    o_ref, *refs = refs
    q_refs, scr = refs[:-1], refs[-1]
    tensor = me_ref[2]
    land_heads(me_ref, piece_refs, o_ref, block_len, 1, 3 if fused else 0)
    part = matmul(g_ref[...], down_ref[0]) if fused else part_ref[...]
    scr[...] = (matmul(o_ref[...], w_ref[0]) + part).astype(BF16)
    for k in range(4):
        q_refs[k][...] = scr[rows(wrap4(tensor + k), block_len), :]


def send_grad_body(block_len, me_ref, x_ref, w_ref, *refs):
    chip, tensor = me_ref[0], me_ref[2]
    quarter_ref, *refs = refs
    quarter_ref[...] = x_ref[rows(tensor, block_len), :]
    for k in range(4):
        value = x_ref[rows(wrap4(chip + k), block_len), :].astype(BF16)
        grad = matmul_nt(value, w_ref[0]).astype(BF16)
        for pair in range(2):
            refs[k][pair] = grad[:, pair * LANES : (pair + 1) * LANES]


def join_body(block_len, me_ref, *refs):
    q_refs, refs = refs[:4], refs[4:]
    w_ref, r_ref, *g_refs = refs
    chip, tensor = me_ref[0], me_ref[2]
    for k in range(4):
        r_ref[rows(wrap4(tensor - k), block_len), :] = q_refs[k][...]
    for k in range(4):
        value = r_ref[rows(wrap4(chip + k), block_len), :]
        grad = matmul_nt(value, w_ref[0]).astype(BF16)
        for pair in range(2):
            g_refs[k][pair] = grad[:, pair * LANES : (pair + 1) * LANES]


def project_back_body(block_len, layer, me_ref, *refs):
    piece_refs, refs = refs[:8], refs[8:]
    w_ref, dm_ref, ag_ref, mg_ref, *refs = refs
    riders, refs = refs[:-8], refs[-8:]
    dp_ref, da_ref, bias_ref, *q_refs, scr = refs
    tensor = me_ref[2]
    land_heads(me_ref, piece_refs, dp_ref, block_len, 3)
    for j in range(3):
        span = slice(j * 2 * LANES, (j + 1) * 2 * LANES)
        bias_ref[j : j + 1, :] = jnp.sum(dp_ref[:, span].astype(F32), axis=0, keepdims=True)
    total = None
    for j in range(3):
        term = matmul_nt(dp_ref[:, j * 2 * LANES : (j + 1) * 2 * LANES], w_ref[0, j])
        total = term if total is None else total + term
    da_ref[...] = total.astype(BF16)
    scr[...] = (total * ag_ref[layer : layer + 1, :] + dm_ref[...] * mg_ref[layer : layer + 1, :]).astype(BF16)
    for k in range(4):
        q_refs[k][0:block_len, :] = scr[rows(wrap4(tensor + k), block_len), :]
        if riders:
            q_refs[k][block_len:, :] = riders[k][...]


def norm_back_body(me_ref, *refs):
    e_ref, x_ref, dy_ref, dx_ref, low_ref, bias_ref = refs
    upstream = dy_ref[...]
    size = upstream.shape[0]
    total = e_ref[0:size, :]
    normed, factor = normalize(x_ref[...])
    inner = jnp.mean(total * normed, axis=-1, keepdims=True)
    result = upstream + factor * (total - jnp.mean(total, axis=-1, keepdims=True) - normed * inner)
    dx_ref[...] = result
    low_ref[0:size, :] = result.astype(BF16)
    if e_ref.shape[0] > size:
        low_ref[size:, :] = e_ref[size:, :].astype(BF16)
    bias_ref[...] = jnp.sum(upstream, axis=0, keepdims=True)


def gains_body(me_ref, x_ref, da_ref, dm_ref, out_ref):
    normed, _ = normalize(x_ref[...])
    da = da_ref[...].astype(F32)
    dm = dm_ref[...]
    out_ref[0:1, :] = jnp.sum(da * normed, axis=0, keepdims=True)
    out_ref[1:2, :] = jnp.sum(da, axis=0, keepdims=True)
    out_ref[2:3, :] = jnp.sum(dm * normed, axis=0, keepdims=True)
    out_ref[3:4, :] = jnp.sum(dm, axis=0, keepdims=True)


def gelu_parts(hidden):
    cdf = 0.5 * (1.0 + lax.erf(hidden * (0.5**0.5)))
    density = jnp.exp(-0.5 * hidden * hidden) * 0.3989422804014327
    return cdf, density


def feed_body(layer, me_ref, m_ref, up_ref, ub_ref, down_ref, g_ref, slope_ref, part_ref):
    size = 2 * LANES
    for step in range(up_ref.shape[2] // size):
        span = slice(step * size, (step + 1) * size)
        hidden = matmul(m_ref[...], up_ref[0, :, span]) + ub_ref[layer : layer + 1, span]
        cdf, density = gelu_parts(hidden)
        g_ref[:, span] = (hidden * cdf).astype(BF16)
        slope_ref[:, span] = cdf + hidden * density
    part_ref[...] = matmul(g_ref[...], down_ref[0])


def feed_back_body(me_ref, r_ref, slope_ref, up_ref, down_ref, dh_ref, dm_ref, bias_ref):
    size = 2 * LANES
    for step in range(down_ref.shape[1] // size):
        span = slice(step * size, (step + 1) * size)
        grad = matmul_nt(r_ref[...], down_ref[0, span, :]) * slope_ref[:, span]
        bias_ref[:, span] = jnp.sum(grad, axis=0, keepdims=True)
        dh_ref[:, span] = grad.astype(BF16)
    dm_ref[...] = matmul_nt(dh_ref[...], up_ref[0])


def feed_both_body(layer, me_ref, m_ref, dy_ref, up_ref, ub_ref, down_ref, g_ref, r_ref, dh_ref, dm_ref, bias_ref):
    size = 2 * LANES
    r_ref[...] = dy_ref[...].astype(BF16)
    for step in range(up_ref.shape[2] // size):
        span = slice(step * size, (step + 1) * size)
        hidden = matmul(m_ref[...], up_ref[0, :, span]) + ub_ref[layer : layer + 1, span]
        cdf, density = gelu_parts(hidden)
        g_ref[:, span] = (hidden * cdf).astype(BF16)
        grad = matmul_nt(r_ref[...], down_ref[0, span, :]) * (cdf + hidden * density)
        bias_ref[:, span] = jnp.sum(grad, axis=0, keepdims=True)
        dh_ref[:, span] = grad.astype(BF16)
    dm_ref[...] = matmul_nt(dh_ref[...], up_ref[0])


def feed_weights_body(me_ref, m_ref, dh_ref, g_ref, r_ref, keep_ref, send_ref):
    core = me_ref[1]
    half = m_ref.shape[1] // 2
    for side, out in ((core, keep_ref), (1 - core, send_ref)):
        out[0:half, :] = matmul_tn(m_ref[:, rows(side, half)], dh_ref[...]).astype(BF16)
        out[half:, :] = matmul_tn(g_ref[:, rows(side, half)], r_ref[...]).astype(BF16)


def head_weights_body(me_ref, a_ref, dp_ref, o_ref, r_ref, keep_ref, send_ref):
    core = me_ref[1]
    half = a_ref.shape[1] // 2
    wide = dp_ref.shape[1]
    for side, out in ((core, keep_ref), (1 - core, send_ref)):
        out[:, 0:wide] = matmul_tn(a_ref[:, rows(side, half)], dp_ref[...]).astype(BF16)
        grad = matmul_tn(o_ref[:, rows(side, LANES)], r_ref[...]).astype(BF16)
        for part in range(4):
            out[part * LANES : (part + 1) * LANES, wide:] = grad[:, part * 2 * LANES : (part + 1) * 2 * LANES]


def feed_weights_whole_body(me_ref, m_ref, dh_ref, g_ref, r_ref, pack_ref):
    high = m_ref.shape[1]
    pack_ref[0:high, :] = matmul_tn(m_ref[...], dh_ref[...]).astype(BF16)
    pack_ref[high:, :] = matmul_tn(g_ref[...], r_ref[...]).astype(BF16)


def head_weights_whole_body(me_ref, a_ref, dp_ref, o_ref, r_ref, before_ref, pack_ref):
    wide = dp_ref.shape[1]
    pack_ref[:, 0:wide] = matmul_tn(a_ref[...], dp_ref[...]).astype(BF16)
    grad = matmul_tn(o_ref[...], r_ref[...]).astype(BF16)
    high, size = grad.shape[0], 2 * LANES
    for part in range(4):
        pack_ref[part * high : (part + 1) * high, wide:] = grad[:, part * size : (part + 1) * size]


def near_far(place):
    return place ^ 1, 3 - place


def halve_body(me_ref, feed_keep, feed_came, head_keep, head_came, *refs):
    outs, feed_scr, head_scr = refs[:4], refs[4], refs[5]
    feed_scr[...] = (feed_keep[...].astype(F32) + feed_came[...].astype(F32)).astype(BF16)
    head_scr[...] = (head_keep[...].astype(F32) + head_came[...].astype(F32)).astype(BF16)
    place = me_ref[3]
    near, far = near_far(place)
    half = head_scr.shape[0]
    size = half // 8
    orders = ((place, far), (near, 3 - near), (4 + place, 4 + near), (4 + far, 4 + (far ^ 1)))
    for ref, order in zip(outs, orders):
        for index, block in enumerate(order):
            at = 3 * size * index
            ref[at : at + size, :] = feed_scr[rows(block, size), :]
            ref[at + size : at + 2 * size, :] = feed_scr[pl.ds(pl.multiple_of(half + block * size, size), size), :]
            ref[at + 2 * size : at + 3 * size, :] = head_scr[rows(block, size), :]


def halve_again_body(me_ref, a_keep, a_came, b_keep, b_came, *outs):
    size = outs[0].shape[0]
    for keep, came, mine, send in ((a_keep, a_came, outs[0], outs[1]), (b_keep, b_came, outs[2], outs[3])):
        total = (keep[...].astype(F32) + came[...].astype(F32)).astype(BF16)
        mine[...] = total[0:size, :]
        send[...] = total[size:, :]


def line_up_body(axis, me_ref, *refs):
    size = refs[4].shape[0] // 4
    for k in range(4):
        refs[4][rows(wrap4(me_ref[axis] - k), size), :] = refs[k][0:size, :]
    if len(refs) > 5:
        even = refs[0][size:, :].astype(F32) + refs[2][size:, :].astype(F32)
        odd = refs[1][size:, :].astype(F32) + refs[3][size:, :].astype(F32)
        refs[5][...] = (even + odd).astype(BF16)


def merge_body(me_ref, a_keep, a_came, b_keep, b_came, small_ref, *refs):
    out_refs, scr = refs[:4], refs[4]
    high = a_keep.shape[0]
    scr[0:high, :] = (a_keep[...].astype(F32) + a_came[...].astype(F32)).astype(BF16)
    scr[high:, :] = (b_keep[...].astype(F32) + b_came[...].astype(F32)).astype(BF16)
    few = high // 6
    for k in range(4):
        part = wrap4(me_ref[0] + k)
        for weight in range(3):
            at = pl.multiple_of((part >> 1) * high + weight * 2 * few + (part & 1) * few, few)
            out_refs[k][weight * few : (weight + 1) * few, :] = scr[pl.ds(at, few), :]
        out_refs[k][3 * few :, :] = small_ref[...]


def settle_body(me_ref, *refs):
    in_refs, (first_ref, second_ref) = refs[:4], refs[4:]
    even = in_refs[0][...].astype(F32) + in_refs[2][...].astype(F32)
    odd = in_refs[1][...].astype(F32) + in_refs[3][...].astype(F32)
    total = (even + odd).astype(BF16)
    few = first_ref.shape[0] // 3
    for weight in range(3):
        for index, ref in enumerate((first_ref, second_ref)):
            at = (2 * weight + index) * few
            ref[weight * few : (weight + 1) * few, :] = total[at : at + few, :]
    second_ref[3 * few :, :] = total[6 * few :, :]


def flush(held, outs, layer, sems):
    copies = [pltpu.make_async_copy(a, b.at[layer], sems.at[i]) for i, (a, b) in enumerate(zip(held, outs))]
    return copies


def unpack_body(few, me_ref, *refs):
    outs, held, sems = refs[24:28], refs[28:32], refs[32]
    up_ref, down_ref, qkv_ref, out_ref = held
    copies = flush(held, outs, 0, sems)
    chip, core, place_z = me_ref[0], me_ref[1], me_ref[3]
    size = 2 * LANES
    half = up_ref.shape[0] // 2
    for weight in range(3):
        for side, group in ((core, refs[:10]), (1 - core, refs[10:20])):
            for along, me in ((0, place_z), (1, chip)):
                pieces = group[5 * along : 5 * along + 5]
                spans = [(pieces[0], me, 0), (pieces[1], me ^ 1, 0), (pieces[2], 3 - me, 0)]
                spans += [(pieces[3], me ^ 2, 0), (pieces[4], me ^ 2, 2)]
                for ref, owner, first in spans:
                    for index in range(ref.shape[0] // (3 * few)):
                        z, x = (owner, first + index) if along == 0 else (first + index, owner)
                        start = (3 * index + weight) * few
                        value = ref[start : start + few, :].astype(F32)
                        row = (z + 4 * (x >> 1)) * (4 * few) + (x & 1) * (2 * few) + along * few
                        place = pl.ds(pl.multiple_of(row + side * half, few), few)
                        if weight < 2:
                            held[weight][place, :] = value
                        else:
                            for j in range(3):
                                qkv_ref[j, place, :] = value[:, j * size : (j + 1) * size]
                            inner = pl.ds(pl.multiple_of((row & (LANES - 1)) + side * LANES, few), few)
                            lanes = pl.ds(pl.multiple_of((row >> 7) * size, size), size)
                            out_ref[inner, lanes] = value[:, 3 * size :]
        for copy in copies[weight : weight + 1] if weight < 2 else copies[2:]:
            copy.start()
    for copy in copies:
        copy.wait()


def add_packs_body(me_ref, feed_keep, feed_came, head_keep, head_came, out_ref):
    high = feed_keep.shape[0]
    out_ref[0:high, :] = (feed_keep[...].astype(F32) + feed_came[...].astype(F32)).astype(BF16)
    out_ref[high:, :] = (head_keep[...].astype(F32) + head_came[...].astype(F32)).astype(BF16)


def unpack_whole_body(me_ref, up_mine, down_mine, head_mine, up_other, down_other, head_other, *outs):
    up_ref, down_ref, qkv_ref, out_ref = outs
    size = 2 * LANES
    for core in range(2):
        mine = me_ref[1] == core
        for ref, first, second in ((up_ref, up_mine, up_other), (down_ref, down_mine, down_other)):
            ref[0, core] = jnp.where(mine, first[...], second[...]).astype(F32)
        head = jnp.where(mine, head_mine[...], head_other[...]).astype(F32)
        for j in range(3):
            qkv_ref[0, j, core] = head[:, j * size : (j + 1) * size]
        out_ref[0, core] = head[:, 3 * size :]


def pack_small_body(me_ref, *refs):
    ins, small_ref = refs[:8], refs[8]
    width = small_ref.shape[1]
    blank = jnp.zeros((1, width), F32)
    shared = [ins[0][...], ins[1][...], ins[2][...], ins[3][...]] + [blank] * 6
    small_ref[0:16, :] = jnp.concatenate(shared, axis=0).astype(BF16)
    local = [ins[6][...], ins[7][...]]
    for ref in ins[4:6]:
        values = ref[...]
        flat = [values[j : j + 1, :] for j in range(3)]
        local.append(jnp.concatenate(flat + [jnp.zeros((1, width - 3 * values.shape[1]), F32)], axis=1))
    small_ref[16:32, :] = jnp.concatenate(local + [blank] * 12, axis=0).astype(BF16)


def add_cut_body(me_ref, mine_ref, came_ref, shared_ref, local_ref):
    total = (mine_ref[...].astype(F32) + came_ref[...].astype(F32)).astype(BF16)
    half = shared_ref.shape[0]
    shared_ref[...] = total[0:half, :]
    local_ref[...] = total[half:, :]


def add_body(count, me_ref, *refs):
    total = refs[0][...].astype(F32)
    for ref in refs[1:count]:
        total = total + ref[...].astype(F32)
    refs[count][...] = total.astype(refs[count].dtype)


def small_out_body(me_ref, mine_ref, came_ref, local_ref, *outs):
    shared = mine_ref[...].astype(F32) + came_ref[...].astype(F32)
    local = local_ref[...].astype(F32)
    for index in range(5):
        outs[index][0:1, :] = shared[index : index + 1, :]
        outs[index][1:2, :] = shared[index + 5 : index + 6, :]
    outs[5][...] = local[0:2, :]
    size = outs[6].shape[2]
    for layer in range(2):
        for j in range(3):
            outs[6][layer, j : j + 1, :] = local[2 + layer : 3 + layer, j * size : (j + 1) * size]


def place_body(block_len, me_ref, *refs):
    q_refs, (x_ref, ob_ref, db_ref, grad_ref, out_ref) = refs[:4], refs[4:]
    shift = ob_ref[1:2, :] + db_ref[1:2, :]
    for k in range(4):
        place = rows(wrap4(me_ref[2] - k), block_len)
        grad_ref[place, :] = q_refs[k][0:block_len, :].astype(F32)
        out_ref[place, :] = x_ref[place, :] + q_refs[k][block_len:, :].astype(F32) + shift


def chip_turn(shift):
    return [(2 * x + c, 2 * ((x + shift) % 4) + c) for x in range(4) for c in range(2)]


CORE_SWAP = [(i, i ^ 1) for i in range(8)]


def over_chips(pieces, beside=()):
    mine, beside = lax.optimization_barrier((over_x(pieces), beside))
    return mine + [swap_core(piece) for piece in mine], beside


def ring_turn(shift):
    return [(i, (i + shift) % 4) for i in range(4)]


def over_tensor(pieces):
    return [pieces[0]] + [lax.ppermute(pieces[k], "tensor", ring_turn(k)) for k in range(1, 4)]


def share_tensor(piece):
    return over_tensor([piece] * 4)


def over_dp(pieces):
    return [pieces[0]] + [lax.ppermute(pieces[k], "dp", ring_turn(k)) for k in range(1, 4)]


def over_x(pieces):
    return [pieces[0]] + [lax.ppermute(pieces[k], "ctx", chip_turn(k)) for k in range(1, 4)]


def swap_core(piece):
    return lax.ppermute(piece, "ctx", CORE_SWAP)


NEXT_PAIR = [(0, 1), (1, 0), (2, 3), (3, 2)]
WRAP_PAIR = [(0, 3), (3, 0), (1, 2), (2, 1)]


def both_ways(to_next, to_wrap):
    return lax.ppermute(to_next, "dp", NEXT_PAIR), lax.ppermute(to_wrap, "dp", WRAP_PAIR)


def chips_of(pairs):
    return [(2 * a + c, 2 * b + c) for a, b in pairs for c in range(2)]


def spread_near(piece, axis):
    name, move = ("dp", lambda pairs: pairs) if axis == "dp" else ("ctx", chips_of)
    return [piece] + [lax.ppermute(piece, name, move(pairs)) for pairs in (NEXT_PAIR, WRAP_PAIR)]


def spread_far(pieces, axis):
    name, move = ("dp", lambda pairs: pairs) if axis == "dp" else ("ctx", chips_of)
    half = pieces[0].shape[0] // 2
    return pieces + [
        lax.ppermute(pieces[1][:half], name, move(WRAP_PAIR)),
        lax.ppermute(pieces[2][half:], name, move(NEXT_PAIR)),
    ]


def tie(first, second):
    return lax.optimization_barrier((first, second))


def after(values, token):
    return lax.optimization_barrier((values, token))[0]


def add_up(pieces):
    total = pieces[0].astype(F32)
    for piece in pieces[1:]:
        total = total + piece.astype(F32)
    return total


def on_device(
    inputs,
    segments,
    attn_gain,
    attn_shift,
    mlp_gain,
    mlp_shift,
    qkv_weight,
    qkv_bias,
    out_weight,
    out_bias,
    up_weight,
    up_bias,
    down_weight,
    down_bias,
    cotangent,
):
    seq_count, block_len, width = inputs.shape
    tokens = seq_count * block_len
    inner = qkv_weight.shape[3]
    hidden = up_weight.shape[2]
    length = block_len * 8
    chunk = 256
    place = lax.axis_index("ctx")
    me = jnp.stack([place // 2, place % 2, lax.axis_index("tensor"), lax.axis_index("dp")]).astype(jnp.int32)
    x0 = inputs.reshape(tokens, width)
    dy1 = cotangent.reshape(tokens, width)
    tok_shape = inputs.shape
    wide = shape_of((tokens, width), BF16)
    norms = (attn_gain, attn_shift, mlp_gain, mlp_shift)
    biases = qkv_bias.transpose(1, 0, 2)

    def project_first(x):
        sources = [x, segments, *norms, qkv_weight, biases]
        held = [v.shape for v in sources[:6]] + [qkv_weight.shape[1:], biases.shape]
        piece = shape_of((2, block_len + 16, 3 * LANES), BF16)
        return run(
            functools.partial(project_first_body, tok_shape),
            me,
            [(v, pl.BlockSpec(memory_space=pltpu.HBM)) for v in sources],
            [shape_of((block_len, width), F32), wide, wide] + [piece] * 4,
            scratch=[pltpu.VMEM((tokens, 3 * inner), F32)]
            + [pltpu.VMEM(size, v.dtype) for size, v in zip(held, sources)]
            + [pltpu.SemaphoreType.DMA((11,))],
            name="norm_project",
            limit=62,
        )

    def project(layer, x, extra):
        piece = shape_of((2, block_len, 3 * LANES), BF16)
        return run(
            functools.partial(project_body, layer, tok_shape),
            me,
            [x, segments, *extra, *norms]
            + [(qkv_weight, layer_spec(qkv_weight, layer)), biases],
            [shape_of((tokens, width), F32), shape_of((block_len, width), F32), wide, wide] + [piece] * 4,
            scratch=[pltpu.VMEM((tokens, 3 * inner), F32)],
            name="norm_project",
            limit=24,
        )

    def feed(layer, m):
        return run(
            functools.partial(feed_body, layer),
            me,
            [m, (up_weight, layer_spec(up_weight, layer)), up_bias, (down_weight, layer_spec(down_weight, layer))],
            [shape_of((tokens, hidden), BF16), shape_of((tokens, hidden), F32), shape_of((tokens, width), F32)],
            name="feed", limit=24,
        )

    def feed_back(layer, r, slope):
        return run(
            feed_back_body,
            me,
            [r, slope, (up_weight, layer_spec(up_weight, layer)), (down_weight, layer_spec(down_weight, layer))],
            [shape_of((tokens, hidden), BF16), shape_of((tokens, width), F32), shape_of((1, hidden), F32)],
            name="feed_back", limit=24,
        )

    def feed_both(layer, m, dy):
        return run(
            functools.partial(feed_both_body, layer),
            me,
            [m, dy, (up_weight, layer_spec(up_weight, layer)), up_bias, (down_weight, layer_spec(down_weight, layer))],
            [shape_of((tokens, hidden), BF16), wide, shape_of((tokens, hidden), BF16)]
            + [shape_of((tokens, width), F32), shape_of((1, hidden), F32)],
            name="feed_both", limit=24,
        )

    def combine(layer, pieces, part, active=None):
        fused = part is None
        got = run(
            functools.partial(combine_body, block_len, fused),
            me,
            [*pieces, (out_weight, layer_spec(out_weight, layer))]
            + ([active, (down_weight, layer_spec(down_weight, layer))] if fused else [part]),
            [shape_of((tokens, inner), BF16)] + [shape_of((block_len, width), BF16)] * 4,
            scratch=[pltpu.VMEM((tokens, width), BF16)],
            name="combine", limit=20,
        )
        return got[0], got[1:]

    def add_all(values, dtype=BF16):
        out = shape_of(values[0].shape, dtype)
        return run(functools.partial(add_body, len(values)), me, values, [out], name="add_all", limit=16)[0]

    def line_up(axis, values, size):
        extra = values[0].shape[0] - size
        small = [shape_of((extra, width), BF16)] if extra else []
        outs = [shape_of((4 * size, width), BF16)] + small
        return run(functools.partial(line_up_body, axis), me, values, outs, name="line_up", limit=8)

    seq_bf16 = pltpu.VMEM((length, LANES), BF16)
    seq_f32 = pltpu.VMEM((length, LANES), F32)
    o_shapes = [shape_of((2, block_len, LANES), BF16)] * 4

    def attend_both(pieces, grads, seg_rows, with_out):
        return run(
            functools.partial(attend_both_body, block_len, chunk, with_out),
            me,
            [*pieces, *grads, seg_rows],
            [shape_of((2, block_len, (4 if with_out else 3) * LANES), BF16)] * 4,
            scratch=([pltpu.VMEM((3, length, LANES), BF16)] if with_out else [])
            + [seq_bf16, pltpu.VMEM((2, LANES, length), BF16), seq_bf16]
            + [seq_f32] * 3,
            name="attend_both", limit=24,
        )

    def project_back(layer, pieces, dm, riders=()):
        got = run(
            functools.partial(project_back_body, block_len, layer),
            me,
            [*pieces, (qkv_weight, layer_spec(qkv_weight, layer)), dm, attn_gain, mlp_gain, *riders],
            [shape_of((tokens, 3 * inner), BF16), wide, shape_of((3, inner), F32)]
            + [shape_of((block_len * (2 if riders else 1), width), BF16)] * 4,
            scratch=[pltpu.VMEM((tokens, width), BF16)],
            name="project_back", limit=24,
        )
        return got[0], got[1], got[2], got[3:]

    def norm_back(pieces, x, dy):
        quarter = shape_of((block_len, width), F32)
        return run(
            norm_back_body,
            me,
            [add_up(pieces), x, dy],
            [quarter, shape_of(pieces[0].shape, BF16), shape_of((1, width), F32)],
            name="norm_back",
            limit=10,
        )

    def gains(x, da, dm):
        return run(gains_body, me, [x, da, dm], [shape_of((4, width), F32)], name="gains", limit=16)[0]

    half = width // 2
    columns = [[8 * z + 2 * chip + core for z in range(4) for chip in range(4)] for core in range(2)]

    def feed_weights(m, dh, active, r):
        pack = shape_of((2 * half, width), BF16)
        return run(feed_weights_body, me, [m, dh, active, r], [pack] * 2, name="feed_weights", limit=24)

    def head_weights(attn_in, dproj, attended, r):
        pack = shape_of((half, width), BF16)
        return run(head_weights_body, me, [attn_in, dproj, attended, r], [pack] * 2, name="head_weights", limit=20)

    x0_quarter, a0, m0, *pieces = project_first(x0)
    fed0 = feed(0, m0)
    pieces0, (active0, slope0, part0) = over_chips(pieces, fed0)
    got = run(
        functools.partial(attend_body, block_len, chunk),
        me,
        pieces0,
        [shape_of((8, length), F32), shape_of((3, length, LANES), BF16)] + o_shapes,
        scratch=[pltpu.VMEM((LANES, length), BF16), seq_bf16],
        name="attend", limit=20,
    )
    seg_rows, qkv0 = got[:2]
    out0, _ = over_chips(got[2:])
    attended0, u0 = combine(0, out0, part0)
    dy1_quarter, *grads1 = run(
        functools.partial(send_grad_body, block_len),
        me,
        [after(dy1, u0[0]), (out_weight, layer_spec(out_weight, 1))],
        [shape_of((block_len, width), F32)] + o_shapes,
        name="out_back", limit=14,
    )
    grads1 = over_x(grads1)
    u0 = share_tensor(add_up(over_tensor(u0)).astype(BF16))
    u0, grads1 = tie(u0, grads1)
    grads1_other = [swap_core(piece) for piece in grads1]

    x1, x1_quarter, a1, m1, *pieces = project(1, x0, [*u0, out_bias, down_bias])
    fed1 = feed_both(1, m1, dy1)
    pieces1, ((active1, r1, dh1, dm1, up_b1), grads1_other) = over_chips(pieces, (fed1, grads1_other))
    got = attend_both(pieces1, grads1 + grads1_other, seg_rows, True)
    feed_pack1 = feed_weights(after(m1, got[0]), dh1, active1, r1)
    back1, feed_pack1 = over_chips(got, feed_pack1)
    dproj1, da1, qkv_b1, e1 = project_back(1, back1, dm1)
    back1, (feed_keep, feed_send) = after((back1, feed_pack1), e1[0])
    attended1, u1 = combine(1, back1, None, active1)
    head_keep, head_send = head_weights(a1, dproj1, attended1, r1)
    e1, (u1, head_keep, head_send, feed_came) = tie(over_tensor(e1), (u1, head_keep, head_send, swap_core(feed_send)))
    pack1 = run(
        add_packs_body,
        me,
        [feed_keep, feed_came, head_keep, swap_core(head_send)],
        [shape_of((3 * half, width), BF16)],
        name="add_packs",
        limit=16,
    )[0]
    part1 = lax.psum_scatter(pack1, ("dp", "ctx"), axis_index_groups=columns, tiled=True)
    dx1, low1, bias1 = norm_back(e1, x1_quarter, dy1_quarter)
    gains1 = gains(after(x1, low1), da1, dm1)
    quarters, gains1 = tie(share_tensor(low1), gains1)

    r0, *grads0 = run(
        functools.partial(join_body, block_len),
        me,
        [*quarters, (out_weight, layer_spec(out_weight, 0))],
        [wide] + o_shapes,
        name="join_out_back", limit=14,
    )
    dh0, dm0, up_b0 = feed_back(0, r0, slope0)
    grads0, (dh0, dm0) = over_chips(grads0, (dh0, dm0))
    back0 = attend_both([qkv0], grads0, seg_rows, False)
    feed_pack0 = feed_weights(after(m0, back0[0]), dh0, active0, r0)
    back0, (feed_keep, feed_send) = over_chips(back0, feed_pack0)
    dproj0, da0, qkv_b0, e0 = project_back(0, back0, dm0, u1)
    head_keep, head_send = head_weights(a0, dproj0, attended0, r0)
    e0 = after(e0, head_keep)
    way = shape_of((3 * half // 4, width), BF16)
    a_keep, a_send, b_keep, b_send = run(
        halve_body,
        me,
        [feed_keep, swap_core(feed_send), head_keep, swap_core(head_send)],
        [way] * 4,
        scratch=[pltpu.VMEM((2 * half, width), BF16), pltpu.VMEM((half, width), BF16)],
        name="halve",
        limit=20,
    )
    gains0 = gains(after(x0, a_send), da0, dm0)
    a_came, b_came = both_ways(a_send, b_send)
    e0, (gains0, a_came, b_came) = tie(over_tensor(e0), (gains0, a_came, b_came))
    way = shape_of((3 * half // 8, width), BF16)
    a_keep, a_send, b_keep, b_send = run(
        halve_again_body, me, [a_keep, a_came, b_keep, b_came], [way] * 4, name="halve_again", limit=12
    )
    b_came, a_came = both_ways(b_send, a_send)
    part1 = after(part1, a_send)
    pack1 = lax.all_gather(part1, ("dp", "ctx"), axis_index_groups=columns, tiled=True)
    dx0, low0, bias0 = norm_back(after(e0, a_send), x0_quarter, dx1)
    last = share_tensor(low0)
    small = run(
        pack_small_body,
        me,
        [gains0, bias0, gains1, bias1, qkv_b0, qkv_b1, up_b0, up_b1],
        [shape_of((32, width), BF16)],
        name="pack_small",
        limit=8,
    )[0]

    few = half // 32
    cut = run(
        merge_body,
        me,
        [a_keep, a_came, b_keep, b_came, small],
        [shape_of((6 * few + 32, width), BF16)] * 4,
        scratch=[pltpu.VMEM((24 * few, width), BF16)],
        name="merge",
        limit=12,
    )
    input_grad, output = run(
        functools.partial(place_body, block_len),
        me,
        [*last, x1, out_bias, down_bias],
        [shape_of((tokens, width), F32)] * 2,
        name="place",
        limit=20,
    )
    cut, (input_grad, output) = tie(over_x(cut), (input_grad, output))
    pieces = [shape_of((3 * few, width), BF16), shape_of((3 * few + 32, width), BF16)]
    first, second = run(settle_body, me, cut, pieces, name="settle", limit=8)
    first, second = tie(over_x([first] * 4), over_dp([second] * 4))
    second, small = line_up(3, second, 3 * few)
    first = line_up(0, first, 3 * few)[0]
    near = (spread_near(first, "dp"), spread_near(second, "x"))

    pack1 = after(pack1, first)
    heavy = [
        shape_of((2, width, hidden), F32),
        shape_of((2, hidden, width), F32),
        shape_of((2, 3, width, inner), F32),
        shape_of((2, inner, width), F32),
    ]
    quarter = half // 4
    views = [(2, 2, half, width)] * 2 + [(2, 3, 2, half, inner), (2, 2, LANES, width)]
    first_outs = run(
        unpack_whole_body,
        me,
        [
            (pack, pl.BlockSpec((quarter, width), lambda i, *_, part=part: (4 * part + i, 0)))
            for pack in (pack1, swap_core(pack1))
            for part in range(3)
        ],
        [shape_of(view, F32) for view in views],
        name="unpack_whole",
        limit=24,
        out_specs=[
            pl.BlockSpec((1, 2, quarter, width), lambda i, *_: (1, 0, i, 0)),
            pl.BlockSpec((1, 2, quarter, width), lambda i, *_: (1, 0, i, 0)),
            pl.BlockSpec((1, 3, 2, quarter, inner), lambda i, *_: (1, 0, 0, i, 0)),
            pl.BlockSpec((1, 2, LANES, 2 * LANES), lambda i, *_: (1, 0, 0, i)),
        ],
        grid=4,
    )
    first_outs = [v.reshape(like.shape) for v, like in zip(first_outs, heavy)]
    row_block = shape_of((16, width), BF16)
    shared, local = run(add_cut_body, me, [small, swap_core(small)], [row_block] * 2, name="add_cut", limit=8)
    shared_came = lax.ppermute(shared, "tensor", NEXT_PAIR)
    near, shared_came = tie(near, shared_came)
    far = (spread_far(near[0], "dp"), spread_far(near[1], "x"))
    other = [swap_core(v) for v in near[0] + near[1]]
    shared = add_all([shared, shared_came])
    shared_came = lax.ppermute(shared, "tensor", WRAP_PAIR)
    row_pair = shape_of((2, width), F32)
    small = run(
        small_out_body,
        me,
        [shared, shared_came, local],
        [row_pair] * 6 + [shape_of((2, 3, inner), F32)],
        name="small_out",
        limit=8,
    )
    mine, (small, other, first_outs) = tie(far[0] + far[1], (small, other, first_outs))
    far = [swap_core(v) for v in mine[3:5] + mine[8:10]]
    other = other[0:3] + far[0:2] + other[3:6] + far[2:4]
    in_place = pl.BlockSpec(memory_space=pl.ANY)
    held = [pltpu.VMEM(v.shape[1:], F32) for v in heavy] + [pltpu.SemaphoreType.DMA((4,))]
    up_grad, down_grad, qkv_grad, out_grad = run(
        functools.partial(unpack_body, few),
        me,
        mine + other + [(v, in_place) for v in first_outs],
        heavy,
        name="unpack",
        limit=28,
        out_specs=[in_place] * 4,
        scratch=held,
        aliases={21 + index: index for index in range(4)},
    )
    return (
        output.reshape(tok_shape),
        input_grad.reshape(tok_shape),
        small[0],
        small[1],
        small[2],
        small[3],
        qkv_grad,
        small[6],
        out_grad,
        small[4],
        up_grad,
        small[5],
        down_grad,
        small[4],
    )


def solution(mesh):
    in_specs = (
        P("dp", "ctx", None),
        P("dp", "ctx"),
        P(),
        P(),
        P(),
        P(),
        P(None, None, None, "tensor"),
        P(None, None, "tensor"),
        P(None, "tensor", None),
        P(),
        P(None, None, "tensor"),
        P(None, "tensor"),
        P(None, "tensor", None),
        P(),
        P("dp", "ctx", None),
    )
    out_specs = (
        P("dp", "ctx", None),
        P("dp", "ctx", None),
        P(),
        P(),
        P(),
        P(),
        P(None, None, None, "tensor"),
        P(None, None, "tensor"),
        P(None, "tensor", None),
        P(),
        P(None, None, "tensor"),
        P(None, "tensor"),
        P(None, "tensor", None),
        P(),
    )
    return jax.shard_map(
        on_device, mesh=mesh, in_specs=in_specs, out_specs=out_specs, check_vma=False
    )
```

```python
import functools

import jax
import jax.numpy as jnp
from jax import lax
from jax.experimental import pallas as pl
from jax.experimental.pallas import tpu as pltpu
from jax.sharding import PartitionSpec as P

HEAD = 64
ROT = 16
LAYERS = 2
LANES = 128
F32 = jnp.float32
BF16 = jnp.bfloat16


def shape_of(shape, dtype):
    return jax.ShapeDtypeStruct(tuple(shape), dtype)


def whole(array):
    rank = array.ndim
    return pl.BlockSpec(array.shape, lambda i, *_: (0,) * rank, pipeline_mode=pl.Buffered(1))


def layer_spec(array, layer):
    rank = array.ndim
    return pl.BlockSpec(
        (1,) + array.shape[1:], lambda i, *_: (layer,) + (0,) * (rank - 1), pipeline_mode=pl.Buffered(1)
    )


def run(body, me, operands, outs, scratch=(), name=None, limit=32, out_specs=None, aliases=None, grid=1):
    arrays, specs = [], []
    for operand in operands:
        array, spec = operand if isinstance(operand, tuple) else (operand, None)
        arrays.append(array)
        specs.append(whole(array) if spec is None else spec)
    return pl.pallas_call(
        body,
        grid_spec=pltpu.PrefetchScalarGridSpec(
            num_scalar_prefetch=1,
            grid=(grid,),
            in_specs=specs,
            out_specs=[whole(o) for o in outs] if out_specs is None else out_specs,
            scratch_shapes=list(scratch),
        ),
        out_shape=list(outs),
        input_output_aliases=aliases or {},
        compiler_params=pltpu.CompilerParams(vmem_limit_bytes=limit * 1024 * 1024),
        cost_estimate=pl.CostEstimate(flops=1, bytes_accessed=1, transcendentals=0),
        name=name,
    )(me, *arrays)


def matmul(left, right):
    return jnp.dot(left, right, preferred_element_type=F32)


def matmul_nt(left, right):
    return lax.dot_general(left, right, (((1,), (1,)), ((), ())), preferred_element_type=F32)


def matmul_tn(left, right):
    return lax.dot_general(left, right, (((0,), (0,)), ((), ())), preferred_element_type=F32)


def normalize(values):
    average = jnp.mean(values, axis=-1, keepdims=True)
    centred = values - average
    factor = lax.rsqrt(jnp.mean(centred * centred, axis=-1, keepdims=True) + 1e-05)
    return centred * factor, factor


def wrap4(value):
    return lax.rem(value + 4, 4)


def rows(index, size):
    return pl.ds(pl.multiple_of(index * size, size), size)


def rotary_rows(place_row):
    count = place_row.shape[1]
    which = lax.broadcasted_iota(jnp.int32, (8, count), 0)
    frequency = jnp.zeros((8, count), F32)
    for index in range(8):
        frequency = jnp.where(which == index, 10000.0 ** (-2.0 * index / ROT), frequency)
    angles = frequency * place_row
    trig = jnp.concatenate([jnp.cos(angles), jnp.sin(angles)], axis=0)
    row = lax.broadcasted_iota(jnp.int32, (16, LANES), 0)
    lane = lax.broadcasted_iota(jnp.int32, (16, LANES), 1) & (HEAD - 1)
    same = (lane & 7) == (row & 7)
    is_cos = row < 8
    pick_cos = jnp.where(is_cos & same & (lane < 16), 1.0, 0.0)
    pick_low = jnp.where((row >= 8) & same & (lane < 8), 1.0, 0.0)
    pick_high = jnp.where((row >= 8) & same & (lane >= 8) & (lane < 16), 1.0, 0.0)
    picks = jnp.concatenate([pick_cos, pick_low, pick_high], axis=1).astype(F32)
    spread = lax.dot_general(
        trig, picks, (((0,), (0,)), ((), ())), preferred_element_type=F32, precision=lax.Precision.HIGHEST
    )
    lane_row = lax.broadcasted_iota(jnp.int32, (1, LANES), 1) & (HEAD - 1)
    cos_table = spread[:, :LANES] + jnp.where(lane_row >= ROT, 1.0, 0.0)
    return cos_table, spread[:, LANES : 2 * LANES], spread[:, 2 * LANES :]


def rotate(values, tables, back=False):
    cos_table, low_sin, high_sin = tables
    below = pltpu.roll(values, LANES - ROT // 2, 1) * low_sin
    above = pltpu.roll(values, ROT // 2, 1) * high_sin
    turned = below - above if back else above - below
    return values * cos_table + turned


def project_rows(layer, tok_shape, me_ref, seg_ref, weight, bias, a_ref, p_refs, proj_ref, with_seg):
    seq_count, block_len, width = tok_shape
    chip, core = me_ref[0], me_ref[1]
    base = (chip * 2 + core) * block_len
    for j in range(3):
        proj_ref[:, j * 2 * LANES : (j + 1) * 2 * LANES] = matmul(a_ref[...], weight(j)) + bias[j, layer : layer + 1, :]
    for k in range(4):
        seq = wrap4(chip + k)
        place = rows(seq, block_len)
        seg_row = seg_ref[pl.ds(seq, 1), :]
        spots = lax.broadcasted_iota(jnp.int32, (1, block_len), 1) + base
        tables = rotary_rows((spots - seg_row).astype(F32))
        for j in range(3):
            for pair in range(2):
                at = (2 * j + pair) * LANES
                part = proj_ref[place, at : at + LANES]
                if j < 2:
                    part = rotate(part, tables)
                p_refs[k][pair, 0:block_len, j * LANES : (j + 1) * LANES] = part.astype(BF16)
        if with_seg:
            coded = seg_row.astype(F32)
            high = jnp.floor(coded * 0.125)
            packed = jnp.concatenate([high, coded - 8.0 * high, jnp.zeros_like(high)], axis=1)
            packed = jnp.broadcast_to(packed, (16, 3 * LANES)).astype(BF16)
            for pair in range(2):
                p_refs[k][pair, block_len : block_len + 16, :] = packed


def project_first_body(tok_shape, me_ref, *refs):
    seq_count, block_len, width = tok_shape
    in_refs, refs = refs[:8], refs[8:]
    xq_ref, a_ref, m_ref, *p_refs = refs[:7]
    proj_ref, *held, sems = refs[7:]
    x_ref, seg_ref, ag_ref, as_ref, mg_ref, ms_ref, w_ref, b_ref = held
    copies = []
    for index in (1, 2, 3, 4, 5):
        copies.append(pltpu.make_async_copy(in_refs[index], held[index], sems.at[len(copies)]))
    copies.append(pltpu.make_async_copy(in_refs[7], b_ref, sems.at[len(copies)]))
    small_count = len(copies)
    for seq in range(seq_count):
        place = pl.ds(seq * block_len, block_len)
        copies.append(pltpu.make_async_copy(in_refs[0].at[place], x_ref.at[place], sems.at[len(copies)]))
    copies.append(pltpu.make_async_copy(in_refs[6].at[0], w_ref, sems.at[len(copies)]))
    for copy in copies:
        copy.start()
    for copy in copies[:small_count]:
        copy.wait()
    for seq in range(seq_count):
        copies[small_count + seq].wait()
        place = slice(seq * block_len, (seq + 1) * block_len)
        normed, _ = normalize(x_ref[place, :])
        a_ref[place, :] = (normed * ag_ref[0:1, :] + as_ref[0:1, :]).astype(BF16)
        m_ref[place, :] = (normed * mg_ref[0:1, :] + ms_ref[0:1, :]).astype(BF16)
    xq_ref[...] = x_ref[rows(me_ref[2], block_len), :]
    copies[-1].wait()
    project_rows(0, tok_shape, me_ref, seg_ref, lambda j: w_ref[j], b_ref, a_ref, p_refs, proj_ref, True)


def project_body(layer, tok_shape, me_ref, *refs):
    seq_count, block_len, width = tok_shape
    x_ref, seg_ref, *refs = refs
    u_refs, refs = refs[:4], refs[4:]
    ob_ref, db_ref, ag_ref, as_ref, mg_ref, ms_ref, w_ref, b_ref, x_out, xq_ref, a_ref, m_ref, *p_refs, proj_ref = refs
    tensor = me_ref[2]
    shift = ob_ref[layer - 1 : layer, :] + db_ref[layer - 1 : layer, :]
    for k in range(4):
        place = rows(wrap4(tensor - k), block_len)
        value = x_ref[place, :] + u_refs[k][...].astype(F32) + shift
        x_out[place, :] = value
        if k == 0:
            xq_ref[...] = value
        normed, _ = normalize(value)
        a_ref[place, :] = (normed * ag_ref[layer : layer + 1, :] + as_ref[layer : layer + 1, :]).astype(BF16)
        m_ref[place, :] = (normed * mg_ref[layer : layer + 1, :] + ms_ref[layer : layer + 1, :]).astype(BF16)
    project_rows(layer, tok_shape, me_ref, seg_ref, lambda j: w_ref[0, j], b_ref, a_ref, p_refs, proj_ref, False)


def gather_pieces(me_ref, refs, targets, block_len, seg_target=None):
    chip, core = me_ref[0], me_ref[1]
    for k in range(4):
        owner = wrap4(chip - k)
        for side, ref in ((core, refs[k]), (1 - core, refs[4 + k])):
            place = rows(owner * 2 + side, block_len)
            for index, target in enumerate(targets):
                target[place, :] = ref[core, 0:block_len, index * LANES : (index + 1) * LANES]
            if seg_target is not None:
                row = ref[core, block_len : block_len + 16, :].astype(F32)[0:1, :]
                starts = row[:, 0:LANES] * 8.0 + row[:, LANES : 2 * LANES]
                seg_target[:, place] = jnp.broadcast_to(starts, (8, block_len))


def head_stack(values):
    lane = lax.broadcasted_iota(jnp.int32, values.shape, 1)
    zero = jnp.zeros_like(values)
    return jnp.concatenate(
        [jnp.where(lane < HEAD, values, zero), jnp.where(lane >= HEAD, values, zero)], axis=0
    )


def own_halves(product, width):
    return jnp.concatenate([product[0:HEAD, 0:width], product[HEAD:, width : 2 * width]], axis=0)


def chances_t(q_ref, k_ref, seg_ref, step, chunk):
    start, keys = step * chunk, (step + 1) * chunk
    stacked = head_stack(q_ref[start:keys, :]) * jnp.asarray(HEAD ** (-0.5), BF16)
    scores = matmul_nt(k_ref[0:keys, :], stacked)
    key_place = lax.broadcasted_iota(jnp.int32, (keys, 2 * chunk), 0).astype(F32)
    query_place = (lax.broadcasted_iota(jnp.int32, (1, 2 * chunk), 1) & (chunk - 1)).astype(F32) + start
    seg_row = seg_ref[0:1, start:keys]
    seg_row = jnp.concatenate([seg_row, seg_row], axis=1)
    allowed = (key_place >= seg_row) & (key_place <= query_place)
    scores = jnp.where(allowed, scores, -1e30)
    raised = jnp.exp(scores - jnp.max(scores, axis=0, keepdims=True))
    total = jnp.sum(raised, axis=0, keepdims=True)
    return raised * (1.0 / total), stacked


def attend_body(block_len, chunk, me_ref, *refs):
    piece_refs, refs = refs[:8], refs[8:]
    seg_out, qkv_ref, *refs = refs
    o_refs, refs = refs[:4], refs[4:]
    vt_ref, o_ref = refs
    q_ref, k_ref, v_ref = qkv_ref.at[0], qkv_ref.at[1], qkv_ref.at[2]
    gather_pieces(me_ref, piece_refs, (q_ref, k_ref, v_ref), block_len, seg_out)
    vt_ref[...] = v_ref[...].T
    length = q_ref.shape[0]
    for step in range(length // chunk):
        keys = (step + 1) * chunk
        chances, _ = chances_t(q_ref, k_ref, seg_out, step, chunk)
        mixed = matmul(vt_ref[:, 0:keys], chances.astype(BF16))
        o_ref[step * chunk : keys, :] = own_halves(mixed, chunk).T.astype(BF16)
    send_blocks(me_ref, o_ref, o_refs, block_len)


def send_blocks(me_ref, source, targets, block_len):
    chip = me_ref[0]
    for k in range(4):
        dest = wrap4(chip + k)
        for side in range(2):
            targets[k][side] = source[rows(dest * 2 + side, block_len), :]


def attend_both_body(block_len, chunk, with_out, me_ref, *refs):
    if with_out:
        piece_refs, refs = refs[:8], refs[8:]
    else:
        qkv_ref, *refs = refs
    grad_refs, refs = refs[:8], refs[8:]
    seg_ref, *refs = refs
    d_refs, refs = refs[:4], refs[4:]
    if with_out:
        qkv_ref, *refs = refs
    q_ref, k_ref, v_ref = qkv_ref.at[0], qkv_ref.at[1], qkv_ref.at[2]
    g_ref, t_ref, o_ref, dq_ref, dk_ref, dv_ref = refs
    if with_out:
        gather_pieces(me_ref, piece_refs, (q_ref, k_ref, v_ref), block_len)
    gather_pieces(me_ref, grad_refs, (g_ref,), block_len)
    length = q_ref.shape[0]
    t_ref[0] = k_ref[...].T
    if with_out:
        t_ref[1] = v_ref[...].T
    dk_ref[...] = jnp.zeros_like(dk_ref)
    dv_ref[...] = jnp.zeros_like(dv_ref)
    for step in range(length // chunk):
        start, keys = step * chunk, (step + 1) * chunk
        chances, stacked = chances_t(q_ref, k_ref, seg_ref, step, chunk)
        low = chances.astype(BF16)
        if with_out:
            mixed = matmul(t_ref[1, :, 0:keys], low)
            o_ref[start:keys, :] = own_halves(mixed, chunk).T.astype(BF16)
        grads = head_stack(g_ref[start:keys, :])
        chance_grad = matmul_nt(v_ref[0:keys, :], grads)
        delta = jnp.sum(chances * chance_grad, axis=0, keepdims=True)
        score_grad = (chances * (chance_grad - delta)).astype(BF16)
        dv_ref[0:keys, :] += matmul(low, grads)
        dk_ref[0:keys, :] += matmul(score_grad, stacked)
        query = matmul(t_ref[0, :, 0:keys], score_grad)
        dq_ref[start:keys, :] = own_halves(query, chunk).T * HEAD ** (-0.5)
    chip = me_ref[0]
    for k in range(4):
        dest = wrap4(chip + k)
        for side in range(2):
            place = rows(dest * 2 + side, block_len)
            spots = (lax.broadcasted_iota(jnp.int32, (1, block_len), 1) + (dest * 2 + side) * block_len).astype(F32)
            tables = rotary_rows(spots - seg_ref[0:1, place])
            d_refs[k][side, :, 0:LANES] = rotate(dq_ref[place, :], tables, True).astype(BF16)
            d_refs[k][side, :, LANES : 2 * LANES] = rotate(dk_ref[place, :], tables, True).astype(BF16)
            d_refs[k][side, :, 2 * LANES : 3 * LANES] = dv_ref[place, :].astype(BF16)
            if with_out:
                d_refs[k][side, :, 3 * LANES :] = o_ref[place, :]


def land_heads(me_ref, refs, target, block_len, groups, first=0):
    chip, core = me_ref[0], me_ref[1]
    for k in range(4):
        place = rows(wrap4(chip - k), block_len)
        mine, other = refs[k][core], refs[4 + k][core]
        is_low = core == 0
        for group in range(groups):
            span = slice((first + group) * LANES, (first + group + 1) * LANES)
            at = group * 2 * LANES
            target[place, at : at + LANES] = jnp.where(is_low, mine[:, span], other[:, span])
            target[place, at + LANES : at + 2 * LANES] = jnp.where(is_low, other[:, span], mine[:, span])


def combine_body(block_len, fused, me_ref, *refs):
    piece_refs, refs = refs[:8], refs[8:]
    w_ref, *refs = refs
    if fused:
        g_ref, down_ref, *refs = refs
    else:
        part_ref, *refs = refs
    o_ref, *refs = refs
    q_refs, scr = refs[:-1], refs[-1]
    tensor = me_ref[2]
    land_heads(me_ref, piece_refs, o_ref, block_len, 1, 3 if fused else 0)
    part = matmul(g_ref[...], down_ref[0]) if fused else part_ref[...]
    scr[...] = (matmul(o_ref[...], w_ref[0]) + part).astype(BF16)
    if fused:
        near, far = near_far(tensor)
        size = block_len // 2
        orders = ((tensor, far), (near, 3 - near), (tensor, near), (far, far ^ 1))
        for way, (ref, order) in enumerate(zip(q_refs, orders)):
            for index, quarter in enumerate(order):
                at = pl.multiple_of(quarter * block_len + (way >> 1) * size, size)
                ref[index * size : (index + 1) * size, :] = scr[pl.ds(at, size), :]
        return
    for k in range(4):
        q_refs[k][...] = scr[rows(wrap4(tensor + k), block_len), :]


def send_grad_body(block_len, me_ref, x_ref, w_ref, *refs):
    chip, tensor = me_ref[0], me_ref[2]
    quarter_ref, *refs = refs
    quarter_ref[...] = x_ref[rows(tensor, block_len), :]
    for k in range(4):
        value = x_ref[rows(wrap4(chip + k), block_len), :].astype(BF16)
        grad = matmul_nt(value, w_ref[0]).astype(BF16)
        for pair in range(2):
            refs[k][pair] = grad[:, pair * LANES : (pair + 1) * LANES]


def join_body(block_len, me_ref, *refs):
    q_refs, refs = refs[:4], refs[4:]
    w_ref, r_ref, *g_refs = refs
    chip, tensor = me_ref[0], me_ref[2]
    for k in range(4):
        r_ref[rows(wrap4(tensor - k), block_len), :] = q_refs[k][...]
    for k in range(4):
        value = r_ref[rows(wrap4(chip + k), block_len), :]
        grad = matmul_nt(value, w_ref[0]).astype(BF16)
        for pair in range(2):
            g_refs[k][pair] = grad[:, pair * LANES : (pair + 1) * LANES]


def project_back_body(block_len, layer, me_ref, *refs):
    piece_refs, refs = refs[:8], refs[8:]
    w_ref, dm_ref, ag_ref, mg_ref, *refs = refs
    riders, refs = refs[:-8], refs[-8:]
    dp_ref, da_ref, bias_ref, *q_refs, scr = refs
    tensor = me_ref[2]
    land_heads(me_ref, piece_refs, dp_ref, block_len, 3)
    for j in range(3):
        span = slice(j * 2 * LANES, (j + 1) * 2 * LANES)
        bias_ref[j : j + 1, :] = jnp.sum(dp_ref[:, span].astype(F32), axis=0, keepdims=True)
    total = None
    for j in range(3):
        term = matmul_nt(dp_ref[:, j * 2 * LANES : (j + 1) * 2 * LANES], w_ref[0, j])
        total = term if total is None else total + term
    da_ref[...] = total.astype(BF16)
    scr[...] = (total * ag_ref[layer : layer + 1, :] + dm_ref[...] * mg_ref[layer : layer + 1, :]).astype(BF16)
    for k in range(4):
        q_refs[k][0:block_len, :] = scr[rows(wrap4(tensor + k), block_len), :]
        if riders:
            q_refs[k][block_len:, :] = riders[k][...]


def norm_back_body(me_ref, *refs):
    e_ref, x_ref, dy_ref, dx_ref, low_ref, bias_ref = refs
    upstream = dy_ref[...]
    size = upstream.shape[0]
    total = e_ref[0:size, :]
    normed, factor = normalize(x_ref[...])
    inner = jnp.mean(total * normed, axis=-1, keepdims=True)
    result = upstream + factor * (total - jnp.mean(total, axis=-1, keepdims=True) - normed * inner)
    dx_ref[...] = result
    low_ref[0:size, :] = result.astype(BF16)
    if e_ref.shape[0] > size:
        low_ref[size:, :] = e_ref[size:, :].astype(BF16)
    bias_ref[...] = jnp.sum(upstream, axis=0, keepdims=True)


def gains_body(me_ref, x_ref, da_ref, dm_ref, out_ref):
    normed, _ = normalize(x_ref[...])
    da = da_ref[...].astype(F32)
    dm = dm_ref[...]
    out_ref[0:1, :] = jnp.sum(da * normed, axis=0, keepdims=True)
    out_ref[1:2, :] = jnp.sum(da, axis=0, keepdims=True)
    out_ref[2:3, :] = jnp.sum(dm * normed, axis=0, keepdims=True)
    out_ref[3:4, :] = jnp.sum(dm, axis=0, keepdims=True)


def gelu_parts(hidden):
    cdf = 0.5 * (1.0 + lax.erf(hidden * (0.5**0.5)))
    density = jnp.exp(-0.5 * hidden * hidden) * 0.3989422804014327
    return cdf, density


def feed_body(layer, me_ref, m_ref, up_ref, ub_ref, down_ref, g_ref, slope_ref, part_ref):
    size = 2 * LANES
    for step in range(up_ref.shape[2] // size):
        span = slice(step * size, (step + 1) * size)
        hidden = matmul(m_ref[...], up_ref[0, :, span]) + ub_ref[layer : layer + 1, span]
        cdf, density = gelu_parts(hidden)
        g_ref[:, span] = (hidden * cdf).astype(BF16)
        slope_ref[:, span] = cdf + hidden * density
    part_ref[...] = matmul(g_ref[...], down_ref[0])


def feed_back_body(me_ref, r_ref, slope_ref, up_ref, down_ref, dh_ref, dm_ref, bias_ref):
    size = 2 * LANES
    for step in range(down_ref.shape[1] // size):
        span = slice(step * size, (step + 1) * size)
        grad = matmul_nt(r_ref[...], down_ref[0, span, :]) * slope_ref[:, span]
        bias_ref[:, span] = jnp.sum(grad, axis=0, keepdims=True)
        dh_ref[:, span] = grad.astype(BF16)
    dm_ref[...] = matmul_nt(dh_ref[...], up_ref[0])


def feed_both_body(layer, me_ref, m_ref, dy_ref, up_ref, ub_ref, down_ref, g_ref, r_ref, dh_ref, dm_ref, bias_ref):
    size = 2 * LANES
    r_ref[...] = dy_ref[...].astype(BF16)
    for step in range(up_ref.shape[2] // size):
        span = slice(step * size, (step + 1) * size)
        hidden = matmul(m_ref[...], up_ref[0, :, span]) + ub_ref[layer : layer + 1, span]
        cdf, density = gelu_parts(hidden)
        g_ref[:, span] = (hidden * cdf).astype(BF16)
        grad = matmul_nt(r_ref[...], down_ref[0, span, :]) * (cdf + hidden * density)
        bias_ref[:, span] = jnp.sum(grad, axis=0, keepdims=True)
        dh_ref[:, span] = grad.astype(BF16)
    dm_ref[...] = matmul_nt(dh_ref[...], up_ref[0])


def feed_weights_body(me_ref, m_ref, dh_ref, g_ref, r_ref, keep_ref, send_ref):
    core = me_ref[1]
    half = m_ref.shape[1] // 2
    for side, out in ((core, keep_ref), (1 - core, send_ref)):
        out[0:half, :] = matmul_tn(m_ref[:, rows(side, half)], dh_ref[...]).astype(BF16)
        out[half:, :] = matmul_tn(g_ref[:, rows(side, half)], r_ref[...]).astype(BF16)


def head_weights_body(me_ref, a_ref, dp_ref, o_ref, r_ref, keep_ref, send_ref):
    core = me_ref[1]
    half = a_ref.shape[1] // 2
    wide = dp_ref.shape[1]
    for side, out in ((core, keep_ref), (1 - core, send_ref)):
        out[:, 0:wide] = matmul_tn(a_ref[:, rows(side, half)], dp_ref[...]).astype(BF16)
        grad = matmul_tn(o_ref[:, rows(side, LANES)], r_ref[...]).astype(BF16)
        for part in range(4):
            out[part * LANES : (part + 1) * LANES, wide:] = grad[:, part * 2 * LANES : (part + 1) * 2 * LANES]


def feed_weights_whole_body(me_ref, m_ref, dh_ref, g_ref, r_ref, pack_ref):
    high = m_ref.shape[1]
    pack_ref[0:high, :] = matmul_tn(m_ref[...], dh_ref[...]).astype(BF16)
    pack_ref[high:, :] = matmul_tn(g_ref[...], r_ref[...]).astype(BF16)


def head_weights_whole_body(me_ref, a_ref, dp_ref, o_ref, r_ref, before_ref, pack_ref):
    wide = dp_ref.shape[1]
    pack_ref[:, 0:wide] = matmul_tn(a_ref[...], dp_ref[...]).astype(BF16)
    grad = matmul_tn(o_ref[...], r_ref[...]).astype(BF16)
    high, size = grad.shape[0], 2 * LANES
    for part in range(4):
        pack_ref[part * high : (part + 1) * high, wide:] = grad[:, part * size : (part + 1) * size]


def near_far(place):
    return place ^ 1, 3 - place


def halve_body(me_ref, feed_keep, feed_came, head_keep, head_came, *refs):
    outs, feed_scr, head_scr = refs[:4], refs[4], refs[5]
    feed_scr[...] = (feed_keep[...].astype(F32) + feed_came[...].astype(F32)).astype(BF16)
    head_scr[...] = (head_keep[...].astype(F32) + head_came[...].astype(F32)).astype(BF16)
    place = me_ref[3]
    near, far = near_far(place)
    half = head_scr.shape[0]
    size = half // 8
    orders = ((place, far), (near, 3 - near), (4 + place, 4 + near), (4 + far, 4 + (far ^ 1)))
    for ref, order in zip(outs, orders):
        for index, block in enumerate(order):
            at = 3 * size * index
            ref[at : at + size, :] = feed_scr[rows(block, size), :]
            ref[at + size : at + 2 * size, :] = feed_scr[pl.ds(pl.multiple_of(half + block * size, size), size), :]
            ref[at + 2 * size : at + 3 * size, :] = head_scr[rows(block, size), :]


def halve_again_body(me_ref, a_keep, a_came, b_keep, b_came, *outs):
    size = outs[0].shape[0]
    for keep, came, mine, send in ((a_keep, a_came, outs[0], outs[1]), (b_keep, b_came, outs[2], outs[3])):
        total = (keep[...].astype(F32) + came[...].astype(F32)).astype(BF16)
        mine[...] = total[0:size, :]
        send[...] = total[size:, :]


def line_up_body(axis, me_ref, *refs):
    size = refs[4].shape[0] // 4
    for k in range(4):
        refs[4][rows(wrap4(me_ref[axis] - k), size), :] = refs[k][0:size, :]
    if len(refs) > 5:
        even = refs[0][size:, :].astype(F32) + refs[2][size:, :].astype(F32)
        odd = refs[1][size:, :].astype(F32) + refs[3][size:, :].astype(F32)
        refs[5][...] = (even + odd).astype(BF16)


def merge_body(me_ref, a_keep, a_came, b_keep, b_came, small_ref, *refs):
    out_refs, scr = refs[:4], refs[4]
    high = a_keep.shape[0]
    scr[0:high, :] = (a_keep[...].astype(F32) + a_came[...].astype(F32)).astype(BF16)
    scr[high:, :] = (b_keep[...].astype(F32) + b_came[...].astype(F32)).astype(BF16)
    few = high // 6
    for k in range(4):
        part = wrap4(me_ref[0] + k)
        for weight in range(3):
            at = pl.multiple_of((part >> 1) * high + weight * 2 * few + (part & 1) * few, few)
            out_refs[k][weight * few : (weight + 1) * few, :] = scr[pl.ds(at, few), :]
        out_refs[k][3 * few :, :] = small_ref[...]


def settle_body(me_ref, *refs):
    in_refs, (first_ref, second_ref) = refs[:4], refs[4:]
    even = in_refs[0][...].astype(F32) + in_refs[2][...].astype(F32)
    odd = in_refs[1][...].astype(F32) + in_refs[3][...].astype(F32)
    total = (even + odd).astype(BF16)
    few = first_ref.shape[0] // 3
    for weight in range(3):
        for index, ref in enumerate((first_ref, second_ref)):
            at = (2 * weight + index) * few
            ref[weight * few : (weight + 1) * few, :] = total[at : at + few, :]
    second_ref[3 * few :, :] = total[6 * few :, :]


def flush(held, outs, layer, sems):
    copies = [pltpu.make_async_copy(a, b.at[layer], sems.at[i]) for i, (a, b) in enumerate(zip(held, outs))]
    return copies


def unpack_body(few, me_ref, *refs):
    outs, held, sems = refs[24:28], refs[28:32], refs[32]
    up_ref, down_ref, qkv_ref, out_ref = held
    copies = flush(held, outs, 0, sems)
    chip, core, place_z = me_ref[0], me_ref[1], me_ref[3]
    size = 2 * LANES
    half = up_ref.shape[0] // 2
    for weight in range(3):
        for side, group in ((core, refs[:10]), (1 - core, refs[10:20])):
            for along, me in ((0, place_z), (1, chip)):
                pieces = group[5 * along : 5 * along + 5]
                spans = [(pieces[0], me, 0), (pieces[1], me ^ 1, 0), (pieces[2], 3 - me, 0)]
                spans += [(pieces[3], me ^ 2, 0), (pieces[4], me ^ 2, 2)]
                for ref, owner, first in spans:
                    for index in range(ref.shape[0] // (3 * few)):
                        z, x = (owner, first + index) if along == 0 else (first + index, owner)
                        start = (3 * index + weight) * few
                        value = ref[start : start + few, :].astype(F32)
                        row = (z + 4 * (x >> 1)) * (4 * few) + (x & 1) * (2 * few) + along * few
                        place = pl.ds(pl.multiple_of(row + side * half, few), few)
                        if weight < 2:
                            held[weight][place, :] = value
                        else:
                            for j in range(3):
                                qkv_ref[j, place, :] = value[:, j * size : (j + 1) * size]
                            inner = pl.ds(pl.multiple_of((row & (LANES - 1)) + side * LANES, few), few)
                            lanes = pl.ds(pl.multiple_of((row >> 7) * size, size), size)
                            out_ref[inner, lanes] = value[:, 3 * size :]
        for copy in copies[weight : weight + 1] if weight < 2 else copies[2:]:
            copy.start()
    for copy in copies:
        copy.wait()


def add_packs_body(me_ref, feed_keep, feed_came, head_keep, head_came, out_ref):
    high = feed_keep.shape[0]
    out_ref[0:high, :] = (feed_keep[...].astype(F32) + feed_came[...].astype(F32)).astype(BF16)
    out_ref[high:, :] = (head_keep[...].astype(F32) + head_came[...].astype(F32)).astype(BF16)


def unpack_whole_body(me_ref, up_mine, down_mine, head_mine, up_other, down_other, head_other, *outs):
    up_ref, down_ref, qkv_ref, out_ref = outs
    size = 2 * LANES
    for core in range(2):
        mine = me_ref[1] == core
        for ref, first, second in ((up_ref, up_mine, up_other), (down_ref, down_mine, down_other)):
            ref[0, core] = jnp.where(mine, first[...], second[...]).astype(F32)
        head = jnp.where(mine, head_mine[...], head_other[...]).astype(F32)
        for j in range(3):
            qkv_ref[0, j, core] = head[:, j * size : (j + 1) * size]
        out_ref[0, core] = head[:, 3 * size :]


def pack_small_body(me_ref, *refs):
    ins, small_ref = refs[:8], refs[8]
    width = small_ref.shape[1]
    blank = jnp.zeros((1, width), F32)
    shared = [ins[0][...], ins[1][...], ins[2][...], ins[3][...]] + [blank] * 6
    small_ref[0:16, :] = jnp.concatenate(shared, axis=0).astype(BF16)
    local = [ins[6][...], ins[7][...]]
    for ref in ins[4:6]:
        values = ref[...]
        flat = [values[j : j + 1, :] for j in range(3)]
        local.append(jnp.concatenate(flat + [jnp.zeros((1, width - 3 * values.shape[1]), F32)], axis=1))
    small_ref[16:32, :] = jnp.concatenate(local + [blank] * 12, axis=0).astype(BF16)


def add_halves_body(me_ref, a_keep, a_came, b_keep, b_came, out_ref):
    size = a_keep.shape[0]
    out_ref[0:size, :] = (a_keep[...].astype(F32) + a_came[...].astype(F32)).astype(BF16)
    out_ref[size:, :] = (b_keep[...].astype(F32) + b_came[...].astype(F32)).astype(BF16)


def add_cut_body(me_ref, mine_ref, came_ref, shared_ref, local_ref):
    total = (mine_ref[...].astype(F32) + came_ref[...].astype(F32)).astype(BF16)
    half = shared_ref.shape[0]
    shared_ref[...] = total[0:half, :]
    local_ref[...] = total[half:, :]


def add_body(count, me_ref, *refs):
    total = refs[0][...].astype(F32)
    for ref in refs[1:count]:
        total = total + ref[...].astype(F32)
    refs[count][...] = total.astype(refs[count].dtype)


def small_out_body(me_ref, mine_ref, came_ref, local_ref, *outs):
    shared = mine_ref[...].astype(F32) + came_ref[...].astype(F32)
    local = local_ref[...].astype(F32)
    for index in range(5):
        outs[index][0:1, :] = shared[index : index + 1, :]
        outs[index][1:2, :] = shared[index + 5 : index + 6, :]
    outs[5][...] = local[0:2, :]
    size = outs[6].shape[2]
    for layer in range(2):
        for j in range(3):
            outs[6][layer, j : j + 1, :] = local[2 + layer : 3 + layer, j * size : (j + 1) * size]


def place_body(block_len, me_ref, *refs):
    q_refs, u_refs, (x_ref, ob_ref, db_ref, grad_ref, out_ref) = refs[:4], refs[4:9], refs[9:]
    shift = ob_ref[1:2, :] + db_ref[1:2, :]
    me = me_ref[2]
    for k in range(4):
        grad_ref[rows(wrap4(me - k), block_len), :] = q_refs[k][...].astype(F32)
    half = block_len // 2
    spots = ((me, 0), (me ^ 1, 0), (3 - me, 0), (me ^ 2, 0), (me ^ 2, half))
    for ref, (quarter, offset) in zip(u_refs, spots):
        count = ref.shape[0]
        place = pl.ds(pl.multiple_of(quarter * block_len + offset, half), count)
        out_ref[place, :] = x_ref[place, :] + ref[...].astype(F32) + shift


def chip_turn(shift):
    return [(2 * x + c, 2 * ((x + shift) % 4) + c) for x in range(4) for c in range(2)]


CORE_SWAP = [(i, i ^ 1) for i in range(8)]


def over_chips(pieces, beside=()):
    mine, beside = lax.optimization_barrier((over_x(pieces), beside))
    return mine + [swap_core(piece) for piece in mine], beside


def ring_turn(shift):
    return [(i, (i + shift) % 4) for i in range(4)]


def over_tensor(pieces):
    return [pieces[0]] + [lax.ppermute(pieces[k], "tensor", ring_turn(k)) for k in range(1, 4)]


def share_tensor(piece):
    return over_tensor([piece] * 4)


def over_dp(pieces):
    return [pieces[0]] + [lax.ppermute(pieces[k], "dp", ring_turn(k)) for k in range(1, 4)]


def over_x(pieces):
    return [pieces[0]] + [lax.ppermute(pieces[k], "ctx", chip_turn(k)) for k in range(1, 4)]


def swap_core(piece):
    return lax.ppermute(piece, "ctx", CORE_SWAP)


NEXT_PAIR = [(0, 1), (1, 0), (2, 3), (3, 2)]
WRAP_PAIR = [(0, 3), (3, 0), (1, 2), (2, 1)]


def both_ways(to_next, to_wrap, axis="dp"):
    return lax.ppermute(to_next, axis, NEXT_PAIR), lax.ppermute(to_wrap, axis, WRAP_PAIR)


def chips_of(pairs):
    return [(2 * a + c, 2 * b + c) for a, b in pairs for c in range(2)]


def along(axis):
    return ("ctx", chips_of) if axis == "x" else (axis, lambda pairs: pairs)


def spread_near(piece, axis):
    name, move = along(axis)
    return [piece] + [lax.ppermute(piece, name, move(pairs)) for pairs in (NEXT_PAIR, WRAP_PAIR)]


def spread_far(pieces, axis):
    name, move = along(axis)
    half = pieces[0].shape[0] // 2
    return pieces + [
        lax.ppermute(pieces[1][:half], name, move(WRAP_PAIR)),
        lax.ppermute(pieces[2][half:], name, move(NEXT_PAIR)),
    ]


def tie(first, second):
    return lax.optimization_barrier((first, second))


def after(values, token):
    return lax.optimization_barrier((values, token))[0]


def add_up(pieces):
    total = pieces[0].astype(F32)
    for piece in pieces[1:]:
        total = total + piece.astype(F32)
    return total


def on_device(
    inputs,
    segments,
    attn_gain,
    attn_shift,
    mlp_gain,
    mlp_shift,
    qkv_weight,
    qkv_bias,
    out_weight,
    out_bias,
    up_weight,
    up_bias,
    down_weight,
    down_bias,
    cotangent,
):
    seq_count, block_len, width = inputs.shape
    tokens = seq_count * block_len
    inner = qkv_weight.shape[3]
    hidden = up_weight.shape[2]
    length = block_len * 8
    chunk = 256
    place = lax.axis_index("ctx")
    me = jnp.stack([place // 2, place % 2, lax.axis_index("tensor"), lax.axis_index("dp")]).astype(jnp.int32)
    x0 = inputs.reshape(tokens, width)
    dy1 = cotangent.reshape(tokens, width)
    tok_shape = inputs.shape
    wide = shape_of((tokens, width), BF16)
    norms = (attn_gain, attn_shift, mlp_gain, mlp_shift)
    biases = qkv_bias.transpose(1, 0, 2)

    def project_first(x):
        sources = [x, segments, *norms, qkv_weight, biases]
        held = [v.shape for v in sources[:6]] + [qkv_weight.shape[1:], biases.shape]
        piece = shape_of((2, block_len + 16, 3 * LANES), BF16)
        return run(
            functools.partial(project_first_body, tok_shape),
            me,
            [(v, pl.BlockSpec(memory_space=pltpu.HBM)) for v in sources],
            [shape_of((block_len, width), F32), wide, wide] + [piece] * 4,
            scratch=[pltpu.VMEM((tokens, 3 * inner), F32)]
            + [pltpu.VMEM(size, v.dtype) for size, v in zip(held, sources)]
            + [pltpu.SemaphoreType.DMA((11,))],
            name="norm_project",
            limit=62,
        )

    def project(layer, x, extra):
        piece = shape_of((2, block_len, 3 * LANES), BF16)
        return run(
            functools.partial(project_body, layer, tok_shape),
            me,
            [x, segments, *extra, *norms]
            + [(qkv_weight, layer_spec(qkv_weight, layer)), biases],
            [shape_of((tokens, width), F32), shape_of((block_len, width), F32), wide, wide] + [piece] * 4,
            scratch=[pltpu.VMEM((tokens, 3 * inner), F32)],
            name="norm_project",
            limit=24,
        )

    def feed(layer, m):
        return run(
            functools.partial(feed_body, layer),
            me,
            [m, (up_weight, layer_spec(up_weight, layer)), up_bias, (down_weight, layer_spec(down_weight, layer))],
            [shape_of((tokens, hidden), BF16), shape_of((tokens, hidden), F32), shape_of((tokens, width), F32)],
            name="feed", limit=24,
        )

    def feed_back(layer, r, slope):
        return run(
            feed_back_body,
            me,
            [r, slope, (up_weight, layer_spec(up_weight, layer)), (down_weight, layer_spec(down_weight, layer))],
            [shape_of((tokens, hidden), BF16), shape_of((tokens, width), F32), shape_of((1, hidden), F32)],
            name="feed_back", limit=24,
        )

    def feed_both(layer, m, dy):
        return run(
            functools.partial(feed_both_body, layer),
            me,
            [m, dy, (up_weight, layer_spec(up_weight, layer)), up_bias, (down_weight, layer_spec(down_weight, layer))],
            [shape_of((tokens, hidden), BF16), wide, shape_of((tokens, hidden), BF16)]
            + [shape_of((tokens, width), F32), shape_of((1, hidden), F32)],
            name="feed_both", limit=24,
        )

    def combine(layer, pieces, part, active=None):
        fused = part is None
        got = run(
            functools.partial(combine_body, block_len, fused),
            me,
            [*pieces, (out_weight, layer_spec(out_weight, layer))]
            + ([active, (down_weight, layer_spec(down_weight, layer))] if fused else [part]),
            [shape_of((tokens, inner), BF16)] + [shape_of((block_len, width), BF16)] * 4,
            scratch=[pltpu.VMEM((tokens, width), BF16)],
            name="combine", limit=20,
        )
        return got[0], got[1:]

    def add_all(values, dtype=BF16):
        out = shape_of(values[0].shape, dtype)
        return run(functools.partial(add_body, len(values)), me, values, [out], name="add_all", limit=16)[0]

    def line_up(axis, values, size):
        extra = values[0].shape[0] - size
        small = [shape_of((extra, width), BF16)] if extra else []
        outs = [shape_of((4 * size, width), BF16)] + small
        return run(functools.partial(line_up_body, axis), me, values, outs, name="line_up", limit=8)

    seq_bf16 = pltpu.VMEM((length, LANES), BF16)
    seq_f32 = pltpu.VMEM((length, LANES), F32)
    o_shapes = [shape_of((2, block_len, LANES), BF16)] * 4

    def attend_both(pieces, grads, seg_rows, with_out):
        return run(
            functools.partial(attend_both_body, block_len, chunk, with_out),
            me,
            [*pieces, *grads, seg_rows],
            [shape_of((2, block_len, (4 if with_out else 3) * LANES), BF16)] * 4,
            scratch=([pltpu.VMEM((3, length, LANES), BF16)] if with_out else [])
            + [seq_bf16, pltpu.VMEM((2, LANES, length), BF16), seq_bf16]
            + [seq_f32] * 3,
            name="attend_both", limit=24,
        )

    def project_back(layer, pieces, dm, riders=()):
        got = run(
            functools.partial(project_back_body, block_len, layer),
            me,
            [*pieces, (qkv_weight, layer_spec(qkv_weight, layer)), dm, attn_gain, mlp_gain, *riders],
            [shape_of((tokens, 3 * inner), BF16), wide, shape_of((3, inner), F32)]
            + [shape_of((block_len * (2 if riders else 1), width), BF16)] * 4,
            scratch=[pltpu.VMEM((tokens, width), BF16)],
            name="project_back", limit=24,
        )
        return got[0], got[1], got[2], got[3:]

    def norm_back(pieces, x, dy):
        quarter = shape_of((block_len, width), F32)
        return run(
            norm_back_body,
            me,
            [add_up(pieces), x, dy],
            [quarter, shape_of(pieces[0].shape, BF16), shape_of((1, width), F32)],
            name="norm_back",
            limit=10,
        )

    def gains(x, da, dm):
        return run(gains_body, me, [x, da, dm], [shape_of((4, width), F32)], name="gains", limit=16)[0]

    half = width // 2
    columns = [[8 * z + 2 * chip + core for z in range(4) for chip in range(4)] for core in range(2)]

    def feed_weights(m, dh, active, r):
        pack = shape_of((2 * half, width), BF16)
        return run(feed_weights_body, me, [m, dh, active, r], [pack] * 2, name="feed_weights", limit=24)

    def head_weights(attn_in, dproj, attended, r):
        pack = shape_of((half, width), BF16)
        return run(head_weights_body, me, [attn_in, dproj, attended, r], [pack] * 2, name="head_weights", limit=20)

    x0_quarter, a0, m0, *pieces = project_first(x0)
    fed0 = feed(0, m0)
    pieces0, (active0, slope0, part0) = over_chips(pieces, fed0)
    got = run(
        functools.partial(attend_body, block_len, chunk),
        me,
        pieces0,
        [shape_of((8, length), F32), shape_of((3, length, LANES), BF16)] + o_shapes,
        scratch=[pltpu.VMEM((LANES, length), BF16), seq_bf16],
        name="attend", limit=20,
    )
    seg_rows, qkv0 = got[:2]
    out0, _ = over_chips(got[2:])
    attended0, u0 = combine(0, out0, part0)
    dy1_quarter, *grads1 = run(
        functools.partial(send_grad_body, block_len),
        me,
        [after(dy1, u0[0]), (out_weight, layer_spec(out_weight, 1))],
        [shape_of((block_len, width), F32)] + o_shapes,
        name="out_back", limit=14,
    )
    u0, grads1 = tie(over_tensor(u0), over_x(grads1))
    u0 = share_tensor(add_up(u0).astype(BF16))
    u0, grads1_other = tie(u0, [swap_core(piece) for piece in grads1])

    x1, x1_quarter, a1, m1, *pieces = project(1, x0, [*u0, out_bias, down_bias])
    fed1 = feed_both(1, m1, dy1)
    pieces1, (active1, r1, dh1, dm1, up_b1) = over_chips(pieces, fed1)
    got = attend_both(pieces1, grads1 + grads1_other, seg_rows, True)
    feed_pack1 = feed_weights(after(m1, got[0]), dh1, active1, r1)
    back1, feed_pack1 = over_chips(got, feed_pack1)
    dproj1, da1, qkv_b1, e1 = project_back(1, back1, dm1)
    back1, (feed_keep, feed_send) = after((back1, feed_pack1), e1[0])
    attended1, u1 = combine(1, back1, None, active1)
    head_keep, head_send = head_weights(a1, dproj1, attended1, r1)
    e1, (u1, head_keep, head_send, feed_came) = tie(over_tensor(e1), (u1, head_keep, head_send, swap_core(feed_send)))
    pack1 = run(
        add_packs_body,
        me,
        [feed_keep, feed_came, head_keep, swap_core(head_send)],
        [shape_of((3 * half, width), BF16)],
        name="add_packs",
        limit=16,
    )[0]
    part1 = lax.psum_scatter(pack1, ("dp", "ctx"), axis_index_groups=columns, tiled=True)
    dx1, low1, bias1 = norm_back(e1, x1_quarter, dy1_quarter)
    gains1 = gains(after(x1, low1), da1, dm1)
    quarters, gains1 = tie(share_tensor(low1), gains1)

    r0, *grads0 = run(
        functools.partial(join_body, block_len),
        me,
        [*quarters, (out_weight, layer_spec(out_weight, 0))],
        [wide] + o_shapes,
        name="join_out_back", limit=14,
    )
    ua_keep, ua_send, ub_keep, ub_send = after(u1, r0)
    ua_came, ub_came = both_ways(ua_send, ub_send, "tensor")
    grads0, (ua_came, ub_came) = over_chips(grads0, (ua_came, ub_came))
    back0 = attend_both([qkv0], grads0, seg_rows, False)
    r0_late, u_parts = after((r0, [ua_keep, ua_came, ub_keep, ub_came]), back0[0])
    dh0, dm0, up_b0 = feed_back(0, r0_late, slope0)
    feed_pack0 = feed_weights(m0, dh0, active0, r0)
    u_part = shape_of((block_len // 2, width), BF16)
    ua_keep, ua_send, ub_keep, ub_send = run(
        halve_again_body, me, u_parts, [u_part] * 4, name="halve_again", limit=8
    )
    ub_came, ua_came = both_ways(ub_send, ua_send, "tensor")
    back0, (feed_keep, feed_send, dm0, up_b0, u1) = over_chips(
        back0, (*feed_pack0, dm0, up_b0, [ua_keep, ua_came, ub_keep, ub_came])
    )
    dproj0, da0, qkv_b0, e0 = project_back(0, back0, dm0)
    head_keep, head_send = head_weights(a0, dproj0, attended0, r0)
    e0 = after(e0, head_keep)
    way = shape_of((3 * half // 4, width), BF16)
    a_keep, a_send, b_keep, b_send = run(
        halve_body,
        me,
        [feed_keep, swap_core(feed_send), head_keep, swap_core(head_send)],
        [way] * 4,
        scratch=[pltpu.VMEM((2 * half, width), BF16), pltpu.VMEM((half, width), BF16)],
        name="halve",
        limit=20,
    )
    gains0 = gains(after(x0, a_send), da0, dm0)
    a_came, b_came = both_ways(a_send, b_send)
    e0, (gains0, a_came, b_came) = tie(over_tensor(e0), (gains0, a_came, b_came))
    way = shape_of((3 * half // 8, width), BF16)
    a_keep, a_send, b_keep, b_send = run(
        halve_again_body, me, [a_keep, a_came, b_keep, b_came], [way] * 4, name="halve_again", limit=12
    )
    b_came, a_came = both_ways(b_send, a_send)
    part1 = after(part1, a_send)
    pack1 = lax.all_gather(part1, ("dp", "ctx"), axis_index_groups=columns, tiled=True)
    dx0, low0, bias0 = norm_back(after(e0, a_send), x0_quarter, dx1)
    last = share_tensor(low0)
    (a_came, b_came), last = tie((a_came, b_came), last)
    small = run(
        pack_small_body,
        me,
        [gains0, bias0, gains1, bias1, qkv_b0, qkv_b1, up_b0, up_b1],
        [shape_of((32, width), BF16)],
        name="pack_small",
        limit=8,
    )[0]

    few = half // 32
    cut = run(
        merge_body,
        me,
        [a_keep, a_came, b_keep, b_came, small],
        [shape_of((6 * few + 32, width), BF16)] * 4,
        scratch=[pltpu.VMEM((24 * few, width), BF16)],
        name="merge",
        limit=12,
    )
    u1 = run(
        add_halves_body, me, after(u1, cut[0]), [shape_of((block_len, width), BF16)], name="add_halves", limit=8
    )[0]
    cut, u1 = tie(over_x(cut), spread_near(u1, "tensor"))
    pieces = [shape_of((3 * few, width), BF16), shape_of((3 * few + 32, width), BF16)]
    first, second = run(settle_body, me, cut, pieces, name="settle", limit=8)
    first, second = tie(over_x([first] * 4), over_dp([second] * 4))
    second, small = line_up(3, second, 3 * few)
    first = line_up(0, first, 3 * few)[0]
    near = (spread_near(first, "dp"), spread_near(second, "x"))

    u1 = spread_far(u1, "tensor")
    last, u1 = after((last, u1), first)
    input_grad, output = run(
        functools.partial(place_body, block_len),
        me,
        [*last, *u1, x1, out_bias, down_bias],
        [shape_of((tokens, width), F32)] * 2,
        name="place",
        limit=20,
    )
    heavy = [
        shape_of((2, width, hidden), F32),
        shape_of((2, hidden, width), F32),
        shape_of((2, 3, width, inner), F32),
        shape_of((2, inner, width), F32),
    ]
    row_block = shape_of((16, width), BF16)
    shared, local = run(add_cut_body, me, [small, swap_core(small)], [row_block] * 2, name="add_cut", limit=8)
    shared_came = lax.ppermute(shared, "tensor", NEXT_PAIR)
    pack1 = after(pack1, shared)
    pack1_came = swap_core(pack1)
    near, (shared_came, pack1_came, input_grad, output) = tie(near, (shared_came, pack1_came, input_grad, output))
    quarter = half // 4
    views = [(2, 2, half, width)] * 2 + [(2, 3, 2, half, inner), (2, 2, LANES, width)]
    first_outs = run(
        unpack_whole_body,
        me,
        [
            (pack, pl.BlockSpec((quarter, width), lambda i, *_, part=part: (4 * part + i, 0)))
            for pack in (pack1, pack1_came)
            for part in range(3)
        ],
        [shape_of(view, F32) for view in views],
        name="unpack_whole",
        limit=24,
        out_specs=[
            pl.BlockSpec((1, 2, quarter, width), lambda i, *_: (1, 0, i, 0)),
            pl.BlockSpec((1, 2, quarter, width), lambda i, *_: (1, 0, i, 0)),
            pl.BlockSpec((1, 3, 2, quarter, inner), lambda i, *_: (1, 0, 0, i, 0)),
            pl.BlockSpec((1, 2, LANES, 2 * LANES), lambda i, *_: (1, 0, 0, i)),
        ],
        grid=4,
    )
    first_outs = [v.reshape(like.shape) for v, like in zip(first_outs, heavy)]
    far = (spread_far(near[0], "dp"), spread_far(near[1], "x"))
    other = [swap_core(v) for v in near[0] + near[1]]
    shared = add_all([shared, shared_came])
    shared_came = lax.ppermute(shared, "tensor", WRAP_PAIR)
    row_pair = shape_of((2, width), F32)
    small = run(
        small_out_body,
        me,
        [shared, shared_came, local],
        [row_pair] * 6 + [shape_of((2, 3, inner), F32)],
        name="small_out",
        limit=8,
    )
    mine, (small, other, first_outs) = tie(far[0] + far[1], (small, other, first_outs))
    far = [swap_core(v) for v in mine[3:5] + mine[8:10]]
    other = other[0:3] + far[0:2] + other[3:6] + far[2:4]
    in_place = pl.BlockSpec(memory_space=pl.ANY)
    held = [pltpu.VMEM(v.shape[1:], F32) for v in heavy] + [pltpu.SemaphoreType.DMA((4,))]
    up_grad, down_grad, qkv_grad, out_grad = run(
        functools.partial(unpack_body, few),
        me,
        mine + other + [(v, in_place) for v in first_outs],
        heavy,
        name="unpack",
        limit=28,
        out_specs=[in_place] * 4,
        scratch=held,
        aliases={21 + index: index for index in range(4)},
    )
    return (
        output.reshape(tok_shape),
        input_grad.reshape(tok_shape),
        small[0],
        small[1],
        small[2],
        small[3],
        qkv_grad,
        small[6],
        out_grad,
        small[4],
        up_grad,
        small[5],
        down_grad,
        small[4],
    )


def solution(mesh):
    in_specs = (
        P("dp", "ctx", None),
        P("dp", "ctx"),
        P(),
        P(),
        P(),
        P(),
        P(None, None, None, "tensor"),
        P(None, None, "tensor"),
        P(None, "tensor", None),
        P(),
        P(None, None, "tensor"),
        P(None, "tensor"),
        P(None, "tensor", None),
        P(),
        P("dp", "ctx", None),
    )
    out_specs = (
        P("dp", "ctx", None),
        P("dp", "ctx", None),
        P(),
        P(),
        P(),
        P(),
        P(None, None, None, "tensor"),
        P(None, None, "tensor"),
        P(None, "tensor", None),
        P(),
        P(None, None, "tensor"),
        P(None, "tensor"),
        P(None, "tensor", None),
        P(),
    )
    return jax.shard_map(
        on_device, mesh=mesh, in_specs=in_specs, out_specs=out_specs, check_vma=False
    )
```

```python
import functools

import jax
import jax.numpy as jnp
from jax import lax
from jax.experimental import pallas as pl
from jax.experimental.pallas import tpu as pltpu
from jax.sharding import PartitionSpec as P

HEAD = 64
ROT = 16
LAYERS = 2
LANES = 128
F32 = jnp.float32
BF16 = jnp.bfloat16


def shape_of(shape, dtype):
    return jax.ShapeDtypeStruct(tuple(shape), dtype)


def whole(array):
    rank = array.ndim
    return pl.BlockSpec(array.shape, lambda i, *_: (0,) * rank, pipeline_mode=pl.Buffered(1))


def layer_spec(array, layer):
    rank = array.ndim
    return pl.BlockSpec(
        (1,) + array.shape[1:], lambda i, *_: (layer,) + (0,) * (rank - 1), pipeline_mode=pl.Buffered(1)
    )


def run(body, me, operands, outs, scratch=(), name=None, limit=32, out_specs=None, aliases=None, grid=1):
    arrays, specs = [], []
    for operand in operands:
        array, spec = operand if isinstance(operand, tuple) else (operand, None)
        arrays.append(array)
        specs.append(whole(array) if spec is None else spec)
    return pl.pallas_call(
        body,
        grid_spec=pltpu.PrefetchScalarGridSpec(
            num_scalar_prefetch=1,
            grid=(grid,),
            in_specs=specs,
            out_specs=[whole(o) for o in outs] if out_specs is None else out_specs,
            scratch_shapes=list(scratch),
        ),
        out_shape=list(outs),
        input_output_aliases=aliases or {},
        compiler_params=pltpu.CompilerParams(vmem_limit_bytes=limit * 1024 * 1024),
        cost_estimate=pl.CostEstimate(flops=1, bytes_accessed=1, transcendentals=0),
        name=name,
    )(me, *arrays)


def matmul(left, right):
    return jnp.dot(left, right, preferred_element_type=F32)


def matmul_nt(left, right):
    return lax.dot_general(left, right, (((1,), (1,)), ((), ())), preferred_element_type=F32)


def matmul_tn(left, right):
    return lax.dot_general(left, right, (((0,), (0,)), ((), ())), preferred_element_type=F32)


def normalize(values):
    average = jnp.mean(values, axis=-1, keepdims=True)
    centred = values - average
    factor = lax.rsqrt(jnp.mean(centred * centred, axis=-1, keepdims=True) + 1e-05)
    return centred * factor, factor


def wrap4(value):
    return lax.rem(value + 4, 4)


def rows(index, size):
    return pl.ds(pl.multiple_of(index * size, size), size)


def rotary_rows(place_row):
    count = place_row.shape[1]
    which = lax.broadcasted_iota(jnp.int32, (8, count), 0)
    frequency = jnp.zeros((8, count), F32)
    for index in range(8):
        frequency = jnp.where(which == index, 10000.0 ** (-2.0 * index / ROT), frequency)
    angles = frequency * place_row
    trig = jnp.concatenate([jnp.cos(angles), jnp.sin(angles)], axis=0)
    row = lax.broadcasted_iota(jnp.int32, (16, LANES), 0)
    lane = lax.broadcasted_iota(jnp.int32, (16, LANES), 1) & (HEAD - 1)
    same = (lane & 7) == (row & 7)
    is_cos = row < 8
    pick_cos = jnp.where(is_cos & same & (lane < 16), 1.0, 0.0)
    pick_low = jnp.where((row >= 8) & same & (lane < 8), 1.0, 0.0)
    pick_high = jnp.where((row >= 8) & same & (lane >= 8) & (lane < 16), 1.0, 0.0)
    picks = jnp.concatenate([pick_cos, pick_low, pick_high], axis=1).astype(F32)
    spread = lax.dot_general(
        trig, picks, (((0,), (0,)), ((), ())), preferred_element_type=F32, precision=lax.Precision.HIGHEST
    )
    lane_row = lax.broadcasted_iota(jnp.int32, (1, LANES), 1) & (HEAD - 1)
    cos_table = spread[:, :LANES] + jnp.where(lane_row >= ROT, 1.0, 0.0)
    return cos_table, spread[:, LANES : 2 * LANES], spread[:, 2 * LANES :]


def rotate(values, tables, back=False):
    cos_table, low_sin, high_sin = tables
    below = pltpu.roll(values, LANES - ROT // 2, 1) * low_sin
    above = pltpu.roll(values, ROT // 2, 1) * high_sin
    turned = below - above if back else above - below
    return values * cos_table + turned


def project_rows(layer, tok_shape, me_ref, seg_ref, weight, bias, a_ref, p_refs, proj_ref, with_seg):
    seq_count, block_len, width = tok_shape
    chip, core = me_ref[0], me_ref[1]
    base = (chip * 2 + core) * block_len
    for j in range(3):
        proj_ref[:, j * 2 * LANES : (j + 1) * 2 * LANES] = matmul(a_ref[...], weight(j)) + bias[j, layer : layer + 1, :]
    for k in range(4):
        seq = wrap4(chip + k)
        place = rows(seq, block_len)
        seg_row = seg_ref[pl.ds(seq, 1), :]
        spots = lax.broadcasted_iota(jnp.int32, (1, block_len), 1) + base
        tables = rotary_rows((spots - seg_row).astype(F32))
        for j in range(3):
            for pair in range(2):
                at = (2 * j + pair) * LANES
                part = proj_ref[place, at : at + LANES]
                if j < 2:
                    part = rotate(part, tables)
                p_refs[k][pair, 0:block_len, j * LANES : (j + 1) * LANES] = part.astype(BF16)
        if with_seg:
            coded = seg_row.astype(F32)
            high = jnp.floor(coded * 0.125)
            packed = jnp.concatenate([high, coded - 8.0 * high, jnp.zeros_like(high)], axis=1)
            packed = jnp.broadcast_to(packed, (16, 3 * LANES)).astype(BF16)
            for pair in range(2):
                p_refs[k][pair, block_len : block_len + 16, :] = packed


def project_first_body(tok_shape, me_ref, *refs):
    seq_count, block_len, width = tok_shape
    in_refs, refs = refs[:8], refs[8:]
    xq_ref, a_ref, m_ref, *p_refs = refs[:7]
    proj_ref, *held, sems = refs[7:]
    x_ref, seg_ref, ag_ref, as_ref, mg_ref, ms_ref, w_ref, b_ref = held
    copies = []
    for index in (1, 2, 3, 4, 5):
        copies.append(pltpu.make_async_copy(in_refs[index], held[index], sems.at[len(copies)]))
    copies.append(pltpu.make_async_copy(in_refs[7], b_ref, sems.at[len(copies)]))
    small_count = len(copies)
    for seq in range(seq_count):
        place = pl.ds(seq * block_len, block_len)
        copies.append(pltpu.make_async_copy(in_refs[0].at[place], x_ref.at[place], sems.at[len(copies)]))
    copies.append(pltpu.make_async_copy(in_refs[6].at[0], w_ref, sems.at[len(copies)]))
    for copy in copies:
        copy.start()
    for copy in copies[:small_count]:
        copy.wait()
    for seq in range(seq_count):
        copies[small_count + seq].wait()
        place = slice(seq * block_len, (seq + 1) * block_len)
        normed, _ = normalize(x_ref[place, :])
        a_ref[place, :] = (normed * ag_ref[0:1, :] + as_ref[0:1, :]).astype(BF16)
        m_ref[place, :] = (normed * mg_ref[0:1, :] + ms_ref[0:1, :]).astype(BF16)
    xq_ref[...] = x_ref[rows(me_ref[2], block_len), :]
    copies[-1].wait()
    project_rows(0, tok_shape, me_ref, seg_ref, lambda j: w_ref[j], b_ref, a_ref, p_refs, proj_ref, True)


def project_body(layer, tok_shape, me_ref, *refs):
    seq_count, block_len, width = tok_shape
    x_ref, seg_ref, *refs = refs
    u_refs, refs = refs[:4], refs[4:]
    ob_ref, db_ref, ag_ref, as_ref, mg_ref, ms_ref, w_ref, b_ref, x_out, xq_ref, a_ref, m_ref, *p_refs, proj_ref = refs
    tensor = me_ref[2]
    shift = ob_ref[layer - 1 : layer, :] + db_ref[layer - 1 : layer, :]
    for k in range(4):
        place = rows(wrap4(tensor - k), block_len)
        value = x_ref[place, :] + u_refs[k][...].astype(F32) + shift
        x_out[place, :] = value
        if k == 0:
            xq_ref[...] = value
        normed, _ = normalize(value)
        a_ref[place, :] = (normed * ag_ref[layer : layer + 1, :] + as_ref[layer : layer + 1, :]).astype(BF16)
        m_ref[place, :] = (normed * mg_ref[layer : layer + 1, :] + ms_ref[layer : layer + 1, :]).astype(BF16)
    project_rows(layer, tok_shape, me_ref, seg_ref, lambda j: w_ref[0, j], b_ref, a_ref, p_refs, proj_ref, False)


def gather_pieces(me_ref, refs, targets, block_len, seg_target=None):
    chip, core = me_ref[0], me_ref[1]
    for k in range(4):
        owner = wrap4(chip - k)
        for side, ref in ((core, refs[k]), (1 - core, refs[4 + k])):
            place = rows(owner * 2 + side, block_len)
            for index, target in enumerate(targets):
                target[place, :] = ref[core, 0:block_len, index * LANES : (index + 1) * LANES]
            if seg_target is not None:
                row = ref[core, block_len : block_len + 16, :].astype(F32)[0:1, :]
                starts = row[:, 0:LANES] * 8.0 + row[:, LANES : 2 * LANES]
                seg_target[:, place] = jnp.broadcast_to(starts, (8, block_len))


def head_stack(values):
    lane = lax.broadcasted_iota(jnp.int32, values.shape, 1)
    zero = jnp.zeros_like(values)
    return jnp.concatenate(
        [jnp.where(lane < HEAD, values, zero), jnp.where(lane >= HEAD, values, zero)], axis=0
    )


def own_halves(product, width):
    return jnp.concatenate([product[0:HEAD, 0:width], product[HEAD:, width : 2 * width]], axis=0)


def chances_t(q_ref, k_ref, seg_ref, step, chunk):
    start, keys = step * chunk, (step + 1) * chunk
    stacked = head_stack(q_ref[start:keys, :]) * jnp.asarray(HEAD ** (-0.5), BF16)
    scores = matmul_nt(k_ref[0:keys, :], stacked)
    key_place = lax.broadcasted_iota(jnp.int32, (keys, 2 * chunk), 0).astype(F32)
    query_place = (lax.broadcasted_iota(jnp.int32, (1, 2 * chunk), 1) & (chunk - 1)).astype(F32) + start
    seg_row = seg_ref[0:1, start:keys]
    seg_row = jnp.concatenate([seg_row, seg_row], axis=1)
    allowed = (key_place >= seg_row) & (key_place <= query_place)
    scores = jnp.where(allowed, scores, -1e30)
    raised = jnp.exp(scores - jnp.max(scores, axis=0, keepdims=True))
    total = jnp.sum(raised, axis=0, keepdims=True)
    return raised * (1.0 / total), stacked


def attend_body(block_len, chunk, me_ref, *refs):
    piece_refs, refs = refs[:8], refs[8:]
    seg_out, qkv_ref, *refs = refs
    o_refs, refs = refs[:4], refs[4:]
    vt_ref, o_ref = refs
    q_ref, k_ref, v_ref = qkv_ref.at[0], qkv_ref.at[1], qkv_ref.at[2]
    gather_pieces(me_ref, piece_refs, (q_ref, k_ref, v_ref), block_len, seg_out)
    vt_ref[...] = v_ref[...].T
    length = q_ref.shape[0]
    for step in range(length // chunk):
        keys = (step + 1) * chunk
        chances, _ = chances_t(q_ref, k_ref, seg_out, step, chunk)
        mixed = matmul(vt_ref[:, 0:keys], chances.astype(BF16))
        o_ref[step * chunk : keys, :] = own_halves(mixed, chunk).T.astype(BF16)
    send_blocks(me_ref, o_ref, o_refs, block_len)


def send_blocks(me_ref, source, targets, block_len):
    chip = me_ref[0]
    for k in range(4):
        dest = wrap4(chip + k)
        for side in range(2):
            targets[k][side] = source[rows(dest * 2 + side, block_len), :]


def attend_both_body(block_len, chunk, with_out, me_ref, *refs):
    if with_out:
        piece_refs, refs = refs[:8], refs[8:]
    else:
        qkv_ref, *refs = refs
    grad_refs, refs = refs[:8], refs[8:]
    seg_ref, *refs = refs
    d_refs, refs = refs[:4], refs[4:]
    if with_out:
        qkv_ref, *refs = refs
    q_ref, k_ref, v_ref = qkv_ref.at[0], qkv_ref.at[1], qkv_ref.at[2]
    g_ref, t_ref, o_ref, dq_ref, dk_ref, dv_ref = refs
    if with_out:
        gather_pieces(me_ref, piece_refs, (q_ref, k_ref, v_ref), block_len)
    gather_pieces(me_ref, grad_refs, (g_ref,), block_len)
    length = q_ref.shape[0]
    t_ref[0] = k_ref[...].T
    if with_out:
        t_ref[1] = v_ref[...].T
    dk_ref[...] = jnp.zeros_like(dk_ref)
    dv_ref[...] = jnp.zeros_like(dv_ref)
    for step in range(length // chunk):
        start, keys = step * chunk, (step + 1) * chunk
        chances, stacked = chances_t(q_ref, k_ref, seg_ref, step, chunk)
        low = chances.astype(BF16)
        if with_out:
            mixed = matmul(t_ref[1, :, 0:keys], low)
            o_ref[start:keys, :] = own_halves(mixed, chunk).T.astype(BF16)
        grads = head_stack(g_ref[start:keys, :])
        chance_grad = matmul_nt(v_ref[0:keys, :], grads)
        delta = jnp.sum(chances * chance_grad, axis=0, keepdims=True)
        score_grad = (chances * (chance_grad - delta)).astype(BF16)
        dv_ref[0:keys, :] += matmul(low, grads)
        dk_ref[0:keys, :] += matmul(score_grad, stacked)
        query = matmul(t_ref[0, :, 0:keys], score_grad)
        dq_ref[start:keys, :] = own_halves(query, chunk).T * HEAD ** (-0.5)
    chip = me_ref[0]
    for k in range(4):
        dest = wrap4(chip + k)
        for side in range(2):
            place = rows(dest * 2 + side, block_len)
            spots = (lax.broadcasted_iota(jnp.int32, (1, block_len), 1) + (dest * 2 + side) * block_len).astype(F32)
            tables = rotary_rows(spots - seg_ref[0:1, place])
            d_refs[k][side, :, 0:LANES] = rotate(dq_ref[place, :], tables, True).astype(BF16)
            d_refs[k][side, :, LANES : 2 * LANES] = rotate(dk_ref[place, :], tables, True).astype(BF16)
            d_refs[k][side, :, 2 * LANES : 3 * LANES] = dv_ref[place, :].astype(BF16)
            if with_out:
                d_refs[k][side, :, 3 * LANES :] = o_ref[place, :]


def land_heads(me_ref, refs, target, block_len, groups, first=0):
    chip, core = me_ref[0], me_ref[1]
    for k in range(4):
        place = rows(wrap4(chip - k), block_len)
        mine, other = refs[k][core], refs[4 + k][core]
        is_low = core == 0
        for group in range(groups):
            span = slice((first + group) * LANES, (first + group + 1) * LANES)
            at = group * 2 * LANES
            target[place, at : at + LANES] = jnp.where(is_low, mine[:, span], other[:, span])
            target[place, at + LANES : at + 2 * LANES] = jnp.where(is_low, other[:, span], mine[:, span])


def combine_body(block_len, fused, me_ref, *refs):
    piece_refs, refs = refs[:8], refs[8:]
    w_ref, *refs = refs
    if fused:
        g_ref, down_ref, *refs = refs
    else:
        part_ref, *refs = refs
    o_ref, *refs = refs
    q_refs, scr = refs[:-1], refs[-1]
    tensor = me_ref[2]
    land_heads(me_ref, piece_refs, o_ref, block_len, 1, 3 if fused else 0)
    part = matmul(g_ref[...], down_ref[0]) if fused else part_ref[...]
    scr[...] = (matmul(o_ref[...], w_ref[0]) + part).astype(BF16)
    if fused:
        near, far = near_far(tensor)
        size = block_len // 2
        orders = ((tensor, far), (near, 3 - near), (tensor, near), (far, far ^ 1))
        for way, (ref, order) in enumerate(zip(q_refs, orders)):
            for index, quarter in enumerate(order):
                at = pl.multiple_of(quarter * block_len + (way >> 1) * size, size)
                ref[index * size : (index + 1) * size, :] = scr[pl.ds(at, size), :]
        return
    for k in range(4):
        q_refs[k][...] = scr[rows(wrap4(tensor + k), block_len), :]


def send_grad_body(block_len, me_ref, x_ref, w_ref, *refs):
    chip, tensor = me_ref[0], me_ref[2]
    quarter_ref, *refs = refs
    quarter_ref[...] = x_ref[rows(tensor, block_len), :]
    for k in range(4):
        value = x_ref[rows(wrap4(chip + k), block_len), :].astype(BF16)
        grad = matmul_nt(value, w_ref[0]).astype(BF16)
        for pair in range(2):
            refs[k][pair] = grad[:, pair * LANES : (pair + 1) * LANES]


def join_body(block_len, me_ref, *refs):
    q_refs, refs = refs[:4], refs[4:]
    w_ref, r_ref, *g_refs = refs
    chip, tensor = me_ref[0], me_ref[2]
    for k in range(4):
        r_ref[rows(wrap4(tensor - k), block_len), :] = q_refs[k][...]
    for k in range(4):
        value = r_ref[rows(wrap4(chip + k), block_len), :]
        grad = matmul_nt(value, w_ref[0]).astype(BF16)
        for pair in range(2):
            g_refs[k][pair] = grad[:, pair * LANES : (pair + 1) * LANES]


def project_back_body(block_len, layer, me_ref, *refs):
    piece_refs, refs = refs[:8], refs[8:]
    w_ref, dm_ref, ag_ref, mg_ref, *refs = refs
    riders, refs = refs[:-8], refs[-8:]
    dp_ref, da_ref, bias_ref, *q_refs, scr = refs
    tensor = me_ref[2]
    land_heads(me_ref, piece_refs, dp_ref, block_len, 3)
    for j in range(3):
        span = slice(j * 2 * LANES, (j + 1) * 2 * LANES)
        bias_ref[j : j + 1, :] = jnp.sum(dp_ref[:, span].astype(F32), axis=0, keepdims=True)
    total = None
    for j in range(3):
        term = matmul_nt(dp_ref[:, j * 2 * LANES : (j + 1) * 2 * LANES], w_ref[0, j])
        total = term if total is None else total + term
    da_ref[...] = total.astype(BF16)
    scr[...] = (total * ag_ref[layer : layer + 1, :] + dm_ref[...] * mg_ref[layer : layer + 1, :]).astype(BF16)
    for k in range(4):
        q_refs[k][0:block_len, :] = scr[rows(wrap4(tensor + k), block_len), :]
        if riders:
            q_refs[k][block_len:, :] = riders[k][...]


def norm_back_body(me_ref, *refs):
    e_ref, x_ref, dy_ref, *gain_refs, dx_ref, low_ref, bias_ref = refs
    upstream = dy_ref[...]
    size = upstream.shape[0]
    total = e_ref[0:size, :]
    normed, factor = normalize(x_ref[...])
    inner = jnp.mean(total * normed, axis=-1, keepdims=True)
    result = upstream + factor * (total - jnp.mean(total, axis=-1, keepdims=True) - normed * inner)
    dx_ref[...] = result
    low_ref[0:size, :] = result.astype(BF16)
    bias = jnp.sum(upstream, axis=0, keepdims=True)
    bias_ref[...] = bias
    if gain_refs:
        mine, other, other_bias = gain_refs
        blank = jnp.zeros((6, bias.shape[1]), F32)
        rows_here = jnp.concatenate([mine[...], bias, other[...], other_bias[...], blank], axis=0)
        low_ref[size:, :] = rows_here.astype(BF16)


def gains_body(me_ref, x_ref, da_ref, dm_ref, out_ref):
    normed, _ = normalize(x_ref[...])
    da = da_ref[...].astype(F32)
    dm = dm_ref[...]
    out_ref[0:1, :] = jnp.sum(da * normed, axis=0, keepdims=True)
    out_ref[1:2, :] = jnp.sum(da, axis=0, keepdims=True)
    out_ref[2:3, :] = jnp.sum(dm * normed, axis=0, keepdims=True)
    out_ref[3:4, :] = jnp.sum(dm, axis=0, keepdims=True)


def gelu_parts(hidden):
    cdf = 0.5 * (1.0 + lax.erf(hidden * (0.5**0.5)))
    density = jnp.exp(-0.5 * hidden * hidden) * 0.3989422804014327
    return cdf, density


def feed_body(layer, me_ref, m_ref, up_ref, ub_ref, down_ref, g_ref, slope_ref, part_ref):
    size = 2 * LANES
    for step in range(up_ref.shape[2] // size):
        span = slice(step * size, (step + 1) * size)
        hidden = matmul(m_ref[...], up_ref[0, :, span]) + ub_ref[layer : layer + 1, span]
        cdf, density = gelu_parts(hidden)
        g_ref[:, span] = (hidden * cdf).astype(BF16)
        slope_ref[:, span] = cdf + hidden * density
    part_ref[...] = matmul(g_ref[...], down_ref[0])


def feed_back_body(me_ref, r_ref, slope_ref, up_ref, down_ref, dh_ref, dm_ref, bias_ref):
    size = 2 * LANES
    for step in range(down_ref.shape[1] // size):
        span = slice(step * size, (step + 1) * size)
        grad = matmul_nt(r_ref[...], down_ref[0, span, :]) * slope_ref[:, span]
        bias_ref[:, span] = jnp.sum(grad, axis=0, keepdims=True)
        dh_ref[:, span] = grad.astype(BF16)
    dm_ref[...] = matmul_nt(dh_ref[...], up_ref[0])


def feed_both_body(layer, me_ref, m_ref, dy_ref, up_ref, ub_ref, down_ref, g_ref, r_ref, dh_ref, dm_ref, bias_ref):
    size = 2 * LANES
    r_ref[...] = dy_ref[...].astype(BF16)
    for step in range(up_ref.shape[2] // size):
        span = slice(step * size, (step + 1) * size)
        hidden = matmul(m_ref[...], up_ref[0, :, span]) + ub_ref[layer : layer + 1, span]
        cdf, density = gelu_parts(hidden)
        g_ref[:, span] = (hidden * cdf).astype(BF16)
        grad = matmul_nt(r_ref[...], down_ref[0, span, :]) * (cdf + hidden * density)
        bias_ref[:, span] = jnp.sum(grad, axis=0, keepdims=True)
        dh_ref[:, span] = grad.astype(BF16)
    dm_ref[...] = matmul_nt(dh_ref[...], up_ref[0])


def feed_weights_body(me_ref, m_ref, dh_ref, g_ref, r_ref, keep_ref, send_ref):
    core = me_ref[1]
    half = m_ref.shape[1] // 2
    for side, out in ((core, keep_ref), (1 - core, send_ref)):
        out[0:half, :] = matmul_tn(m_ref[:, rows(side, half)], dh_ref[...]).astype(BF16)
        out[half:, :] = matmul_tn(g_ref[:, rows(side, half)], r_ref[...]).astype(BF16)


def head_weights_body(me_ref, a_ref, dp_ref, o_ref, r_ref, keep_ref, send_ref):
    core = me_ref[1]
    half = a_ref.shape[1] // 2
    wide = dp_ref.shape[1]
    for side, out in ((core, keep_ref), (1 - core, send_ref)):
        out[:, 0:wide] = matmul_tn(a_ref[:, rows(side, half)], dp_ref[...]).astype(BF16)
        grad = matmul_tn(o_ref[:, rows(side, LANES)], r_ref[...]).astype(BF16)
        for part in range(4):
            out[part * LANES : (part + 1) * LANES, wide:] = grad[:, part * 2 * LANES : (part + 1) * 2 * LANES]


def feed_weights_whole_body(me_ref, m_ref, dh_ref, g_ref, r_ref, pack_ref):
    high = m_ref.shape[1]
    pack_ref[0:high, :] = matmul_tn(m_ref[...], dh_ref[...]).astype(BF16)
    pack_ref[high:, :] = matmul_tn(g_ref[...], r_ref[...]).astype(BF16)


def head_weights_whole_body(me_ref, a_ref, dp_ref, o_ref, r_ref, before_ref, pack_ref):
    wide = dp_ref.shape[1]
    pack_ref[:, 0:wide] = matmul_tn(a_ref[...], dp_ref[...]).astype(BF16)
    grad = matmul_tn(o_ref[...], r_ref[...]).astype(BF16)
    high, size = grad.shape[0], 2 * LANES
    for part in range(4):
        pack_ref[part * high : (part + 1) * high, wide:] = grad[:, part * size : (part + 1) * size]


def near_far(place):
    return place ^ 1, 3 - place


def halve_body(me_ref, feed_keep, feed_came, head_keep, head_came, *refs):
    outs, feed_scr, head_scr = refs[:4], refs[4], refs[5]
    feed_scr[...] = (feed_keep[...].astype(F32) + feed_came[...].astype(F32)).astype(BF16)
    head_scr[...] = (head_keep[...].astype(F32) + head_came[...].astype(F32)).astype(BF16)
    place = me_ref[3]
    near, far = near_far(place)
    half = head_scr.shape[0]
    size = half // 8
    orders = ((place, far), (near, 3 - near), (4 + place, 4 + near), (4 + far, 4 + (far ^ 1)))
    for ref, order in zip(outs, orders):
        for index, block in enumerate(order):
            at = 3 * size * index
            ref[at : at + size, :] = feed_scr[rows(block, size), :]
            ref[at + size : at + 2 * size, :] = feed_scr[pl.ds(pl.multiple_of(half + block * size, size), size), :]
            ref[at + 2 * size : at + 3 * size, :] = head_scr[rows(block, size), :]


def halve_again_body(me_ref, a_keep, a_came, b_keep, b_came, *outs):
    size = outs[0].shape[0]
    for keep, came, mine, send in ((a_keep, a_came, outs[0], outs[1]), (b_keep, b_came, outs[2], outs[3])):
        total = (keep[...].astype(F32) + came[...].astype(F32)).astype(BF16)
        mine[...] = total[0:size, :]
        send[...] = total[size:, :]


def line_up_body(axis, me_ref, *refs):
    size = refs[4].shape[0] // 4
    for k in range(4):
        refs[4][rows(wrap4(me_ref[axis] - k), size), :] = refs[k][0:size, :]
    if len(refs) > 5:
        even = refs[0][size:, :].astype(F32) + refs[2][size:, :].astype(F32)
        odd = refs[1][size:, :].astype(F32) + refs[3][size:, :].astype(F32)
        refs[5][...] = (even + odd).astype(BF16)


def merge_body(me_ref, a_keep, a_came, b_keep, b_came, *refs):
    last_refs, local_ref, out_refs, scr = refs[:4], refs[4], refs[5:9], refs[9]
    count = local_ref.shape[0]
    shared = [ref[ref.shape[0] - count :, :].astype(F32) for ref in last_refs]
    shared = ((shared[0] + shared[2]) + (shared[1] + shared[3])).astype(BF16)
    high = a_keep.shape[0]
    scr[0:high, :] = (a_keep[...].astype(F32) + a_came[...].astype(F32)).astype(BF16)
    scr[high:, :] = (b_keep[...].astype(F32) + b_came[...].astype(F32)).astype(BF16)
    few = high // 6
    for k in range(4):
        part = wrap4(me_ref[0] + k)
        for weight in range(3):
            at = pl.multiple_of((part >> 1) * high + weight * 2 * few + (part & 1) * few, few)
            out_refs[k][weight * few : (weight + 1) * few, :] = scr[pl.ds(at, few), :]
        out_refs[k][3 * few : 3 * few + count, :] = shared
        out_refs[k][3 * few + count :, :] = local_ref[...]


def settle_body(me_ref, *refs):
    in_refs, (first_ref, second_ref) = refs[:4], refs[4:]
    even = in_refs[0][...].astype(F32) + in_refs[2][...].astype(F32)
    odd = in_refs[1][...].astype(F32) + in_refs[3][...].astype(F32)
    total = (even + odd).astype(BF16)
    few = first_ref.shape[0] // 3
    for weight in range(3):
        for index, ref in enumerate((first_ref, second_ref)):
            at = (2 * weight + index) * few
            ref[weight * few : (weight + 1) * few, :] = total[at : at + few, :]
    second_ref[3 * few :, :] = total[6 * few :, :]


def flush(held, outs, layer, sems):
    copies = [pltpu.make_async_copy(a, b.at[layer], sems.at[i]) for i, (a, b) in enumerate(zip(held, outs))]
    return copies


def unpack_body(few, me_ref, *refs):
    outs, held, sems = refs[24:28], refs[28:32], refs[32]
    up_ref, down_ref, qkv_ref, out_ref = held
    copies = flush(held, outs, 0, sems)
    chip, core, place_z = me_ref[0], me_ref[1], me_ref[3]
    size = 2 * LANES
    half = up_ref.shape[0] // 2
    for weight in range(3):
        for side, group in ((core, refs[:10]), (1 - core, refs[10:20])):
            for along, me in ((0, place_z), (1, chip)):
                pieces = group[5 * along : 5 * along + 5]
                spans = [(pieces[0], me, 0), (pieces[1], me ^ 1, 0), (pieces[2], 3 - me, 0)]
                spans += [(pieces[3], me ^ 2, 0), (pieces[4], me ^ 2, 2)]
                for ref, owner, first in spans:
                    for index in range(ref.shape[0] // (3 * few)):
                        z, x = (owner, first + index) if along == 0 else (first + index, owner)
                        start = (3 * index + weight) * few
                        value = ref[start : start + few, :].astype(F32)
                        row = (z + 4 * (x >> 1)) * (4 * few) + (x & 1) * (2 * few) + along * few
                        place = pl.ds(pl.multiple_of(row + side * half, few), few)
                        if weight < 2:
                            held[weight][place, :] = value
                        else:
                            for j in range(3):
                                qkv_ref[j, place, :] = value[:, j * size : (j + 1) * size]
                            inner = pl.ds(pl.multiple_of((row & (LANES - 1)) + side * LANES, few), few)
                            lanes = pl.ds(pl.multiple_of((row >> 7) * size, size), size)
                            out_ref[inner, lanes] = value[:, 3 * size :]
        for copy in copies[weight : weight + 1] if weight < 2 else copies[2:]:
            copy.start()
    for copy in copies:
        copy.wait()


def add_packs_body(me_ref, feed_keep, feed_came, head_keep, head_came, out_ref):
    high = feed_keep.shape[0]
    out_ref[0:high, :] = (feed_keep[...].astype(F32) + feed_came[...].astype(F32)).astype(BF16)
    out_ref[high:, :] = (head_keep[...].astype(F32) + head_came[...].astype(F32)).astype(BF16)


def unpack_whole_body(me_ref, up_mine, down_mine, head_mine, up_other, down_other, head_other, *outs):
    up_ref, down_ref, qkv_ref, out_ref = outs
    size = 2 * LANES
    for core in range(2):
        mine = me_ref[1] == core
        for ref, first, second in ((up_ref, up_mine, up_other), (down_ref, down_mine, down_other)):
            ref[0, core] = jnp.where(mine, first[...], second[...]).astype(F32)
        head = jnp.where(mine, head_mine[...], head_other[...]).astype(F32)
        for j in range(3):
            qkv_ref[0, j, core] = head[:, j * size : (j + 1) * size]
        out_ref[0, core] = head[:, 3 * size :]


def pack_small_body(me_ref, *refs):
    ins, local_ref = refs[:4], refs[4]
    width = local_ref.shape[1]
    local = [ins[2][...], ins[3][...]]
    for ref in ins[0:2]:
        values = ref[...]
        flat = [values[j : j + 1, :] for j in range(3)]
        local.append(jnp.concatenate(flat + [jnp.zeros((1, width - 3 * values.shape[1]), F32)], axis=1))
    local_ref[...] = jnp.concatenate(local + [jnp.zeros((12, width), F32)], axis=0).astype(BF16)


def add_halves_body(me_ref, a_keep, a_came, b_keep, b_came, out_ref):
    size = a_keep.shape[0]
    out_ref[0:size, :] = (a_keep[...].astype(F32) + a_came[...].astype(F32)).astype(BF16)
    out_ref[size:, :] = (b_keep[...].astype(F32) + b_came[...].astype(F32)).astype(BF16)


def add_body(count, me_ref, *refs):
    total = refs[0][...].astype(F32)
    for ref in refs[1:count]:
        total = total + ref[...].astype(F32)
    refs[count][...] = total.astype(refs[count].dtype)


def small_out_body(me_ref, mine_ref, came_ref, *outs):
    total = mine_ref[...].astype(F32) + came_ref[...].astype(F32)
    shared, local = total[0:16, :], total[16:32, :]
    for index in range(5):
        outs[index][0:1, :] = shared[index : index + 1, :]
        outs[index][1:2, :] = shared[index + 5 : index + 6, :]
    outs[5][...] = local[0:2, :]
    size = outs[6].shape[2]
    for layer in range(2):
        for j in range(3):
            outs[6][layer, j : j + 1, :] = local[2 + layer : 3 + layer, j * size : (j + 1) * size]


def place_body(block_len, me_ref, *refs):
    q_refs, u_refs, (x_ref, ob_ref, db_ref, grad_ref, out_ref) = refs[:4], refs[4:9], refs[9:]
    shift = ob_ref[1:2, :] + db_ref[1:2, :]
    me = me_ref[2]
    for k in range(4):
        grad_ref[rows(wrap4(me - k), block_len), :] = q_refs[k][0:block_len, :].astype(F32)
    half = block_len // 2
    spots = ((me, 0), (me ^ 1, 0), (3 - me, 0), (me ^ 2, 0), (me ^ 2, half))
    for ref, (quarter, offset) in zip(u_refs, spots):
        count = ref.shape[0]
        place = pl.ds(pl.multiple_of(quarter * block_len + offset, half), count)
        out_ref[place, :] = x_ref[place, :] + ref[...].astype(F32) + shift


def chip_turn(shift):
    return [(2 * x + c, 2 * ((x + shift) % 4) + c) for x in range(4) for c in range(2)]


CORE_SWAP = [(i, i ^ 1) for i in range(8)]


def over_chips(pieces, beside=()):
    mine, beside = lax.optimization_barrier((over_x(pieces), beside))
    return mine + [swap_core(piece) for piece in mine], beside


def ring_turn(shift):
    return [(i, (i + shift) % 4) for i in range(4)]


def over_tensor(pieces):
    return [pieces[0]] + [lax.ppermute(pieces[k], "tensor", ring_turn(k)) for k in range(1, 4)]


def share_tensor(piece):
    return over_tensor([piece] * 4)


def over_dp(pieces):
    return [pieces[0]] + [lax.ppermute(pieces[k], "dp", ring_turn(k)) for k in range(1, 4)]


def over_x(pieces):
    return [pieces[0]] + [lax.ppermute(pieces[k], "ctx", chip_turn(k)) for k in range(1, 4)]


def swap_core(piece):
    return lax.ppermute(piece, "ctx", CORE_SWAP)


NEXT_PAIR = [(0, 1), (1, 0), (2, 3), (3, 2)]
WRAP_PAIR = [(0, 3), (3, 0), (1, 2), (2, 1)]


def both_ways(to_next, to_wrap, axis="dp"):
    return lax.ppermute(to_next, axis, NEXT_PAIR), lax.ppermute(to_wrap, axis, WRAP_PAIR)


def chips_of(pairs):
    return [(2 * a + c, 2 * b + c) for a, b in pairs for c in range(2)]


def along(axis):
    return ("ctx", chips_of) if axis == "x" else (axis, lambda pairs: pairs)


def spread_near(piece, axis):
    name, move = along(axis)
    return [piece] + [lax.ppermute(piece, name, move(pairs)) for pairs in (NEXT_PAIR, WRAP_PAIR)]


def spread_far(pieces, axis):
    name, move = along(axis)
    half = pieces[0].shape[0] // 2
    return pieces + [
        lax.ppermute(pieces[1][:half], name, move(WRAP_PAIR)),
        lax.ppermute(pieces[2][half:], name, move(NEXT_PAIR)),
    ]


def tie(first, second):
    return lax.optimization_barrier((first, second))


def after(values, token):
    return lax.optimization_barrier((values, token))[0]


def add_up(pieces):
    total = pieces[0].astype(F32)
    for piece in pieces[1:]:
        total = total + piece.astype(F32)
    return total


def on_device(
    inputs,
    segments,
    attn_gain,
    attn_shift,
    mlp_gain,
    mlp_shift,
    qkv_weight,
    qkv_bias,
    out_weight,
    out_bias,
    up_weight,
    up_bias,
    down_weight,
    down_bias,
    cotangent,
):
    seq_count, block_len, width = inputs.shape
    tokens = seq_count * block_len
    inner = qkv_weight.shape[3]
    hidden = up_weight.shape[2]
    length = block_len * 8
    chunk = 256
    place = lax.axis_index("ctx")
    me = jnp.stack([place // 2, place % 2, lax.axis_index("tensor"), lax.axis_index("dp")]).astype(jnp.int32)
    x0 = inputs.reshape(tokens, width)
    dy1 = cotangent.reshape(tokens, width)
    tok_shape = inputs.shape
    wide = shape_of((tokens, width), BF16)
    norms = (attn_gain, attn_shift, mlp_gain, mlp_shift)
    biases = qkv_bias.transpose(1, 0, 2)

    def project_first(x):
        sources = [x, segments, *norms, qkv_weight, biases]
        held = [v.shape for v in sources[:6]] + [qkv_weight.shape[1:], biases.shape]
        piece = shape_of((2, block_len + 16, 3 * LANES), BF16)
        return run(
            functools.partial(project_first_body, tok_shape),
            me,
            [(v, pl.BlockSpec(memory_space=pltpu.HBM)) for v in sources],
            [shape_of((block_len, width), F32), wide, wide] + [piece] * 4,
            scratch=[pltpu.VMEM((tokens, 3 * inner), F32)]
            + [pltpu.VMEM(size, v.dtype) for size, v in zip(held, sources)]
            + [pltpu.SemaphoreType.DMA((11,))],
            name="norm_project",
            limit=62,
        )

    def project(layer, x, extra):
        piece = shape_of((2, block_len, 3 * LANES), BF16)
        return run(
            functools.partial(project_body, layer, tok_shape),
            me,
            [x, segments, *extra, *norms]
            + [(qkv_weight, layer_spec(qkv_weight, layer)), biases],
            [shape_of((tokens, width), F32), shape_of((block_len, width), F32), wide, wide] + [piece] * 4,
            scratch=[pltpu.VMEM((tokens, 3 * inner), F32)],
            name="norm_project",
            limit=24,
        )

    def feed(layer, m):
        return run(
            functools.partial(feed_body, layer),
            me,
            [m, (up_weight, layer_spec(up_weight, layer)), up_bias, (down_weight, layer_spec(down_weight, layer))],
            [shape_of((tokens, hidden), BF16), shape_of((tokens, hidden), F32), shape_of((tokens, width), F32)],
            name="feed", limit=24,
        )

    def feed_back(layer, r, slope):
        return run(
            feed_back_body,
            me,
            [r, slope, (up_weight, layer_spec(up_weight, layer)), (down_weight, layer_spec(down_weight, layer))],
            [shape_of((tokens, hidden), BF16), shape_of((tokens, width), F32), shape_of((1, hidden), F32)],
            name="feed_back", limit=24,
        )

    def feed_both(layer, m, dy):
        return run(
            functools.partial(feed_both_body, layer),
            me,
            [m, dy, (up_weight, layer_spec(up_weight, layer)), up_bias, (down_weight, layer_spec(down_weight, layer))],
            [shape_of((tokens, hidden), BF16), wide, shape_of((tokens, hidden), BF16)]
            + [shape_of((tokens, width), F32), shape_of((1, hidden), F32)],
            name="feed_both", limit=24,
        )

    def combine(layer, pieces, part, active=None):
        fused = part is None
        got = run(
            functools.partial(combine_body, block_len, fused),
            me,
            [*pieces, (out_weight, layer_spec(out_weight, layer))]
            + ([active, (down_weight, layer_spec(down_weight, layer))] if fused else [part]),
            [shape_of((tokens, inner), BF16)] + [shape_of((block_len, width), BF16)] * 4,
            scratch=[pltpu.VMEM((tokens, width), BF16)],
            name="combine", limit=20,
        )
        return got[0], got[1:]

    def add_all(values, dtype=BF16):
        out = shape_of(values[0].shape, dtype)
        return run(functools.partial(add_body, len(values)), me, values, [out], name="add_all", limit=16)[0]

    def line_up(axis, values, size):
        extra = values[0].shape[0] - size
        small = [shape_of((extra, width), BF16)] if extra else []
        outs = [shape_of((4 * size, width), BF16)] + small
        return run(functools.partial(line_up_body, axis), me, values, outs, name="line_up", limit=60)

    seq_bf16 = pltpu.VMEM((length, LANES), BF16)
    seq_f32 = pltpu.VMEM((length, LANES), F32)
    o_shapes = [shape_of((2, block_len, LANES), BF16)] * 4

    def attend_both(pieces, grads, seg_rows, with_out):
        return run(
            functools.partial(attend_both_body, block_len, chunk, with_out),
            me,
            [*pieces, *grads, seg_rows],
            [shape_of((2, block_len, (4 if with_out else 3) * LANES), BF16)] * 4,
            scratch=([pltpu.VMEM((3, length, LANES), BF16)] if with_out else [])
            + [seq_bf16, pltpu.VMEM((2, LANES, length), BF16), seq_bf16]
            + [seq_f32] * 3,
            name="attend_both", limit=24,
        )

    def project_back(layer, pieces, dm, riders=()):
        got = run(
            functools.partial(project_back_body, block_len, layer),
            me,
            [*pieces, (qkv_weight, layer_spec(qkv_weight, layer)), dm, attn_gain, mlp_gain, *riders],
            [shape_of((tokens, 3 * inner), BF16), wide, shape_of((3, inner), F32)]
            + [shape_of((block_len * (2 if riders else 1), width), BF16)] * 4,
            scratch=[pltpu.VMEM((tokens, width), BF16)],
            name="project_back", limit=24,
        )
        return got[0], got[1], got[2], got[3:]

    def norm_back(pieces, x, dy, riders=()):
        quarter = shape_of((block_len, width), F32)
        low = shape_of((block_len + (16 if riders else 0), width), BF16)
        return run(
            norm_back_body,
            me,
            [add_up(pieces), x, dy, *riders],
            [quarter, low, shape_of((1, width), F32)],
            name="norm_back",
            limit=60,
        )

    def gains(x, da, dm):
        return run(gains_body, me, [x, da, dm], [shape_of((4, width), F32)], name="gains", limit=16)[0]

    half = width // 2
    columns = [[8 * z + 2 * chip + core for z in range(4) for chip in range(4)] for core in range(2)]

    def feed_weights(m, dh, active, r):
        pack = shape_of((2 * half, width), BF16)
        return run(feed_weights_body, me, [m, dh, active, r], [pack] * 2, name="feed_weights", limit=24)

    def head_weights(attn_in, dproj, attended, r):
        pack = shape_of((half, width), BF16)
        return run(head_weights_body, me, [attn_in, dproj, attended, r], [pack] * 2, name="head_weights", limit=20)

    x0_quarter, a0, m0, *pieces = project_first(x0)
    fed0 = feed(0, m0)
    pieces0, (active0, slope0, part0) = over_chips(pieces, fed0)
    got = run(
        functools.partial(attend_body, block_len, chunk),
        me,
        pieces0,
        [shape_of((8, length), F32), shape_of((3, length, LANES), BF16)] + o_shapes,
        scratch=[pltpu.VMEM((LANES, length), BF16), seq_bf16],
        name="attend", limit=20,
    )
    seg_rows, qkv0 = got[:2]
    out0, _ = over_chips(got[2:])
    attended0, u0 = combine(0, out0, part0)
    dy1_quarter, *grads1 = run(
        functools.partial(send_grad_body, block_len),
        me,
        [after(dy1, u0[0]), (out_weight, layer_spec(out_weight, 1))],
        [shape_of((block_len, width), F32)] + o_shapes,
        name="out_back", limit=14,
    )
    u0, grads1 = tie(over_tensor(u0), over_x(grads1))
    u0 = share_tensor(add_up(u0).astype(BF16))
    u0, grads1_other = tie(u0, [swap_core(piece) for piece in grads1])

    x1, x1_quarter, a1, m1, *pieces = project(1, x0, [*u0, out_bias, down_bias])
    fed1 = feed_both(1, m1, dy1)
    pieces1, (active1, r1, dh1, dm1, up_b1) = over_chips(pieces, fed1)
    got = attend_both(pieces1, grads1 + grads1_other, seg_rows, True)
    feed_pack1 = feed_weights(after(m1, got[0]), dh1, active1, r1)
    back1, feed_pack1 = over_chips(got, feed_pack1)
    dproj1, da1, qkv_b1, e1 = project_back(1, back1, dm1)
    back1, (feed_keep, feed_send) = after((back1, feed_pack1), e1[0])
    attended1, u1 = combine(1, back1, None, active1)
    head_keep, head_send = head_weights(a1, dproj1, attended1, r1)
    e1, (u1, head_keep, head_send, feed_came) = tie(over_tensor(e1), (u1, head_keep, head_send, swap_core(feed_send)))
    pack1 = run(
        add_packs_body,
        me,
        [feed_keep, feed_came, head_keep, swap_core(head_send)],
        [shape_of((3 * half, width), BF16)],
        name="add_packs",
        limit=16,
    )[0]
    part1 = lax.psum_scatter(pack1, ("dp", "ctx"), axis_index_groups=columns, tiled=True)
    dx1, low1, bias1 = norm_back(e1, x1_quarter, dy1_quarter)
    gains1 = gains(after(x1, low1), da1, dm1)
    quarters, gains1 = tie(share_tensor(low1), gains1)

    r0, *grads0 = run(
        functools.partial(join_body, block_len),
        me,
        [*quarters, (out_weight, layer_spec(out_weight, 0))],
        [wide] + o_shapes,
        name="join_out_back", limit=14,
    )
    ua_keep, ua_send, ub_keep, ub_send = after(u1, r0)
    ua_came, ub_came = both_ways(ua_send, ub_send, "tensor")
    dh0, dm0, up_b0 = feed_back(0, r0, slope0)
    grads0, (ua_came, ub_came, dh0, dm0, up_b0) = over_chips(grads0, (ua_came, ub_came, dh0, dm0, up_b0))
    back0 = attend_both([qkv0], grads0, seg_rows, False)
    m0_late, u_parts = after((m0, [ua_keep, ua_came, ub_keep, ub_came]), back0[0])
    feed_pack0 = feed_weights(m0_late, dh0, active0, r0)
    u_part = shape_of((block_len // 2, width), BF16)
    ua_keep, ua_send, ub_keep, ub_send = run(
        halve_again_body, me, u_parts, [u_part] * 4, name="halve_again", limit=60
    )
    ub_came, ua_came = both_ways(ub_send, ua_send, "tensor")
    back0, (feed_keep, feed_send, u1) = over_chips(back0, (*feed_pack0, [ua_keep, ua_came, ub_keep, ub_came]))
    dproj0, da0, qkv_b0, e0 = project_back(0, back0, dm0)
    head_keep, head_send = head_weights(a0, dproj0, attended0, r0)
    e0 = after(e0, head_keep)
    way = shape_of((3 * half // 4, width), BF16)
    a_keep, a_send, b_keep, b_send = run(
        halve_body,
        me,
        [feed_keep, swap_core(feed_send), head_keep, swap_core(head_send)],
        [way] * 4,
        scratch=[pltpu.VMEM((2 * half, width), BF16), pltpu.VMEM((half, width), BF16)],
        name="halve",
        limit=60,
    )
    gains0 = gains(after(x0, a_send), da0, dm0)
    a_came, b_came = both_ways(a_send, b_send)
    e0, (gains0, a_came, b_came) = tie(over_tensor(e0), (gains0, a_came, b_came))
    way = shape_of((3 * half // 8, width), BF16)
    a_keep, a_send, b_keep, b_send = run(
        halve_again_body, me, [a_keep, a_came, b_keep, b_came], [way] * 4, name="halve_again", limit=60
    )
    b_came, a_came = both_ways(b_send, a_send)
    part1 = after(part1, a_send)
    pack1 = lax.all_gather(part1, ("dp", "ctx"), axis_index_groups=columns, tiled=True)
    dx0, low0, bias0 = norm_back(after(e0, a_send), x0_quarter, dx1, (gains0, gains1, bias1))
    last = share_tensor(low0)
    (a_came, b_came), last = tie((a_came, b_came), last)
    local = run(
        pack_small_body,
        me,
        [qkv_b0, qkv_b1, up_b0, up_b1],
        [shape_of((16, width), BF16)],
        name="pack_small",
        limit=60,
    )[0]

    few = half // 32
    cut = run(
        merge_body,
        me,
        [a_keep, a_came, b_keep, b_came, *last, local],
        [shape_of((6 * few + 32, width), BF16)] * 4,
        scratch=[pltpu.VMEM((24 * few, width), BF16)],
        name="merge",
        limit=60,
    )
    u1 = run(
        add_halves_body, me, after(u1, cut[0]), [shape_of((block_len, width), BF16)], name="add_halves", limit=60
    )[0]
    cut, u1 = tie(over_x(cut), spread_near(u1, "tensor"))
    pieces = [shape_of((3 * few, width), BF16), shape_of((3 * few + 32, width), BF16)]
    first, second = run(settle_body, me, cut, pieces, name="settle", limit=60)
    first, second = tie(over_x([first] * 4), over_dp([second] * 4))
    second, small = line_up(3, second, 3 * few)
    first = line_up(0, first, 3 * few)[0]
    near = (spread_near(first, "dp"), spread_near(second, "x"))

    u1 = spread_far(u1, "tensor")
    last, u1 = after((last, u1), first)
    input_grad, output = run(
        functools.partial(place_body, block_len),
        me,
        [*last, *u1, x1, out_bias, down_bias],
        [shape_of((tokens, width), F32)] * 2,
        name="place",
        limit=60,
    )
    heavy = [
        shape_of((2, width, hidden), F32),
        shape_of((2, hidden, width), F32),
        shape_of((2, 3, width, inner), F32),
        shape_of((2, inner, width), F32),
    ]
    small_came = swap_core(small)
    pack1_came = swap_core(after(pack1, first))
    quarter = half // 4
    views = [(2, 2, half, width)] * 2 + [(2, 3, 2, half, inner), (2, 2, LANES, width)]
    first_outs = run(
        unpack_whole_body,
        me,
        [
            (pack, pl.BlockSpec((quarter, width), lambda i, *_, part=part: (4 * part + i, 0)))
            for pack in (pack1, pack1_came)
            for part in range(3)
        ],
        [shape_of(view, F32) for view in views],
        name="unpack_whole",
        limit=60,
        out_specs=[
            pl.BlockSpec((1, 2, quarter, width), lambda i, *_: (1, 0, i, 0)),
            pl.BlockSpec((1, 2, quarter, width), lambda i, *_: (1, 0, i, 0)),
            pl.BlockSpec((1, 3, 2, quarter, inner), lambda i, *_: (1, 0, 0, i, 0)),
            pl.BlockSpec((1, 2, LANES, 2 * LANES), lambda i, *_: (1, 0, 0, i)),
        ],
        grid=4,
    )
    first_outs = [v.reshape(like.shape) for v, like in zip(first_outs, heavy)]
    near, (first_outs, small_came, input_grad, output) = tie(near, (first_outs, small_came, input_grad, output))
    far = (spread_far(near[0], "dp"), spread_far(near[1], "x"))
    other = [swap_core(v) for v in near[0] + near[1]]
    row_pair = shape_of((2, width), F32)
    small = run(
        small_out_body,
        me,
        [small, small_came],
        [row_pair] * 6 + [shape_of((2, 3, inner), F32)],
        name="small_out",
        limit=60,
    )
    mine, (small, other) = tie(far[0] + far[1], (small, other))
    far = [swap_core(v) for v in mine[3:5] + mine[8:10]]
    other = other[0:3] + far[0:2] + other[3:6] + far[2:4]
    in_place = pl.BlockSpec(memory_space=pl.ANY)
    held = [pltpu.VMEM(v.shape[1:], F32) for v in heavy] + [pltpu.SemaphoreType.DMA((4,))]
    up_grad, down_grad, qkv_grad, out_grad = run(
        functools.partial(unpack_body, few),
        me,
        mine + other + [(v, in_place) for v in first_outs],
        heavy,
        name="unpack",
        limit=60,
        out_specs=[in_place] * 4,
        scratch=held,
        aliases={21 + index: index for index in range(4)},
    )
    return (
        output.reshape(tok_shape),
        input_grad.reshape(tok_shape),
        small[0],
        small[1],
        small[2],
        small[3],
        qkv_grad,
        small[6],
        out_grad,
        small[4],
        up_grad,
        small[5],
        down_grad,
        small[4],
    )


def solution(mesh):
    in_specs = (
        P("dp", "ctx", None),
        P("dp", "ctx"),
        P(),
        P(),
        P(),
        P(),
        P(None, None, None, "tensor"),
        P(None, None, "tensor"),
        P(None, "tensor", None),
        P(),
        P(None, None, "tensor"),
        P(None, "tensor"),
        P(None, "tensor", None),
        P(),
        P("dp", "ctx", None),
    )
    out_specs = (
        P("dp", "ctx", None),
        P("dp", "ctx", None),
        P(),
        P(),
        P(),
        P(),
        P(None, None, None, "tensor"),
        P(None, None, "tensor"),
        P(None, "tensor", None),
        P(),
        P(None, None, "tensor"),
        P(None, "tensor"),
        P(None, "tensor", None),
        P(),
    )
    return jax.shard_map(
        on_device, mesh=mesh, in_specs=in_specs, out_specs=out_specs, check_vma=False
    )
```

```python
import functools

import jax
import jax.numpy as jnp
from jax import lax
from jax.experimental import pallas as pl
from jax.experimental.pallas import tpu as pltpu
from jax.sharding import PartitionSpec as P

HEAD = 64
ROT = 16
LAYERS = 2
LANES = 128
F32 = jnp.float32
BF16 = jnp.bfloat16


def shape_of(shape, dtype):
    return jax.ShapeDtypeStruct(tuple(shape), dtype)


def whole(array):
    rank = array.ndim
    return pl.BlockSpec(array.shape, lambda i, *_: (0,) * rank, pipeline_mode=pl.Buffered(1))


def layer_spec(array, layer):
    rank = array.ndim
    return pl.BlockSpec(
        (1,) + array.shape[1:], lambda i, *_: (layer,) + (0,) * (rank - 1), pipeline_mode=pl.Buffered(1)
    )


def run(body, me, operands, outs, scratch=(), name=None, limit=32, out_specs=None, aliases=None, grid=1):
    arrays, specs = [], []
    for operand in operands:
        array, spec = operand if isinstance(operand, tuple) else (operand, None)
        arrays.append(array)
        specs.append(whole(array) if spec is None else spec)
    return pl.pallas_call(
        body,
        grid_spec=pltpu.PrefetchScalarGridSpec(
            num_scalar_prefetch=1,
            grid=(grid,),
            in_specs=specs,
            out_specs=[whole(o) for o in outs] if out_specs is None else out_specs,
            scratch_shapes=list(scratch),
        ),
        out_shape=list(outs),
        input_output_aliases=aliases or {},
        compiler_params=pltpu.CompilerParams(vmem_limit_bytes=limit * 1024 * 1024),
        cost_estimate=pl.CostEstimate(flops=1, bytes_accessed=1, transcendentals=0),
        name=name,
    )(me, *arrays)


def matmul(left, right):
    return jnp.dot(left, right, preferred_element_type=F32)


def matmul_nt(left, right):
    return lax.dot_general(left, right, (((1,), (1,)), ((), ())), preferred_element_type=F32)


def matmul_tn(left, right):
    return lax.dot_general(left, right, (((0,), (0,)), ((), ())), preferred_element_type=F32)


def normalize(values):
    average = jnp.mean(values, axis=-1, keepdims=True)
    centred = values - average
    factor = lax.rsqrt(jnp.mean(centred * centred, axis=-1, keepdims=True) + 1e-05)
    return centred * factor, factor


def wrap4(value):
    return lax.rem(value + 4, 4)


def rows(index, size):
    return pl.ds(pl.multiple_of(index * size, size), size)


def rotary_rows(place_row):
    count = place_row.shape[1]
    which = lax.broadcasted_iota(jnp.int32, (8, count), 0)
    frequency = jnp.zeros((8, count), F32)
    for index in range(8):
        frequency = jnp.where(which == index, 10000.0 ** (-2.0 * index / ROT), frequency)
    angles = frequency * place_row
    trig = jnp.concatenate([jnp.cos(angles), jnp.sin(angles)], axis=0)
    row = lax.broadcasted_iota(jnp.int32, (16, LANES), 0)
    lane = lax.broadcasted_iota(jnp.int32, (16, LANES), 1) & (HEAD - 1)
    same = (lane & 7) == (row & 7)
    is_cos = row < 8
    pick_cos = jnp.where(is_cos & same & (lane < 16), 1.0, 0.0)
    pick_low = jnp.where((row >= 8) & same & (lane < 8), 1.0, 0.0)
    pick_high = jnp.where((row >= 8) & same & (lane >= 8) & (lane < 16), 1.0, 0.0)
    picks = jnp.concatenate([pick_cos, pick_low, pick_high], axis=1).astype(F32)
    spread = lax.dot_general(
        trig, picks, (((0,), (0,)), ((), ())), preferred_element_type=F32, precision=lax.Precision.HIGHEST
    )
    lane_row = lax.broadcasted_iota(jnp.int32, (1, LANES), 1) & (HEAD - 1)
    cos_table = spread[:, :LANES] + jnp.where(lane_row >= ROT, 1.0, 0.0)
    return cos_table, spread[:, LANES : 2 * LANES], spread[:, 2 * LANES :]


def rotate(values, tables, back=False):
    cos_table, low_sin, high_sin = tables
    below = pltpu.roll(values, LANES - ROT // 2, 1) * low_sin
    above = pltpu.roll(values, ROT // 2, 1) * high_sin
    turned = below - above if back else above - below
    return values * cos_table + turned


def project_rows(layer, tok_shape, me_ref, seg_ref, weight, bias, a_ref, p_refs, proj_ref, with_seg):
    seq_count, block_len, width = tok_shape
    chip, core = me_ref[0], me_ref[1]
    base = (chip * 2 + core) * block_len
    for j in range(3):
        proj_ref[:, j * 2 * LANES : (j + 1) * 2 * LANES] = matmul(a_ref[...], weight(j)) + bias[j, layer : layer + 1, :]
    for k in range(4):
        seq = wrap4(chip + k)
        place = rows(seq, block_len)
        seg_row = seg_ref[pl.ds(seq, 1), :]
        spots = lax.broadcasted_iota(jnp.int32, (1, block_len), 1) + base
        tables = rotary_rows((spots - seg_row).astype(F32))
        for j in range(3):
            for pair in range(2):
                at = (2 * j + pair) * LANES
                part = proj_ref[place, at : at + LANES]
                if j < 2:
                    part = rotate(part, tables)
                p_refs[k][pair, 0:block_len, j * LANES : (j + 1) * LANES] = part.astype(BF16)
        if with_seg:
            coded = seg_row.astype(F32)
            high = jnp.floor(coded * 0.125)
            packed = jnp.concatenate([high, coded - 8.0 * high, jnp.zeros_like(high)], axis=1)
            packed = jnp.broadcast_to(packed, (16, 3 * LANES)).astype(BF16)
            for pair in range(2):
                p_refs[k][pair, block_len : block_len + 16, :] = packed


def project_first_body(tok_shape, me_ref, *refs):
    seq_count, block_len, width = tok_shape
    in_refs, refs = refs[:8], refs[8:]
    xq_ref, a_ref, m_ref, *p_refs = refs[:7]
    proj_ref, *held, sems = refs[7:]
    x_ref, seg_ref, ag_ref, as_ref, mg_ref, ms_ref, w_ref, b_ref = held
    copies = []
    for index in (1, 2, 3, 4, 5):
        copies.append(pltpu.make_async_copy(in_refs[index], held[index], sems.at[len(copies)]))
    copies.append(pltpu.make_async_copy(in_refs[7], b_ref, sems.at[len(copies)]))
    small_count = len(copies)
    for seq in range(seq_count):
        place = pl.ds(seq * block_len, block_len)
        copies.append(pltpu.make_async_copy(in_refs[0].at[place], x_ref.at[place], sems.at[len(copies)]))
    copies.append(pltpu.make_async_copy(in_refs[6].at[0], w_ref, sems.at[len(copies)]))
    for copy in copies:
        copy.start()
    for copy in copies[:small_count]:
        copy.wait()
    for seq in range(seq_count):
        copies[small_count + seq].wait()
        place = slice(seq * block_len, (seq + 1) * block_len)
        normed, _ = normalize(x_ref[place, :])
        a_ref[place, :] = (normed * ag_ref[0:1, :] + as_ref[0:1, :]).astype(BF16)
        m_ref[place, :] = (normed * mg_ref[0:1, :] + ms_ref[0:1, :]).astype(BF16)
    xq_ref[...] = x_ref[rows(me_ref[2], block_len), :]
    copies[-1].wait()
    project_rows(0, tok_shape, me_ref, seg_ref, lambda j: w_ref[j], b_ref, a_ref, p_refs, proj_ref, True)


def project_body(layer, tok_shape, me_ref, *refs):
    seq_count, block_len, width = tok_shape
    x_ref, seg_ref, *refs = refs
    u_refs, refs = refs[:4], refs[4:]
    ob_ref, db_ref, ag_ref, as_ref, mg_ref, ms_ref, w_ref, b_ref, x_out, xq_ref, a_ref, m_ref, *p_refs, proj_ref = refs
    tensor = me_ref[2]
    shift = ob_ref[layer - 1 : layer, :] + db_ref[layer - 1 : layer, :]
    for k in range(4):
        place = rows(wrap4(tensor - k), block_len)
        value = x_ref[place, :] + u_refs[k][...].astype(F32) + shift
        x_out[place, :] = value
        if k == 0:
            xq_ref[...] = value
        normed, _ = normalize(value)
        a_ref[place, :] = (normed * ag_ref[layer : layer + 1, :] + as_ref[layer : layer + 1, :]).astype(BF16)
        m_ref[place, :] = (normed * mg_ref[layer : layer + 1, :] + ms_ref[layer : layer + 1, :]).astype(BF16)
    project_rows(layer, tok_shape, me_ref, seg_ref, lambda j: w_ref[0, j], b_ref, a_ref, p_refs, proj_ref, False)


def gather_pieces(me_ref, refs, targets, block_len, seg_target=None):
    chip, core = me_ref[0], me_ref[1]
    for k in range(4):
        owner = wrap4(chip - k)
        for side, ref in ((core, refs[k]), (1 - core, refs[4 + k])):
            place = rows(owner * 2 + side, block_len)
            for index, target in enumerate(targets):
                target[place, :] = ref[core, 0:block_len, index * LANES : (index + 1) * LANES]
            if seg_target is not None:
                row = ref[core, block_len : block_len + 16, :].astype(F32)[0:1, :]
                starts = row[:, 0:LANES] * 8.0 + row[:, LANES : 2 * LANES]
                seg_target[:, place] = jnp.broadcast_to(starts, (8, block_len))


def head_stack(values):
    lane = lax.broadcasted_iota(jnp.int32, values.shape, 1)
    zero = jnp.zeros_like(values)
    return jnp.concatenate(
        [jnp.where(lane < HEAD, values, zero), jnp.where(lane >= HEAD, values, zero)], axis=0
    )


def own_halves(product, width):
    return jnp.concatenate([product[0:HEAD, 0:width], product[HEAD:, width : 2 * width]], axis=0)


def chances_t(q_ref, k_ref, seg_ref, step, chunk):
    start, keys = step * chunk, (step + 1) * chunk
    stacked = head_stack(q_ref[start:keys, :]) * jnp.asarray(HEAD ** (-0.5), BF16)
    scores = matmul_nt(k_ref[0:keys, :], stacked)
    key_place = lax.broadcasted_iota(jnp.int32, (keys, 2 * chunk), 0).astype(F32)
    query_place = (lax.broadcasted_iota(jnp.int32, (1, 2 * chunk), 1) & (chunk - 1)).astype(F32) + start
    seg_row = seg_ref[0:1, start:keys]
    seg_row = jnp.concatenate([seg_row, seg_row], axis=1)
    allowed = (key_place >= seg_row) & (key_place <= query_place)
    scores = jnp.where(allowed, scores, -1e30)
    raised = jnp.exp(scores - jnp.max(scores, axis=0, keepdims=True))
    total = jnp.sum(raised, axis=0, keepdims=True)
    return raised * (1.0 / total), stacked


def attend_body(block_len, chunk, me_ref, *refs):
    piece_refs, refs = refs[:8], refs[8:]
    seg_out, qkv_ref, *refs = refs
    o_refs, refs = refs[:4], refs[4:]
    vt_ref, o_ref = refs
    q_ref, k_ref, v_ref = qkv_ref.at[0], qkv_ref.at[1], qkv_ref.at[2]
    gather_pieces(me_ref, piece_refs, (q_ref, k_ref, v_ref), block_len, seg_out)
    vt_ref[...] = v_ref[...].T
    length = q_ref.shape[0]
    for step in range(length // chunk):
        keys = (step + 1) * chunk
        chances, _ = chances_t(q_ref, k_ref, seg_out, step, chunk)
        mixed = matmul(vt_ref[:, 0:keys], chances.astype(BF16))
        o_ref[step * chunk : keys, :] = own_halves(mixed, chunk).T.astype(BF16)
    send_blocks(me_ref, o_ref, o_refs, block_len)


def send_blocks(me_ref, source, targets, block_len):
    chip = me_ref[0]
    for k in range(4):
        dest = wrap4(chip + k)
        for side in range(2):
            targets[k][side] = source[rows(dest * 2 + side, block_len), :]


def attend_both_body(block_len, chunk, with_out, me_ref, *refs):
    if with_out:
        piece_refs, refs = refs[:8], refs[8:]
    else:
        qkv_ref, *refs = refs
    grad_refs, refs = refs[:8], refs[8:]
    seg_ref, *refs = refs
    d_refs, refs = refs[:4], refs[4:]
    if with_out:
        qkv_ref, *refs = refs
    q_ref, k_ref, v_ref = qkv_ref.at[0], qkv_ref.at[1], qkv_ref.at[2]
    g_ref, t_ref, o_ref, dq_ref, dk_ref, dv_ref = refs
    if with_out:
        gather_pieces(me_ref, piece_refs, (q_ref, k_ref, v_ref), block_len)
    gather_pieces(me_ref, grad_refs, (g_ref,), block_len)
    length = q_ref.shape[0]
    t_ref[0] = k_ref[...].T
    if with_out:
        t_ref[1] = v_ref[...].T
    dk_ref[...] = jnp.zeros_like(dk_ref)
    dv_ref[...] = jnp.zeros_like(dv_ref)
    for step in range(length // chunk):
        start, keys = step * chunk, (step + 1) * chunk
        chances, stacked = chances_t(q_ref, k_ref, seg_ref, step, chunk)
        low = chances.astype(BF16)
        if with_out:
            mixed = matmul(t_ref[1, :, 0:keys], low)
            o_ref[start:keys, :] = own_halves(mixed, chunk).T.astype(BF16)
        grads = head_stack(g_ref[start:keys, :])
        chance_grad = matmul_nt(v_ref[0:keys, :], grads)
        delta = jnp.sum(chances * chance_grad, axis=0, keepdims=True)
        score_grad = (chances * (chance_grad - delta)).astype(BF16)
        dv_ref[0:keys, :] += matmul(low, grads)
        dk_ref[0:keys, :] += matmul(score_grad, stacked)
        query = matmul(t_ref[0, :, 0:keys], score_grad)
        dq_ref[start:keys, :] = own_halves(query, chunk).T * HEAD ** (-0.5)
    chip = me_ref[0]
    for k in range(4):
        dest = wrap4(chip + k)
        for side in range(2):
            place = rows(dest * 2 + side, block_len)
            spots = (lax.broadcasted_iota(jnp.int32, (1, block_len), 1) + (dest * 2 + side) * block_len).astype(F32)
            tables = rotary_rows(spots - seg_ref[0:1, place])
            d_refs[k][side, :, 0:LANES] = rotate(dq_ref[place, :], tables, True).astype(BF16)
            d_refs[k][side, :, LANES : 2 * LANES] = rotate(dk_ref[place, :], tables, True).astype(BF16)
            d_refs[k][side, :, 2 * LANES : 3 * LANES] = dv_ref[place, :].astype(BF16)
            if with_out:
                d_refs[k][side, :, 3 * LANES :] = o_ref[place, :]


def land_heads(me_ref, refs, target, block_len, groups, first=0):
    chip, core = me_ref[0], me_ref[1]
    for k in range(4):
        place = rows(wrap4(chip - k), block_len)
        mine, other = refs[k][core], refs[4 + k][core]
        is_low = core == 0
        for group in range(groups):
            span = slice((first + group) * LANES, (first + group + 1) * LANES)
            at = group * 2 * LANES
            target[place, at : at + LANES] = jnp.where(is_low, mine[:, span], other[:, span])
            target[place, at + LANES : at + 2 * LANES] = jnp.where(is_low, other[:, span], mine[:, span])


def combine_body(block_len, fused, me_ref, *refs):
    piece_refs, refs = refs[:8], refs[8:]
    w_ref, *refs = refs
    if fused:
        g_ref, down_ref, *refs = refs
    else:
        part_ref, *refs = refs
    o_ref, *refs = refs
    q_refs, scr = refs[:-1], refs[-1]
    tensor = me_ref[2]
    land_heads(me_ref, piece_refs, o_ref, block_len, 1, 3 if fused else 0)
    part = matmul(g_ref[...], down_ref[0]) if fused else part_ref[...]
    scr[...] = (matmul(o_ref[...], w_ref[0]) + part).astype(BF16)
    if fused:
        near, far = near_far(tensor)
        size = block_len // 2
        orders = ((tensor, far), (near, 3 - near), (tensor, near), (far, far ^ 1))
        for way, (ref, order) in enumerate(zip(q_refs, orders)):
            for index, quarter in enumerate(order):
                at = pl.multiple_of(quarter * block_len + (way >> 1) * size, size)
                ref[index * size : (index + 1) * size, :] = scr[pl.ds(at, size), :]
        return
    for k in range(4):
        q_refs[k][...] = scr[rows(wrap4(tensor + k), block_len), :]


def send_grad_body(block_len, me_ref, x_ref, w_ref, *refs):
    chip, tensor = me_ref[0], me_ref[2]
    quarter_ref, *refs = refs
    quarter_ref[...] = x_ref[rows(tensor, block_len), :]
    for k in range(4):
        value = x_ref[rows(wrap4(chip + k), block_len), :].astype(BF16)
        grad = matmul_nt(value, w_ref[0]).astype(BF16)
        for pair in range(2):
            refs[k][pair] = grad[:, pair * LANES : (pair + 1) * LANES]


def join_body(block_len, me_ref, *refs):
    q_refs, refs = refs[:4], refs[4:]
    w_ref, r_ref, *g_refs = refs
    chip, tensor = me_ref[0], me_ref[2]
    for k in range(4):
        r_ref[rows(wrap4(tensor - k), block_len), :] = q_refs[k][...]
    for k in range(4):
        value = r_ref[rows(wrap4(chip + k), block_len), :]
        grad = matmul_nt(value, w_ref[0]).astype(BF16)
        for pair in range(2):
            g_refs[k][pair] = grad[:, pair * LANES : (pair + 1) * LANES]


def project_back_body(block_len, layer, me_ref, *refs):
    piece_refs, refs = refs[:8], refs[8:]
    w_ref, dm_ref, ag_ref, mg_ref, *refs = refs
    riders, refs = refs[:-8], refs[-8:]
    dp_ref, da_ref, bias_ref, *q_refs, scr = refs
    tensor = me_ref[2]
    land_heads(me_ref, piece_refs, dp_ref, block_len, 3)
    for j in range(3):
        span = slice(j * 2 * LANES, (j + 1) * 2 * LANES)
        bias_ref[j : j + 1, :] = jnp.sum(dp_ref[:, span].astype(F32), axis=0, keepdims=True)
    total = None
    for j in range(3):
        term = matmul_nt(dp_ref[:, j * 2 * LANES : (j + 1) * 2 * LANES], w_ref[0, j])
        total = term if total is None else total + term
    da_ref[...] = total.astype(BF16)
    scr[...] = (total * ag_ref[layer : layer + 1, :] + dm_ref[...] * mg_ref[layer : layer + 1, :]).astype(BF16)
    for k in range(4):
        q_refs[k][0:block_len, :] = scr[rows(wrap4(tensor + k), block_len), :]
        if riders:
            q_refs[k][block_len:, :] = riders[k][...]


def norm_back_body(me_ref, *refs):
    e_ref, x_ref, dy_ref, *gain_refs, dx_ref, low_ref, bias_ref = refs
    upstream = dy_ref[...]
    size = upstream.shape[0]
    total = e_ref[0:size, :]
    normed, factor = normalize(x_ref[...])
    inner = jnp.mean(total * normed, axis=-1, keepdims=True)
    result = upstream + factor * (total - jnp.mean(total, axis=-1, keepdims=True) - normed * inner)
    dx_ref[...] = result
    low_ref[0:size, :] = result.astype(BF16)
    bias = jnp.sum(upstream, axis=0, keepdims=True)
    bias_ref[...] = bias
    if gain_refs:
        mine, other, other_bias = gain_refs
        blank = jnp.zeros((6, bias.shape[1]), F32)
        rows_here = jnp.concatenate([mine[...], bias, other[...], other_bias[...], blank], axis=0)
        low_ref[size:, :] = rows_here.astype(BF16)


def gains_body(me_ref, x_ref, da_ref, dm_ref, out_ref):
    normed, _ = normalize(x_ref[...])
    da = da_ref[...].astype(F32)
    dm = dm_ref[...]
    out_ref[0:1, :] = jnp.sum(da * normed, axis=0, keepdims=True)
    out_ref[1:2, :] = jnp.sum(da, axis=0, keepdims=True)
    out_ref[2:3, :] = jnp.sum(dm * normed, axis=0, keepdims=True)
    out_ref[3:4, :] = jnp.sum(dm, axis=0, keepdims=True)


def gelu_parts(hidden):
    cdf = 0.5 * (1.0 + lax.erf(hidden * (0.5**0.5)))
    density = jnp.exp(-0.5 * hidden * hidden) * 0.3989422804014327
    return cdf, density


def feed_body(layer, me_ref, m_ref, up_ref, ub_ref, down_ref, g_ref, slope_ref, part_ref):
    size = 2 * LANES
    for step in range(up_ref.shape[2] // size):
        span = slice(step * size, (step + 1) * size)
        hidden = matmul(m_ref[...], up_ref[0, :, span]) + ub_ref[layer : layer + 1, span]
        cdf, density = gelu_parts(hidden)
        g_ref[:, span] = (hidden * cdf).astype(BF16)
        slope_ref[:, span] = cdf + hidden * density
    part_ref[...] = matmul(g_ref[...], down_ref[0])


def feed_back_body(me_ref, r_ref, slope_ref, up_ref, down_ref, dh_ref, dm_ref, bias_ref):
    size = 2 * LANES
    for step in range(down_ref.shape[1] // size):
        span = slice(step * size, (step + 1) * size)
        grad = matmul_nt(r_ref[...], down_ref[0, span, :]) * slope_ref[:, span]
        bias_ref[:, span] = jnp.sum(grad, axis=0, keepdims=True)
        dh_ref[:, span] = grad.astype(BF16)
    dm_ref[...] = matmul_nt(dh_ref[...], up_ref[0])


def feed_both_body(layer, me_ref, m_ref, dy_ref, up_ref, ub_ref, down_ref, g_ref, r_ref, dh_ref, dm_ref, bias_ref):
    size = 2 * LANES
    r_ref[...] = dy_ref[...].astype(BF16)
    for step in range(up_ref.shape[2] // size):
        span = slice(step * size, (step + 1) * size)
        hidden = matmul(m_ref[...], up_ref[0, :, span]) + ub_ref[layer : layer + 1, span]
        cdf, density = gelu_parts(hidden)
        g_ref[:, span] = (hidden * cdf).astype(BF16)
        grad = matmul_nt(r_ref[...], down_ref[0, span, :]) * (cdf + hidden * density)
        bias_ref[:, span] = jnp.sum(grad, axis=0, keepdims=True)
        dh_ref[:, span] = grad.astype(BF16)
    dm_ref[...] = matmul_nt(dh_ref[...], up_ref[0])


def feed_weights_body(me_ref, m_ref, dh_ref, g_ref, r_ref, keep_ref, send_ref):
    core = me_ref[1]
    half = m_ref.shape[1] // 2
    for side, out in ((core, keep_ref), (1 - core, send_ref)):
        out[0:half, :] = matmul_tn(m_ref[:, rows(side, half)], dh_ref[...]).astype(BF16)
        out[half:, :] = matmul_tn(g_ref[:, rows(side, half)], r_ref[...]).astype(BF16)


def head_weights_body(me_ref, a_ref, dp_ref, o_ref, r_ref, keep_ref, send_ref):
    core = me_ref[1]
    half = a_ref.shape[1] // 2
    wide = dp_ref.shape[1]
    for side, out in ((core, keep_ref), (1 - core, send_ref)):
        out[:, 0:wide] = matmul_tn(a_ref[:, rows(side, half)], dp_ref[...]).astype(BF16)
        grad = matmul_tn(o_ref[:, rows(side, LANES)], r_ref[...]).astype(BF16)
        for part in range(4):
            out[part * LANES : (part + 1) * LANES, wide:] = grad[:, part * 2 * LANES : (part + 1) * 2 * LANES]


def feed_weights_whole_body(me_ref, m_ref, dh_ref, g_ref, r_ref, pack_ref):
    high = m_ref.shape[1]
    pack_ref[0:high, :] = matmul_tn(m_ref[...], dh_ref[...]).astype(BF16)
    pack_ref[high:, :] = matmul_tn(g_ref[...], r_ref[...]).astype(BF16)


def head_weights_whole_body(me_ref, a_ref, dp_ref, o_ref, r_ref, before_ref, pack_ref):
    wide = dp_ref.shape[1]
    pack_ref[:, 0:wide] = matmul_tn(a_ref[...], dp_ref[...]).astype(BF16)
    grad = matmul_tn(o_ref[...], r_ref[...]).astype(BF16)
    high, size = grad.shape[0], 2 * LANES
    for part in range(4):
        pack_ref[part * high : (part + 1) * high, wide:] = grad[:, part * size : (part + 1) * size]


def near_far(place):
    return place ^ 1, 3 - place


def halve_body(me_ref, feed_keep, feed_came, head_keep, head_came, *refs):
    outs, feed_scr, head_scr = refs[:4], refs[4], refs[5]
    feed_scr[...] = (feed_keep[...].astype(F32) + feed_came[...].astype(F32)).astype(BF16)
    head_scr[...] = (head_keep[...].astype(F32) + head_came[...].astype(F32)).astype(BF16)
    place = me_ref[3]
    near, far = near_far(place)
    half = head_scr.shape[0]
    size = half // 8
    orders = ((place, far), (near, 3 - near), (4 + place, 4 + near), (4 + far, 4 + (far ^ 1)))
    for ref, order in zip(outs, orders):
        for index, block in enumerate(order):
            at = 3 * size * index
            ref[at : at + size, :] = feed_scr[rows(block, size), :]
            ref[at + size : at + 2 * size, :] = feed_scr[pl.ds(pl.multiple_of(half + block * size, size), size), :]
            ref[at + 2 * size : at + 3 * size, :] = head_scr[rows(block, size), :]


def halve_again_body(me_ref, a_keep, a_came, b_keep, b_came, *outs):
    size = outs[0].shape[0]
    for keep, came, mine, send in ((a_keep, a_came, outs[0], outs[1]), (b_keep, b_came, outs[2], outs[3])):
        total = (keep[...].astype(F32) + came[...].astype(F32)).astype(BF16)
        mine[...] = total[0:size, :]
        send[...] = total[size:, :]


def line_up_body(axis, me_ref, *refs):
    size = refs[4].shape[0] // 4
    for k in range(4):
        refs[4][rows(wrap4(me_ref[axis] - k), size), :] = refs[k][0:size, :]
    if len(refs) > 5:
        even = refs[0][size:, :].astype(F32) + refs[2][size:, :].astype(F32)
        odd = refs[1][size:, :].astype(F32) + refs[3][size:, :].astype(F32)
        refs[5][...] = (even + odd).astype(BF16)


def merge_body(me_ref, a_keep, a_came, b_keep, b_came, *refs):
    last_refs, local_ref, out_refs, scr = refs[:4], refs[4], refs[5:9], refs[9]
    count = local_ref.shape[0]
    shared = [ref[ref.shape[0] - count :, :].astype(F32) for ref in last_refs]
    shared = ((shared[0] + shared[2]) + (shared[1] + shared[3])).astype(BF16)
    high = a_keep.shape[0]
    scr[0:high, :] = (a_keep[...].astype(F32) + a_came[...].astype(F32)).astype(BF16)
    scr[high:, :] = (b_keep[...].astype(F32) + b_came[...].astype(F32)).astype(BF16)
    few = high // 6
    for k in range(4):
        part = wrap4(me_ref[0] + k)
        for weight in range(3):
            at = pl.multiple_of((part >> 1) * high + weight * 2 * few + (part & 1) * few, few)
            out_refs[k][weight * few : (weight + 1) * few, :] = scr[pl.ds(at, few), :]
        out_refs[k][3 * few : 3 * few + count, :] = shared
        out_refs[k][3 * few + count :, :] = local_ref[...]


def settle_body(me_ref, *refs):
    in_refs, (first_ref, second_ref) = refs[:4], refs[4:]
    even = in_refs[0][...].astype(F32) + in_refs[2][...].astype(F32)
    odd = in_refs[1][...].astype(F32) + in_refs[3][...].astype(F32)
    total = (even + odd).astype(BF16)
    few = first_ref.shape[0] // 3
    for weight in range(3):
        for index, ref in enumerate((first_ref, second_ref)):
            at = (2 * weight + index) * few
            ref[weight * few : (weight + 1) * few, :] = total[at : at + few, :]
    second_ref[3 * few :, :] = total[6 * few :, :]


def flush(held, outs, layer, sems):
    copies = [pltpu.make_async_copy(a, b.at[layer], sems.at[i]) for i, (a, b) in enumerate(zip(held, outs))]
    return copies


def unpack_body(few, me_ref, *refs):
    outs, held, sems = refs[24:28], refs[28:32], refs[32]
    up_ref, down_ref, qkv_ref, out_ref = held
    copies = flush(held, outs, 0, sems)
    chip, core, place_z = me_ref[0], me_ref[1], me_ref[3]
    size = 2 * LANES
    half = up_ref.shape[0] // 2
    for weight in range(3):
        for side, group in ((core, refs[:10]), (1 - core, refs[10:20])):
            for along, me in ((0, place_z), (1, chip)):
                pieces = group[5 * along : 5 * along + 5]
                spans = [(pieces[0], me, 0), (pieces[1], me ^ 1, 0), (pieces[2], 3 - me, 0)]
                spans += [(pieces[3], me ^ 2, 0), (pieces[4], me ^ 2, 2)]
                for ref, owner, first in spans:
                    for index in range(ref.shape[0] // (3 * few)):
                        z, x = (owner, first + index) if along == 0 else (first + index, owner)
                        start = (3 * index + weight) * few
                        value = ref[start : start + few, :].astype(F32)
                        row = (z + 4 * (x >> 1)) * (4 * few) + (x & 1) * (2 * few) + along * few
                        place = pl.ds(pl.multiple_of(row + side * half, few), few)
                        if weight < 2:
                            held[weight][place, :] = value
                        else:
                            for j in range(3):
                                qkv_ref[j, place, :] = value[:, j * size : (j + 1) * size]
                            inner = pl.ds(pl.multiple_of((row & (LANES - 1)) + side * LANES, few), few)
                            lanes = pl.ds(pl.multiple_of((row >> 7) * size, size), size)
                            out_ref[inner, lanes] = value[:, 3 * size :]
        for copy in copies[weight : weight + 1] if weight < 2 else copies[2:]:
            copy.start()
    for copy in copies:
        copy.wait()


def add_packs_body(me_ref, feed_keep, feed_came, head_keep, head_came, out_ref):
    high = feed_keep.shape[0]
    out_ref[0:high, :] = (feed_keep[...].astype(F32) + feed_came[...].astype(F32)).astype(BF16)
    out_ref[high:, :] = (head_keep[...].astype(F32) + head_came[...].astype(F32)).astype(BF16)


def unpack_whole_body(me_ref, up_mine, down_mine, head_mine, up_other, down_other, head_other, *outs):
    up_ref, down_ref, qkv_ref, out_ref = outs
    size = 2 * LANES
    for core in range(2):
        mine = me_ref[1] == core
        for ref, first, second in ((up_ref, up_mine, up_other), (down_ref, down_mine, down_other)):
            ref[0, core] = jnp.where(mine, first[...], second[...]).astype(F32)
        head = jnp.where(mine, head_mine[...], head_other[...]).astype(F32)
        for j in range(3):
            qkv_ref[0, j, core] = head[:, j * size : (j + 1) * size]
        out_ref[0, core] = head[:, 3 * size :]


def pack_small_body(me_ref, *refs):
    ins, local_ref = refs[:4], refs[4]
    width = local_ref.shape[1]
    local = [ins[2][...], ins[3][...]]
    for ref in ins[0:2]:
        values = ref[...]
        flat = [values[j : j + 1, :] for j in range(3)]
        local.append(jnp.concatenate(flat + [jnp.zeros((1, width - 3 * values.shape[1]), F32)], axis=1))
    local_ref[...] = jnp.concatenate(local + [jnp.zeros((12, width), F32)], axis=0).astype(BF16)


def add_halves_body(me_ref, a_keep, a_came, b_keep, b_came, out_ref):
    size = a_keep.shape[0]
    out_ref[0:size, :] = (a_keep[...].astype(F32) + a_came[...].astype(F32)).astype(BF16)
    out_ref[size:, :] = (b_keep[...].astype(F32) + b_came[...].astype(F32)).astype(BF16)


def add_body(count, me_ref, *refs):
    total = refs[0][...].astype(F32)
    for ref in refs[1:count]:
        total = total + ref[...].astype(F32)
    refs[count][...] = total.astype(refs[count].dtype)


def small_out_body(me_ref, mine_ref, came_ref, *outs):
    total = mine_ref[...].astype(F32) + came_ref[...].astype(F32)
    shared, local = total[0:16, :], total[16:32, :]
    for index in range(5):
        outs[index][0:1, :] = shared[index : index + 1, :]
        outs[index][1:2, :] = shared[index + 5 : index + 6, :]
    outs[5][...] = local[0:2, :]
    size = outs[6].shape[2]
    for layer in range(2):
        for j in range(3):
            outs[6][layer, j : j + 1, :] = local[2 + layer : 3 + layer, j * size : (j + 1) * size]


def place_body(block_len, me_ref, *refs):
    q_refs, u_refs, (x_ref, ob_ref, db_ref, grad_ref, out_ref) = refs[:4], refs[4:9], refs[9:]
    shift = ob_ref[1:2, :] + db_ref[1:2, :]
    me = me_ref[2]
    for k in range(4):
        grad_ref[rows(wrap4(me - k), block_len), :] = q_refs[k][0:block_len, :].astype(F32)
    half = block_len // 2
    spots = ((me, 0), (me ^ 1, 0), (3 - me, 0), (me ^ 2, 0), (me ^ 2, half))
    for ref, (quarter, offset) in zip(u_refs, spots):
        count = ref.shape[0]
        place = pl.ds(pl.multiple_of(quarter * block_len + offset, half), count)
        out_ref[place, :] = x_ref[place, :] + ref[...].astype(F32) + shift


def chip_turn(shift):
    return [(2 * x + c, 2 * ((x + shift) % 4) + c) for x in range(4) for c in range(2)]


CORE_SWAP = [(i, i ^ 1) for i in range(8)]


def over_chips(pieces, beside=()):
    mine, beside = lax.optimization_barrier((over_x(pieces), beside))
    return mine + [swap_core(piece) for piece in mine], beside


def ring_turn(shift):
    return [(i, (i + shift) % 4) for i in range(4)]


def over_tensor(pieces):
    return [pieces[0]] + [lax.ppermute(pieces[k], "tensor", ring_turn(k)) for k in range(1, 4)]


def share_tensor(piece):
    return over_tensor([piece] * 4)


def over_dp(pieces):
    return [pieces[0]] + [lax.ppermute(pieces[k], "dp", ring_turn(k)) for k in range(1, 4)]


def over_x(pieces):
    return [pieces[0]] + [lax.ppermute(pieces[k], "ctx", chip_turn(k)) for k in range(1, 4)]


def swap_core(piece):
    return lax.ppermute(piece, "ctx", CORE_SWAP)


NEXT_PAIR = [(0, 1), (1, 0), (2, 3), (3, 2)]
WRAP_PAIR = [(0, 3), (3, 0), (1, 2), (2, 1)]


def both_ways(to_next, to_wrap, axis="dp"):
    return lax.ppermute(to_next, axis, NEXT_PAIR), lax.ppermute(to_wrap, axis, WRAP_PAIR)


def chips_of(pairs):
    return [(2 * a + c, 2 * b + c) for a, b in pairs for c in range(2)]


def along(axis):
    return ("ctx", chips_of) if axis == "x" else (axis, lambda pairs: pairs)


def spread_near(piece, axis):
    name, move = along(axis)
    return [piece] + [lax.ppermute(piece, name, move(pairs)) for pairs in (NEXT_PAIR, WRAP_PAIR)]


def spread_far(pieces, axis):
    name, move = along(axis)
    half = pieces[0].shape[0] // 2
    return pieces + [
        lax.ppermute(pieces[1][:half], name, move(WRAP_PAIR)),
        lax.ppermute(pieces[2][half:], name, move(NEXT_PAIR)),
    ]


def tie(first, second):
    return lax.optimization_barrier((first, second))


def after(values, token):
    return lax.optimization_barrier((values, token))[0]


def add_up(pieces):
    total = pieces[0].astype(F32)
    for piece in pieces[1:]:
        total = total + piece.astype(F32)
    return total


def on_device(
    inputs,
    segments,
    attn_gain,
    attn_shift,
    mlp_gain,
    mlp_shift,
    qkv_weight,
    qkv_bias,
    out_weight,
    out_bias,
    up_weight,
    up_bias,
    down_weight,
    down_bias,
    cotangent,
):
    seq_count, block_len, width = inputs.shape
    tokens = seq_count * block_len
    inner = qkv_weight.shape[3]
    hidden = up_weight.shape[2]
    length = block_len * 8
    chunk = 256
    place = lax.axis_index("ctx")
    me = jnp.stack([place // 2, place % 2, lax.axis_index("tensor"), lax.axis_index("dp")]).astype(jnp.int32)
    x0 = inputs.reshape(tokens, width)
    dy1 = cotangent.reshape(tokens, width)
    tok_shape = inputs.shape
    wide = shape_of((tokens, width), BF16)
    norms = (attn_gain, attn_shift, mlp_gain, mlp_shift)
    biases = qkv_bias.transpose(1, 0, 2)

    def project_first(x):
        sources = [x, segments, *norms, qkv_weight, biases]
        held = [v.shape for v in sources[:6]] + [qkv_weight.shape[1:], biases.shape]
        piece = shape_of((2, block_len + 16, 3 * LANES), BF16)
        return run(
            functools.partial(project_first_body, tok_shape),
            me,
            [(v, pl.BlockSpec(memory_space=pltpu.HBM)) for v in sources],
            [shape_of((block_len, width), F32), wide, wide] + [piece] * 4,
            scratch=[pltpu.VMEM((tokens, 3 * inner), F32)]
            + [pltpu.VMEM(size, v.dtype) for size, v in zip(held, sources)]
            + [pltpu.SemaphoreType.DMA((11,))],
            name="norm_project",
            limit=62,
        )

    def project(layer, x, extra):
        piece = shape_of((2, block_len, 3 * LANES), BF16)
        return run(
            functools.partial(project_body, layer, tok_shape),
            me,
            [x, segments, *extra, *norms]
            + [(qkv_weight, layer_spec(qkv_weight, layer)), biases],
            [shape_of((tokens, width), F32), shape_of((block_len, width), F32), wide, wide] + [piece] * 4,
            scratch=[pltpu.VMEM((tokens, 3 * inner), F32)],
            name="norm_project",
            limit=24,
        )

    def feed(layer, m):
        return run(
            functools.partial(feed_body, layer),
            me,
            [m, (up_weight, layer_spec(up_weight, layer)), up_bias, (down_weight, layer_spec(down_weight, layer))],
            [shape_of((tokens, hidden), BF16), shape_of((tokens, hidden), F32), shape_of((tokens, width), F32)],
            name="feed", limit=24,
        )

    def feed_back(layer, r, slope):
        return run(
            feed_back_body,
            me,
            [r, slope, (up_weight, layer_spec(up_weight, layer)), (down_weight, layer_spec(down_weight, layer))],
            [shape_of((tokens, hidden), BF16), shape_of((tokens, width), F32), shape_of((1, hidden), F32)],
            name="feed_back", limit=24,
        )

    def feed_both(layer, m, dy):
        return run(
            functools.partial(feed_both_body, layer),
            me,
            [m, dy, (up_weight, layer_spec(up_weight, layer)), up_bias, (down_weight, layer_spec(down_weight, layer))],
            [shape_of((tokens, hidden), BF16), wide, shape_of((tokens, hidden), BF16)]
            + [shape_of((tokens, width), F32), shape_of((1, hidden), F32)],
            name="feed_both", limit=24,
        )

    def combine(layer, pieces, part, active=None):
        fused = part is None
        got = run(
            functools.partial(combine_body, block_len, fused),
            me,
            [*pieces, (out_weight, layer_spec(out_weight, layer))]
            + ([active, (down_weight, layer_spec(down_weight, layer))] if fused else [part]),
            [shape_of((tokens, inner), BF16)] + [shape_of((block_len, width), BF16)] * 4,
            scratch=[pltpu.VMEM((tokens, width), BF16)],
            name="combine", limit=20,
        )
        return got[0], got[1:]

    def add_all(values, dtype=BF16):
        out = shape_of(values[0].shape, dtype)
        return run(functools.partial(add_body, len(values)), me, values, [out], name="add_all", limit=16)[0]

    def line_up(axis, values, size):
        extra = values[0].shape[0] - size
        small = [shape_of((extra, width), BF16)] if extra else []
        outs = [shape_of((4 * size, width), BF16)] + small
        return run(functools.partial(line_up_body, axis), me, values, outs, name="line_up", limit=8)

    seq_bf16 = pltpu.VMEM((length, LANES), BF16)
    seq_f32 = pltpu.VMEM((length, LANES), F32)
    o_shapes = [shape_of((2, block_len, LANES), BF16)] * 4

    def attend_both(pieces, grads, seg_rows, with_out):
        return run(
            functools.partial(attend_both_body, block_len, chunk, with_out),
            me,
            [*pieces, *grads, seg_rows],
            [shape_of((2, block_len, (4 if with_out else 3) * LANES), BF16)] * 4,
            scratch=([pltpu.VMEM((3, length, LANES), BF16)] if with_out else [])
            + [seq_bf16, pltpu.VMEM((2, LANES, length), BF16), seq_bf16]
            + [seq_f32] * 3,
            name="attend_both", limit=24,
        )

    def project_back(layer, pieces, dm, riders=()):
        got = run(
            functools.partial(project_back_body, block_len, layer),
            me,
            [*pieces, (qkv_weight, layer_spec(qkv_weight, layer)), dm, attn_gain, mlp_gain, *riders],
            [shape_of((tokens, 3 * inner), BF16), wide, shape_of((3, inner), F32)]
            + [shape_of((block_len * (2 if riders else 1), width), BF16)] * 4,
            scratch=[pltpu.VMEM((tokens, width), BF16)],
            name="project_back", limit=24,
        )
        return got[0], got[1], got[2], got[3:]

    def norm_back(pieces, x, dy, riders=()):
        quarter = shape_of((block_len, width), F32)
        low = shape_of((block_len + (16 if riders else 0), width), BF16)
        return run(
            norm_back_body,
            me,
            [add_up(pieces), x, dy, *riders],
            [quarter, low, shape_of((1, width), F32)],
            name="norm_back",
            limit=10,
        )

    def gains(x, da, dm):
        return run(gains_body, me, [x, da, dm], [shape_of((4, width), F32)], name="gains", limit=16)[0]

    half = width // 2
    columns = [[8 * z + 2 * chip + core for z in range(4) for chip in range(4)] for core in range(2)]

    def feed_weights(m, dh, active, r):
        pack = shape_of((2 * half, width), BF16)
        return run(feed_weights_body, me, [m, dh, active, r], [pack] * 2, name="feed_weights", limit=24)

    def head_weights(attn_in, dproj, attended, r):
        pack = shape_of((half, width), BF16)
        return run(head_weights_body, me, [attn_in, dproj, attended, r], [pack] * 2, name="head_weights", limit=20)

    x0_quarter, a0, m0, *pieces = project_first(x0)
    fed0 = feed(0, m0)
    pieces0, (active0, slope0, part0) = over_chips(pieces, fed0)
    got = run(
        functools.partial(attend_body, block_len, chunk),
        me,
        pieces0,
        [shape_of((8, length), F32), shape_of((3, length, LANES), BF16)] + o_shapes,
        scratch=[pltpu.VMEM((LANES, length), BF16), seq_bf16],
        name="attend", limit=20,
    )
    seg_rows, qkv0 = got[:2]
    out0, _ = over_chips(got[2:])
    attended0, u0 = combine(0, out0, part0)
    dy1_quarter, *grads1 = run(
        functools.partial(send_grad_body, block_len),
        me,
        [after(dy1, u0[0]), (out_weight, layer_spec(out_weight, 1))],
        [shape_of((block_len, width), F32)] + o_shapes,
        name="out_back", limit=14,
    )
    u0, grads1 = tie(over_tensor(u0), over_x(grads1))
    u0 = share_tensor(add_up(u0).astype(BF16))
    u0, grads1_other = tie(u0, [swap_core(piece) for piece in grads1])

    x1, x1_quarter, a1, m1, *pieces = project(1, x0, [*u0, out_bias, down_bias])
    fed1 = feed_both(1, m1, dy1)
    pieces1, (active1, r1, dh1, dm1, up_b1) = over_chips(pieces, fed1)
    got = attend_both(pieces1, grads1 + grads1_other, seg_rows, True)
    feed_pack1 = feed_weights(after(m1, got[0]), dh1, active1, r1)
    back1, feed_pack1 = over_chips(got, feed_pack1)
    dproj1, da1, qkv_b1, e1 = project_back(1, back1, dm1)
    back1, (feed_keep, feed_send) = after((back1, feed_pack1), e1[0])
    attended1, u1 = combine(1, back1, None, active1)
    head_keep, head_send = head_weights(a1, dproj1, attended1, r1)
    e1, (u1, head_keep, head_send, feed_came) = tie(over_tensor(e1), (u1, head_keep, head_send, swap_core(feed_send)))
    pack1 = run(
        add_packs_body,
        me,
        [feed_keep, feed_came, head_keep, swap_core(head_send)],
        [shape_of((3 * half, width), BF16)],
        name="add_packs",
        limit=16,
    )[0]
    part1 = lax.psum_scatter(pack1, ("dp", "ctx"), axis_index_groups=columns, tiled=True)
    dx1, low1, bias1 = norm_back(e1, x1_quarter, dy1_quarter)
    gains1 = gains(after(x1, low1), da1, dm1)
    quarters, gains1 = tie(share_tensor(low1), gains1)

    r0, *grads0 = run(
        functools.partial(join_body, block_len),
        me,
        [*quarters, (out_weight, layer_spec(out_weight, 0))],
        [wide] + o_shapes,
        name="join_out_back", limit=14,
    )
    ua_keep, ua_send, ub_keep, ub_send = after(u1, r0)
    ua_came, ub_came = both_ways(ua_send, ub_send, "tensor")
    dh0, dm0, up_b0 = feed_back(0, r0, slope0)
    grads0, (ua_came, ub_came, dh0, dm0, up_b0) = over_chips(grads0, (ua_came, ub_came, dh0, dm0, up_b0))
    back0 = attend_both([qkv0], grads0, seg_rows, False)
    m0_late, u_parts = after((m0, [ua_keep, ua_came, ub_keep, ub_came]), back0[0])
    feed_pack0 = feed_weights(m0_late, dh0, active0, r0)
    u_part = shape_of((block_len // 2, width), BF16)
    ua_keep, ua_send, ub_keep, ub_send = run(
        halve_again_body, me, u_parts, [u_part] * 4, name="halve_again", limit=10
    )
    ub_came, ua_came = both_ways(ub_send, ua_send, "tensor")
    back0, (feed_keep, feed_send, u1) = over_chips(back0, (*feed_pack0, [ua_keep, ua_came, ub_keep, ub_came]))
    dproj0, da0, qkv_b0, e0 = project_back(0, back0, dm0)
    head_keep, head_send = head_weights(a0, dproj0, attended0, r0)
    e0 = after(e0, head_keep)
    way = shape_of((3 * half // 4, width), BF16)
    a_keep, a_send, b_keep, b_send = run(
        halve_body,
        me,
        [feed_keep, swap_core(feed_send), head_keep, swap_core(head_send)],
        [way] * 4,
        scratch=[pltpu.VMEM((2 * half, width), BF16), pltpu.VMEM((half, width), BF16)],
        name="halve",
        limit=20,
    )
    gains0 = gains(after(x0, a_send), da0, dm0)
    a_came, b_came = both_ways(a_send, b_send)
    e0, (gains0, a_came, b_came) = tie(over_tensor(e0), (gains0, a_came, b_came))
    way = shape_of((3 * half // 8, width), BF16)
    a_keep, a_send, b_keep, b_send = run(
        halve_again_body, me, [a_keep, a_came, b_keep, b_came], [way] * 4, name="halve_again", limit=10
    )
    b_came, a_came = both_ways(b_send, a_send)
    part1 = after(part1, a_send)
    pack1 = lax.all_gather(part1, ("dp", "ctx"), axis_index_groups=columns, tiled=True)
    dx0, low0, bias0 = norm_back(after(e0, a_send), x0_quarter, dx1, (gains0, gains1, bias1))
    last = share_tensor(low0)
    (a_came, b_came), last = tie((a_came, b_came), last)
    local = run(
        pack_small_body,
        me,
        [qkv_b0, qkv_b1, up_b0, up_b1],
        [shape_of((16, width), BF16)],
        name="pack_small",
        limit=8,
    )[0]

    few = half // 32
    cut = run(
        merge_body,
        me,
        [a_keep, a_came, b_keep, b_came, *last, local],
        [shape_of((6 * few + 32, width), BF16)] * 4,
        scratch=[pltpu.VMEM((24 * few, width), BF16)],
        name="merge",
        limit=12,
    )
    u1 = run(
        add_halves_body, me, after(u1, cut[0]), [shape_of((block_len, width), BF16)], name="add_halves", limit=8
    )[0]
    cut, u1 = tie(over_x(cut), spread_near(u1, "tensor"))
    pieces = [shape_of((3 * few, width), BF16), shape_of((3 * few + 32, width), BF16)]
    first, second = run(settle_body, me, cut, pieces, name="settle", limit=8)
    first, second = tie(over_x([first] * 4), over_dp([second] * 4))
    second, small = line_up(3, second, 3 * few)
    first = line_up(0, first, 3 * few)[0]
    near = (spread_near(first, "dp"), spread_near(second, "x"))

    u1 = spread_far(u1, "tensor")
    last, u1 = after((last, u1), first)
    input_grad, output = run(
        functools.partial(place_body, block_len),
        me,
        [*last, *u1, x1, out_bias, down_bias],
        [shape_of((tokens, width), F32)] * 2,
        name="place",
        limit=20,
    )
    heavy = [
        shape_of((2, width, hidden), F32),
        shape_of((2, hidden, width), F32),
        shape_of((2, 3, width, inner), F32),
        shape_of((2, inner, width), F32),
    ]
    small_came = swap_core(small)
    pack1_came = swap_core(after(pack1, first))
    quarter = half // 4
    views = [(2, 2, half, width)] * 2 + [(2, 3, 2, half, inner), (2, 2, LANES, width)]
    first_outs = run(
        unpack_whole_body,
        me,
        [
            (pack, pl.BlockSpec((quarter, width), lambda i, *_, part=part: (4 * part + i, 0)))
            for pack in (pack1, pack1_came)
            for part in range(3)
        ],
        [shape_of(view, F32) for view in views],
        name="unpack_whole",
        limit=24,
        out_specs=[
            pl.BlockSpec((1, 2, quarter, width), lambda i, *_: (1, 0, i, 0)),
            pl.BlockSpec((1, 2, quarter, width), lambda i, *_: (1, 0, i, 0)),
            pl.BlockSpec((1, 3, 2, quarter, inner), lambda i, *_: (1, 0, 0, i, 0)),
            pl.BlockSpec((1, 2, LANES, 2 * LANES), lambda i, *_: (1, 0, 0, i)),
        ],
        grid=4,
    )
    first_outs = [v.reshape(like.shape) for v, like in zip(first_outs, heavy)]
    near, (first_outs, small_came, input_grad, output) = tie(near, (first_outs, small_came, input_grad, output))
    far = (spread_far(near[0], "dp"), spread_far(near[1], "x"))
    other = [swap_core(v) for v in near[0] + near[1]]
    row_pair = shape_of((2, width), F32)
    small = run(
        small_out_body,
        me,
        [small, small_came],
        [row_pair] * 6 + [shape_of((2, 3, inner), F32)],
        name="small_out",
        limit=8,
    )
    mine, (small, other) = tie(far[0] + far[1], (small, other))
    far = [swap_core(v) for v in mine[3:5] + mine[8:10]]
    other = other[0:3] + far[0:2] + other[3:6] + far[2:4]
    in_place = pl.BlockSpec(memory_space=pl.ANY)
    held = [pltpu.VMEM(v.shape[1:], F32) for v in heavy] + [pltpu.SemaphoreType.DMA((4,))]
    up_grad, down_grad, qkv_grad, out_grad = run(
        functools.partial(unpack_body, few),
        me,
        mine + other + [(v, in_place) for v in first_outs],
        heavy,
        name="unpack",
        limit=28,
        out_specs=[in_place] * 4,
        scratch=held,
        aliases={21 + index: index for index in range(4)},
    )
    return (
        output.reshape(tok_shape),
        input_grad.reshape(tok_shape),
        small[0],
        small[1],
        small[2],
        small[3],
        qkv_grad,
        small[6],
        out_grad,
        small[4],
        up_grad,
        small[5],
        down_grad,
        small[4],
    )


def solution(mesh):
    in_specs = (
        P("dp", "ctx", None),
        P("dp", "ctx"),
        P(),
        P(),
        P(),
        P(),
        P(None, None, None, "tensor"),
        P(None, None, "tensor"),
        P(None, "tensor", None),
        P(),
        P(None, None, "tensor"),
        P(None, "tensor"),
        P(None, "tensor", None),
        P(),
        P("dp", "ctx", None),
    )
    out_specs = (
        P("dp", "ctx", None),
        P("dp", "ctx", None),
        P(),
        P(),
        P(),
        P(),
        P(None, None, None, "tensor"),
        P(None, None, "tensor"),
        P(None, "tensor", None),
        P(),
        P(None, None, "tensor"),
        P(None, "tensor"),
        P(None, "tensor", None),
        P(),
    )
    return jax.shard_map(
        on_device, mesh=mesh, in_specs=in_specs, out_specs=out_specs, check_vma=False
    )
```

```python
import functools

import jax
import jax.numpy as jnp
from jax import lax
from jax.experimental import pallas as pl
from jax.experimental.pallas import tpu as pltpu
from jax.sharding import PartitionSpec as P

HEAD = 64
ROT = 16
LAYERS = 2
LANES = 128
F32 = jnp.float32
BF16 = jnp.bfloat16


def shape_of(shape, dtype):
    return jax.ShapeDtypeStruct(tuple(shape), dtype)


def whole(array):
    rank = array.ndim
    return pl.BlockSpec(array.shape, lambda i, *_: (0,) * rank, pipeline_mode=pl.Buffered(1))


def layer_spec(array, layer):
    rank = array.ndim
    return pl.BlockSpec(
        (1,) + array.shape[1:], lambda i, *_: (layer,) + (0,) * (rank - 1), pipeline_mode=pl.Buffered(1)
    )


def run(body, me, operands, outs, scratch=(), name=None, limit=32, out_specs=None, aliases=None, grid=1):
    arrays, specs = [], []
    for operand in operands:
        array, spec = operand if isinstance(operand, tuple) else (operand, None)
        arrays.append(array)
        specs.append(whole(array) if spec is None else spec)
    return pl.pallas_call(
        body,
        grid_spec=pltpu.PrefetchScalarGridSpec(
            num_scalar_prefetch=1,
            grid=(grid,),
            in_specs=specs,
            out_specs=[whole(o) for o in outs] if out_specs is None else out_specs,
            scratch_shapes=list(scratch),
        ),
        out_shape=list(outs),
        input_output_aliases=aliases or {},
        compiler_params=pltpu.CompilerParams(vmem_limit_bytes=limit * 1024 * 1024),
        cost_estimate=pl.CostEstimate(flops=1, bytes_accessed=1, transcendentals=0),
        name=name,
    )(me, *arrays)


def matmul(left, right):
    return jnp.dot(left, right, preferred_element_type=F32)


def matmul_nt(left, right):
    return lax.dot_general(left, right, (((1,), (1,)), ((), ())), preferred_element_type=F32)


def matmul_tn(left, right):
    return lax.dot_general(left, right, (((0,), (0,)), ((), ())), preferred_element_type=F32)


def normalize(values):
    average = jnp.mean(values, axis=-1, keepdims=True)
    centred = values - average
    factor = lax.rsqrt(jnp.mean(centred * centred, axis=-1, keepdims=True) + 1e-05)
    return centred * factor, factor


def wrap4(value):
    return lax.rem(value + 4, 4)


def rows(index, size):
    return pl.ds(pl.multiple_of(index * size, size), size)


def rotary_rows(place_row):
    count = place_row.shape[1]
    which = lax.broadcasted_iota(jnp.int32, (8, count), 0)
    frequency = jnp.zeros((8, count), F32)
    for index in range(8):
        frequency = jnp.where(which == index, 10000.0 ** (-2.0 * index / ROT), frequency)
    angles = frequency * place_row
    trig = jnp.concatenate([jnp.cos(angles), jnp.sin(angles)], axis=0)
    row = lax.broadcasted_iota(jnp.int32, (16, LANES), 0)
    lane = lax.broadcasted_iota(jnp.int32, (16, LANES), 1) & (HEAD - 1)
    same = (lane & 7) == (row & 7)
    is_cos = row < 8
    pick_cos = jnp.where(is_cos & same & (lane < 16), 1.0, 0.0)
    pick_low = jnp.where((row >= 8) & same & (lane < 8), 1.0, 0.0)
    pick_high = jnp.where((row >= 8) & same & (lane >= 8) & (lane < 16), 1.0, 0.0)
    picks = jnp.concatenate([pick_cos, pick_low, pick_high], axis=1).astype(F32)
    spread = lax.dot_general(
        trig, picks, (((0,), (0,)), ((), ())), preferred_element_type=F32, precision=lax.Precision.HIGHEST
    )
    lane_row = lax.broadcasted_iota(jnp.int32, (1, LANES), 1) & (HEAD - 1)
    cos_table = spread[:, :LANES] + jnp.where(lane_row >= ROT, 1.0, 0.0)
    return cos_table, spread[:, LANES : 2 * LANES], spread[:, 2 * LANES :]


def rotate(values, tables, back=False):
    cos_table, low_sin, high_sin = tables
    below = pltpu.roll(values, LANES - ROT // 2, 1) * low_sin
    above = pltpu.roll(values, ROT // 2, 1) * high_sin
    turned = below - above if back else above - below
    return values * cos_table + turned


def project_rows(layer, tok_shape, me_ref, seg_ref, weight, bias, a_ref, p_refs, proj_ref, with_seg):
    seq_count, block_len, width = tok_shape
    chip, core = me_ref[0], me_ref[1]
    base = (chip * 2 + core) * block_len
    for j in range(3):
        proj_ref[:, j * 2 * LANES : (j + 1) * 2 * LANES] = matmul(a_ref[...], weight(j)) + bias[j, layer : layer + 1, :]
    for k in range(4):
        seq = wrap4(chip + k)
        place = rows(seq, block_len)
        seg_row = seg_ref[pl.ds(seq, 1), :]
        spots = lax.broadcasted_iota(jnp.int32, (1, block_len), 1) + base
        tables = rotary_rows((spots - seg_row).astype(F32))
        for j in range(3):
            for pair in range(2):
                at = (2 * j + pair) * LANES
                part = proj_ref[place, at : at + LANES]
                if j < 2:
                    part = rotate(part, tables)
                p_refs[k][pair, 0:block_len, j * LANES : (j + 1) * LANES] = part.astype(BF16)
        if with_seg:
            coded = seg_row.astype(F32)
            high = jnp.floor(coded * 0.125)
            packed = jnp.concatenate([high, coded - 8.0 * high, jnp.zeros_like(high)], axis=1)
            packed = jnp.broadcast_to(packed, (16, 3 * LANES)).astype(BF16)
            for pair in range(2):
                p_refs[k][pair, block_len : block_len + 16, :] = packed


def project_first_body(tok_shape, me_ref, *refs):
    seq_count, block_len, width = tok_shape
    in_refs, refs = refs[:8], refs[8:]
    xq_ref, a_ref, m_ref, *p_refs = refs[:7]
    proj_ref, *held, sems = refs[7:]
    x_ref, seg_ref, ag_ref, as_ref, mg_ref, ms_ref, w_ref, b_ref = held
    copies = []
    for index in (1, 2, 3, 4, 5):
        copies.append(pltpu.make_async_copy(in_refs[index], held[index], sems.at[len(copies)]))
    copies.append(pltpu.make_async_copy(in_refs[7], b_ref, sems.at[len(copies)]))
    small_count = len(copies)
    for seq in range(seq_count):
        place = pl.ds(seq * block_len, block_len)
        copies.append(pltpu.make_async_copy(in_refs[0].at[place], x_ref.at[place], sems.at[len(copies)]))
    copies.append(pltpu.make_async_copy(in_refs[6].at[0], w_ref, sems.at[len(copies)]))
    for copy in copies:
        copy.start()
    for copy in copies[:small_count]:
        copy.wait()
    for seq in range(seq_count):
        copies[small_count + seq].wait()
        place = slice(seq * block_len, (seq + 1) * block_len)
        normed, _ = normalize(x_ref[place, :])
        a_ref[place, :] = (normed * ag_ref[0:1, :] + as_ref[0:1, :]).astype(BF16)
        m_ref[place, :] = (normed * mg_ref[0:1, :] + ms_ref[0:1, :]).astype(BF16)
    xq_ref[...] = x_ref[rows(me_ref[2], block_len), :]
    copies[-1].wait()
    project_rows(0, tok_shape, me_ref, seg_ref, lambda j: w_ref[j], b_ref, a_ref, p_refs, proj_ref, True)


def project_body(layer, tok_shape, me_ref, *refs):
    seq_count, block_len, width = tok_shape
    x_ref, seg_ref, *refs = refs
    u_refs, refs = refs[:4], refs[4:]
    ob_ref, db_ref, ag_ref, as_ref, mg_ref, ms_ref, w_ref, b_ref, x_out, xq_ref, a_ref, m_ref, *p_refs, proj_ref = refs
    tensor = me_ref[2]
    shift = ob_ref[layer - 1 : layer, :] + db_ref[layer - 1 : layer, :]
    for k in range(4):
        place = rows(wrap4(tensor - k), block_len)
        value = x_ref[place, :] + u_refs[k][...].astype(F32) + shift
        x_out[place, :] = value
        if k == 0:
            xq_ref[...] = value
        normed, _ = normalize(value)
        a_ref[place, :] = (normed * ag_ref[layer : layer + 1, :] + as_ref[layer : layer + 1, :]).astype(BF16)
        m_ref[place, :] = (normed * mg_ref[layer : layer + 1, :] + ms_ref[layer : layer + 1, :]).astype(BF16)
    project_rows(layer, tok_shape, me_ref, seg_ref, lambda j: w_ref[0, j], b_ref, a_ref, p_refs, proj_ref, False)


def gather_pieces(me_ref, refs, targets, block_len, seg_target=None):
    chip, core = me_ref[0], me_ref[1]
    for k in range(4):
        owner = wrap4(chip - k)
        for side, ref in ((core, refs[k]), (1 - core, refs[4 + k])):
            place = rows(owner * 2 + side, block_len)
            for index, target in enumerate(targets):
                target[place, :] = ref[core, 0:block_len, index * LANES : (index + 1) * LANES]
            if seg_target is not None:
                row = ref[core, block_len : block_len + 16, :].astype(F32)[0:1, :]
                starts = row[:, 0:LANES] * 8.0 + row[:, LANES : 2 * LANES]
                seg_target[:, place] = jnp.broadcast_to(starts, (8, block_len))


def head_stack(values):
    lane = lax.broadcasted_iota(jnp.int32, values.shape, 1)
    zero = jnp.zeros_like(values)
    return jnp.concatenate(
        [jnp.where(lane < HEAD, values, zero), jnp.where(lane >= HEAD, values, zero)], axis=0
    )


def own_halves(product, width):
    return jnp.concatenate([product[0:HEAD, 0:width], product[HEAD:, width : 2 * width]], axis=0)


def chances_t(q_ref, k_ref, seg_ref, step, chunk):
    start, keys = step * chunk, (step + 1) * chunk
    stacked = head_stack(q_ref[start:keys, :]) * jnp.asarray(HEAD ** (-0.5), BF16)
    scores = matmul_nt(k_ref[0:keys, :], stacked)
    key_place = lax.broadcasted_iota(jnp.int32, (keys, 2 * chunk), 0).astype(F32)
    query_place = (lax.broadcasted_iota(jnp.int32, (1, 2 * chunk), 1) & (chunk - 1)).astype(F32) + start
    seg_row = seg_ref[0:1, start:keys]
    seg_row = jnp.concatenate([seg_row, seg_row], axis=1)
    allowed = (key_place >= seg_row) & (key_place <= query_place)
    scores = jnp.where(allowed, scores, -1e30)
    raised = jnp.exp(scores - jnp.max(scores, axis=0, keepdims=True))
    total = jnp.sum(raised, axis=0, keepdims=True)
    return raised * (1.0 / total), stacked


def attend_body(block_len, chunk, me_ref, *refs):
    piece_refs, refs = refs[:8], refs[8:]
    seg_out, qkv_ref, *refs = refs
    o_refs, refs = refs[:4], refs[4:]
    vt_ref, o_ref = refs
    q_ref, k_ref, v_ref = qkv_ref.at[0], qkv_ref.at[1], qkv_ref.at[2]
    gather_pieces(me_ref, piece_refs, (q_ref, k_ref, v_ref), block_len, seg_out)
    vt_ref[...] = v_ref[...].T
    length = q_ref.shape[0]
    for step in range(length // chunk):
        keys = (step + 1) * chunk
        chances, _ = chances_t(q_ref, k_ref, seg_out, step, chunk)
        mixed = matmul(vt_ref[:, 0:keys], chances.astype(BF16))
        o_ref[step * chunk : keys, :] = own_halves(mixed, chunk).T.astype(BF16)
    send_blocks(me_ref, o_ref, o_refs, block_len)


def send_blocks(me_ref, source, targets, block_len):
    chip = me_ref[0]
    for k in range(4):
        dest = wrap4(chip + k)
        for side in range(2):
            targets[k][side] = source[rows(dest * 2 + side, block_len), :]


def attend_both_body(block_len, chunk, with_out, me_ref, *refs):
    if with_out:
        piece_refs, refs = refs[:8], refs[8:]
    else:
        qkv_ref, *refs = refs
    grad_refs, refs = refs[:8], refs[8:]
    seg_ref, *refs = refs
    d_refs, refs = refs[:4], refs[4:]
    if with_out:
        qkv_ref, *refs = refs
    q_ref, k_ref, v_ref = qkv_ref.at[0], qkv_ref.at[1], qkv_ref.at[2]
    g_ref, t_ref, o_ref, dq_ref, dk_ref, dv_ref = refs
    if with_out:
        gather_pieces(me_ref, piece_refs, (q_ref, k_ref, v_ref), block_len)
    gather_pieces(me_ref, grad_refs, (g_ref,), block_len)
    length = q_ref.shape[0]
    t_ref[0] = k_ref[...].T
    if with_out:
        t_ref[1] = v_ref[...].T
    dk_ref[...] = jnp.zeros_like(dk_ref)
    dv_ref[...] = jnp.zeros_like(dv_ref)
    for step in range(length // chunk):
        start, keys = step * chunk, (step + 1) * chunk
        chances, stacked = chances_t(q_ref, k_ref, seg_ref, step, chunk)
        low = chances.astype(BF16)
        if with_out:
            mixed = matmul(t_ref[1, :, 0:keys], low)
            o_ref[start:keys, :] = own_halves(mixed, chunk).T.astype(BF16)
        grads = head_stack(g_ref[start:keys, :])
        chance_grad = matmul_nt(v_ref[0:keys, :], grads)
        delta = jnp.sum(chances * chance_grad, axis=0, keepdims=True)
        score_grad = (chances * (chance_grad - delta)).astype(BF16)
        dv_ref[0:keys, :] += matmul(low, grads)
        dk_ref[0:keys, :] += matmul(score_grad, stacked)
        query = matmul(t_ref[0, :, 0:keys], score_grad)
        dq_ref[start:keys, :] = own_halves(query, chunk).T * HEAD ** (-0.5)
    chip = me_ref[0]
    for k in range(4):
        dest = wrap4(chip + k)
        for side in range(2):
            place = rows(dest * 2 + side, block_len)
            spots = (lax.broadcasted_iota(jnp.int32, (1, block_len), 1) + (dest * 2 + side) * block_len).astype(F32)
            tables = rotary_rows(spots - seg_ref[0:1, place])
            d_refs[k][side, :, 0:LANES] = rotate(dq_ref[place, :], tables, True).astype(BF16)
            d_refs[k][side, :, LANES : 2 * LANES] = rotate(dk_ref[place, :], tables, True).astype(BF16)
            d_refs[k][side, :, 2 * LANES : 3 * LANES] = dv_ref[place, :].astype(BF16)
            if with_out:
                d_refs[k][side, :, 3 * LANES :] = o_ref[place, :]


def land_heads(me_ref, refs, target, block_len, groups, first=0):
    chip, core = me_ref[0], me_ref[1]
    for k in range(4):
        place = rows(wrap4(chip - k), block_len)
        mine, other = refs[k][core], refs[4 + k][core]
        is_low = core == 0
        for group in range(groups):
            span = slice((first + group) * LANES, (first + group + 1) * LANES)
            at = group * 2 * LANES
            target[place, at : at + LANES] = jnp.where(is_low, mine[:, span], other[:, span])
            target[place, at + LANES : at + 2 * LANES] = jnp.where(is_low, other[:, span], mine[:, span])


def combine_body(block_len, fused, me_ref, *refs):
    piece_refs, refs = refs[:8], refs[8:]
    w_ref, *refs = refs
    if fused:
        g_ref, down_ref, *refs = refs
    else:
        part_ref, *refs = refs
    o_ref, *refs = refs
    q_refs, scr = refs[:-1], refs[-1]
    tensor = me_ref[2]
    land_heads(me_ref, piece_refs, o_ref, block_len, 1, 3 if fused else 0)
    part = matmul(g_ref[...], down_ref[0]) if fused else part_ref[...]
    scr[...] = (matmul(o_ref[...], w_ref[0]) + part).astype(BF16)
    if fused:
        near, far = near_far(tensor)
        size = block_len // 2
        orders = ((tensor, far), (near, 3 - near), (tensor, near), (far, far ^ 1))
        for way, (ref, order) in enumerate(zip(q_refs, orders)):
            for index, quarter in enumerate(order):
                at = pl.multiple_of(quarter * block_len + (way >> 1) * size, size)
                ref[index * size : (index + 1) * size, :] = scr[pl.ds(at, size), :]
        return
    for k in range(4):
        q_refs[k][...] = scr[rows(wrap4(tensor + k), block_len), :]


def send_grad_body(block_len, me_ref, x_ref, w_ref, *refs):
    chip, tensor = me_ref[0], me_ref[2]
    quarter_ref, *refs = refs
    quarter_ref[...] = x_ref[rows(tensor, block_len), :]
    for k in range(4):
        value = x_ref[rows(wrap4(chip + k), block_len), :].astype(BF16)
        grad = matmul_nt(value, w_ref[0]).astype(BF16)
        for pair in range(2):
            refs[k][pair] = grad[:, pair * LANES : (pair + 1) * LANES]


def join_body(block_len, me_ref, *refs):
    q_refs, refs = refs[:4], refs[4:]
    w_ref, r_ref, *g_refs = refs
    chip, tensor = me_ref[0], me_ref[2]
    for k in range(4):
        r_ref[rows(wrap4(tensor - k), block_len), :] = q_refs[k][...]
    for k in range(4):
        value = r_ref[rows(wrap4(chip + k), block_len), :]
        grad = matmul_nt(value, w_ref[0]).astype(BF16)
        for pair in range(2):
            g_refs[k][pair] = grad[:, pair * LANES : (pair + 1) * LANES]


def project_back_body(block_len, layer, me_ref, *refs):
    piece_refs, refs = refs[:8], refs[8:]
    w_ref, dm_ref, ag_ref, mg_ref, *refs = refs
    riders, refs = refs[:-8], refs[-8:]
    dp_ref, da_ref, bias_ref, *q_refs, scr = refs
    tensor = me_ref[2]
    land_heads(me_ref, piece_refs, dp_ref, block_len, 3)
    for j in range(3):
        span = slice(j * 2 * LANES, (j + 1) * 2 * LANES)
        bias_ref[j : j + 1, :] = jnp.sum(dp_ref[:, span].astype(F32), axis=0, keepdims=True)
    total = None
    for j in range(3):
        term = matmul_nt(dp_ref[:, j * 2 * LANES : (j + 1) * 2 * LANES], w_ref[0, j])
        total = term if total is None else total + term
    da_ref[...] = total.astype(BF16)
    scr[...] = (total * ag_ref[layer : layer + 1, :] + dm_ref[...] * mg_ref[layer : layer + 1, :]).astype(BF16)
    for k in range(4):
        q_refs[k][0:block_len, :] = scr[rows(wrap4(tensor + k), block_len), :]
        if riders:
            q_refs[k][block_len:, :] = riders[k][...]


def norm_back_body(me_ref, *refs):
    e_ref, x_ref, dy_ref, *gain_refs, dx_ref, low_ref, bias_ref = refs
    upstream = dy_ref[...]
    size = upstream.shape[0]
    total = e_ref[0:size, :]
    normed, factor = normalize(x_ref[...])
    inner = jnp.mean(total * normed, axis=-1, keepdims=True)
    result = upstream + factor * (total - jnp.mean(total, axis=-1, keepdims=True) - normed * inner)
    dx_ref[...] = result
    low_ref[0:size, :] = result.astype(BF16)
    bias = jnp.sum(upstream, axis=0, keepdims=True)
    bias_ref[...] = bias
    if gain_refs:
        mine, other, other_bias = gain_refs
        blank = jnp.zeros((6, bias.shape[1]), F32)
        rows_here = jnp.concatenate([mine[...], bias, other[...], other_bias[...], blank], axis=0)
        low_ref[size:, :] = rows_here.astype(BF16)


def gains_body(me_ref, x_ref, da_ref, dm_ref, out_ref):
    normed, _ = normalize(x_ref[...])
    da = da_ref[...].astype(F32)
    dm = dm_ref[...]
    out_ref[0:1, :] = jnp.sum(da * normed, axis=0, keepdims=True)
    out_ref[1:2, :] = jnp.sum(da, axis=0, keepdims=True)
    out_ref[2:3, :] = jnp.sum(dm * normed, axis=0, keepdims=True)
    out_ref[3:4, :] = jnp.sum(dm, axis=0, keepdims=True)


def gelu_parts(hidden):
    cdf = 0.5 * (1.0 + lax.erf(hidden * (0.5**0.5)))
    density = jnp.exp(-0.5 * hidden * hidden) * 0.3989422804014327
    return cdf, density


def feed_body(layer, me_ref, m_ref, up_ref, ub_ref, down_ref, g_ref, slope_ref, part_ref):
    size = 2 * LANES
    for step in range(up_ref.shape[2] // size):
        span = slice(step * size, (step + 1) * size)
        hidden = matmul(m_ref[...], up_ref[0, :, span]) + ub_ref[layer : layer + 1, span]
        cdf, density = gelu_parts(hidden)
        g_ref[:, span] = (hidden * cdf).astype(BF16)
        slope_ref[:, span] = cdf + hidden * density
    part_ref[...] = matmul(g_ref[...], down_ref[0])


def feed_back_body(me_ref, r_ref, slope_ref, up_ref, down_ref, dh_ref, dm_ref, bias_ref):
    size = 2 * LANES
    for step in range(down_ref.shape[1] // size):
        span = slice(step * size, (step + 1) * size)
        grad = matmul_nt(r_ref[...], down_ref[0, span, :]) * slope_ref[:, span]
        bias_ref[:, span] = jnp.sum(grad, axis=0, keepdims=True)
        dh_ref[:, span] = grad.astype(BF16)
    dm_ref[...] = matmul_nt(dh_ref[...], up_ref[0])


def feed_both_body(layer, me_ref, m_ref, dy_ref, up_ref, ub_ref, down_ref, g_ref, r_ref, dh_ref, dm_ref, bias_ref):
    size = 2 * LANES
    r_ref[...] = dy_ref[...].astype(BF16)
    for step in range(up_ref.shape[2] // size):
        span = slice(step * size, (step + 1) * size)
        hidden = matmul(m_ref[...], up_ref[0, :, span]) + ub_ref[layer : layer + 1, span]
        cdf, density = gelu_parts(hidden)
        g_ref[:, span] = (hidden * cdf).astype(BF16)
        grad = matmul_nt(r_ref[...], down_ref[0, span, :]) * (cdf + hidden * density)
        bias_ref[:, span] = jnp.sum(grad, axis=0, keepdims=True)
        dh_ref[:, span] = grad.astype(BF16)
    dm_ref[...] = matmul_nt(dh_ref[...], up_ref[0])


def feed_weights_body(me_ref, m_ref, dh_ref, g_ref, r_ref, keep_ref, send_ref):
    core = me_ref[1]
    half = m_ref.shape[1] // 2
    for side, out in ((core, keep_ref), (1 - core, send_ref)):
        out[0:half, :] = matmul_tn(m_ref[:, rows(side, half)], dh_ref[...]).astype(BF16)
        out[half:, :] = matmul_tn(g_ref[:, rows(side, half)], r_ref[...]).astype(BF16)


def head_weights_body(me_ref, a_ref, dp_ref, o_ref, r_ref, keep_ref, send_ref):
    core = me_ref[1]
    half = a_ref.shape[1] // 2
    wide = dp_ref.shape[1]
    for side, out in ((core, keep_ref), (1 - core, send_ref)):
        out[:, 0:wide] = matmul_tn(a_ref[:, rows(side, half)], dp_ref[...]).astype(BF16)
        grad = matmul_tn(o_ref[:, rows(side, LANES)], r_ref[...]).astype(BF16)
        for part in range(4):
            out[part * LANES : (part + 1) * LANES, wide:] = grad[:, part * 2 * LANES : (part + 1) * 2 * LANES]


def feed_weights_whole_body(me_ref, m_ref, dh_ref, g_ref, r_ref, pack_ref):
    high = m_ref.shape[1]
    pack_ref[0:high, :] = matmul_tn(m_ref[...], dh_ref[...]).astype(BF16)
    pack_ref[high:, :] = matmul_tn(g_ref[...], r_ref[...]).astype(BF16)


def head_weights_whole_body(me_ref, a_ref, dp_ref, o_ref, r_ref, before_ref, pack_ref):
    wide = dp_ref.shape[1]
    pack_ref[:, 0:wide] = matmul_tn(a_ref[...], dp_ref[...]).astype(BF16)
    grad = matmul_tn(o_ref[...], r_ref[...]).astype(BF16)
    high, size = grad.shape[0], 2 * LANES
    for part in range(4):
        pack_ref[part * high : (part + 1) * high, wide:] = grad[:, part * size : (part + 1) * size]


def near_far(place):
    return place ^ 1, 3 - place


def halve_body(me_ref, feed_keep, feed_came, head_keep, head_came, *refs):
    outs, feed_scr, head_scr = refs[:4], refs[4], refs[5]
    feed_scr[...] = (feed_keep[...].astype(F32) + feed_came[...].astype(F32)).astype(BF16)
    head_scr[...] = (head_keep[...].astype(F32) + head_came[...].astype(F32)).astype(BF16)
    place = me_ref[3]
    near, far = near_far(place)
    half = head_scr.shape[0]
    size = half // 8
    orders = ((place, far), (near, 3 - near), (4 + place, 4 + near), (4 + far, 4 + (far ^ 1)))
    for ref, order in zip(outs, orders):
        for index, block in enumerate(order):
            at = 3 * size * index
            ref[at : at + size, :] = feed_scr[rows(block, size), :]
            ref[at + size : at + 2 * size, :] = feed_scr[pl.ds(pl.multiple_of(half + block * size, size), size), :]
            ref[at + 2 * size : at + 3 * size, :] = head_scr[rows(block, size), :]


def halve_again_body(me_ref, a_keep, a_came, b_keep, b_came, *outs):
    size = outs[0].shape[0]
    for keep, came, mine, send in ((a_keep, a_came, outs[0], outs[1]), (b_keep, b_came, outs[2], outs[3])):
        total = (keep[...].astype(F32) + came[...].astype(F32)).astype(BF16)
        mine[...] = total[0:size, :]
        send[...] = total[size:, :]


def line_up_body(axis, me_ref, *refs):
    size = refs[4].shape[0] // 4
    for k in range(4):
        refs[4][rows(wrap4(me_ref[axis] - k), size), :] = refs[k][0:size, :]
    if len(refs) > 5:
        even = refs[0][size:, :].astype(F32) + refs[2][size:, :].astype(F32)
        odd = refs[1][size:, :].astype(F32) + refs[3][size:, :].astype(F32)
        refs[5][...] = (even + odd).astype(BF16)


def merge_body(me_ref, a_keep, a_came, b_keep, b_came, *refs):
    out_refs, scr = refs[:4], refs[4]
    high = a_keep.shape[0]
    scr[0:high, :] = (a_keep[...].astype(F32) + a_came[...].astype(F32)).astype(BF16)
    scr[high:, :] = (b_keep[...].astype(F32) + b_came[...].astype(F32)).astype(BF16)
    few = high // 6
    for k in range(4):
        part = wrap4(me_ref[0] + k)
        for weight in range(3):
            at = pl.multiple_of((part >> 1) * high + weight * 2 * few + (part & 1) * few, few)
            out_refs[k][weight * few : (weight + 1) * few, :] = scr[pl.ds(at, few), :]


def settle_body(me_ref, *refs):
    in_refs, last_refs, local_ref, (first_ref, second_ref) = refs[:4], refs[4:8], refs[8], refs[9:]
    total = in_refs[0][...].astype(F32)
    for ref in in_refs[1:]:
        total = total + ref[...].astype(F32)
    total = total.astype(BF16)
    few = second_ref.shape[0] // 3
    for weight in range(3):
        for index, ref in enumerate((first_ref, second_ref)):
            at = (2 * weight + index) * few
            ref[weight * few : (weight + 1) * few, :] = total[at : at + few, :]
    count = local_ref.shape[0]
    shared = [ref[ref.shape[0] - count :, :].astype(F32) for ref in last_refs]
    shared = ((shared[0] + shared[2]) + (shared[1] + shared[3])).astype(BF16)
    first_ref[3 * few : 3 * few + count, :] = shared
    first_ref[3 * few + count :, :] = local_ref[...]


def flush(held, outs, layer, sems):
    copies = [pltpu.make_async_copy(a, b.at[layer], sems.at[i]) for i, (a, b) in enumerate(zip(held, outs))]
    return copies


def unpack_body(few, me_ref, *refs):
    outs, small_outs, held, sems = refs[24:28], refs[28:35], refs[35:39], refs[39]
    up_ref, down_ref, qkv_ref, out_ref = held
    copies = flush(held, outs, 0, sems)
    chip, core, place_z = me_ref[0], me_ref[1], me_ref[3]
    size = 2 * LANES
    half = up_ref.shape[0] // 2
    for weight in range(3):
        for side, group in ((core, refs[:10]), (1 - core, refs[10:20])):
            for along, me in ((0, place_z), (1, chip)):
                pieces = group[5 * along : 5 * along + 5]
                cut = pieces[3].shape[0] // few
                spans = [(pieces[0], me, 0, 12), (pieces[1], me ^ 1, 0, 12), (pieces[2], 3 - me, 0, 12)]
                spans += [(pieces[3], me ^ 2, 0, cut), (pieces[4], me ^ 2, cut, 12)]
                for ref, owner, first, stop in spans:
                    for index in range(first, stop):
                        if index % 3 != weight:
                            continue
                        z, x = (owner, wrap4(chip - index // 3)) if along == 0 else (wrap4(place_z - index // 3), owner)
                        start = (index - first) * few
                        value = ref[start : start + few, :].astype(F32)
                        row = (z + 4 * (x >> 1)) * (4 * few) + (x & 1) * (2 * few) + along * few
                        place = pl.ds(pl.multiple_of(row + side * half, few), few)
                        if weight < 2:
                            held[weight][place, :] = value
                        else:
                            for j in range(3):
                                qkv_ref[j, place, :] = value[:, j * size : (j + 1) * size]
                            inner = pl.ds(pl.multiple_of((row & (LANES - 1)) + side * LANES, few), few)
                            lanes = pl.ds(pl.multiple_of((row >> 7) * size, size), size)
                            out_ref[inner, lanes] = value[:, 3 * size :]
        for copy in copies[weight : weight + 1] if weight < 2 else copies[2:]:
            copy.start()
    parts = []
    for group in (refs[:10], refs[10:20]):
        count = group[0].shape[0] - 12 * few
        rows_of = [ref[ref.shape[0] - count :, :].astype(F32) for ref in (group[0], group[4], group[1], group[2])]
        parts.append((rows_of[0] + rows_of[1]) + (rows_of[2] + rows_of[3]))
    small_out(parts[0] + parts[1], small_outs)
    for copy in copies:
        copy.wait()


def add_packs_body(me_ref, feed_keep, feed_came, head_keep, head_came, out_ref):
    high = feed_keep.shape[0]
    out_ref[0:high, :] = (feed_keep[...].astype(F32) + feed_came[...].astype(F32)).astype(BF16)
    out_ref[high:, :] = (head_keep[...].astype(F32) + head_came[...].astype(F32)).astype(BF16)


def unpack_whole_body(me_ref, up_mine, down_mine, head_mine, up_other, down_other, head_other, *outs):
    up_ref, down_ref, qkv_ref, out_ref = outs
    size = 2 * LANES
    for core in range(2):
        mine = me_ref[1] == core
        for ref, first, second in ((up_ref, up_mine, up_other), (down_ref, down_mine, down_other)):
            ref[0, core] = jnp.where(mine, first[...], second[...]).astype(F32)
        head = jnp.where(mine, head_mine[...], head_other[...]).astype(F32)
        for j in range(3):
            qkv_ref[0, j, core] = head[:, j * size : (j + 1) * size]
        out_ref[0, core] = head[:, 3 * size :]


def pack_small_body(me_ref, *refs):
    ins, local_ref = refs[:4], refs[4]
    width = local_ref.shape[1]
    local = [ins[2][...], ins[3][...]]
    for ref in ins[0:2]:
        values = ref[...]
        flat = [values[j : j + 1, :] for j in range(3)]
        local.append(jnp.concatenate(flat + [jnp.zeros((1, width - 3 * values.shape[1]), F32)], axis=1))
    local_ref[...] = jnp.concatenate(local + [jnp.zeros((12, width), F32)], axis=0).astype(BF16)


def add_halves_body(me_ref, a_keep, a_came, b_keep, b_came, out_ref):
    size = a_keep.shape[0]
    out_ref[0:size, :] = (a_keep[...].astype(F32) + a_came[...].astype(F32)).astype(BF16)
    out_ref[size:, :] = (b_keep[...].astype(F32) + b_came[...].astype(F32)).astype(BF16)


def add_body(count, me_ref, *refs):
    total = refs[0][...].astype(F32)
    for ref in refs[1:count]:
        total = total + ref[...].astype(F32)
    refs[count][...] = total.astype(refs[count].dtype)


def small_out(total, outs):
    shared, local = total[0:16, :], total[16:32, :]
    for index in range(5):
        outs[index][0:1, :] = shared[index : index + 1, :]
        outs[index][1:2, :] = shared[index + 5 : index + 6, :]
    outs[5][...] = local[0:2, :]
    size = outs[6].shape[2]
    for layer in range(2):
        for j in range(3):
            outs[6][j, layer : layer + 1, :] = local[2 + layer : 3 + layer, j * size : (j + 1) * size]


def place_grad_body(block_len, me_ref, *refs):
    q_refs, grad_ref = refs[:4], refs[4]
    for k in range(4):
        grad_ref[rows(wrap4(me_ref[2] - k), block_len), :] = q_refs[k][0:block_len, :].astype(F32)


def place_output_body(block_len, me_ref, *refs):
    u_refs, (x_ref, ob_ref, db_ref, out_ref) = refs[:4], refs[4:]
    shift = ob_ref[1:2, :] + db_ref[1:2, :]
    me = me_ref[2]
    for ref, quarter in zip(u_refs, (me, me ^ 1, 3 - me, me ^ 2)):
        place = rows(quarter, block_len)
        out_ref[place, :] = x_ref[place, :] + ref[...].astype(F32) + shift


def chip_turn(shift):
    return [(2 * x + c, 2 * ((x + shift) % 4) + c) for x in range(4) for c in range(2)]


CORE_SWAP = [(i, i ^ 1) for i in range(8)]


def over_chips(pieces, beside=()):
    mine, beside = lax.optimization_barrier((over_x(pieces), beside))
    return mine + [swap_core(piece) for piece in mine], beside


def ring_turn(shift):
    return [(i, (i + shift) % 4) for i in range(4)]


def over_tensor(pieces):
    return [pieces[0]] + [lax.ppermute(pieces[k], "tensor", ring_turn(k)) for k in range(1, 4)]


def share_tensor(piece):
    return over_tensor([piece] * 4)


def over_dp(pieces):
    return [pieces[0]] + [lax.ppermute(pieces[k], "dp", ring_turn(k)) for k in range(1, 4)]


def over_x(pieces):
    return [pieces[0]] + [lax.ppermute(pieces[k], "ctx", chip_turn(k)) for k in range(1, 4)]


def swap_core(piece):
    return lax.ppermute(piece, "ctx", CORE_SWAP)


NEXT_PAIR = [(0, 1), (1, 0), (2, 3), (3, 2)]
WRAP_PAIR = [(0, 3), (3, 0), (1, 2), (2, 1)]


def both_ways(to_next, to_wrap, axis="dp"):
    return lax.ppermute(to_next, axis, NEXT_PAIR), lax.ppermute(to_wrap, axis, WRAP_PAIR)


def chips_of(pairs):
    return [(2 * a + c, 2 * b + c) for a, b in pairs for c in range(2)]


def along(axis):
    return ("ctx", chips_of) if axis == "x" else (axis, lambda pairs: pairs)


def spread_near(piece, axis):
    name, move = along(axis)
    return [piece] + [lax.ppermute(piece, name, move(pairs)) for pairs in (NEXT_PAIR, WRAP_PAIR)]


def spread_far(pieces, axis):
    name, move = along(axis)
    half = pieces[0].shape[0] // 2
    return pieces + [
        lax.ppermute(pieces[1][:half], name, move(WRAP_PAIR)),
        lax.ppermute(pieces[2][half:], name, move(NEXT_PAIR)),
    ]


def tie(first, second):
    return lax.optimization_barrier((first, second))


def after(values, token):
    return lax.optimization_barrier((values, token))[0]


def add_up(pieces):
    total = pieces[0].astype(F32)
    for piece in pieces[1:]:
        total = total + piece.astype(F32)
    return total


def on_device(
    inputs,
    segments,
    attn_gain,
    attn_shift,
    mlp_gain,
    mlp_shift,
    qkv_weight,
    qkv_bias,
    out_weight,
    out_bias,
    up_weight,
    up_bias,
    down_weight,
    down_bias,
    cotangent,
):
    seq_count, block_len, width = inputs.shape
    tokens = seq_count * block_len
    inner = qkv_weight.shape[3]
    hidden = up_weight.shape[2]
    length = block_len * 8
    chunk = 256
    place = lax.axis_index("ctx")
    me = jnp.stack([place // 2, place % 2, lax.axis_index("tensor"), lax.axis_index("dp")]).astype(jnp.int32)
    x0 = inputs.reshape(tokens, width)
    dy1 = cotangent.reshape(tokens, width)
    tok_shape = inputs.shape
    wide = shape_of((tokens, width), BF16)
    norms = (attn_gain, attn_shift, mlp_gain, mlp_shift)
    biases = qkv_bias.transpose(1, 0, 2)

    def project_first(x):
        sources = [x, segments, *norms, qkv_weight, biases]
        held = [v.shape for v in sources[:6]] + [qkv_weight.shape[1:], biases.shape]
        piece = shape_of((2, block_len + 16, 3 * LANES), BF16)
        return run(
            functools.partial(project_first_body, tok_shape),
            me,
            [(v, pl.BlockSpec(memory_space=pltpu.HBM)) for v in sources],
            [shape_of((block_len, width), F32), wide, wide] + [piece] * 4,
            scratch=[pltpu.VMEM((tokens, 3 * inner), F32)]
            + [pltpu.VMEM(size, v.dtype) for size, v in zip(held, sources)]
            + [pltpu.SemaphoreType.DMA((11,))],
            name="norm_project",
            limit=62,
        )

    def project(layer, x, extra):
        piece = shape_of((2, block_len, 3 * LANES), BF16)
        return run(
            functools.partial(project_body, layer, tok_shape),
            me,
            [x, segments, *extra, *norms]
            + [(qkv_weight, layer_spec(qkv_weight, layer)), biases],
            [shape_of((tokens, width), F32), shape_of((block_len, width), F32), wide, wide] + [piece] * 4,
            scratch=[pltpu.VMEM((tokens, 3 * inner), F32)],
            name="norm_project",
            limit=24,
        )

    def feed(layer, m):
        return run(
            functools.partial(feed_body, layer),
            me,
            [m, (up_weight, layer_spec(up_weight, layer)), up_bias, (down_weight, layer_spec(down_weight, layer))],
            [shape_of((tokens, hidden), BF16), shape_of((tokens, hidden), F32), shape_of((tokens, width), F32)],
            name="feed", limit=24,
        )

    def feed_back(layer, r, slope):
        return run(
            feed_back_body,
            me,
            [r, slope, (up_weight, layer_spec(up_weight, layer)), (down_weight, layer_spec(down_weight, layer))],
            [shape_of((tokens, hidden), BF16), shape_of((tokens, width), F32), shape_of((1, hidden), F32)],
            name="feed_back", limit=24,
        )

    def feed_both(layer, m, dy):
        return run(
            functools.partial(feed_both_body, layer),
            me,
            [m, dy, (up_weight, layer_spec(up_weight, layer)), up_bias, (down_weight, layer_spec(down_weight, layer))],
            [shape_of((tokens, hidden), BF16), wide, shape_of((tokens, hidden), BF16)]
            + [shape_of((tokens, width), F32), shape_of((1, hidden), F32)],
            name="feed_both", limit=24,
        )

    def combine(layer, pieces, part, active=None):
        fused = part is None
        got = run(
            functools.partial(combine_body, block_len, fused),
            me,
            [*pieces, (out_weight, layer_spec(out_weight, layer))]
            + ([active, (down_weight, layer_spec(down_weight, layer))] if fused else [part]),
            [shape_of((tokens, inner), BF16)] + [shape_of((block_len, width), BF16)] * 4,
            scratch=[pltpu.VMEM((tokens, width), BF16)],
            name="combine", limit=20,
        )
        return got[0], got[1:]

    def add_all(values, dtype=BF16):
        out = shape_of(values[0].shape, dtype)
        return run(functools.partial(add_body, len(values)), me, values, [out], name="add_all", limit=16)[0]

    def line_up(axis, values, size):
        extra = values[0].shape[0] - size
        small = [shape_of((extra, width), BF16)] if extra else []
        outs = [shape_of((4 * size, width), BF16)] + small
        return run(functools.partial(line_up_body, axis), me, values, outs, name="line_up", limit=8)

    seq_bf16 = pltpu.VMEM((length, LANES), BF16)
    seq_f32 = pltpu.VMEM((length, LANES), F32)
    o_shapes = [shape_of((2, block_len, LANES), BF16)] * 4

    def attend_both(pieces, grads, seg_rows, with_out):
        return run(
            functools.partial(attend_both_body, block_len, chunk, with_out),
            me,
            [*pieces, *grads, seg_rows],
            [shape_of((2, block_len, (4 if with_out else 3) * LANES), BF16)] * 4,
            scratch=([pltpu.VMEM((3, length, LANES), BF16)] if with_out else [])
            + [seq_bf16, pltpu.VMEM((2, LANES, length), BF16), seq_bf16]
            + [seq_f32] * 3,
            name="attend_both", limit=24,
        )

    def project_back(layer, pieces, dm, riders=()):
        got = run(
            functools.partial(project_back_body, block_len, layer),
            me,
            [*pieces, (qkv_weight, layer_spec(qkv_weight, layer)), dm, attn_gain, mlp_gain, *riders],
            [shape_of((tokens, 3 * inner), BF16), wide, shape_of((3, inner), F32)]
            + [shape_of((block_len * (2 if riders else 1), width), BF16)] * 4,
            scratch=[pltpu.VMEM((tokens, width), BF16)],
            name="project_back", limit=24,
        )
        return got[0], got[1], got[2], got[3:]

    def norm_back(pieces, x, dy, riders=()):
        quarter = shape_of((block_len, width), F32)
        low = shape_of((block_len + (16 if riders else 0), width), BF16)
        return run(
            norm_back_body,
            me,
            [add_up(pieces), x, dy, *riders],
            [quarter, low, shape_of((1, width), F32)],
            name="norm_back",
            limit=10,
        )

    def gains(x, da, dm):
        return run(gains_body, me, [x, da, dm], [shape_of((4, width), F32)], name="gains", limit=16)[0]

    half = width // 2
    columns = [[8 * z + 2 * chip + core for z in range(4) for chip in range(4)] for core in range(2)]

    def feed_weights(m, dh, active, r):
        pack = shape_of((2 * half, width), BF16)
        return run(feed_weights_body, me, [m, dh, active, r], [pack] * 2, name="feed_weights", limit=24)

    def head_weights(attn_in, dproj, attended, r):
        pack = shape_of((half, width), BF16)
        return run(head_weights_body, me, [attn_in, dproj, attended, r], [pack] * 2, name="head_weights", limit=20)

    x0_quarter, a0, m0, *pieces = project_first(x0)
    fed0 = feed(0, m0)
    pieces0, (active0, slope0, part0) = over_chips(pieces, fed0)
    got = run(
        functools.partial(attend_body, block_len, chunk),
        me,
        pieces0,
        [shape_of((8, length), F32), shape_of((3, length, LANES), BF16)] + o_shapes,
        scratch=[pltpu.VMEM((LANES, length), BF16), seq_bf16],
        name="attend", limit=20,
    )
    seg_rows, qkv0 = got[:2]
    out0, _ = over_chips(got[2:])
    attended0, u0 = combine(0, out0, part0)
    dy1_quarter, *grads1 = run(
        functools.partial(send_grad_body, block_len),
        me,
        [after(dy1, u0[0]), (out_weight, layer_spec(out_weight, 1))],
        [shape_of((block_len, width), F32)] + o_shapes,
        name="out_back", limit=14,
    )
    u0, grads1 = tie(over_tensor(u0), over_x(grads1))
    u0 = share_tensor(add_up(u0).astype(BF16))
    u0, grads1_other = tie(u0, [swap_core(piece) for piece in grads1])

    x1, x1_quarter, a1, m1, *pieces = project(1, x0, [*u0, out_bias, down_bias])
    fed1 = feed_both(1, m1, dy1)
    pieces1, (active1, r1, dh1, dm1, up_b1) = over_chips(pieces, fed1)
    got = attend_both(pieces1, grads1 + grads1_other, seg_rows, True)
    feed_pack1 = feed_weights(after(m1, got[0]), dh1, active1, r1)
    back1, feed_pack1 = over_chips(got, feed_pack1)
    dproj1, da1, qkv_b1, e1 = project_back(1, back1, dm1)
    back1, (feed_keep, feed_send) = after((back1, feed_pack1), e1[0])
    attended1, u1 = combine(1, back1, None, active1)
    head_keep, head_send = head_weights(a1, dproj1, attended1, r1)
    e1, (u1, head_keep, head_send, feed_came) = tie(over_tensor(e1), (u1, head_keep, head_send, swap_core(feed_send)))
    pack1 = run(
        add_packs_body,
        me,
        [feed_keep, feed_came, head_keep, swap_core(head_send)],
        [shape_of((3 * half, width), BF16)],
        name="add_packs",
        limit=16,
    )[0]
    part1 = lax.psum_scatter(pack1, ("dp", "ctx"), axis_index_groups=columns, tiled=True)
    dx1, low1, bias1 = norm_back(e1, x1_quarter, dy1_quarter)
    gains1 = gains(after(x1, low1), da1, dm1)
    quarters, gains1 = tie(share_tensor(low1), gains1)

    r0, *grads0 = run(
        functools.partial(join_body, block_len),
        me,
        [*quarters, (out_weight, layer_spec(out_weight, 0))],
        [wide] + o_shapes,
        name="join_out_back", limit=14,
    )
    ua_keep, ua_send, ub_keep, ub_send = after(u1, r0)
    ua_came, ub_came = both_ways(ua_send, ub_send, "tensor")
    dh0, dm0, up_b0 = feed_back(0, r0, slope0)
    grads0, (ua_came, ub_came, dh0, dm0, up_b0) = over_chips(grads0, (ua_came, ub_came, dh0, dm0, up_b0))
    back0 = attend_both([qkv0], grads0, seg_rows, False)
    m0_late, u_parts = after((m0, [ua_keep, ua_came, ub_keep, ub_came]), back0[0])
    feed_pack0 = feed_weights(m0_late, dh0, active0, r0)
    u_part = shape_of((block_len // 2, width), BF16)
    ua_keep, ua_send, ub_keep, ub_send = run(
        halve_again_body, me, u_parts, [u_part] * 4, name="halve_again", limit=10
    )
    ub_came, ua_came = both_ways(ub_send, ua_send, "tensor")
    back0, (feed_keep, feed_send, u1) = over_chips(back0, (*feed_pack0, [ua_keep, ua_came, ub_keep, ub_came]))
    dproj0, da0, qkv_b0, e0 = project_back(0, back0, dm0)
    head_keep, head_send = head_weights(a0, dproj0, attended0, r0)
    e0 = after(e0, head_keep)
    way = shape_of((3 * half // 4, width), BF16)
    a_keep, a_send, b_keep, b_send = run(
        halve_body,
        me,
        [feed_keep, swap_core(feed_send), head_keep, swap_core(head_send)],
        [way] * 4,
        scratch=[pltpu.VMEM((2 * half, width), BF16), pltpu.VMEM((half, width), BF16)],
        name="halve",
        limit=20,
    )
    gains0 = gains(after(x0, a_send), da0, dm0)
    a_came, b_came = both_ways(a_send, b_send)
    e0, (gains0, a_came, b_came) = tie(over_tensor(e0), (gains0, a_came, b_came))
    dx0, low0, bias0 = norm_back(e0, x0_quarter, dx1, (gains0, gains1, bias1))
    last = share_tensor(low0)
    way = shape_of((3 * half // 8, width), BF16)
    a_keep, a_send, b_keep, b_send = run(
        halve_again_body, me, after([a_keep, a_came, b_keep, b_came], low0), [way] * 4, name="halve_again", limit=10
    )
    b_came, a_came = both_ways(b_send, a_send)
    part1 = after(part1, a_send)
    pack1 = lax.all_gather(part1, ("dp", "ctx"), axis_index_groups=columns, tiled=True)
    (a_came, b_came), last = tie((a_came, b_came), last)
    local = run(
        pack_small_body,
        me,
        [qkv_b0, qkv_b1, up_b0, up_b1],
        [shape_of((16, width), BF16)],
        name="pack_small",
        limit=8,
    )[0]

    few = half // 32
    cut = run(
        merge_body,
        me,
        [a_keep, a_came, b_keep, b_came],
        [shape_of((6 * few, width), BF16)] * 4,
        scratch=[pltpu.VMEM((24 * few, width), BF16)],
        name="merge",
        limit=10,
    )
    u1 = run(
        add_halves_body, me, after(u1, cut[0]), [shape_of((block_len, width), BF16)], name="add_halves", limit=8
    )[0]
    input_grad = run(
        functools.partial(place_grad_body, block_len),
        me,
        after(last, cut[0]),
        [shape_of((tokens, width), F32)],
        name="place_grad",
        limit=12,
    )[0]
    cut, (u1, input_grad) = tie(over_x(cut), (spread_near(u1, "tensor"), input_grad))
    pieces = [shape_of((3 * few + 32, width), BF16), shape_of((3 * few, width), BF16)]
    first, second = run(settle_body, me, [*cut, *last, local], pieces, name="settle", limit=10)
    first, second = tie(over_x([first] * 4), over_dp([second] * 4))
    small = [piece[3 * few :].astype(F32) for piece in first]
    small = ((small[0] + small[2]) + (small[1] + small[3])).astype(BF16)
    first = jnp.concatenate([piece[: 3 * few] for piece in first] + [small], axis=0)
    second = jnp.concatenate(second, axis=0)
    near = (spread_near(first, "dp"), spread_near(second, "x"))

    u1 = after(u1, near[0][1])
    u1 = u1 + [lax.ppermute(u1[1], "tensor", WRAP_PAIR)]
    output = run(
        functools.partial(place_output_body, block_len),
        me,
        [*u1, x1, out_bias, down_bias],
        [shape_of((tokens, width), F32)],
        name="place_output",
        limit=16,
    )[0]
    heavy = [
        shape_of((2, width, hidden), F32),
        shape_of((2, hidden, width), F32),
        shape_of((2, 3, width, inner), F32),
        shape_of((2, inner, width), F32),
    ]
    pack1_came = swap_core(after(pack1, first))
    quarter = half // 4
    views = [(2, 2, half, width)] * 2 + [(2, 3, 2, half, inner), (2, 2, LANES, width)]
    first_outs = run(
        unpack_whole_body,
        me,
        [
            (pack, pl.BlockSpec((quarter, width), lambda i, *_, part=part: (4 * part + i, 0)))
            for pack in (pack1, pack1_came)
            for part in range(3)
        ],
        [shape_of(view, F32) for view in views],
        name="unpack_whole",
        limit=24,
        out_specs=[
            pl.BlockSpec((1, 2, quarter, width), lambda i, *_: (1, 0, i, 0)),
            pl.BlockSpec((1, 2, quarter, width), lambda i, *_: (1, 0, i, 0)),
            pl.BlockSpec((1, 3, 2, quarter, inner), lambda i, *_: (1, 0, 0, i, 0)),
            pl.BlockSpec((1, 2, LANES, 2 * LANES), lambda i, *_: (1, 0, 0, i)),
        ],
        grid=4,
    )
    first_outs = [v.reshape(like.shape) for v, like in zip(first_outs, heavy)]
    near, first_outs = tie(near, first_outs)
    far = (spread_far(near[0], "dp"), spread_far(near[1], "x"))
    other = [swap_core(v) for v in near[0] + near[1]]
    mine, (other, output) = tie(far[0] + far[1], (other, output))
    far = [swap_core(v) for v in mine[3:5] + mine[8:10]]
    other = other[0:3] + far[0:2] + other[3:6] + far[2:4]
    in_place = pl.BlockSpec(memory_space=pl.ANY)
    held = [pltpu.VMEM(v.shape[1:], F32) for v in heavy] + [pltpu.SemaphoreType.DMA((4,))]
    small_shapes = [shape_of((2, width), F32)] * 6 + [shape_of((3, 2, inner), F32)]
    up_grad, down_grad, qkv_grad, out_grad, *small = run(
        functools.partial(unpack_body, few),
        me,
        mine + other + [(v, in_place) for v in first_outs],
        heavy + small_shapes,
        name="unpack",
        limit=28,
        out_specs=[in_place] * 4 + [whole(v) for v in small_shapes],
        scratch=held,
        aliases={21 + index: index for index in range(4)},
    )
    return (
        output.reshape(tok_shape),
        input_grad.reshape(tok_shape),
        small[0],
        small[1],
        small[2],
        small[3],
        qkv_grad,
        small[6].transpose(1, 0, 2),
        out_grad,
        small[4],
        up_grad,
        small[5],
        down_grad,
        small[4],
    )


def solution(mesh):
    in_specs = (
        P("dp", "ctx", None),
        P("dp", "ctx"),
        P(),
        P(),
        P(),
        P(),
        P(None, None, None, "tensor"),
        P(None, None, "tensor"),
        P(None, "tensor", None),
        P(),
        P(None, None, "tensor"),
        P(None, "tensor"),
        P(None, "tensor", None),
        P(),
        P("dp", "ctx", None),
    )
    out_specs = (
        P("dp", "ctx", None),
        P("dp", "ctx", None),
        P(),
        P(),
        P(),
        P(),
        P(None, None, None, "tensor"),
        P(None, None, "tensor"),
        P(None, "tensor", None),
        P(),
        P(None, None, "tensor"),
        P(None, "tensor"),
        P(None, "tensor", None),
        P(),
    )
    return jax.shard_map(
        on_device, mesh=mesh, in_specs=in_specs, out_specs=out_specs, check_vma=False
    )
```

```python
import functools

import jax
import jax.numpy as jnp
from jax import lax
from jax.experimental import pallas as pl
from jax.experimental.pallas import tpu as pltpu
from jax.sharding import PartitionSpec as P

HEAD = 64
ROT = 16
LAYERS = 2
LANES = 128
F32 = jnp.float32
BF16 = jnp.bfloat16


def shape_of(shape, dtype):
    return jax.ShapeDtypeStruct(tuple(shape), dtype)


def whole(array):
    rank = array.ndim
    return pl.BlockSpec(array.shape, lambda i, *_: (0,) * rank, pipeline_mode=pl.Buffered(1))


def layer_spec(array, layer):
    rank = array.ndim
    return pl.BlockSpec(
        (1,) + array.shape[1:], lambda i, *_: (layer,) + (0,) * (rank - 1), pipeline_mode=pl.Buffered(1)
    )


def run(body, me, operands, outs, scratch=(), name=None, limit=32, out_specs=None, aliases=None, grid=1):
    arrays, specs = [], []
    for operand in operands:
        array, spec = operand if isinstance(operand, tuple) else (operand, None)
        arrays.append(array)
        specs.append(whole(array) if spec is None else spec)
    return pl.pallas_call(
        body,
        grid_spec=pltpu.PrefetchScalarGridSpec(
            num_scalar_prefetch=1,
            grid=(grid,),
            in_specs=specs,
            out_specs=[whole(o) for o in outs] if out_specs is None else out_specs,
            scratch_shapes=list(scratch),
        ),
        out_shape=list(outs),
        input_output_aliases=aliases or {},
        compiler_params=pltpu.CompilerParams(vmem_limit_bytes=limit * 1024 * 1024),
        cost_estimate=pl.CostEstimate(flops=1, bytes_accessed=1, transcendentals=0),
        name=name,
    )(me, *arrays)


def matmul(left, right):
    return jnp.dot(left, right, preferred_element_type=F32)


def matmul_nt(left, right):
    return lax.dot_general(left, right, (((1,), (1,)), ((), ())), preferred_element_type=F32)


def matmul_tn(left, right):
    return lax.dot_general(left, right, (((0,), (0,)), ((), ())), preferred_element_type=F32)


def normalize(values):
    average = jnp.mean(values, axis=-1, keepdims=True)
    centred = values - average
    factor = lax.rsqrt(jnp.mean(centred * centred, axis=-1, keepdims=True) + 1e-05)
    return centred * factor, factor


def wrap4(value):
    return lax.rem(value + 4, 4)


def rows(index, size):
    return pl.ds(pl.multiple_of(index * size, size), size)


def rotary_rows(place_row):
    count = place_row.shape[1]
    which = lax.broadcasted_iota(jnp.int32, (8, count), 0)
    frequency = jnp.zeros((8, count), F32)
    for index in range(8):
        frequency = jnp.where(which == index, 10000.0 ** (-2.0 * index / ROT), frequency)
    angles = frequency * place_row
    trig = jnp.concatenate([jnp.cos(angles), jnp.sin(angles)], axis=0)
    row = lax.broadcasted_iota(jnp.int32, (16, LANES), 0)
    lane = lax.broadcasted_iota(jnp.int32, (16, LANES), 1) & (HEAD - 1)
    same = (lane & 7) == (row & 7)
    is_cos = row < 8
    pick_cos = jnp.where(is_cos & same & (lane < 16), 1.0, 0.0)
    pick_low = jnp.where((row >= 8) & same & (lane < 8), 1.0, 0.0)
    pick_high = jnp.where((row >= 8) & same & (lane >= 8) & (lane < 16), 1.0, 0.0)
    picks = jnp.concatenate([pick_cos, pick_low, pick_high], axis=1).astype(F32)
    spread = lax.dot_general(
        trig, picks, (((0,), (0,)), ((), ())), preferred_element_type=F32, precision=lax.Precision.HIGHEST
    )
    lane_row = lax.broadcasted_iota(jnp.int32, (1, LANES), 1) & (HEAD - 1)
    cos_table = spread[:, :LANES] + jnp.where(lane_row >= ROT, 1.0, 0.0)
    return cos_table, spread[:, LANES : 2 * LANES], spread[:, 2 * LANES :]


def rotate(values, tables, back=False):
    cos_table, low_sin, high_sin = tables
    below = pltpu.roll(values, LANES - ROT // 2, 1) * low_sin
    above = pltpu.roll(values, ROT // 2, 1) * high_sin
    turned = below - above if back else above - below
    return values * cos_table + turned


def project_rows(layer, tok_shape, me_ref, seg_ref, weight, bias, a_ref, p_refs, proj_ref, with_seg):
    seq_count, block_len, width = tok_shape
    chip, core = me_ref[0], me_ref[1]
    base = (chip * 2 + core) * block_len
    for j in range(3):
        proj_ref[:, j * 2 * LANES : (j + 1) * 2 * LANES] = matmul(a_ref[...], weight(j)) + bias[j, layer : layer + 1, :]
    for k in range(4):
        seq = wrap4(chip + k)
        place = rows(seq, block_len)
        seg_row = seg_ref[pl.ds(seq, 1), :]
        spots = lax.broadcasted_iota(jnp.int32, (1, block_len), 1) + base
        tables = rotary_rows((spots - seg_row).astype(F32))
        for j in range(3):
            for pair in range(2):
                at = (2 * j + pair) * LANES
                part = proj_ref[place, at : at + LANES]
                if j < 2:
                    part = rotate(part, tables)
                p_refs[k][pair, 0:block_len, j * LANES : (j + 1) * LANES] = part.astype(BF16)
        if with_seg:
            coded = seg_row.astype(F32)
            high = jnp.floor(coded * 0.125)
            packed = jnp.concatenate([high, coded - 8.0 * high, jnp.zeros_like(high)], axis=1)
            packed = jnp.broadcast_to(packed, (16, 3 * LANES)).astype(BF16)
            for pair in range(2):
                p_refs[k][pair, block_len : block_len + 16, :] = packed


def project_first_body(tok_shape, me_ref, *refs):
    seq_count, block_len, width = tok_shape
    in_refs, refs = refs[:8], refs[8:]
    xq_ref, a_ref, m_ref, *p_refs = refs[:7]
    proj_ref, *held, sems = refs[7:]
    x_ref, seg_ref, ag_ref, as_ref, mg_ref, ms_ref, w_ref, b_ref = held
    copies = []
    for index in (1, 2, 3, 4, 5):
        copies.append(pltpu.make_async_copy(in_refs[index], held[index], sems.at[len(copies)]))
    copies.append(pltpu.make_async_copy(in_refs[7], b_ref, sems.at[len(copies)]))
    small_count = len(copies)
    for seq in range(seq_count):
        place = pl.ds(seq * block_len, block_len)
        copies.append(pltpu.make_async_copy(in_refs[0].at[place], x_ref.at[place], sems.at[len(copies)]))
    copies.append(pltpu.make_async_copy(in_refs[6].at[0], w_ref, sems.at[len(copies)]))
    for copy in copies:
        copy.start()
    for copy in copies[:small_count]:
        copy.wait()
    for seq in range(seq_count):
        copies[small_count + seq].wait()
        place = slice(seq * block_len, (seq + 1) * block_len)
        normed, _ = normalize(x_ref[place, :])
        a_ref[place, :] = (normed * ag_ref[0:1, :] + as_ref[0:1, :]).astype(BF16)
        m_ref[place, :] = (normed * mg_ref[0:1, :] + ms_ref[0:1, :]).astype(BF16)
    xq_ref[...] = x_ref[rows(me_ref[2], block_len), :]
    copies[-1].wait()
    project_rows(0, tok_shape, me_ref, seg_ref, lambda j: w_ref[j], b_ref, a_ref, p_refs, proj_ref, True)


def project_body(layer, tok_shape, me_ref, *refs):
    seq_count, block_len, width = tok_shape
    x_ref, seg_ref, *refs = refs
    u_refs, refs = refs[:4], refs[4:]
    ob_ref, db_ref, ag_ref, as_ref, mg_ref, ms_ref, w_ref, b_ref, x_out, xq_ref, a_ref, m_ref, *p_refs, proj_ref = refs
    tensor = me_ref[2]
    shift = ob_ref[layer - 1 : layer, :] + db_ref[layer - 1 : layer, :]
    for k in range(4):
        place = rows(wrap4(tensor - k), block_len)
        value = x_ref[place, :] + u_refs[k][...].astype(F32) + shift
        x_out[place, :] = value
        if k == 0:
            xq_ref[...] = value
        normed, _ = normalize(value)
        a_ref[place, :] = (normed * ag_ref[layer : layer + 1, :] + as_ref[layer : layer + 1, :]).astype(BF16)
        m_ref[place, :] = (normed * mg_ref[layer : layer + 1, :] + ms_ref[layer : layer + 1, :]).astype(BF16)
    project_rows(layer, tok_shape, me_ref, seg_ref, lambda j: w_ref[0, j], b_ref, a_ref, p_refs, proj_ref, False)


def gather_pieces(me_ref, refs, targets, block_len, seg_target=None):
    chip, core = me_ref[0], me_ref[1]
    for k in range(4):
        owner = wrap4(chip - k)
        for side, ref in ((core, refs[k]), (1 - core, refs[4 + k])):
            place = rows(owner * 2 + side, block_len)
            for index, target in enumerate(targets):
                target[place, :] = ref[core, 0:block_len, index * LANES : (index + 1) * LANES]
            if seg_target is not None:
                row = ref[core, block_len : block_len + 16, :].astype(F32)[0:1, :]
                starts = row[:, 0:LANES] * 8.0 + row[:, LANES : 2 * LANES]
                seg_target[:, place] = jnp.broadcast_to(starts, (8, block_len))


def head_stack(values):
    lane = lax.broadcasted_iota(jnp.int32, values.shape, 1)
    zero = jnp.zeros_like(values)
    return jnp.concatenate(
        [jnp.where(lane < HEAD, values, zero), jnp.where(lane >= HEAD, values, zero)], axis=0
    )


def own_halves(product, width):
    return jnp.concatenate([product[0:HEAD, 0:width], product[HEAD:, width : 2 * width]], axis=0)


def chances_t(q_ref, k_ref, seg_ref, step, chunk):
    start, keys = step * chunk, (step + 1) * chunk
    stacked = head_stack(q_ref[start:keys, :]) * jnp.asarray(HEAD ** (-0.5), BF16)
    scores = matmul_nt(k_ref[0:keys, :], stacked)
    key_place = lax.broadcasted_iota(jnp.int32, (keys, 2 * chunk), 0).astype(F32)
    query_place = (lax.broadcasted_iota(jnp.int32, (1, 2 * chunk), 1) & (chunk - 1)).astype(F32) + start
    seg_row = seg_ref[0:1, start:keys]
    seg_row = jnp.concatenate([seg_row, seg_row], axis=1)
    allowed = (key_place >= seg_row) & (key_place <= query_place)
    scores = jnp.where(allowed, scores, -1e30)
    raised = jnp.exp(scores - jnp.max(scores, axis=0, keepdims=True))
    total = jnp.sum(raised, axis=0, keepdims=True)
    return raised * (1.0 / total), stacked


def attend_body(block_len, chunk, me_ref, *refs):
    piece_refs, refs = refs[:8], refs[8:]
    seg_out, qkv_ref, *refs = refs
    o_refs, refs = refs[:4], refs[4:]
    vt_ref, o_ref = refs
    q_ref, k_ref, v_ref = qkv_ref.at[0], qkv_ref.at[1], qkv_ref.at[2]
    gather_pieces(me_ref, piece_refs, (q_ref, k_ref, v_ref), block_len, seg_out)
    vt_ref[...] = v_ref[...].T
    length = q_ref.shape[0]
    for step in range(length // chunk):
        keys = (step + 1) * chunk
        chances, _ = chances_t(q_ref, k_ref, seg_out, step, chunk)
        mixed = matmul(vt_ref[:, 0:keys], chances.astype(BF16))
        o_ref[step * chunk : keys, :] = own_halves(mixed, chunk).T.astype(BF16)
    send_blocks(me_ref, o_ref, o_refs, block_len)


def send_blocks(me_ref, source, targets, block_len):
    chip = me_ref[0]
    for k in range(4):
        dest = wrap4(chip + k)
        for side in range(2):
            targets[k][side] = source[rows(dest * 2 + side, block_len), :]


def attend_both_body(block_len, chunk, with_out, me_ref, *refs):
    if with_out:
        piece_refs, refs = refs[:8], refs[8:]
    else:
        qkv_ref, *refs = refs
    grad_refs, refs = refs[:8], refs[8:]
    seg_ref, *refs = refs
    d_refs, refs = refs[:4], refs[4:]
    if with_out:
        qkv_ref, *refs = refs
    q_ref, k_ref, v_ref = qkv_ref.at[0], qkv_ref.at[1], qkv_ref.at[2]
    g_ref, t_ref, o_ref, dq_ref, dk_ref, dv_ref = refs
    if with_out:
        gather_pieces(me_ref, piece_refs, (q_ref, k_ref, v_ref), block_len)
    gather_pieces(me_ref, grad_refs, (g_ref,), block_len)
    length = q_ref.shape[0]
    t_ref[0] = k_ref[...].T
    if with_out:
        t_ref[1] = v_ref[...].T
    dk_ref[...] = jnp.zeros_like(dk_ref)
    dv_ref[...] = jnp.zeros_like(dv_ref)
    for step in range(length // chunk):
        start, keys = step * chunk, (step + 1) * chunk
        chances, stacked = chances_t(q_ref, k_ref, seg_ref, step, chunk)
        low = chances.astype(BF16)
        if with_out:
            mixed = matmul(t_ref[1, :, 0:keys], low)
            o_ref[start:keys, :] = own_halves(mixed, chunk).T.astype(BF16)
        grads = head_stack(g_ref[start:keys, :])
        chance_grad = matmul_nt(v_ref[0:keys, :], grads)
        delta = jnp.sum(chances * chance_grad, axis=0, keepdims=True)
        score_grad = (chances * (chance_grad - delta)).astype(BF16)
        dv_ref[0:keys, :] += matmul(low, grads)
        dk_ref[0:keys, :] += matmul(score_grad, stacked)
        query = matmul(t_ref[0, :, 0:keys], score_grad)
        dq_ref[start:keys, :] = own_halves(query, chunk).T * HEAD ** (-0.5)
    chip = me_ref[0]
    for k in range(4):
        dest = wrap4(chip + k)
        for side in range(2):
            place = rows(dest * 2 + side, block_len)
            spots = (lax.broadcasted_iota(jnp.int32, (1, block_len), 1) + (dest * 2 + side) * block_len).astype(F32)
            tables = rotary_rows(spots - seg_ref[0:1, place])
            d_refs[k][side, :, 0:LANES] = rotate(dq_ref[place, :], tables, True).astype(BF16)
            d_refs[k][side, :, LANES : 2 * LANES] = rotate(dk_ref[place, :], tables, True).astype(BF16)
            d_refs[k][side, :, 2 * LANES : 3 * LANES] = dv_ref[place, :].astype(BF16)
            if with_out:
                d_refs[k][side, :, 3 * LANES :] = o_ref[place, :]


def land_heads(me_ref, refs, target, block_len, groups, first=0):
    chip, core = me_ref[0], me_ref[1]
    for k in range(4):
        place = rows(wrap4(chip - k), block_len)
        mine, other = refs[k][core], refs[4 + k][core]
        is_low = core == 0
        for group in range(groups):
            span = slice((first + group) * LANES, (first + group + 1) * LANES)
            at = group * 2 * LANES
            target[place, at : at + LANES] = jnp.where(is_low, mine[:, span], other[:, span])
            target[place, at + LANES : at + 2 * LANES] = jnp.where(is_low, other[:, span], mine[:, span])


def combine_body(block_len, fused, me_ref, *refs):
    piece_refs, refs = refs[:8], refs[8:]
    w_ref, *refs = refs
    if fused:
        g_ref, down_ref, *refs = refs
    else:
        part_ref, *refs = refs
    o_ref, *refs = refs
    q_refs, scr = refs[:-1], refs[-1]
    tensor = me_ref[2]
    land_heads(me_ref, piece_refs, o_ref, block_len, 1, 3 if fused else 0)
    part = matmul(g_ref[...], down_ref[0]) if fused else part_ref[...]
    scr[...] = (matmul(o_ref[...], w_ref[0]) + part).astype(BF16)
    if fused:
        near, far = near_far(tensor)
        size = block_len // 2
        orders = ((tensor, far), (near, 3 - near), (tensor, near), (far, far ^ 1))
        for way, (ref, order) in enumerate(zip(q_refs, orders)):
            for index, quarter in enumerate(order):
                at = pl.multiple_of(quarter * block_len + (way >> 1) * size, size)
                ref[index * size : (index + 1) * size, :] = scr[pl.ds(at, size), :]
        return
    for k in range(4):
        q_refs[k][...] = scr[rows(wrap4(tensor + k), block_len), :]


def send_grad_body(block_len, me_ref, x_ref, w_ref, *refs):
    chip, tensor = me_ref[0], me_ref[2]
    quarter_ref, *refs = refs
    quarter_ref[...] = x_ref[rows(tensor, block_len), :]
    for k in range(4):
        value = x_ref[rows(wrap4(chip + k), block_len), :].astype(BF16)
        grad = matmul_nt(value, w_ref[0]).astype(BF16)
        for pair in range(2):
            refs[k][pair] = grad[:, pair * LANES : (pair + 1) * LANES]


def join_body(block_len, me_ref, *refs):
    q_refs, refs = refs[:4], refs[4:]
    w_ref, r_ref, *g_refs = refs
    chip, tensor = me_ref[0], me_ref[2]
    for k in range(4):
        r_ref[rows(wrap4(tensor - k), block_len), :] = q_refs[k][...]
    for k in range(4):
        value = r_ref[rows(wrap4(chip + k), block_len), :]
        grad = matmul_nt(value, w_ref[0]).astype(BF16)
        for pair in range(2):
            g_refs[k][pair] = grad[:, pair * LANES : (pair + 1) * LANES]


def project_back_body(block_len, layer, me_ref, *refs):
    piece_refs, refs = refs[:8], refs[8:]
    w_ref, dm_ref, ag_ref, mg_ref, *refs = refs
    riders, refs = refs[:-8], refs[-8:]
    dp_ref, da_ref, bias_ref, *q_refs, scr = refs
    tensor = me_ref[2]
    land_heads(me_ref, piece_refs, dp_ref, block_len, 3)
    for j in range(3):
        span = slice(j * 2 * LANES, (j + 1) * 2 * LANES)
        bias_ref[j : j + 1, :] = jnp.sum(dp_ref[:, span].astype(F32), axis=0, keepdims=True)
    total = None
    for j in range(3):
        term = matmul_nt(dp_ref[:, j * 2 * LANES : (j + 1) * 2 * LANES], w_ref[0, j])
        total = term if total is None else total + term
    da_ref[...] = total.astype(BF16)
    scr[...] = (total * ag_ref[layer : layer + 1, :] + dm_ref[...] * mg_ref[layer : layer + 1, :]).astype(BF16)
    for k in range(4):
        q_refs[k][0:block_len, :] = scr[rows(wrap4(tensor + k), block_len), :]
        if riders:
            q_refs[k][block_len:, :] = riders[k][...]


def norm_back_body(me_ref, *refs):
    e_ref, x_ref, dy_ref, *gain_refs, dx_ref, low_ref, bias_ref = refs
    upstream = dy_ref[...]
    size = upstream.shape[0]
    total = e_ref[0:size, :]
    normed, factor = normalize(x_ref[...])
    inner = jnp.mean(total * normed, axis=-1, keepdims=True)
    result = upstream + factor * (total - jnp.mean(total, axis=-1, keepdims=True) - normed * inner)
    dx_ref[...] = result
    low_ref[0:size, :] = result.astype(BF16)
    bias = jnp.sum(upstream, axis=0, keepdims=True)
    bias_ref[...] = bias
    if gain_refs:
        mine, other, other_bias = gain_refs
        blank = jnp.zeros((6, bias.shape[1]), F32)
        rows_here = jnp.concatenate([mine[...], bias, other[...], other_bias[...], blank], axis=0)
        low_ref[size:, :] = rows_here.astype(BF16)


def gains_body(me_ref, x_ref, da_ref, dm_ref, out_ref):
    normed, _ = normalize(x_ref[...])
    da = da_ref[...].astype(F32)
    dm = dm_ref[...]
    out_ref[0:1, :] = jnp.sum(da * normed, axis=0, keepdims=True)
    out_ref[1:2, :] = jnp.sum(da, axis=0, keepdims=True)
    out_ref[2:3, :] = jnp.sum(dm * normed, axis=0, keepdims=True)
    out_ref[3:4, :] = jnp.sum(dm, axis=0, keepdims=True)


def gelu_parts(hidden):
    cdf = 0.5 * (1.0 + lax.erf(hidden * (0.5**0.5)))
    density = jnp.exp(-0.5 * hidden * hidden) * 0.3989422804014327
    return cdf, density


def feed_body(layer, me_ref, m_ref, up_ref, ub_ref, down_ref, g_ref, slope_ref, part_ref):
    size = 2 * LANES
    for step in range(up_ref.shape[2] // size):
        span = slice(step * size, (step + 1) * size)
        hidden = matmul(m_ref[...], up_ref[0, :, span]) + ub_ref[layer : layer + 1, span]
        cdf, density = gelu_parts(hidden)
        g_ref[:, span] = (hidden * cdf).astype(BF16)
        slope_ref[:, span] = cdf + hidden * density
    part_ref[...] = matmul(g_ref[...], down_ref[0])


def feed_back_body(me_ref, r_ref, slope_ref, up_ref, down_ref, dh_ref, dm_ref, bias_ref):
    size = 2 * LANES
    for step in range(down_ref.shape[1] // size):
        span = slice(step * size, (step + 1) * size)
        grad = matmul_nt(r_ref[...], down_ref[0, span, :]) * slope_ref[:, span]
        bias_ref[:, span] = jnp.sum(grad, axis=0, keepdims=True)
        dh_ref[:, span] = grad.astype(BF16)
    dm_ref[...] = matmul_nt(dh_ref[...], up_ref[0])


def feed_both_body(layer, me_ref, m_ref, dy_ref, up_ref, ub_ref, down_ref, g_ref, r_ref, dh_ref, dm_ref, bias_ref):
    size = 2 * LANES
    r_ref[...] = dy_ref[...].astype(BF16)
    for step in range(up_ref.shape[2] // size):
        span = slice(step * size, (step + 1) * size)
        hidden = matmul(m_ref[...], up_ref[0, :, span]) + ub_ref[layer : layer + 1, span]
        cdf, density = gelu_parts(hidden)
        g_ref[:, span] = (hidden * cdf).astype(BF16)
        grad = matmul_nt(r_ref[...], down_ref[0, span, :]) * (cdf + hidden * density)
        bias_ref[:, span] = jnp.sum(grad, axis=0, keepdims=True)
        dh_ref[:, span] = grad.astype(BF16)
    dm_ref[...] = matmul_nt(dh_ref[...], up_ref[0])


def feed_weights_body(me_ref, m_ref, dh_ref, g_ref, r_ref, keep_ref, send_ref):
    core = me_ref[1]
    half = m_ref.shape[1] // 2
    for side, out in ((core, keep_ref), (1 - core, send_ref)):
        out[0:half, :] = matmul_tn(m_ref[:, rows(side, half)], dh_ref[...]).astype(BF16)
        out[half:, :] = matmul_tn(g_ref[:, rows(side, half)], r_ref[...]).astype(BF16)


def head_weights_body(me_ref, a_ref, dp_ref, o_ref, r_ref, keep_ref, send_ref):
    core = me_ref[1]
    half = a_ref.shape[1] // 2
    wide = dp_ref.shape[1]
    for side, out in ((core, keep_ref), (1 - core, send_ref)):
        out[:, 0:wide] = matmul_tn(a_ref[:, rows(side, half)], dp_ref[...]).astype(BF16)
        grad = matmul_tn(o_ref[:, rows(side, LANES)], r_ref[...]).astype(BF16)
        for part in range(4):
            out[part * LANES : (part + 1) * LANES, wide:] = grad[:, part * 2 * LANES : (part + 1) * 2 * LANES]


def feed_weights_whole_body(me_ref, m_ref, dh_ref, g_ref, r_ref, pack_ref):
    high = m_ref.shape[1]
    pack_ref[0:high, :] = matmul_tn(m_ref[...], dh_ref[...]).astype(BF16)
    pack_ref[high:, :] = matmul_tn(g_ref[...], r_ref[...]).astype(BF16)


def head_weights_whole_body(me_ref, a_ref, dp_ref, o_ref, r_ref, before_ref, pack_ref):
    wide = dp_ref.shape[1]
    pack_ref[:, 0:wide] = matmul_tn(a_ref[...], dp_ref[...]).astype(BF16)
    grad = matmul_tn(o_ref[...], r_ref[...]).astype(BF16)
    high, size = grad.shape[0], 2 * LANES
    for part in range(4):
        pack_ref[part * high : (part + 1) * high, wide:] = grad[:, part * size : (part + 1) * size]


def near_far(place):
    return place ^ 1, 3 - place


def halve_body(me_ref, feed_keep, feed_came, head_keep, head_came, *refs):
    outs, feed_scr, head_scr = refs[:4], refs[4], refs[5]
    feed_scr[...] = (feed_keep[...].astype(F32) + feed_came[...].astype(F32)).astype(BF16)
    head_scr[...] = (head_keep[...].astype(F32) + head_came[...].astype(F32)).astype(BF16)
    place = me_ref[3]
    near, far = near_far(place)
    half = head_scr.shape[0]
    size = half // 8
    orders = ((place, far), (near, 3 - near), (4 + place, 4 + near), (4 + far, 4 + (far ^ 1)))
    for ref, order in zip(outs, orders):
        for index, block in enumerate(order):
            at = 3 * size * index
            ref[at : at + size, :] = feed_scr[rows(block, size), :]
            ref[at + size : at + 2 * size, :] = feed_scr[pl.ds(pl.multiple_of(half + block * size, size), size), :]
            ref[at + 2 * size : at + 3 * size, :] = head_scr[rows(block, size), :]


def halve_again_body(me_ref, a_keep, a_came, b_keep, b_came, *outs):
    size = outs[0].shape[0]
    for keep, came, mine, send in ((a_keep, a_came, outs[0], outs[1]), (b_keep, b_came, outs[2], outs[3])):
        total = (keep[...].astype(F32) + came[...].astype(F32)).astype(BF16)
        mine[...] = total[0:size, :]
        send[...] = total[size:, :]


def line_up_body(axis, me_ref, *refs):
    size = refs[4].shape[0] // 4
    for k in range(4):
        refs[4][rows(wrap4(me_ref[axis] - k), size), :] = refs[k][0:size, :]
    if len(refs) > 5:
        even = refs[0][size:, :].astype(F32) + refs[2][size:, :].astype(F32)
        odd = refs[1][size:, :].astype(F32) + refs[3][size:, :].astype(F32)
        refs[5][...] = (even + odd).astype(BF16)


def merge_body(me_ref, a_keep, a_came, b_keep, b_came, *refs):
    out_refs, scr = refs[:4], refs[4]
    high = a_keep.shape[0]
    scr[0:high, :] = (a_keep[...].astype(F32) + a_came[...].astype(F32)).astype(BF16)
    scr[high:, :] = (b_keep[...].astype(F32) + b_came[...].astype(F32)).astype(BF16)
    few = high // 6
    for k in range(4):
        part = wrap4(me_ref[0] + k)
        for weight in range(3):
            at = pl.multiple_of((part >> 1) * high + weight * 2 * few + (part & 1) * few, few)
            out_refs[k][weight * few : (weight + 1) * few, :] = scr[pl.ds(at, few), :]


def settle_body(me_ref, *refs):
    in_refs, last_refs, local_ref, (first_ref, second_ref) = refs[:4], refs[4:8], refs[8], refs[9:]
    total = in_refs[0][...].astype(F32)
    for ref in in_refs[1:]:
        total = total + ref[...].astype(F32)
    total = total.astype(BF16)
    few = second_ref.shape[0] // 3
    for weight in range(3):
        for index, ref in enumerate((first_ref, second_ref)):
            at = (2 * weight + index) * few
            ref[weight * few : (weight + 1) * few, :] = total[at : at + few, :]
    count = local_ref.shape[0]
    shared = [ref[ref.shape[0] - count :, :].astype(F32) for ref in last_refs]
    shared = ((shared[0] + shared[2]) + (shared[1] + shared[3])).astype(BF16)
    first_ref[3 * few : 3 * few + count, :] = shared
    first_ref[3 * few + count :, :] = local_ref[...]


def flush(held, outs, layer, sems):
    copies = [pltpu.make_async_copy(a, b.at[layer], sems.at[i]) for i, (a, b) in enumerate(zip(held, outs))]
    return copies


def unpack_body(few, me_ref, *refs):
    outs, small_outs, held, sems = refs[24:28], refs[28:36], refs[36:40], refs[40]
    up_ref, down_ref, qkv_ref, out_ref = held
    copies = flush(held, outs, 0, sems)
    chip, core, place_z = me_ref[0], me_ref[1], me_ref[3]
    size = 2 * LANES
    half = up_ref.shape[0] // 2
    for weight in range(3):
        for side, group in ((core, refs[:10]), (1 - core, refs[10:20])):
            for along, me in ((0, place_z), (1, chip)):
                pieces = group[5 * along : 5 * along + 5]
                cut = pieces[3].shape[0] // few
                spans = [(pieces[0], me, 0, 12), (pieces[1], me ^ 1, 0, 12), (pieces[2], 3 - me, 0, 12)]
                spans += [(pieces[3], me ^ 2, 0, cut), (pieces[4], me ^ 2, cut, 12)]
                for ref, owner, first, stop in spans:
                    for index in range(first, stop):
                        if index % 3 != weight:
                            continue
                        z, x = (owner, wrap4(chip - index // 3)) if along == 0 else (wrap4(place_z - index // 3), owner)
                        start = (index - first) * few
                        value = ref[start : start + few, :].astype(F32)
                        row = (z + 4 * (x >> 1)) * (4 * few) + (x & 1) * (2 * few) + along * few
                        place = pl.ds(pl.multiple_of(row + side * half, few), few)
                        if weight < 2:
                            held[weight][place, :] = value
                        else:
                            for j in range(3):
                                qkv_ref[j, place, :] = value[:, j * size : (j + 1) * size]
                            inner = pl.ds(pl.multiple_of((row & (LANES - 1)) + side * LANES, few), few)
                            lanes = pl.ds(pl.multiple_of((row >> 7) * size, size), size)
                            out_ref[inner, lanes] = value[:, 3 * size :]
        for copy in copies[weight : weight + 1] if weight < 2 else copies[2:]:
            copy.start()
    parts = []
    for group in (refs[:10], refs[10:20]):
        count = group[0].shape[0] - 12 * few
        rows_of = [ref[ref.shape[0] - count :, :].astype(F32) for ref in (group[0], group[4], group[1], group[2])]
        parts.append((rows_of[0] + rows_of[1]) + (rows_of[2] + rows_of[3]))
    small_out(parts[0] + parts[1], small_outs)
    for copy in copies:
        copy.wait()


def add_packs_body(me_ref, feed_keep, feed_came, head_keep, head_came, out_ref):
    high = feed_keep.shape[0]
    out_ref[0:high, :] = (feed_keep[...].astype(F32) + feed_came[...].astype(F32)).astype(BF16)
    out_ref[high:, :] = (head_keep[...].astype(F32) + head_came[...].astype(F32)).astype(BF16)


def unpack_whole_body(me_ref, up_mine, down_mine, head_mine, up_other, down_other, head_other, *outs):
    up_ref, down_ref, qkv_ref, out_ref = outs
    size = 2 * LANES
    for core in range(2):
        mine = me_ref[1] == core
        for ref, first, second in ((up_ref, up_mine, up_other), (down_ref, down_mine, down_other)):
            ref[0, core] = jnp.where(mine, first[...], second[...]).astype(F32)
        head = jnp.where(mine, head_mine[...], head_other[...]).astype(F32)
        for j in range(3):
            qkv_ref[0, j, core] = head[:, j * size : (j + 1) * size]
        out_ref[0, core] = head[:, 3 * size :]


def pack_small_body(me_ref, *refs):
    ins, local_ref = refs[:4], refs[4]
    width = local_ref.shape[1]
    local = [ins[2][...], ins[3][...]]
    for ref in ins[0:2]:
        values = ref[...]
        flat = [values[j : j + 1, :] for j in range(3)]
        local.append(jnp.concatenate(flat + [jnp.zeros((1, width - 3 * values.shape[1]), F32)], axis=1))
    local_ref[...] = jnp.concatenate(local + [jnp.zeros((12, width), F32)], axis=0).astype(BF16)


def add_halves_body(me_ref, a_keep, a_came, b_keep, b_came, out_ref):
    size = a_keep.shape[0]
    out_ref[0:size, :] = (a_keep[...].astype(F32) + a_came[...].astype(F32)).astype(BF16)
    out_ref[size:, :] = (b_keep[...].astype(F32) + b_came[...].astype(F32)).astype(BF16)


def add_body(count, me_ref, *refs):
    total = refs[0][...].astype(F32)
    for ref in refs[1:count]:
        total = total + ref[...].astype(F32)
    refs[count][...] = total.astype(refs[count].dtype)


def small_out(total, outs):
    shared, local = total[0:16, :], total[16:32, :]
    for index in range(5):
        outs[index][0:1, :] = shared[index : index + 1, :]
        outs[index][1:2, :] = shared[index + 5 : index + 6, :]
    outs[7][...] = outs[4][...]
    outs[5][...] = local[0:2, :]
    size = outs[6].shape[2]
    for layer in range(2):
        for j in range(3):
            outs[6][j, layer : layer + 1, :] = local[2 + layer : 3 + layer, j * size : (j + 1) * size]


def place_grad_body(block_len, me_ref, *refs):
    q_refs, grad_ref = refs[:4], refs[4]
    for k in range(4):
        grad_ref[rows(wrap4(me_ref[2] - k), block_len), :] = q_refs[k][0:block_len, :].astype(F32)


def place_output_body(block_len, me_ref, *refs):
    u_refs, (x_ref, ob_ref, db_ref, out_ref) = refs[:4], refs[4:]
    shift = ob_ref[1:2, :] + db_ref[1:2, :]
    me = me_ref[2]
    for ref, quarter in zip(u_refs, (me, me ^ 1, 3 - me, me ^ 2)):
        place = rows(quarter, block_len)
        out_ref[place, :] = x_ref[place, :] + ref[...].astype(F32) + shift


def chip_turn(shift):
    return [(2 * x + c, 2 * ((x + shift) % 4) + c) for x in range(4) for c in range(2)]


CORE_SWAP = [(i, i ^ 1) for i in range(8)]


def over_chips(pieces, beside=()):
    mine, beside = lax.optimization_barrier((over_x(pieces), beside))
    return mine + [swap_core(piece) for piece in mine], beside


def ring_turn(shift):
    return [(i, (i + shift) % 4) for i in range(4)]


def over_tensor(pieces):
    return [pieces[0]] + [lax.ppermute(pieces[k], "tensor", ring_turn(k)) for k in range(1, 4)]


def share_tensor(piece):
    return over_tensor([piece] * 4)


def over_dp(pieces):
    return [pieces[0]] + [lax.ppermute(pieces[k], "dp", ring_turn(k)) for k in range(1, 4)]


def over_x(pieces):
    return [pieces[0]] + [lax.ppermute(pieces[k], "ctx", chip_turn(k)) for k in range(1, 4)]


def swap_core(piece):
    return lax.ppermute(piece, "ctx", CORE_SWAP)


NEXT_PAIR = [(0, 1), (1, 0), (2, 3), (3, 2)]
WRAP_PAIR = [(0, 3), (3, 0), (1, 2), (2, 1)]


def both_ways(to_next, to_wrap, axis="dp"):
    return lax.ppermute(to_next, axis, NEXT_PAIR), lax.ppermute(to_wrap, axis, WRAP_PAIR)


def chips_of(pairs):
    return [(2 * a + c, 2 * b + c) for a, b in pairs for c in range(2)]


def along(axis):
    return ("ctx", chips_of) if axis == "x" else (axis, lambda pairs: pairs)


def spread_near(piece, axis):
    name, move = along(axis)
    return [piece] + [lax.ppermute(piece, name, move(pairs)) for pairs in (NEXT_PAIR, WRAP_PAIR)]


def spread_far(pieces, axis):
    name, move = along(axis)
    half = pieces[0].shape[0] // 2
    return pieces + [
        lax.ppermute(pieces[1][:half], name, move(WRAP_PAIR)),
        lax.ppermute(pieces[2][half:], name, move(NEXT_PAIR)),
    ]


def tie(first, second):
    return lax.optimization_barrier((first, second))


def after(values, token):
    return lax.optimization_barrier((values, token))[0]


def add_up(pieces):
    total = pieces[0].astype(F32)
    for piece in pieces[1:]:
        total = total + piece.astype(F32)
    return total


def on_device(
    inputs,
    segments,
    attn_gain,
    attn_shift,
    mlp_gain,
    mlp_shift,
    qkv_weight,
    qkv_bias,
    out_weight,
    out_bias,
    up_weight,
    up_bias,
    down_weight,
    down_bias,
    cotangent,
):
    seq_count, block_len, width = inputs.shape
    tokens = seq_count * block_len
    inner = qkv_weight.shape[3]
    hidden = up_weight.shape[2]
    length = block_len * 8
    chunk = 256
    place = lax.axis_index("ctx")
    me = jnp.stack([place // 2, place % 2, lax.axis_index("tensor"), lax.axis_index("dp")]).astype(jnp.int32)
    x0 = inputs.reshape(tokens, width)
    dy1 = cotangent.reshape(tokens, width)
    tok_shape = inputs.shape
    wide = shape_of((tokens, width), BF16)
    norms = (attn_gain, attn_shift, mlp_gain, mlp_shift)
    biases = qkv_bias.transpose(1, 0, 2)

    def project_first(x):
        sources = [x, segments, *norms, qkv_weight, biases]
        held = [v.shape for v in sources[:6]] + [qkv_weight.shape[1:], biases.shape]
        piece = shape_of((2, block_len + 16, 3 * LANES), BF16)
        return run(
            functools.partial(project_first_body, tok_shape),
            me,
            [(v, pl.BlockSpec(memory_space=pltpu.HBM)) for v in sources],
            [shape_of((block_len, width), F32), wide, wide] + [piece] * 4,
            scratch=[pltpu.VMEM((tokens, 3 * inner), F32)]
            + [pltpu.VMEM(size, v.dtype) for size, v in zip(held, sources)]
            + [pltpu.SemaphoreType.DMA((11,))],
            name="norm_project",
            limit=62,
        )

    def project(layer, x, extra):
        piece = shape_of((2, block_len, 3 * LANES), BF16)
        return run(
            functools.partial(project_body, layer, tok_shape),
            me,
            [x, segments, *extra, *norms]
            + [(qkv_weight, layer_spec(qkv_weight, layer)), biases],
            [shape_of((tokens, width), F32), shape_of((block_len, width), F32), wide, wide] + [piece] * 4,
            scratch=[pltpu.VMEM((tokens, 3 * inner), F32)],
            name="norm_project",
            limit=24,
        )

    def feed(layer, m):
        return run(
            functools.partial(feed_body, layer),
            me,
            [m, (up_weight, layer_spec(up_weight, layer)), up_bias, (down_weight, layer_spec(down_weight, layer))],
            [shape_of((tokens, hidden), BF16), shape_of((tokens, hidden), F32), shape_of((tokens, width), F32)],
            name="feed", limit=24,
        )

    def feed_back(layer, r, slope):
        return run(
            feed_back_body,
            me,
            [r, slope, (up_weight, layer_spec(up_weight, layer)), (down_weight, layer_spec(down_weight, layer))],
            [shape_of((tokens, hidden), BF16), shape_of((tokens, width), F32), shape_of((1, hidden), F32)],
            name="feed_back", limit=24,
        )

    def feed_both(layer, m, dy):
        return run(
            functools.partial(feed_both_body, layer),
            me,
            [m, dy, (up_weight, layer_spec(up_weight, layer)), up_bias, (down_weight, layer_spec(down_weight, layer))],
            [shape_of((tokens, hidden), BF16), wide, shape_of((tokens, hidden), BF16)]
            + [shape_of((tokens, width), F32), shape_of((1, hidden), F32)],
            name="feed_both", limit=24,
        )

    def combine(layer, pieces, part, active=None):
        fused = part is None
        got = run(
            functools.partial(combine_body, block_len, fused),
            me,
            [*pieces, (out_weight, layer_spec(out_weight, layer))]
            + ([active, (down_weight, layer_spec(down_weight, layer))] if fused else [part]),
            [shape_of((tokens, inner), BF16)] + [shape_of((block_len, width), BF16)] * 4,
            scratch=[pltpu.VMEM((tokens, width), BF16)],
            name="combine", limit=20,
        )
        return got[0], got[1:]

    def add_all(values, dtype=BF16):
        out = shape_of(values[0].shape, dtype)
        return run(functools.partial(add_body, len(values)), me, values, [out], name="add_all", limit=16)[0]

    def line_up(axis, values, size):
        extra = values[0].shape[0] - size
        small = [shape_of((extra, width), BF16)] if extra else []
        outs = [shape_of((4 * size, width), BF16)] + small
        return run(functools.partial(line_up_body, axis), me, values, outs, name="line_up", limit=8)

    seq_bf16 = pltpu.VMEM((length, LANES), BF16)
    seq_f32 = pltpu.VMEM((length, LANES), F32)
    o_shapes = [shape_of((2, block_len, LANES), BF16)] * 4

    def attend_both(pieces, grads, seg_rows, with_out):
        return run(
            functools.partial(attend_both_body, block_len, chunk, with_out),
            me,
            [*pieces, *grads, seg_rows],
            [shape_of((2, block_len, (4 if with_out else 3) * LANES), BF16)] * 4,
            scratch=([pltpu.VMEM((3, length, LANES), BF16)] if with_out else [])
            + [seq_bf16, pltpu.VMEM((2, LANES, length), BF16), seq_bf16]
            + [seq_f32] * 3,
            name="attend_both", limit=24,
        )

    def project_back(layer, pieces, dm, riders=()):
        got = run(
            functools.partial(project_back_body, block_len, layer),
            me,
            [*pieces, (qkv_weight, layer_spec(qkv_weight, layer)), dm, attn_gain, mlp_gain, *riders],
            [shape_of((tokens, 3 * inner), BF16), wide, shape_of((3, inner), F32)]
            + [shape_of((block_len * (2 if riders else 1), width), BF16)] * 4,
            scratch=[pltpu.VMEM((tokens, width), BF16)],
            name="project_back", limit=24,
        )
        return got[0], got[1], got[2], got[3:]

    def norm_back(pieces, x, dy, riders=()):
        quarter = shape_of((block_len, width), F32)
        low = shape_of((block_len + (16 if riders else 0), width), BF16)
        return run(
            norm_back_body,
            me,
            [add_up(pieces), x, dy, *riders],
            [quarter, low, shape_of((1, width), F32)],
            name="norm_back",
            limit=10,
        )

    def gains(x, da, dm):
        return run(gains_body, me, [x, da, dm], [shape_of((4, width), F32)], name="gains", limit=16)[0]

    half = width // 2
    columns = [[8 * z + 2 * chip + core for z in range(4) for chip in range(4)] for core in range(2)]

    def feed_weights(m, dh, active, r):
        pack = shape_of((2 * half, width), BF16)
        return run(feed_weights_body, me, [m, dh, active, r], [pack] * 2, name="feed_weights", limit=24)

    def head_weights(attn_in, dproj, attended, r):
        pack = shape_of((half, width), BF16)
        return run(head_weights_body, me, [attn_in, dproj, attended, r], [pack] * 2, name="head_weights", limit=20)

    x0_quarter, a0, m0, *pieces = project_first(x0)
    fed0 = feed(0, m0)
    pieces0, (active0, slope0, part0) = over_chips(pieces, fed0)
    got = run(
        functools.partial(attend_body, block_len, chunk),
        me,
        pieces0,
        [shape_of((8, length), F32), shape_of((3, length, LANES), BF16)] + o_shapes,
        scratch=[pltpu.VMEM((LANES, length), BF16), seq_bf16],
        name="attend", limit=20,
    )
    seg_rows, qkv0 = got[:2]
    out0, _ = over_chips(got[2:])
    attended0, u0 = combine(0, out0, part0)
    dy1_quarter, *grads1 = run(
        functools.partial(send_grad_body, block_len),
        me,
        [after(dy1, u0[0]), (out_weight, layer_spec(out_weight, 1))],
        [shape_of((block_len, width), F32)] + o_shapes,
        name="out_back", limit=14,
    )
    u0, grads1 = tie(over_tensor(u0), over_x(grads1))
    u0 = share_tensor(add_up(u0).astype(BF16))
    u0, grads1_other = tie(u0, [swap_core(piece) for piece in grads1])

    x1, x1_quarter, a1, m1, *pieces = project(1, x0, [*u0, out_bias, down_bias])
    fed1 = feed_both(1, m1, dy1)
    pieces1, (active1, r1, dh1, dm1, up_b1) = over_chips(pieces, fed1)
    got = attend_both(pieces1, grads1 + grads1_other, seg_rows, True)
    feed_pack1 = feed_weights(after(m1, got[0]), dh1, active1, r1)
    back1, feed_pack1 = over_chips(got, feed_pack1)
    dproj1, da1, qkv_b1, e1 = project_back(1, back1, dm1)
    back1, (feed_keep, feed_send) = after((back1, feed_pack1), e1[0])
    attended1, u1 = combine(1, back1, None, active1)
    head_keep, head_send = head_weights(a1, dproj1, attended1, r1)
    e1, (u1, head_keep, head_send, feed_came) = tie(over_tensor(e1), (u1, head_keep, head_send, swap_core(feed_send)))
    pack1 = run(
        add_packs_body,
        me,
        [feed_keep, feed_came, head_keep, swap_core(head_send)],
        [shape_of((3 * half, width), BF16)],
        name="add_packs",
        limit=16,
    )[0]
    part1 = lax.psum_scatter(pack1, ("dp", "ctx"), axis_index_groups=columns, tiled=True)
    dx1, low1, bias1 = norm_back(e1, x1_quarter, dy1_quarter)
    gains1 = gains(after(x1, low1), da1, dm1)
    quarters, gains1 = tie(share_tensor(low1), gains1)

    r0, *grads0 = run(
        functools.partial(join_body, block_len),
        me,
        [*quarters, (out_weight, layer_spec(out_weight, 0))],
        [wide] + o_shapes,
        name="join_out_back", limit=14,
    )
    ua_keep, ua_send, ub_keep, ub_send = after(u1, r0)
    ua_came, ub_came = both_ways(ua_send, ub_send, "tensor")
    dh0, dm0, up_b0 = feed_back(0, r0, slope0)
    grads0, (ua_came, ub_came, dh0, dm0, up_b0) = over_chips(grads0, (ua_came, ub_came, dh0, dm0, up_b0))
    back0 = attend_both([qkv0], grads0, seg_rows, False)
    m0_late, u_parts = after((m0, [ua_keep, ua_came, ub_keep, ub_came]), back0[0])
    feed_pack0 = feed_weights(m0_late, dh0, active0, r0)
    u_part = shape_of((block_len // 2, width), BF16)
    ua_keep, ua_send, ub_keep, ub_send = run(
        halve_again_body, me, u_parts, [u_part] * 4, name="halve_again", limit=10
    )
    ub_came, ua_came = both_ways(ub_send, ua_send, "tensor")
    back0, (feed_keep, feed_send, u1) = over_chips(back0, (*feed_pack0, [ua_keep, ua_came, ub_keep, ub_came]))
    dproj0, da0, qkv_b0, e0 = project_back(0, back0, dm0)
    head_keep, head_send = head_weights(a0, dproj0, attended0, r0)
    e0 = after(e0, head_keep)
    way = shape_of((3 * half // 4, width), BF16)
    a_keep, a_send, b_keep, b_send = run(
        halve_body,
        me,
        [feed_keep, swap_core(feed_send), head_keep, swap_core(head_send)],
        [way] * 4,
        scratch=[pltpu.VMEM((2 * half, width), BF16), pltpu.VMEM((half, width), BF16)],
        name="halve",
        limit=20,
    )
    gains0 = gains(after(x0, a_send), da0, dm0)
    a_came, b_came = both_ways(a_send, b_send)
    e0, (gains0, a_came, b_came) = tie(over_tensor(e0), (gains0, a_came, b_came))
    dx0, low0, bias0 = norm_back(e0, x0_quarter, dx1, (gains0, gains1, bias1))
    last = share_tensor(low0)
    way = shape_of((3 * half // 8, width), BF16)
    a_keep, a_send, b_keep, b_send = run(
        halve_again_body, me, after([a_keep, a_came, b_keep, b_came], low0), [way] * 4, name="halve_again", limit=10
    )
    b_came, a_came = both_ways(b_send, a_send)
    part1 = after(part1, a_send)
    pack1 = lax.all_gather(part1, ("dp", "ctx"), axis_index_groups=columns, tiled=True)
    (a_came, b_came), last = tie((a_came, b_came), last)
    local = run(
        pack_small_body,
        me,
        [qkv_b0, qkv_b1, up_b0, up_b1],
        [shape_of((16, width), BF16)],
        name="pack_small",
        limit=8,
    )[0]

    few = half // 32
    cut = run(
        merge_body,
        me,
        [a_keep, a_came, b_keep, b_came],
        [shape_of((6 * few, width), BF16)] * 4,
        scratch=[pltpu.VMEM((24 * few, width), BF16)],
        name="merge",
        limit=10,
    )
    u1 = run(
        add_halves_body, me, after(u1, cut[0]), [shape_of((block_len, width), BF16)], name="add_halves", limit=8
    )[0]
    input_grad = run(
        functools.partial(place_grad_body, block_len),
        me,
        after(last, cut[0]),
        [shape_of((tokens, width), F32)],
        name="place_grad",
        limit=12,
    )[0]
    u1 = spread_near(u1, "tensor")
    u1 = u1 + [lax.ppermute(u1[1], "tensor", WRAP_PAIR)]
    cut, (u1, input_grad) = tie(over_x(cut), (u1, input_grad))
    pieces = [shape_of((3 * few + 32, width), BF16), shape_of((3 * few, width), BF16)]
    first, second = run(settle_body, me, [*cut, *last, local], pieces, name="settle", limit=10)
    first, second = tie(over_x([first] * 4), over_dp([second] * 4))
    small = [piece[3 * few :].astype(F32) for piece in first]
    small = ((small[0] + small[2]) + (small[1] + small[3])).astype(BF16)
    first = jnp.concatenate([piece[: 3 * few] for piece in first] + [small], axis=0)
    second = jnp.concatenate(second, axis=0)

    output = run(
        functools.partial(place_output_body, block_len),
        me,
        [*after(u1, first), x1, out_bias, down_bias],
        [shape_of((tokens, width), F32)],
        name="place_output",
        limit=16,
    )[0]
    heavy = [
        shape_of((2, width, hidden), F32),
        shape_of((2, hidden, width), F32),
        shape_of((2, 3, width, inner), F32),
        shape_of((2, inner, width), F32),
    ]
    pack1_came = swap_core(after(pack1, first))
    quarter = half // 4
    views = [(2, 2, half, width)] * 2 + [(2, 3, 2, half, inner), (2, 2, LANES, width)]
    first_outs = run(
        unpack_whole_body,
        me,
        [
            (pack, pl.BlockSpec((quarter, width), lambda i, *_, part=part: (4 * part + i, 0)))
            for pack in (pack1, pack1_came)
            for part in range(3)
        ],
        [shape_of(view, F32) for view in views],
        name="unpack_whole",
        limit=24,
        out_specs=[
            pl.BlockSpec((1, 2, quarter, width), lambda i, *_: (1, 0, i, 0)),
            pl.BlockSpec((1, 2, quarter, width), lambda i, *_: (1, 0, i, 0)),
            pl.BlockSpec((1, 3, 2, quarter, inner), lambda i, *_: (1, 0, 0, i, 0)),
            pl.BlockSpec((1, 2, LANES, 2 * LANES), lambda i, *_: (1, 0, 0, i)),
        ],
        grid=4,
    )
    first_outs = [v.reshape(like.shape) for v, like in zip(first_outs, heavy)]
    near = (spread_near(first, "dp"), spread_near(second, "x"))
    near, (first_outs, output) = tie(near, (first_outs, output))
    far = (spread_far(near[0], "dp"), spread_far(near[1], "x"))
    other = [swap_core(v) for v in near[0] + near[1]]
    mine, other = tie(far[0] + far[1], other)
    far = [swap_core(v) for v in mine[3:5] + mine[8:10]]
    other = other[0:3] + far[0:2] + other[3:6] + far[2:4]
    in_place = pl.BlockSpec(memory_space=pl.ANY)
    held = [pltpu.VMEM(v.shape[1:], F32) for v in heavy] + [pltpu.SemaphoreType.DMA((4,))]
    small_shapes = [shape_of((2, width), F32)] * 6 + [shape_of((3, 2, inner), F32), shape_of((2, width), F32)]
    up_grad, down_grad, qkv_grad, out_grad, *small = run(
        functools.partial(unpack_body, few),
        me,
        mine + other + [(v, in_place) for v in first_outs],
        heavy + small_shapes,
        name="unpack",
        limit=28,
        out_specs=[in_place] * 4 + [whole(v) for v in small_shapes],
        scratch=held,
        aliases={21 + index: index for index in range(4)},
    )
    return (
        output.reshape(tok_shape),
        input_grad.reshape(tok_shape),
        small[0],
        small[1],
        small[2],
        small[3],
        qkv_grad,
        small[6].transpose(1, 0, 2),
        out_grad,
        small[4],
        up_grad,
        small[5],
        down_grad,
        small[7],
    )


def solution(mesh):
    in_specs = (
        P("dp", "ctx", None),
        P("dp", "ctx"),
        P(),
        P(),
        P(),
        P(),
        P(None, None, None, "tensor"),
        P(None, None, "tensor"),
        P(None, "tensor", None),
        P(),
        P(None, None, "tensor"),
        P(None, "tensor"),
        P(None, "tensor", None),
        P(),
        P("dp", "ctx", None),
    )
    out_specs = (
        P("dp", "ctx", None),
        P("dp", "ctx", None),
        P(),
        P(),
        P(),
        P(),
        P(None, None, None, "tensor"),
        P(None, None, "tensor"),
        P(None, "tensor", None),
        P(),
        P(None, None, "tensor"),
        P(None, "tensor"),
        P(None, "tensor", None),
        P(),
    )
    return jax.shard_map(
        on_device, mesh=mesh, in_specs=in_specs, out_specs=out_specs, check_vma=False
    )
```

```python
import functools

import jax
import jax.numpy as jnp
from jax import lax
from jax.experimental import pallas as pl
from jax.experimental.pallas import tpu as pltpu
from jax.sharding import PartitionSpec as P

HEAD = 64
ROT = 16
LAYERS = 2
LANES = 128
F32 = jnp.float32
BF16 = jnp.bfloat16


def shape_of(shape, dtype):
    return jax.ShapeDtypeStruct(tuple(shape), dtype)


def whole(array):
    rank = array.ndim
    return pl.BlockSpec(array.shape, lambda i, *_: (0,) * rank, pipeline_mode=pl.Buffered(1))


def layer_spec(array, layer):
    rank = array.ndim
    return pl.BlockSpec(
        (1,) + array.shape[1:], lambda i, *_: (layer,) + (0,) * (rank - 1), pipeline_mode=pl.Buffered(1)
    )


def run(body, me, operands, outs, scratch=(), name=None, limit=32, out_specs=None, aliases=None, grid=1):
    arrays, specs = [], []
    for operand in operands:
        array, spec = operand if isinstance(operand, tuple) else (operand, None)
        arrays.append(array)
        specs.append(whole(array) if spec is None else spec)
    return pl.pallas_call(
        body,
        grid_spec=pltpu.PrefetchScalarGridSpec(
            num_scalar_prefetch=1,
            grid=(grid,),
            in_specs=specs,
            out_specs=[whole(o) for o in outs] if out_specs is None else out_specs,
            scratch_shapes=list(scratch),
        ),
        out_shape=list(outs),
        input_output_aliases=aliases or {},
        compiler_params=pltpu.CompilerParams(vmem_limit_bytes=limit * 1024 * 1024),
        cost_estimate=pl.CostEstimate(flops=1, bytes_accessed=1, transcendentals=0),
        name=name,
    )(me, *arrays)


def matmul(left, right):
    return jnp.dot(left, right, preferred_element_type=F32)


def matmul_nt(left, right):
    return lax.dot_general(left, right, (((1,), (1,)), ((), ())), preferred_element_type=F32)


def matmul_tn(left, right):
    return lax.dot_general(left, right, (((0,), (0,)), ((), ())), preferred_element_type=F32)


def normalize(values):
    average = jnp.mean(values, axis=-1, keepdims=True)
    centred = values - average
    factor = lax.rsqrt(jnp.mean(centred * centred, axis=-1, keepdims=True) + 1e-05)
    return centred * factor, factor


def wrap4(value):
    return lax.rem(value + 4, 4)


def rows(index, size):
    return pl.ds(pl.multiple_of(index * size, size), size)


def rotary_rows(place_row):
    count = place_row.shape[1]
    which = lax.broadcasted_iota(jnp.int32, (8, count), 0)
    frequency = jnp.zeros((8, count), F32)
    for index in range(8):
        frequency = jnp.where(which == index, 10000.0 ** (-2.0 * index / ROT), frequency)
    angles = frequency * place_row
    trig = jnp.concatenate([jnp.cos(angles), jnp.sin(angles)], axis=0)
    row = lax.broadcasted_iota(jnp.int32, (16, LANES), 0)
    lane = lax.broadcasted_iota(jnp.int32, (16, LANES), 1) & (HEAD - 1)
    same = (lane & 7) == (row & 7)
    is_cos = row < 8
    pick_cos = jnp.where(is_cos & same & (lane < 16), 1.0, 0.0)
    pick_low = jnp.where((row >= 8) & same & (lane < 8), 1.0, 0.0)
    pick_high = jnp.where((row >= 8) & same & (lane >= 8) & (lane < 16), 1.0, 0.0)
    picks = jnp.concatenate([pick_cos, pick_low, pick_high], axis=1).astype(F32)
    spread = lax.dot_general(
        trig, picks, (((0,), (0,)), ((), ())), preferred_element_type=F32, precision=lax.Precision.HIGHEST
    )
    lane_row = lax.broadcasted_iota(jnp.int32, (1, LANES), 1) & (HEAD - 1)
    cos_table = spread[:, :LANES] + jnp.where(lane_row >= ROT, 1.0, 0.0)
    return cos_table, spread[:, LANES : 2 * LANES], spread[:, 2 * LANES :]


def rotate(values, tables, back=False):
    cos_table, low_sin, high_sin = tables
    below = pltpu.roll(values, LANES - ROT // 2, 1) * low_sin
    above = pltpu.roll(values, ROT // 2, 1) * high_sin
    turned = below - above if back else above - below
    return values * cos_table + turned


def project_rows(layer, tok_shape, me_ref, seg_ref, weight, bias, a_ref, p_refs, proj_ref, with_seg):
    seq_count, block_len, width = tok_shape
    chip, core = me_ref[0], me_ref[1]
    base = (chip * 2 + core) * block_len
    for j in range(3):
        proj_ref[:, j * 2 * LANES : (j + 1) * 2 * LANES] = matmul(a_ref[...], weight(j)) + bias[j, layer : layer + 1, :]
    for k in range(4):
        seq = wrap4(chip + k)
        place = rows(seq, block_len)
        seg_row = seg_ref[pl.ds(seq, 1), :]
        spots = lax.broadcasted_iota(jnp.int32, (1, block_len), 1) + base
        tables = rotary_rows((spots - seg_row).astype(F32))
        for j in range(3):
            for pair in range(2):
                at = (2 * j + pair) * LANES
                part = proj_ref[place, at : at + LANES]
                if j < 2:
                    part = rotate(part, tables)
                p_refs[k][pair, 0:block_len, j * LANES : (j + 1) * LANES] = part.astype(BF16)
        if with_seg:
            coded = seg_row.astype(F32)
            high = jnp.floor(coded * 0.125)
            packed = jnp.concatenate([high, coded - 8.0 * high, jnp.zeros_like(high)], axis=1)
            packed = jnp.broadcast_to(packed, (16, 3 * LANES)).astype(BF16)
            for pair in range(2):
                p_refs[k][pair, block_len : block_len + 16, :] = packed


def project_first_body(tok_shape, me_ref, *refs):
    seq_count, block_len, width = tok_shape
    in_refs, refs = refs[:8], refs[8:]
    xq_ref, a_ref, m_ref, *p_refs = refs[:7]
    proj_ref, *held, sems = refs[7:]
    x_ref, seg_ref, ag_ref, as_ref, mg_ref, ms_ref, w_ref, b_ref = held
    copies = []
    for index in (1, 2, 3, 4, 5):
        copies.append(pltpu.make_async_copy(in_refs[index], held[index], sems.at[len(copies)]))
    copies.append(pltpu.make_async_copy(in_refs[7], b_ref, sems.at[len(copies)]))
    small_count = len(copies)
    for seq in range(seq_count):
        place = pl.ds(seq * block_len, block_len)
        copies.append(pltpu.make_async_copy(in_refs[0].at[place], x_ref.at[place], sems.at[len(copies)]))
    copies.append(pltpu.make_async_copy(in_refs[6].at[0], w_ref, sems.at[len(copies)]))
    for copy in copies:
        copy.start()
    for copy in copies[:small_count]:
        copy.wait()
    for seq in range(seq_count):
        copies[small_count + seq].wait()
        place = slice(seq * block_len, (seq + 1) * block_len)
        normed, _ = normalize(x_ref[place, :])
        a_ref[place, :] = (normed * ag_ref[0:1, :] + as_ref[0:1, :]).astype(BF16)
        m_ref[place, :] = (normed * mg_ref[0:1, :] + ms_ref[0:1, :]).astype(BF16)
    xq_ref[...] = x_ref[rows(me_ref[2], block_len), :]
    copies[-1].wait()
    project_rows(0, tok_shape, me_ref, seg_ref, lambda j: w_ref[j], b_ref, a_ref, p_refs, proj_ref, True)


def project_body(layer, tok_shape, me_ref, *refs):
    seq_count, block_len, width = tok_shape
    x_ref, seg_ref, *refs = refs
    u_refs, refs = refs[:4], refs[4:]
    ob_ref, db_ref, ag_ref, as_ref, mg_ref, ms_ref, w_ref, b_ref, x_out, xq_ref, a_ref, m_ref, *p_refs, proj_ref = refs
    tensor = me_ref[2]
    shift = ob_ref[layer - 1 : layer, :] + db_ref[layer - 1 : layer, :]
    for k in range(4):
        place = rows(wrap4(tensor - k), block_len)
        value = x_ref[place, :] + u_refs[k][...].astype(F32) + shift
        x_out[place, :] = value
        if k == 0:
            xq_ref[...] = value
        normed, _ = normalize(value)
        a_ref[place, :] = (normed * ag_ref[layer : layer + 1, :] + as_ref[layer : layer + 1, :]).astype(BF16)
        m_ref[place, :] = (normed * mg_ref[layer : layer + 1, :] + ms_ref[layer : layer + 1, :]).astype(BF16)
    project_rows(layer, tok_shape, me_ref, seg_ref, lambda j: w_ref[0, j], b_ref, a_ref, p_refs, proj_ref, False)


def gather_pieces(me_ref, refs, targets, block_len, seg_target=None):
    chip, core = me_ref[0], me_ref[1]
    for k in range(4):
        owner = wrap4(chip - k)
        for side, ref in ((core, refs[k]), (1 - core, refs[4 + k])):
            place = rows(owner * 2 + side, block_len)
            for index, target in enumerate(targets):
                target[place, :] = ref[core, 0:block_len, index * LANES : (index + 1) * LANES]
            if seg_target is not None:
                row = ref[core, block_len : block_len + 16, :].astype(F32)[0:1, :]
                starts = row[:, 0:LANES] * 8.0 + row[:, LANES : 2 * LANES]
                seg_target[:, place] = jnp.broadcast_to(starts, (8, block_len))


def head_stack(values):
    lane = lax.broadcasted_iota(jnp.int32, values.shape, 1)
    zero = jnp.zeros_like(values)
    return jnp.concatenate(
        [jnp.where(lane < HEAD, values, zero), jnp.where(lane >= HEAD, values, zero)], axis=0
    )


def own_halves(product, width):
    return jnp.concatenate([product[0:HEAD, 0:width], product[HEAD:, width : 2 * width]], axis=0)


def chances_t(q_ref, k_ref, seg_ref, step, chunk):
    start, keys = step * chunk, (step + 1) * chunk
    stacked = head_stack(q_ref[start:keys, :]) * jnp.asarray(HEAD ** (-0.5), BF16)
    scores = matmul_nt(k_ref[0:keys, :], stacked)
    key_place = lax.broadcasted_iota(jnp.int32, (keys, 2 * chunk), 0).astype(F32)
    query_place = (lax.broadcasted_iota(jnp.int32, (1, 2 * chunk), 1) & (chunk - 1)).astype(F32) + start
    seg_row = seg_ref[0:1, start:keys]
    seg_row = jnp.concatenate([seg_row, seg_row], axis=1)
    allowed = (key_place >= seg_row) & (key_place <= query_place)
    scores = jnp.where(allowed, scores, -1e30)
    raised = jnp.exp(scores - jnp.max(scores, axis=0, keepdims=True))
    total = jnp.sum(raised, axis=0, keepdims=True)
    return raised * (1.0 / total), stacked


def attend_body(block_len, chunk, me_ref, *refs):
    piece_refs, refs = refs[:8], refs[8:]
    seg_out, qkv_ref, *refs = refs
    o_refs, refs = refs[:4], refs[4:]
    vt_ref, o_ref = refs
    q_ref, k_ref, v_ref = qkv_ref.at[0], qkv_ref.at[1], qkv_ref.at[2]
    gather_pieces(me_ref, piece_refs, (q_ref, k_ref, v_ref), block_len, seg_out)
    vt_ref[...] = v_ref[...].T
    length = q_ref.shape[0]
    for step in range(length // chunk):
        keys = (step + 1) * chunk
        chances, _ = chances_t(q_ref, k_ref, seg_out, step, chunk)
        mixed = matmul(vt_ref[:, 0:keys], chances.astype(BF16))
        o_ref[step * chunk : keys, :] = own_halves(mixed, chunk).T.astype(BF16)
    send_blocks(me_ref, o_ref, o_refs, block_len)


def send_blocks(me_ref, source, targets, block_len):
    chip = me_ref[0]
    for k in range(4):
        dest = wrap4(chip + k)
        for side in range(2):
            targets[k][side] = source[rows(dest * 2 + side, block_len), :]


def attend_both_body(block_len, chunk, with_out, me_ref, *refs):
    if with_out:
        piece_refs, refs = refs[:8], refs[8:]
    else:
        qkv_ref, *refs = refs
    grad_refs, refs = refs[:8], refs[8:]
    seg_ref, *refs = refs
    d_refs, refs = refs[:4], refs[4:]
    if with_out:
        qkv_ref, *refs = refs
    q_ref, k_ref, v_ref = qkv_ref.at[0], qkv_ref.at[1], qkv_ref.at[2]
    g_ref, t_ref, o_ref, dq_ref, dk_ref, dv_ref = refs
    if with_out:
        gather_pieces(me_ref, piece_refs, (q_ref, k_ref, v_ref), block_len)
    gather_pieces(me_ref, grad_refs, (g_ref,), block_len)
    length = q_ref.shape[0]
    t_ref[0] = k_ref[...].T
    if with_out:
        t_ref[1] = v_ref[...].T
    dk_ref[...] = jnp.zeros_like(dk_ref)
    dv_ref[...] = jnp.zeros_like(dv_ref)
    for step in range(length // chunk):
        start, keys = step * chunk, (step + 1) * chunk
        chances, stacked = chances_t(q_ref, k_ref, seg_ref, step, chunk)
        low = chances.astype(BF16)
        if with_out:
            mixed = matmul(t_ref[1, :, 0:keys], low)
            o_ref[start:keys, :] = own_halves(mixed, chunk).T.astype(BF16)
        grads = head_stack(g_ref[start:keys, :])
        chance_grad = matmul_nt(v_ref[0:keys, :], grads)
        delta = jnp.sum(chances * chance_grad, axis=0, keepdims=True)
        score_grad = (chances * (chance_grad - delta)).astype(BF16)
        dv_ref[0:keys, :] += matmul(low, grads)
        dk_ref[0:keys, :] += matmul(score_grad, stacked)
        query = matmul(t_ref[0, :, 0:keys], score_grad)
        dq_ref[start:keys, :] = own_halves(query, chunk).T * HEAD ** (-0.5)
    chip = me_ref[0]
    for k in range(4):
        dest = wrap4(chip + k)
        for side in range(2):
            place = rows(dest * 2 + side, block_len)
            spots = (lax.broadcasted_iota(jnp.int32, (1, block_len), 1) + (dest * 2 + side) * block_len).astype(F32)
            tables = rotary_rows(spots - seg_ref[0:1, place])
            d_refs[k][side, :, 0:LANES] = rotate(dq_ref[place, :], tables, True).astype(BF16)
            d_refs[k][side, :, LANES : 2 * LANES] = rotate(dk_ref[place, :], tables, True).astype(BF16)
            d_refs[k][side, :, 2 * LANES : 3 * LANES] = dv_ref[place, :].astype(BF16)
            if with_out:
                d_refs[k][side, :, 3 * LANES :] = o_ref[place, :]


def land_heads(me_ref, refs, target, block_len, groups, first=0):
    chip, core = me_ref[0], me_ref[1]
    for k in range(4):
        place = rows(wrap4(chip - k), block_len)
        mine, other = refs[k][core], refs[4 + k][core]
        is_low = core == 0
        for group in range(groups):
            span = slice((first + group) * LANES, (first + group + 1) * LANES)
            at = group * 2 * LANES
            target[place, at : at + LANES] = jnp.where(is_low, mine[:, span], other[:, span])
            target[place, at + LANES : at + 2 * LANES] = jnp.where(is_low, other[:, span], mine[:, span])


def combine_body(block_len, fused, me_ref, *refs):
    piece_refs, refs = refs[:8], refs[8:]
    w_ref, *refs = refs
    if fused:
        g_ref, down_ref, *refs = refs
    else:
        part_ref, *refs = refs
    o_ref, *refs = refs
    q_refs, scr = refs[:-1], refs[-1]
    tensor = me_ref[2]
    land_heads(me_ref, piece_refs, o_ref, block_len, 1, 3 if fused else 0)
    part = matmul(g_ref[...], down_ref[0]) if fused else part_ref[...]
    scr[...] = (matmul(o_ref[...], w_ref[0]) + part).astype(BF16)
    if fused:
        near, far = near_far(tensor)
        size = block_len // 2
        orders = ((tensor, far), (near, 3 - near), (tensor, near), (far, far ^ 1))
        for way, (ref, order) in enumerate(zip(q_refs, orders)):
            for index, quarter in enumerate(order):
                at = pl.multiple_of(quarter * block_len + (way >> 1) * size, size)
                ref[index * size : (index + 1) * size, :] = scr[pl.ds(at, size), :]
        return
    for k in range(4):
        q_refs[k][...] = scr[rows(wrap4(tensor + k), block_len), :]


def send_grad_body(block_len, me_ref, x_ref, w_ref, *refs):
    chip, tensor = me_ref[0], me_ref[2]
    quarter_ref, *refs = refs
    quarter_ref[...] = x_ref[rows(tensor, block_len), :]
    for k in range(4):
        value = x_ref[rows(wrap4(chip + k), block_len), :].astype(BF16)
        grad = matmul_nt(value, w_ref[0]).astype(BF16)
        for pair in range(2):
            refs[k][pair] = grad[:, pair * LANES : (pair + 1) * LANES]


def join_body(block_len, me_ref, *refs):
    q_refs, refs = refs[:4], refs[4:]
    w_ref, r_ref, *g_refs = refs
    chip, tensor = me_ref[0], me_ref[2]
    for k in range(4):
        r_ref[rows(wrap4(tensor - k), block_len), :] = q_refs[k][...]
    for k in range(4):
        value = r_ref[rows(wrap4(chip + k), block_len), :]
        grad = matmul_nt(value, w_ref[0]).astype(BF16)
        for pair in range(2):
            g_refs[k][pair] = grad[:, pair * LANES : (pair + 1) * LANES]


def project_back_body(block_len, layer, me_ref, *refs):
    piece_refs, refs = refs[:8], refs[8:]
    w_ref, dm_ref, ag_ref, mg_ref, *refs = refs
    riders, refs = refs[:-8], refs[-8:]
    dp_ref, da_ref, bias_ref, *q_refs, scr = refs
    tensor = me_ref[2]
    land_heads(me_ref, piece_refs, dp_ref, block_len, 3)
    for j in range(3):
        span = slice(j * 2 * LANES, (j + 1) * 2 * LANES)
        bias_ref[j : j + 1, :] = jnp.sum(dp_ref[:, span].astype(F32), axis=0, keepdims=True)
    total = None
    for j in range(3):
        term = matmul_nt(dp_ref[:, j * 2 * LANES : (j + 1) * 2 * LANES], w_ref[0, j])
        total = term if total is None else total + term
    da_ref[...] = total.astype(BF16)
    scr[...] = (total * ag_ref[layer : layer + 1, :] + dm_ref[...] * mg_ref[layer : layer + 1, :]).astype(BF16)
    for k in range(4):
        q_refs[k][0:block_len, :] = scr[rows(wrap4(tensor + k), block_len), :]
        if riders:
            q_refs[k][block_len:, :] = riders[k][...]


def norm_back_body(me_ref, *refs):
    e_ref, x_ref, dy_ref, *gain_refs, dx_ref, low_ref, bias_ref = refs
    upstream = dy_ref[...]
    size = upstream.shape[0]
    total = e_ref[0:size, :]
    normed, factor = normalize(x_ref[...])
    inner = jnp.mean(total * normed, axis=-1, keepdims=True)
    result = upstream + factor * (total - jnp.mean(total, axis=-1, keepdims=True) - normed * inner)
    dx_ref[...] = result
    low_ref[0:size, :] = result.astype(BF16)
    bias = jnp.sum(upstream, axis=0, keepdims=True)
    bias_ref[...] = bias
    if gain_refs:
        mine, other, other_bias = gain_refs
        blank = jnp.zeros((6, bias.shape[1]), F32)
        rows_here = jnp.concatenate([mine[...], bias, other[...], other_bias[...], blank], axis=0)
        low_ref[size:, :] = rows_here.astype(BF16)


def gains_body(me_ref, x_ref, da_ref, dm_ref, out_ref):
    normed, _ = normalize(x_ref[...])
    da = da_ref[...].astype(F32)
    dm = dm_ref[...]
    out_ref[0:1, :] = jnp.sum(da * normed, axis=0, keepdims=True)
    out_ref[1:2, :] = jnp.sum(da, axis=0, keepdims=True)
    out_ref[2:3, :] = jnp.sum(dm * normed, axis=0, keepdims=True)
    out_ref[3:4, :] = jnp.sum(dm, axis=0, keepdims=True)


def gelu_parts(hidden):
    cdf = 0.5 * (1.0 + lax.erf(hidden * (0.5**0.5)))
    density = jnp.exp(-0.5 * hidden * hidden) * 0.3989422804014327
    return cdf, density


def feed_body(layer, me_ref, m_ref, up_ref, ub_ref, down_ref, g_ref, slope_ref, part_ref):
    size = 2 * LANES
    for step in range(up_ref.shape[2] // size):
        span = slice(step * size, (step + 1) * size)
        hidden = matmul(m_ref[...], up_ref[0, :, span]) + ub_ref[layer : layer + 1, span]
        cdf, density = gelu_parts(hidden)
        g_ref[:, span] = (hidden * cdf).astype(BF16)
        slope_ref[:, span] = cdf + hidden * density
    part_ref[...] = matmul(g_ref[...], down_ref[0])


def feed_back_body(me_ref, r_ref, slope_ref, up_ref, down_ref, dh_ref, dm_ref, bias_ref):
    size = 2 * LANES
    for step in range(down_ref.shape[1] // size):
        span = slice(step * size, (step + 1) * size)
        grad = matmul_nt(r_ref[...], down_ref[0, span, :]) * slope_ref[:, span]
        bias_ref[:, span] = jnp.sum(grad, axis=0, keepdims=True)
        dh_ref[:, span] = grad.astype(BF16)
    dm_ref[...] = matmul_nt(dh_ref[...], up_ref[0])


def feed_both_body(layer, me_ref, m_ref, dy_ref, up_ref, ub_ref, down_ref, g_ref, r_ref, dh_ref, dm_ref, bias_ref):
    size = 2 * LANES
    r_ref[...] = dy_ref[...].astype(BF16)
    for step in range(up_ref.shape[2] // size):
        span = slice(step * size, (step + 1) * size)
        hidden = matmul(m_ref[...], up_ref[0, :, span]) + ub_ref[layer : layer + 1, span]
        cdf, density = gelu_parts(hidden)
        g_ref[:, span] = (hidden * cdf).astype(BF16)
        grad = matmul_nt(r_ref[...], down_ref[0, span, :]) * (cdf + hidden * density)
        bias_ref[:, span] = jnp.sum(grad, axis=0, keepdims=True)
        dh_ref[:, span] = grad.astype(BF16)
    dm_ref[...] = matmul_nt(dh_ref[...], up_ref[0])


def feed_weights_body(me_ref, m_ref, dh_ref, g_ref, r_ref, keep_ref, send_ref):
    core = me_ref[1]
    half = m_ref.shape[1] // 2
    for side, out in ((core, keep_ref), (1 - core, send_ref)):
        out[0:half, :] = matmul_tn(m_ref[:, rows(side, half)], dh_ref[...]).astype(BF16)
        out[half:, :] = matmul_tn(g_ref[:, rows(side, half)], r_ref[...]).astype(BF16)


def head_weights_body(me_ref, a_ref, dp_ref, o_ref, r_ref, keep_ref, send_ref):
    core = me_ref[1]
    half = a_ref.shape[1] // 2
    wide = dp_ref.shape[1]
    for side, out in ((core, keep_ref), (1 - core, send_ref)):
        out[:, 0:wide] = matmul_tn(a_ref[:, rows(side, half)], dp_ref[...]).astype(BF16)
        grad = matmul_tn(o_ref[:, rows(side, LANES)], r_ref[...]).astype(BF16)
        for part in range(4):
            out[part * LANES : (part + 1) * LANES, wide:] = grad[:, part * 2 * LANES : (part + 1) * 2 * LANES]


def feed_weights_whole_body(me_ref, m_ref, dh_ref, g_ref, r_ref, pack_ref):
    high = m_ref.shape[1]
    pack_ref[0:high, :] = matmul_tn(m_ref[...], dh_ref[...]).astype(BF16)
    pack_ref[high:, :] = matmul_tn(g_ref[...], r_ref[...]).astype(BF16)


def head_weights_whole_body(me_ref, a_ref, dp_ref, o_ref, r_ref, before_ref, pack_ref):
    wide = dp_ref.shape[1]
    pack_ref[:, 0:wide] = matmul_tn(a_ref[...], dp_ref[...]).astype(BF16)
    grad = matmul_tn(o_ref[...], r_ref[...]).astype(BF16)
    high, size = grad.shape[0], 2 * LANES
    for part in range(4):
        pack_ref[part * high : (part + 1) * high, wide:] = grad[:, part * size : (part + 1) * size]


def near_far(place):
    return place ^ 1, 3 - place


def halve_body(me_ref, feed_keep, feed_came, head_keep, head_came, *refs):
    outs, feed_scr, head_scr = refs[:4], refs[4], refs[5]
    feed_scr[...] = (feed_keep[...].astype(F32) + feed_came[...].astype(F32)).astype(BF16)
    head_scr[...] = (head_keep[...].astype(F32) + head_came[...].astype(F32)).astype(BF16)
    place = me_ref[3]
    near, far = near_far(place)
    half = head_scr.shape[0]
    size = half // 8
    orders = ((place, far), (near, 3 - near), (4 + place, 4 + near), (4 + far, 4 + (far ^ 1)))
    for ref, order in zip(outs, orders):
        for index, block in enumerate(order):
            at = 3 * size * index
            ref[at : at + size, :] = feed_scr[rows(block, size), :]
            ref[at + size : at + 2 * size, :] = feed_scr[pl.ds(pl.multiple_of(half + block * size, size), size), :]
            ref[at + 2 * size : at + 3 * size, :] = head_scr[rows(block, size), :]


def halve_again_body(me_ref, a_keep, a_came, b_keep, b_came, *outs):
    size = outs[0].shape[0]
    for keep, came, mine, send in ((a_keep, a_came, outs[0], outs[1]), (b_keep, b_came, outs[2], outs[3])):
        total = (keep[...].astype(F32) + came[...].astype(F32)).astype(BF16)
        mine[...] = total[0:size, :]
        send[...] = total[size:, :]


def line_up_body(axis, me_ref, *refs):
    size = refs[4].shape[0] // 4
    for k in range(4):
        refs[4][rows(wrap4(me_ref[axis] - k), size), :] = refs[k][0:size, :]
    if len(refs) > 5:
        even = refs[0][size:, :].astype(F32) + refs[2][size:, :].astype(F32)
        odd = refs[1][size:, :].astype(F32) + refs[3][size:, :].astype(F32)
        refs[5][...] = (even + odd).astype(BF16)


def merge_body(me_ref, a_keep, a_came, b_keep, b_came, *refs):
    out_refs, scr = refs[:4], refs[4]
    high = a_keep.shape[0]
    scr[0:high, :] = (a_keep[...].astype(F32) + a_came[...].astype(F32)).astype(BF16)
    scr[high:, :] = (b_keep[...].astype(F32) + b_came[...].astype(F32)).astype(BF16)
    few = high // 6
    for k in range(4):
        part = wrap4(me_ref[0] + k)
        for weight in range(3):
            at = pl.multiple_of((part >> 1) * high + weight * 2 * few + (part & 1) * few, few)
            out_refs[k][weight * few : (weight + 1) * few, :] = scr[pl.ds(at, few), :]


def settle_body(me_ref, *refs):
    in_refs, last_refs, local_ref, (first_ref, second_ref) = refs[:4], refs[4:8], refs[8], refs[9:]
    total = in_refs[0][...].astype(F32)
    for ref in in_refs[1:]:
        total = total + ref[...].astype(F32)
    total = total.astype(BF16)
    few = second_ref.shape[0] // 3
    for weight in range(3):
        for index, ref in enumerate((first_ref, second_ref)):
            at = (2 * weight + index) * few
            ref[weight * few : (weight + 1) * few, :] = total[at : at + few, :]
    count = local_ref.shape[0]
    shared = [ref[ref.shape[0] - count :, :].astype(F32) for ref in last_refs]
    shared = ((shared[0] + shared[2]) + (shared[1] + shared[3])).astype(BF16)
    first_ref[3 * few : 3 * few + count, :] = shared
    first_ref[3 * few + count :, :] = local_ref[...]


def flush(held, outs, layer, sems):
    copies = [pltpu.make_async_copy(a, b.at[layer], sems.at[i]) for i, (a, b) in enumerate(zip(held, outs))]
    return copies


def unpack_body(few, me_ref, *refs):
    outs, small_outs, held, sems = refs[24:28], refs[28:36], refs[36:40], refs[40]
    up_ref, down_ref, qkv_ref, out_ref = held
    copies = flush(held, outs, 0, sems)
    chip, core, place_z = me_ref[0], me_ref[1], me_ref[3]
    size = 2 * LANES
    half = up_ref.shape[0] // 2
    for weight in range(3):
        for side, group in ((core, refs[:10]), (1 - core, refs[10:20])):
            for along, me in ((0, place_z), (1, chip)):
                pieces = group[5 * along : 5 * along + 5]
                cut = pieces[3].shape[0] // few
                spans = [(pieces[0], me, 0, 12), (pieces[1], me ^ 1, 0, 12), (pieces[2], 3 - me, 0, 12)]
                spans += [(pieces[3], me ^ 2, 0, cut), (pieces[4], me ^ 2, cut, 12)]
                for ref, owner, first, stop in spans:
                    for index in range(first, stop):
                        if index % 3 != weight:
                            continue
                        z, x = (owner, wrap4(chip - index // 3)) if along == 0 else (wrap4(place_z - index // 3), owner)
                        start = (index - first) * few
                        value = ref[start : start + few, :].astype(F32)
                        row = (z + 4 * (x >> 1)) * (4 * few) + (x & 1) * (2 * few) + along * few
                        place = pl.ds(pl.multiple_of(row + side * half, few), few)
                        if weight < 2:
                            held[weight][place, :] = value
                        else:
                            for j in range(3):
                                qkv_ref[j, place, :] = value[:, j * size : (j + 1) * size]
                            inner = pl.ds(pl.multiple_of((row & (LANES - 1)) + side * LANES, few), few)
                            lanes = pl.ds(pl.multiple_of((row >> 7) * size, size), size)
                            out_ref[inner, lanes] = value[:, 3 * size :]
        for copy in copies[weight : weight + 1] if weight < 2 else copies[2:]:
            copy.start()
    parts = []
    for group in (refs[:10], refs[10:20]):
        count = group[0].shape[0] - 12 * few
        rows_of = [ref[ref.shape[0] - count :, :].astype(F32) for ref in (group[0], group[4], group[1], group[2])]
        parts.append((rows_of[0] + rows_of[1]) + (rows_of[2] + rows_of[3]))
    small_out(parts[0] + parts[1], small_outs)
    for copy in copies:
        copy.wait()


def add_packs_body(me_ref, feed_keep, feed_came, head_keep, head_came, out_ref):
    high = feed_keep.shape[0]
    out_ref[0:high, :] = (feed_keep[...].astype(F32) + feed_came[...].astype(F32)).astype(BF16)
    out_ref[high:, :] = (head_keep[...].astype(F32) + head_came[...].astype(F32)).astype(BF16)


def unpack_whole_body(me_ref, up_mine, down_mine, head_mine, up_other, down_other, head_other, *outs):
    up_ref, down_ref, qkv_ref, out_ref = outs
    size = 2 * LANES
    for core in range(2):
        mine = me_ref[1] == core
        for ref, first, second in ((up_ref, up_mine, up_other), (down_ref, down_mine, down_other)):
            ref[0, core] = jnp.where(mine, first[...], second[...]).astype(F32)
        head = jnp.where(mine, head_mine[...], head_other[...]).astype(F32)
        for j in range(3):
            qkv_ref[0, j, core] = head[:, j * size : (j + 1) * size]
        out_ref[0, core] = head[:, 3 * size :]


def pack_small_body(me_ref, *refs):
    ins, local_ref = refs[:4], refs[4]
    width = local_ref.shape[1]
    local = [ins[2][...], ins[3][...]]
    for ref in ins[0:2]:
        values = ref[...]
        flat = [values[j : j + 1, :] for j in range(3)]
        local.append(jnp.concatenate(flat + [jnp.zeros((1, width - 3 * values.shape[1]), F32)], axis=1))
    local_ref[...] = jnp.concatenate(local + [jnp.zeros((12, width), F32)], axis=0).astype(BF16)


def add_halves_body(me_ref, a_keep, a_came, b_keep, b_came, out_ref):
    size = a_keep.shape[0]
    out_ref[0:size, :] = (a_keep[...].astype(F32) + a_came[...].astype(F32)).astype(BF16)
    out_ref[size:, :] = (b_keep[...].astype(F32) + b_came[...].astype(F32)).astype(BF16)


def add_body(count, me_ref, *refs):
    total = refs[0][...].astype(F32)
    for ref in refs[1:count]:
        total = total + ref[...].astype(F32)
    refs[count][...] = total.astype(refs[count].dtype)


def small_out(total, outs):
    shared, local = total[0:16, :], total[16:32, :]
    for index in range(5):
        outs[index][0:1, :] = shared[index : index + 1, :]
        outs[index][1:2, :] = shared[index + 5 : index + 6, :]
    outs[7][...] = outs[4][...]
    outs[5][...] = local[0:2, :]
    size = outs[6].shape[2]
    for layer in range(2):
        for j in range(3):
            outs[6][j, layer : layer + 1, :] = local[2 + layer : 3 + layer, j * size : (j + 1) * size]


def place_grad_body(block_len, me_ref, *refs):
    q_refs, grad_ref = refs[:4], refs[4]
    for k in range(4):
        grad_ref[rows(wrap4(me_ref[2] - k), block_len), :] = q_refs[k][0:block_len, :].astype(F32)


def place_output_body(block_len, me_ref, *refs):
    u_refs, (x_ref, ob_ref, db_ref, out_ref) = refs[:4], refs[4:]
    shift = ob_ref[1:2, :] + db_ref[1:2, :]
    me = me_ref[2]
    for ref, quarter in zip(u_refs, (me, me ^ 1, 3 - me, me ^ 2)):
        place = rows(quarter, block_len)
        out_ref[place, :] = x_ref[place, :] + ref[...].astype(F32) + shift


def chip_turn(shift):
    return [(2 * x + c, 2 * ((x + shift) % 4) + c) for x in range(4) for c in range(2)]


CORE_SWAP = [(i, i ^ 1) for i in range(8)]


def over_chips(pieces, beside=()):
    mine, beside = lax.optimization_barrier((over_x(pieces), beside))
    return mine + [swap_core(piece) for piece in mine], beside


def ring_turn(shift):
    return [(i, (i + shift) % 4) for i in range(4)]


def over_tensor(pieces):
    return [pieces[0]] + [lax.ppermute(pieces[k], "tensor", ring_turn(k)) for k in range(1, 4)]


def share_tensor(piece):
    return over_tensor([piece] * 4)


def over_dp(pieces):
    return [pieces[0]] + [lax.ppermute(pieces[k], "dp", ring_turn(k)) for k in range(1, 4)]


def over_x(pieces):
    return [pieces[0]] + [lax.ppermute(pieces[k], "ctx", chip_turn(k)) for k in range(1, 4)]


def swap_core(piece):
    return lax.ppermute(piece, "ctx", CORE_SWAP)


NEXT_PAIR = [(0, 1), (1, 0), (2, 3), (3, 2)]
WRAP_PAIR = [(0, 3), (3, 0), (1, 2), (2, 1)]


def both_ways(to_next, to_wrap, axis="dp"):
    return lax.ppermute(to_next, axis, NEXT_PAIR), lax.ppermute(to_wrap, axis, WRAP_PAIR)


def chips_of(pairs):
    return [(2 * a + c, 2 * b + c) for a, b in pairs for c in range(2)]


def along(axis):
    return ("ctx", chips_of) if axis == "x" else (axis, lambda pairs: pairs)


def spread_near(piece, axis):
    name, move = along(axis)
    return [piece] + [lax.ppermute(piece, name, move(pairs)) for pairs in (NEXT_PAIR, WRAP_PAIR)]


def spread_far(pieces, axis):
    name, move = along(axis)
    half = pieces[0].shape[0] // 2
    return pieces + [
        lax.ppermute(pieces[1][:half], name, move(WRAP_PAIR)),
        lax.ppermute(pieces[2][half:], name, move(NEXT_PAIR)),
    ]


def tie(first, second):
    return lax.optimization_barrier((first, second))


def after(values, token):
    return lax.optimization_barrier((values, token))[0]


def add_up(pieces):
    total = pieces[0].astype(F32)
    for piece in pieces[1:]:
        total = total + piece.astype(F32)
    return total


def on_device(
    inputs,
    segments,
    attn_gain,
    attn_shift,
    mlp_gain,
    mlp_shift,
    qkv_weight,
    qkv_bias,
    out_weight,
    out_bias,
    up_weight,
    up_bias,
    down_weight,
    down_bias,
    cotangent,
):
    seq_count, block_len, width = inputs.shape
    tokens = seq_count * block_len
    inner = qkv_weight.shape[3]
    hidden = up_weight.shape[2]
    length = block_len * 8
    chunk = 256
    place = lax.axis_index("ctx")
    me = jnp.stack([place // 2, place % 2, lax.axis_index("tensor"), lax.axis_index("dp")]).astype(jnp.int32)
    x0 = inputs.reshape(tokens, width)
    dy1 = cotangent.reshape(tokens, width)
    tok_shape = inputs.shape
    wide = shape_of((tokens, width), BF16)
    norms = (attn_gain, attn_shift, mlp_gain, mlp_shift)
    biases = qkv_bias.transpose(1, 0, 2)

    def project_first(x):
        sources = [x, segments, *norms, qkv_weight, biases]
        held = [v.shape for v in sources[:6]] + [qkv_weight.shape[1:], biases.shape]
        piece = shape_of((2, block_len + 16, 3 * LANES), BF16)
        return run(
            functools.partial(project_first_body, tok_shape),
            me,
            [(v, pl.BlockSpec(memory_space=pltpu.HBM)) for v in sources],
            [shape_of((block_len, width), F32), wide, wide] + [piece] * 4,
            scratch=[pltpu.VMEM((tokens, 3 * inner), F32)]
            + [pltpu.VMEM(size, v.dtype) for size, v in zip(held, sources)]
            + [pltpu.SemaphoreType.DMA((11,))],
            name="norm_project",
            limit=62,
        )

    def project(layer, x, extra):
        piece = shape_of((2, block_len, 3 * LANES), BF16)
        return run(
            functools.partial(project_body, layer, tok_shape),
            me,
            [x, segments, *extra, *norms]
            + [(qkv_weight, layer_spec(qkv_weight, layer)), biases],
            [shape_of((tokens, width), F32), shape_of((block_len, width), F32), wide, wide] + [piece] * 4,
            scratch=[pltpu.VMEM((tokens, 3 * inner), F32)],
            name="norm_project",
            limit=24,
        )

    def feed(layer, m):
        return run(
            functools.partial(feed_body, layer),
            me,
            [m, (up_weight, layer_spec(up_weight, layer)), up_bias, (down_weight, layer_spec(down_weight, layer))],
            [shape_of((tokens, hidden), BF16), shape_of((tokens, hidden), F32), shape_of((tokens, width), F32)],
            name="feed", limit=24,
        )

    def feed_back(layer, r, slope):
        return run(
            feed_back_body,
            me,
            [r, slope, (up_weight, layer_spec(up_weight, layer)), (down_weight, layer_spec(down_weight, layer))],
            [shape_of((tokens, hidden), BF16), shape_of((tokens, width), F32), shape_of((1, hidden), F32)],
            name="feed_back", limit=24,
        )

    def feed_both(layer, m, dy):
        return run(
            functools.partial(feed_both_body, layer),
            me,
            [m, dy, (up_weight, layer_spec(up_weight, layer)), up_bias, (down_weight, layer_spec(down_weight, layer))],
            [shape_of((tokens, hidden), BF16), wide, shape_of((tokens, hidden), BF16)]
            + [shape_of((tokens, width), F32), shape_of((1, hidden), F32)],
            name="feed_both", limit=24,
        )

    def combine(layer, pieces, part, active=None):
        fused = part is None
        got = run(
            functools.partial(combine_body, block_len, fused),
            me,
            [*pieces, (out_weight, layer_spec(out_weight, layer))]
            + ([active, (down_weight, layer_spec(down_weight, layer))] if fused else [part]),
            [shape_of((tokens, inner), BF16)] + [shape_of((block_len, width), BF16)] * 4,
            scratch=[pltpu.VMEM((tokens, width), BF16)],
            name="combine", limit=20,
        )
        return got[0], got[1:]

    def add_all(values, dtype=BF16):
        out = shape_of(values[0].shape, dtype)
        return run(functools.partial(add_body, len(values)), me, values, [out], name="add_all", limit=16)[0]

    def line_up(axis, values, size):
        extra = values[0].shape[0] - size
        small = [shape_of((extra, width), BF16)] if extra else []
        outs = [shape_of((4 * size, width), BF16)] + small
        return run(functools.partial(line_up_body, axis), me, values, outs, name="line_up", limit=8)

    seq_bf16 = pltpu.VMEM((length, LANES), BF16)
    seq_f32 = pltpu.VMEM((length, LANES), F32)
    o_shapes = [shape_of((2, block_len, LANES), BF16)] * 4

    def attend_both(pieces, grads, seg_rows, with_out):
        return run(
            functools.partial(attend_both_body, block_len, chunk, with_out),
            me,
            [*pieces, *grads, seg_rows],
            [shape_of((2, block_len, (4 if with_out else 3) * LANES), BF16)] * 4,
            scratch=([pltpu.VMEM((3, length, LANES), BF16)] if with_out else [])
            + [seq_bf16, pltpu.VMEM((2, LANES, length), BF16), seq_bf16]
            + [seq_f32] * 3,
            name="attend_both", limit=24,
        )

    def project_back(layer, pieces, dm, riders=()):
        got = run(
            functools.partial(project_back_body, block_len, layer),
            me,
            [*pieces, (qkv_weight, layer_spec(qkv_weight, layer)), dm, attn_gain, mlp_gain, *riders],
            [shape_of((tokens, 3 * inner), BF16), wide, shape_of((3, inner), F32)]
            + [shape_of((block_len * (2 if riders else 1), width), BF16)] * 4,
            scratch=[pltpu.VMEM((tokens, width), BF16)],
            name="project_back", limit=24,
        )
        return got[0], got[1], got[2], got[3:]

    def norm_back(pieces, x, dy, riders=()):
        quarter = shape_of((block_len, width), F32)
        low = shape_of((block_len + (16 if riders else 0), width), BF16)
        return run(
            norm_back_body,
            me,
            [add_up(pieces), x, dy, *riders],
            [quarter, low, shape_of((1, width), F32)],
            name="norm_back",
            limit=10,
        )

    def gains(x, da, dm):
        return run(gains_body, me, [x, da, dm], [shape_of((4, width), F32)], name="gains", limit=16)[0]

    half = width // 2
    columns = [[8 * z + 2 * chip + core for z in range(4) for chip in range(4)] for core in range(2)]

    def feed_weights(m, dh, active, r):
        pack = shape_of((2 * half, width), BF16)
        return run(feed_weights_body, me, [m, dh, active, r], [pack] * 2, name="feed_weights", limit=24)

    def head_weights(attn_in, dproj, attended, r):
        pack = shape_of((half, width), BF16)
        return run(head_weights_body, me, [attn_in, dproj, attended, r], [pack] * 2, name="head_weights", limit=20)

    x0_quarter, a0, m0, *pieces = project_first(x0)
    fed0 = feed(0, m0)
    pieces0, (active0, slope0, part0) = over_chips(pieces, fed0)
    got = run(
        functools.partial(attend_body, block_len, chunk),
        me,
        pieces0,
        [shape_of((8, length), F32), shape_of((3, length, LANES), BF16)] + o_shapes,
        scratch=[pltpu.VMEM((LANES, length), BF16), seq_bf16],
        name="attend", limit=20,
    )
    seg_rows, qkv0 = got[:2]
    out0, _ = over_chips(got[2:])
    attended0, u0 = combine(0, out0, part0)
    dy1_quarter, *grads1 = run(
        functools.partial(send_grad_body, block_len),
        me,
        [after(dy1, u0[0]), (out_weight, layer_spec(out_weight, 1))],
        [shape_of((block_len, width), F32)] + o_shapes,
        name="out_back", limit=14,
    )
    u0, grads1 = tie(over_tensor(u0), over_x(grads1))
    u0 = share_tensor(add_up(u0).astype(BF16))
    u0, grads1_other = tie(u0, [swap_core(piece) for piece in grads1])

    x1, x1_quarter, a1, m1, *pieces = project(1, x0, [*u0, out_bias, down_bias])
    fed1 = feed_both(1, m1, dy1)
    pieces1, (active1, r1, dh1, dm1, up_b1) = over_chips(pieces, fed1)
    got = attend_both(pieces1, grads1 + grads1_other, seg_rows, True)
    feed_pack1 = feed_weights(after(m1, got[0]), dh1, active1, r1)
    back1, feed_pack1 = over_chips(got, feed_pack1)
    dproj1, da1, qkv_b1, e1 = project_back(1, back1, dm1)
    back1, (feed_keep, feed_send) = after((back1, feed_pack1), e1[0])
    attended1, u1 = combine(1, back1, None, active1)
    head_keep, head_send = head_weights(a1, dproj1, attended1, r1)
    e1, (u1, head_keep, head_send, feed_came) = tie(over_tensor(e1), (u1, head_keep, head_send, swap_core(feed_send)))
    pack1 = run(
        add_packs_body,
        me,
        [feed_keep, feed_came, head_keep, swap_core(head_send)],
        [shape_of((3 * half, width), BF16)],
        name="add_packs",
        limit=16,
    )[0]
    part1 = lax.psum_scatter(pack1, ("dp", "ctx"), axis_index_groups=columns, tiled=True)
    dx1, low1, bias1 = norm_back(e1, x1_quarter, dy1_quarter)
    gains1 = gains(after(x1, low1), da1, dm1)
    quarters, gains1 = tie(share_tensor(low1), gains1)

    r0, *grads0 = run(
        functools.partial(join_body, block_len),
        me,
        [*quarters, (out_weight, layer_spec(out_weight, 0))],
        [wide] + o_shapes,
        name="join_out_back", limit=14,
    )
    ua_keep, ua_send, ub_keep, ub_send = after(u1, r0)
    ua_came, ub_came = both_ways(ua_send, ub_send, "tensor")
    dh0, dm0, up_b0 = feed_back(0, r0, slope0)
    grads0, (ua_came, ub_came, dh0, dm0, up_b0) = over_chips(grads0, (ua_came, ub_came, dh0, dm0, up_b0))
    back0 = attend_both([qkv0], grads0, seg_rows, False)
    m0_late, u_parts = after((m0, [ua_keep, ua_came, ub_keep, ub_came]), back0[0])
    feed_pack0 = feed_weights(m0_late, dh0, active0, r0)
    u_part = shape_of((block_len // 2, width), BF16)
    ua_keep, ua_send, ub_keep, ub_send = run(
        halve_again_body, me, u_parts, [u_part] * 4, name="halve_again", limit=10
    )
    ub_came, ua_came = both_ways(ub_send, ua_send, "tensor")
    back0, (feed_keep, feed_send, u1) = over_chips(back0, (*feed_pack0, [ua_keep, ua_came, ub_keep, ub_came]))
    dproj0, da0, qkv_b0, e0 = project_back(0, back0, dm0)
    head_keep, head_send = head_weights(a0, dproj0, attended0, r0)
    e0 = after(e0, head_keep)
    way = shape_of((3 * half // 4, width), BF16)
    a_keep, a_send, b_keep, b_send = run(
        halve_body,
        me,
        [feed_keep, swap_core(feed_send), head_keep, swap_core(head_send)],
        [way] * 4,
        scratch=[pltpu.VMEM((2 * half, width), BF16), pltpu.VMEM((half, width), BF16)],
        name="halve",
        limit=20,
    )
    gains0 = gains(after(x0, a_send), da0, dm0)
    a_came, b_came = both_ways(a_send, b_send)
    e0, (gains0, a_came, b_came) = tie(over_tensor(e0), (gains0, a_came, b_came))
    dx0, low0, bias0 = norm_back(e0, x0_quarter, dx1, (gains0, gains1, bias1))
    last = share_tensor(low0)
    way = shape_of((3 * half // 8, width), BF16)
    a_keep, a_send, b_keep, b_send = run(
        halve_again_body, me, after([a_keep, a_came, b_keep, b_came], low0), [way] * 4, name="halve_again", limit=10
    )
    b_came, a_came = both_ways(b_send, a_send)
    part1 = after(part1, a_send)
    pack1 = lax.all_gather(part1, ("dp", "ctx"), axis_index_groups=columns, tiled=True)
    (a_came, b_came), last = tie((a_came, b_came), last)
    local = run(
        pack_small_body,
        me,
        [qkv_b0, qkv_b1, up_b0, up_b1],
        [shape_of((16, width), BF16)],
        name="pack_small",
        limit=8,
    )[0]

    few = half // 32
    cut = run(
        merge_body,
        me,
        [a_keep, a_came, b_keep, b_came],
        [shape_of((6 * few, width), BF16)] * 4,
        scratch=[pltpu.VMEM((24 * few, width), BF16)],
        name="merge",
        limit=10,
    )
    u1 = run(
        add_halves_body, me, after(u1, cut[0]), [shape_of((block_len, width), BF16)], name="add_halves", limit=8
    )[0]
    input_grad = run(
        functools.partial(place_grad_body, block_len),
        me,
        after(last, cut[0]),
        [shape_of((tokens, width), F32)],
        name="place_grad",
        limit=12,
    )[0]
    cut, (u1, input_grad) = tie(over_x(cut), (spread_near(u1, "tensor"), input_grad))
    pieces = [shape_of((3 * few + 32, width), BF16), shape_of((3 * few, width), BF16)]
    first, second = run(settle_body, me, [*cut, *last, local], pieces, name="settle", limit=10)
    u_far = lax.ppermute(after(u1[1], first), "tensor", WRAP_PAIR)
    first, (second, u_far) = tie(over_x([first] * 4), (over_dp([second] * 4), u_far))
    u1 = u1 + [u_far]
    small = [piece[3 * few :].astype(F32) for piece in first]
    small = ((small[0] + small[2]) + (small[1] + small[3])).astype(BF16)
    first = jnp.concatenate([piece[: 3 * few] for piece in first] + [small], axis=0)
    second = jnp.concatenate(second, axis=0)

    output = run(
        functools.partial(place_output_body, block_len),
        me,
        [*after(u1, first), x1, out_bias, down_bias],
        [shape_of((tokens, width), F32)],
        name="place_output",
        limit=16,
    )[0]
    heavy = [
        shape_of((2, width, hidden), F32),
        shape_of((2, hidden, width), F32),
        shape_of((2, 3, width, inner), F32),
        shape_of((2, inner, width), F32),
    ]
    pack1_came = swap_core(after(pack1, first))
    quarter = half // 4
    views = [(2, 2, half, width)] * 2 + [(2, 3, 2, half, inner), (2, 2, LANES, width)]
    first_outs = run(
        unpack_whole_body,
        me,
        [
            (pack, pl.BlockSpec((quarter, width), lambda i, *_, part=part: (4 * part + i, 0)))
            for pack in (pack1, pack1_came)
            for part in range(3)
        ],
        [shape_of(view, F32) for view in views],
        name="unpack_whole",
        limit=24,
        out_specs=[
            pl.BlockSpec((1, 2, quarter, width), lambda i, *_: (1, 0, i, 0)),
            pl.BlockSpec((1, 2, quarter, width), lambda i, *_: (1, 0, i, 0)),
            pl.BlockSpec((1, 3, 2, quarter, inner), lambda i, *_: (1, 0, 0, i, 0)),
            pl.BlockSpec((1, 2, LANES, 2 * LANES), lambda i, *_: (1, 0, 0, i)),
        ],
        grid=4,
    )
    first_outs = [v.reshape(like.shape) for v, like in zip(first_outs, heavy)]
    near = (spread_near(first, "dp"), spread_near(second, "x"))
    near, (first_outs, output) = tie(near, (first_outs, output))
    far = (spread_far(near[0], "dp"), spread_far(near[1], "x"))
    other = [swap_core(v) for v in near[0] + near[1]]
    mine, other = tie(far[0] + far[1], other)
    far = [swap_core(v) for v in mine[3:5] + mine[8:10]]
    other = other[0:3] + far[0:2] + other[3:6] + far[2:4]
    in_place = pl.BlockSpec(memory_space=pl.ANY)
    held = [pltpu.VMEM(v.shape[1:], F32) for v in heavy] + [pltpu.SemaphoreType.DMA((4,))]
    small_shapes = [shape_of((2, width), F32)] * 6 + [shape_of((3, 2, inner), F32), shape_of((2, width), F32)]
    up_grad, down_grad, qkv_grad, out_grad, *small = run(
        functools.partial(unpack_body, few),
        me,
        mine + other + [(v, in_place) for v in first_outs],
        heavy + small_shapes,
        name="unpack",
        limit=28,
        out_specs=[in_place] * 4 + [whole(v) for v in small_shapes],
        scratch=held,
        aliases={21 + index: index for index in range(4)},
    )
    return (
        output.reshape(tok_shape),
        input_grad.reshape(tok_shape),
        small[0],
        small[1],
        small[2],
        small[3],
        qkv_grad,
        small[6].transpose(1, 0, 2),
        out_grad,
        small[4],
        up_grad,
        small[5],
        down_grad,
        small[7],
    )


def solution(mesh):
    in_specs = (
        P("dp", "ctx", None),
        P("dp", "ctx"),
        P(),
        P(),
        P(),
        P(),
        P(None, None, None, "tensor"),
        P(None, None, "tensor"),
        P(None, "tensor", None),
        P(),
        P(None, None, "tensor"),
        P(None, "tensor"),
        P(None, "tensor", None),
        P(),
        P("dp", "ctx", None),
    )
    out_specs = (
        P("dp", "ctx", None),
        P("dp", "ctx", None),
        P(),
        P(),
        P(),
        P(),
        P(None, None, None, "tensor"),
        P(None, None, "tensor"),
        P(None, "tensor", None),
        P(),
        P(None, None, "tensor"),
        P(None, "tensor"),
        P(None, "tensor", None),
        P(),
    )
    return jax.shard_map(
        on_device, mesh=mesh, in_specs=in_specs, out_specs=out_specs, check_vma=False
    )
```
